32 devices in a mesh: dp: 8 (over y, x, core), tensor: 4 (over z).
Axes of the slice: x: 2, y: 2, z: 4, core: 2. Of those that a mesh axis runs over, the one named last changes fastest.
Arguments:
- states: float32 [4096, 2048], P('dp'), may hold values from -6 to 6
- w_query: bfloat16 [2048, 2048], P(None, 'tensor'), may hold values from -0.125 to 0.125
- w_key: bfloat16 [2048, 2048], P(None, 'tensor'), may hold values from -0.125 to 0.125
- w_value: bfloat16 [2048, 2048], P(None, 'tensor'), may hold values from -0.125 to 0.125
- w_out: bfloat16 [2048, 2048], P('tensor'), may hold values from -6 to 6
- w_gate: bfloat16 [2048, 8192], P(None, 'tensor'), may hold values from -0.125 to 0.125
- w_up: bfloat16 [2048, 8192], P(None, 'tensor'), may hold values from -0.125 to 0.125
- w_down: bfloat16 [8192, 2048], P('tensor'), may hold values from -0.0625 to 0.0625
- group_id: int32 [8], replicated, may hold values from 0 to 1, as said below
- slice_start: int32 [8], replicated, may hold values from 0 to 1152, as said below
- cont_group: int32 [8], P('dp'), may hold values from 0 to 1
- cotangent: float32 [4096, 2048], P('dp'), may hold values from -6 to 6
Outputs:
- layer_out: float32 [4096, 2048], P('dp')
- input_grad: float32 [4096, 2048], P('dp')
- grad_query: float32 [2048, 2048], P('dp', 'tensor')
- grad_key: float32 [2048, 2048], P('dp', 'tensor')
- grad_value: float32 [2048, 2048], P('dp', 'tensor')
- grad_out: float32 [2048, 2048], P('tensor', 'dp')
- grad_gate: float32 [2048, 8192], P('dp', 'tensor')
- grad_up: float32 [2048, 8192], P('dp', 'tensor')
- grad_down: float32 [8192, 2048], P('tensor', 'dp')
The draws below stay inside these ranges and needn't reach their ends.
Inputs may be any that keep to these rules, and one draw needn't show every extreme that they name: `group_id`: exactly half of the 8 members have each group. `slice_start`: the members of one group have the starts 0, 384, 768, and so on, each once.
All inputs are finite; a program needn't handle non-finite values.
Results may differ from the reference program's by a relative error of at most 0.02.
Values may be sent and summed in bfloat16 or wider, within the bound.
A program may use at most 384 MiB of HBM per device.

```python
import jax
import jax.numpy as jnp
from jax import lax

D = 2048
HEADS = 16
HEAD = 128
FF = 8192
PROMPT_DEV = 384
ROWS = 512
TOKENS = 4096
PROMPT = 1536
N_DP = 8


def member_order(key):
    return jax.random.permutation(key, N_DP).astype(jnp.int32)


def draw_group_id(key, part):
    order = member_order(key)
    return (order % 2).astype(jnp.int32)


def draw_slice_start(key, part):
    order = member_order(key)
    return (order // 2 * PROMPT_DEV).astype(jnp.int32)


def touch_ends(result, rng, low, high):
    index_at = [jax.random.randint(jax.random.fold_in(rng, axis), (), 0, length) for axis, length in enumerate(result.shape)]
    widest = result.shape.index(max(result.shape))
    next_to = index_at[:widest] + [(index_at[widest] + 1) % result.shape[widest]] + index_at[widest + 1:]
    return result.at[tuple(index_at)].set(low).at[tuple(next_to)].set(high)


def raised(values, key, source, target, shards_of, factor):
    owner, partner = [(jnp.arange(values.shape[position]) // (values.shape[position] // shards_of)).reshape([-1 if axis == position else 1 for axis in range(values.ndim)]) for position in (source, target)]
    chosen = jax.random.permutation(key, shards_of)[partner]
    strong = (owner == chosen) | (owner == (partner + shards_of // 2) % shards_of)
    return jnp.where(strong, factor * values, values)


def steps_of(own_key, dims, shards, low, high):
    level = 1.0
    for axis_at, shards_of in shards:
        draws = jax.random.uniform(jax.random.fold_in(jax.random.fold_in(own_key, 6), axis_at), (shards_of,), jnp.float32, low / len(shards), high / len(shards))
        level = level * jnp.repeat(jnp.exp(draws), dims[axis_at] // shards_of).reshape((-1,) + (1,) * (len(dims) - 1 - axis_at))
    return level


def scatter_about(own_key, shape, width, limit, pieces=(), held_as=jnp.bfloat16):
    entries = jax.random.normal(own_key, shape, jnp.float32) * width
    if len(pieces) > 0:
        entries = steps_of(own_key, shape, pieces, -0.22, 0.18) * entries
    return jnp.clip(entries, min=-limit, max=limit).astype(held_as)


def gaussian_with(key, dims, scale, most, shards, heavy, kind=jnp.bfloat16):
    entries = scale * jax.random.normal(key, dims, jnp.float32)
    if shards:
        entries = entries * steps_of(key, dims, shards, -0.22, 0.18)
    return jnp.clip(raised(entries, jax.random.fold_in(key, 3), *heavy), -most, most).astype(kind)


def setup_inputs(seed: int = 0) -> dict:
    seeds = jax.random.split(jax.random.key(seed), 13)
    return {
        "states": scatter_about(seeds[0], (TOKENS, D), 1.0, 6.0, ((0, 8),), jnp.float32),
        "w_query": scatter_about(seeds[1], (D, D), D ** -0.5, 0.125, ((1, 4),)),
        "w_key": scatter_about(seeds[2], (D, D), D ** -0.5, 0.125, ((1, 4),)),
        "w_value": scatter_about(seeds[3], (D, D), D ** -0.5, 0.125, ((1, 4),)),
        "w_out": scatter_about(seeds[4], (D, D), (PROMPT_DEV ** 0.5 * D ** -0.5), 6.0, ((0, 4),)),
        "w_gate": scatter_about(seeds[5], (D, FF), D ** -0.5, 0.125, ((1, 4),)),
        "w_up": scatter_about(seeds[6], (D, FF), D ** -0.5, 0.125, ((1, 4),)),
        "w_down": scatter_about(seeds[7], (FF, D), FF ** -0.5, 0.0625, ((0, 4),)),
        "group_id": draw_group_id(jax.random.fold_in(seeds[12], 71), 0),
        "slice_start": draw_slice_start(jax.random.fold_in(seeds[12], 71), 0),
        "cont_group": touch_ends(jax.random.randint(seeds[10], (N_DP,), 0, 2), jax.random.fold_in(seeds[10], 1), 0, 1).astype(jnp.int32),
        "cotangent": gaussian_with(seeds[11], (TOKENS, D), 1.0, 6.0, ((0, 8),), (0, 1, 8, 2.0), jnp.float32),
    }


@jax.custom_vjp
def low(v):
    return lax.optimization_barrier(v.astype(jnp.bfloat16)).astype(jnp.float32)

@jax.custom_vjp
def low_back(v):
    return v

def low_keep(v):
    return (low(v), None)

def low_pass(kept, grad):
    return (grad,)

def back_keep(v):
    return (v, None)

def back_low(kept, grad):
    return (low(grad),)
low.defvjp(low_keep, low_pass)
low_back.defvjp(back_keep, back_low)
EPSILON = 1e-05
NEGATIVE = -1e+30
HIGHEST = lax.Precision.HIGHEST

def norm_rows(values):
    row_mean = lax.optimization_barrier(jnp.mean(values, axis=-1, keepdims=True))
    centred = values - row_mean
    inverse = lax.rsqrt(lax.optimization_barrier(jnp.mean(centred * centred, axis=-1, keepdims=True)) + EPSILON)
    return centred * inverse

def rotary(values, positions):
    full_width = values.shape[-1]
    half_width = full_width // 2
    frequency = 10000.0 ** (-jnp.arange(half_width, dtype=jnp.float32) * 2.0 / full_width)
    angles = positions.astype(jnp.float32)[:, None] * frequency[None, :]
    cosine = jnp.cos(angles)[:, None, :]
    sine_part = jnp.sin(angles)[:, None, :]
    first_half = values[..., :half_width]
    second_half = values[..., half_width:]
    return jnp.concatenate([first_half * cosine - second_half * sine_part, second_half * cosine + first_half * sine_part], axis=-1)

def product(left_side, right_side):
    return jnp.dot(left_side, right_side, precision=HIGHEST, preferred_element_type=jnp.float32)

def reference(states, w_query, w_key, w_value, w_out, w_gate, w_up, w_down, group_id, slice_start, cont_group, cotangent):
    row_index = jnp.arange(TOKENS, dtype=jnp.int32)
    owner = (row_index // ROWS).astype(jnp.int32)
    offset = (row_index % ROWS).astype(jnp.int32)
    is_prompt = offset < PROMPT_DEV
    positions = jnp.where(is_prompt, slice_start[owner] + offset, PROMPT + offset - PROMPT_DEV).astype(jnp.int32)
    query_tag = jnp.where(is_prompt, group_id[owner], cont_group[owner]).astype(jnp.int32)
    key_tag = jnp.where(is_prompt, group_id[owner], 2 + owner).astype(jnp.int32)

    def forward(states_in, query_w, key_w, value_w, out_w, gate_w, up_w, down_w):
        act_one = low(norm_rows(states_in))
        query_lin = low_back(product(act_one, query_w))
        queries = low(rotary(query_lin.reshape(TOKENS, HEADS, HEAD), positions))
        key_lin = low_back(product(act_one, key_w))
        keys = low(rotary(key_lin.reshape(TOKENS, HEADS, HEAD), positions))
        values = low(low_back(product(act_one, value_w))).reshape(TOKENS, HEADS, HEAD)

        def block(operands):
            block_queries, block_tag, block_pos, block_owner = operands
            scores = jnp.einsum('qhd,khd->hqk', block_queries, keys, precision=HIGHEST) * HEAD ** (-0.5)
            scores = low_back(scores)
            allowed = (positions[None, :] <= block_pos[:, None]) & ((key_tag[None, :] == block_tag[:, None]) | (key_tag[None, :] == 2 + block_owner))
            scores = jnp.where(allowed[None], scores, NEGATIVE)
            row_max = lax.optimization_barrier(jnp.max(scores, axis=-1, keepdims=True))
            weights = jnp.exp(scores - row_max)
            probabilities = low(weights / lax.optimization_barrier(jnp.sum(weights, axis=-1, keepdims=True)))
            return jnp.einsum('hqk,khd->qhd', probabilities, values, precision=HIGHEST)
        stacked = lax.map(jax.checkpoint(block), (queries.reshape(N_DP, ROWS, HEADS, HEAD), query_tag.reshape(N_DP, ROWS), positions.reshape(N_DP, ROWS), jnp.arange(N_DP, dtype=jnp.int32)))
        mixed = low(low_back(stacked.reshape(TOKENS, D)))
        resid = states_in + low_back(product(mixed, out_w))
        act_two = low(norm_rows(resid))
        gate_proj = low_back(product(act_two, gate_w))
        up_proj = low_back(product(act_two, up_w))
        hidden = low(jax.nn.silu(gate_proj) * up_proj)
        return resid + low_back(product(hidden, down_w))
    weights_all = jax.tree.map(lambda matrix: matrix.astype(jnp.float32), (w_query, w_key, w_value, w_out, w_gate, w_up, w_down))
    layer_out, pull = jax.vjp(forward, states, *weights_all)
    grads = pull(cotangent)
    return (layer_out, grads[0], grads[1], grads[2], grads[3], grads[4], grads[5], grads[6], grads[7])
```

```python
import functools

import jax
import jax.numpy as jnp
from jax import lax
from jax.experimental import pallas as pl
from jax.experimental.pallas import tpu as pltpu
from jax.sharding import PartitionSpec as P

HEAD = 128
PROMPT_DEV = 384
EPSILON = 1e-05
NEGATIVE = -1e30
SCALE = HEAD ** (-0.5)
LOW = jnp.bfloat16
WIDE = jnp.float32
MESH = pl.DeviceIdType.MESH
ANY = pl.BlockSpec(memory_space=pl.ANY)
VMEM = pl.BlockSpec(memory_space=pltpu.VMEM)
DMA = pltpu.SemaphoreType.DMA
VMEM_LIMIT = 60 * 2**20


def dot(left, right, left_dim=1, right_dim=0):
    return lax.dot_general(
        left, right, (((left_dim,), (right_dim,)), ((), ())), preferred_element_type=WIDE
    )


def shape(dims, dtype):
    return jax.ShapeDtypeStruct(dims, dtype)


def norm_rows(values):
    row_mean = jnp.mean(values, axis=-1, keepdims=True)
    centred = values - row_mean
    inverse = lax.rsqrt(jnp.mean(centred * centred, axis=-1, keepdims=True) + EPSILON)
    return centred * inverse, inverse


def norm_back(gradient, normed, inverse):
    return inverse * (
        gradient
        - jnp.mean(gradient, axis=-1, keepdims=True)
        - normed * jnp.mean(gradient * normed, axis=-1, keepdims=True)
    )


def rotate(values, cosine, sine):
    return values * cosine + pltpu.roll(values, HEAD // 2, 1) * sine


def flip(index, mask):
    out, bit = index, 1
    while bit <= mask:
        if mask & bit:
            out = out + bit * (1 - 2 * lax.rem(lax.div(index, bit), 2))
        bit *= 2
    return out


def bits_of(count):
    return list(range(count.bit_length() - 1))


def greet(peers):
    barrier = pltpu.get_barrier_semaphore()
    for peer in peers:
        pl.semaphore_signal(barrier, inc=1, device_id=peer, device_id_type=MESH)
    pl.semaphore_wait(barrier, len(peers))


def remote(source, target, send_sem, recv_sem, device):
    return pltpu.make_async_remote_copy(
        src_ref=source,
        dst_ref=target,
        send_sem=send_sem,
        recv_sem=recv_sem,
        device_id=device,
        device_id_type=MESH,
    )


class Line:
    scratch_count = 10

    @staticmethod
    def scratch(count, rows, width):
        return [
            pltpu.VMEM((rows, width), WIDE),
            pltpu.VMEM((count, rows, width), LOW),
            pltpu.VMEM((count, rows, width), LOW),
            pltpu.VMEM((count, rows, width), LOW),
            DMA((count,)),
            DMA((count,)),
            DMA((count,)),
            DMA((count,)),
            DMA((count,)),
            DMA((count,)),
        ]

    def __init__(self, count, refs):
        self.count = count
        (
            self.total,
            self.outgoing,
            self.from_left,
            self.from_right,
            self.out_sem,
            self.left_sem,
            self.right_sem,
            self.to_right_sem,
            self.to_left_sem,
            self.got_sem,
        ) = refs
        self.rows = self.total.shape[0]
        self.here = lax.axis_index("tensor")
        member = lax.axis_index("dp")
        self.right = (member, lax.rem(self.here + 1, count))
        self.left = (member, lax.rem(self.here + count - 1, count))

    def peers(self):
        return [self.left, self.right]

    def rightward(self, chunk):
        return remote(
            self.outgoing.at[chunk],
            self.from_left.at[chunk],
            self.out_sem.at[chunk],
            self.left_sem.at[chunk],
            self.right,
        )

    def leftward(self, chunk):
        return remote(
            self.outgoing.at[chunk],
            self.from_right.at[chunk],
            self.out_sem.at[chunk],
            self.right_sem.at[chunk],
            self.left,
        )

    def scatter_slot(self, slot, part):
        here, count = self.here, self.count

        @pl.when(here <= slot)
        def _():
            chunk = count - 1 + here - slot
            self.total[...] = part(chunk)

            @pl.when(here > 0)
            def _():
                self.rightward(chunk).wait_recv()
                self.total[...] += self.from_left[chunk].astype(WIDE)

            self.outgoing[chunk] = self.total[...].astype(LOW)
            self.rightward(chunk).start()

        @pl.when(count - 1 - here <= slot)
        def _():
            chunk = slot - (count - 1 - here)
            self.total[...] = part(chunk)

            @pl.when(here < count - 1)
            def _():
                self.leftward(chunk).wait_recv()
                self.total[...] += self.from_right[chunk].astype(WIDE)

            self.outgoing[chunk] = self.total[...].astype(LOW)
            self.leftward(chunk).start()

    def scatter_end(self, part):
        here = self.here
        self.total[...] = part(here)

        @pl.when(here > 0)
        def _():
            self.rightward(here).wait_recv()
            self.total[...] += self.from_left[here].astype(WIDE)

        @pl.when(here < self.count - 1)
        def _():
            self.leftward(here).wait_recv()
            self.total[...] += self.from_right[here].astype(WIDE)

    def piece(self, whole, chunk):
        return whole.at[pl.ds(pl.multiple_of(chunk * self.rows, self.rows), self.rows)]

    def passing(self, whole, chunk, right):
        ref = self.piece(whole, chunk)
        return remote(
            ref,
            ref,
            (self.to_right_sem if right else self.to_left_sem).at[chunk],
            self.got_sem.at[chunk],
            self.right if right else self.left,
        )

    def gather_slot(self, whole, distance):
        here, count = self.here, self.count

        @pl.when(here - distance >= 0)
        def _():
            if distance:
                self.passing(whole, here - distance, True).wait_recv()

            @pl.when(here < count - 1)
            def _():
                self.passing(whole, here - distance, True).start()

        @pl.when(here + distance <= count - 1)
        def _():
            if distance:
                self.passing(whole, here + distance, False).wait_recv()

            @pl.when(here > 0)
            def _():
                self.passing(whole, here + distance, False).start()

    def finish(self, whole):
        here, count = self.here, self.count
        for chunk in range(count):

            @pl.when(here != chunk)
            def _(chunk=chunk):
                self.rightward(chunk).wait_send()

            @pl.when((chunk <= here) & (here < count - 1))
            def _(chunk=chunk):
                self.passing(whole, chunk, True).wait_send()

            @pl.when((chunk >= here) & (here > 0))
            def _(chunk=chunk):
                self.passing(whole, chunk, False).wait_send()


class Halving:
    def __init__(self, pairs, order, send, recv, send_sem, recv_sem):
        self.pairs, self.order = pairs, order
        self.send, self.recv = send, recv
        self.send_sem, self.recv_sem = send_sem, recv_sem
        self.member = lax.axis_index("dp")
        self.tensor = lax.axis_index("tensor")
        self.high = lax.div(self.member, 2)

    def stage(self, mask):
        for position, bit in enumerate(self.order):
            if mask >> bit & 1:
                return position
        return len(self.order)

    def sends(self):
        masks = range(1, self.pairs)
        return sorted(masks, key=lambda mask: (self.stage(mask), -mask.bit_count()))

    def copy(self, mask):
        bit = 1 << self.order[self.stage(mask)]
        return remote(
            self.send.at[mask - 1],
            self.recv.at[mask - 1],
            self.send_sem.at[mask - 1],
            self.recv_sem.at[mask - 1],
            (flip(self.member, bit * 2), self.tensor),
        )

    def arrived(self, mask):
        slots = [mask | 1 << bit for bit in self.order[: self.stage(mask)]]
        for slot in slots:
            self.copy(slot).wait_recv()
        return [slot - 1 for slot in slots]

    def target(self, mask):
        return flip(self.high, mask)

    def push(self, mask, own):
        slots = self.arrived(mask)
        own(self.target(mask), slots, self.recv, self.send.at[mask - 1])
        self.copy(mask).start()

    def end(self, own, out):
        own(self.target(0), self.arrived(0), self.recv, out)

    def finish(self):
        for mask in range(1, self.pairs):
            self.copy(mask).wait_send()


class Weight:
    @staticmethod
    def scratch(pairs, rows, block, width, parts):
        return [
            pltpu.VMEM((pairs, 2 * rows, block), LOW),
            pltpu.VMEM((2 * rows, width), LOW),
            pltpu.VMEM((pairs - 1, block, width), LOW),
            pltpu.VMEM((pairs - 1, block, width), LOW),
            DMA((pairs - 1,)),
            DMA((pairs - 1,)),
            DMA((pairs + parts,)),
            DMA((pairs + parts,)),
            DMA((pairs + parts,)),
        ]

    scratch_count = 9

    def __init__(self, pairs, order, left, rights, refs):
        (
            self.lhs,
            self.rhs,
            send,
            recv,
            send_sem,
            recv_sem,
            self.local_sem,
            self.core_send,
            self.core_recv,
        ) = refs
        self.left, self.rights = left, rights
        self.pairs = pairs
        self.rows = self.lhs.shape[1] // 2
        self.block = self.lhs.shape[2]
        self.width = self.rhs.shape[1]
        self.halving = Halving(pairs, order, send, recv, send_sem, recv_sem)
        member = self.halving.member
        self.parity = lax.rem(member, 2)
        self.partner = (flip(member, 1), self.halving.tensor)

    def copies(self):
        out = []
        rows, block = self.rows, self.block

        def columns_of(index):
            if len(self.left.shape) == 3:
                return self.left.at[index]
            return self.left.at[:, pl.ds(pl.multiple_of(index * block, block), block)]

        for pair in range(self.pairs):
            out.append(
                (
                    columns_of(2 * pair + self.parity),
                    self.lhs.at[pair, pl.ds(0, rows)],
                    columns_of(2 * pair + 1 - self.parity),
                    self.lhs.at[pair, pl.ds(rows, rows)],
                )
            )
        at = 0
        for right in self.rights:
            columns = pl.ds(at, right.shape[1])
            at += right.shape[1]
            out.append(
                (
                    right,
                    self.rhs.at[pl.ds(0, rows), columns],
                    right,
                    self.rhs.at[pl.ds(rows, rows), columns],
                )
            )
        local = [
            pltpu.make_async_copy(a, b, self.local_sem.at[i]) for i, (a, b, _, _) in enumerate(out)
        ]
        across = [
            remote(a, b, self.core_send.at[i], self.core_recv.at[i], self.partner)
            for i, (_, _, a, b) in enumerate(out)
        ]
        return local, across

    def start(self):
        local, across = self.copies()
        for copy in across + local:
            copy.start()

    def ready(self):
        local, across = self.copies()
        for copy in local:
            copy.wait()
        for copy in across:
            copy.wait_recv()

    def own(self, target, slots, recv, out):
        tile = 512
        for start in range(0, self.width, tile):
            columns = pl.ds(start, tile)
            total = dot(self.lhs[target], self.rhs[:, columns], 0, 0)
            for slot in slots:
                total += recv[slot, :, columns].astype(WIDE)
            out[:, columns] = total.astype(LOW)

    def push(self, mask):
        self.halving.push(mask, self.own)

    def end(self, out):
        self.halving.end(self.own, out)

    def finish(self):
        self.halving.finish()
        for copy in self.copies()[1]:
            copy.wait_send()


def in_blocks(left, members):
    block = left.shape[1] // members
    if block % 128 == 0:
        return left
    return left.reshape(left.shape[0], members, block).transpose(1, 0, 2)


def member_peers(members):
    member, tensor = lax.axis_index("dp"), lax.axis_index("tensor")
    return [(flip(member, 1 << bit), tensor) for bit in bits_of(members)]


def project_kernel(
    members,
    states,
    w_query,
    w_key,
    w_value,
    cosine,
    sine,
    cotangent,
    act,
    query,
    key,
    value,
    out_low,
    keys_all,
    values_all,
    send_sem,
    recv_sem,
    local_sem,
):
    member, tensor = lax.axis_index("dp"), lax.axis_index("tensor")
    width = query.shape[1]
    greet(member_peers(members))
    rows = 64
    for start in range(0, states.shape[0], rows):
        span = pl.ds(start, rows)
        act[span] = norm_rows(states[span])[0].astype(LOW)

    def turned(weight, out):
        linear = dot(act[...], weight[...])
        for start in range(0, width, HEAD):
            out[:, start : start + HEAD] = rotate(
                linear[:, start : start + HEAD], cosine[...], sine[...]
            ).astype(LOW)

    high = [bit for bit in bits_of(members) if bit]
    orders = (high + [0], high[::-1] + [0])
    owns, alls = (key, value), (keys_all, values_all)

    def copy(flow, mask, bit):
        slot = mask | 1 << bit
        place = alls[flow].at[flip(member, mask)]
        return remote(
            place if mask else owns[flow].at[pl.ds(0, PROMPT_DEV)],
            place,
            send_sem.at[flow, slot],
            recv_sem.at[flow, slot],
            (flip(member, 1 << bit), tensor),
        )

    def forward(flow, mask):
        order = orders[flow]
        last = max([order.index(bit) for bit in order if mask >> bit & 1], default=-1)
        for bit in order[last + 1 :]:
            copy(flow, mask, bit).start()

    def came_by(flow, mask):
        order = orders[flow]
        bit = order[max(order.index(bit) for bit in order if mask >> bit & 1)]
        return copy(flow, mask ^ 1 << bit, bit)

    def keep(flow):
        return pltpu.make_async_copy(
            owns[flow].at[pl.ds(0, PROMPT_DEV)], alls[flow].at[member], local_sem.at[flow]
        )

    turned(w_key, key)
    forward(0, 0)
    value[...] = dot(act[...], w_value[...]).astype(LOW)
    forward(1, 0)
    keep(0).start()
    keep(1).start()
    turned(w_query, query)
    for start in range(0, states.shape[0], rows):
        span = pl.ds(start, rows)
        out_low[span] = cotangent[span].astype(LOW)
    masks = range(1, members)
    inner = sorted([mask for mask in masks if not mask & 1], key=lambda mask: mask.bit_count())
    for mask in inner:
        for flow in (0, 1):
            turn = flow if not mask & 2 else flow
            came_by(turn, mask).wait_recv()
            forward(turn, mask)
    for mask in masks:
        if mask & 1:
            for flow in (0, 1):
                came_by(flow, mask).wait_recv()
    for flow in (0, 1):
        keep(flow).wait()
        for mask in masks:
            came_by(flow, mask).wait_send()


def project(members, states, w_query, w_key, w_value, cosine, sine, cotangent):
    rows, depth = states.shape
    width = w_query.shape[1]
    return pl.pallas_call(
        functools.partial(project_kernel, members),
        out_shape=[
            shape((rows, depth), LOW),
            shape((rows, width), LOW),
            shape((rows, width), LOW),
            shape((rows, width), LOW),
            shape((rows, depth), LOW),
            shape((members, PROMPT_DEV, width), LOW),
            shape((members, PROMPT_DEV, width), LOW),
        ],
        in_specs=[VMEM] * 7,
        out_specs=[VMEM] * 5 + [ANY] * 2,
        scratch_shapes=[DMA((2, members)), DMA((2, members)), DMA((2,))],
        compiler_params=pltpu.CompilerParams(
            collective_id=1, has_side_effects=True, vmem_limit_bytes=VMEM_LIMIT
        ),
        name="project",
    )(states, w_query, w_key, w_value, cosine, sine, cotangent)


def attend_kernel(
    half, plan, query, key, value, keys_all, values_all, mixed, attended, log_total
):
    def part(start, count, steps, offset):
        span = pl.ds(start, count)
        queries = query[span]
        allowed = lax.broadcasted_iota(jnp.int32, (count, count), 0) >= lax.broadcasted_iota(
            jnp.int32, (count, count), 1
        )
        scores = jnp.where(allowed, dot(queries, key[span], 1, 1) * SCALE, NEGATIVE)
        top = jnp.max(scores, axis=-1, keepdims=True)
        weights = jnp.exp(scores - top)
        total = jnp.sum(weights, axis=-1, keepdims=True)
        result = dot(weights.astype(LOW), value[span])

        def step(index, carry):
            top, total, result = carry
            place = plan[offset + index]
            scores = dot(queries, keys_all[place], 1, 1) * SCALE
            higher = jnp.maximum(top, jnp.max(scores, axis=-1, keepdims=True))
            fade = jnp.exp(top - higher)
            weights = jnp.exp(scores - higher)
            total = total * fade + jnp.sum(weights, axis=-1, keepdims=True)
            result = result * fade + dot(weights.astype(LOW), values_all[place])
            return higher, total, result

        top, total, result = lax.fori_loop(0, steps, step, (top, total, result))
        result = result / total
        mixed[span] = result.astype(LOW)
        attended[span] = result
        log_total[span] = jnp.broadcast_to(top + jnp.log(total), (count, HEAD))

    part(0, PROMPT_DEV, plan[0], 1)
    part(PROMPT_DEV, query.shape[0] - PROMPT_DEV, half, 1 + half)


def attend(plan, query, key, value, keys_all, values_all):
    rows, width = query.shape
    members = keys_all.shape[0]
    head = pl.BlockSpec((rows, HEAD), lambda h, _: (0, h))
    every = pl.BlockSpec((members, PROMPT_DEV, HEAD), lambda h, _: (0, 0, h))
    return pl.pallas_call(
        functools.partial(attend_kernel, members // 2),
        out_shape=[
            shape((rows, width), LOW),
            shape((rows, width), WIDE),
            shape((rows, width), WIDE),
        ],
        grid_spec=pltpu.PrefetchScalarGridSpec(
            num_scalar_prefetch=1,
            grid=(width // HEAD,),
            in_specs=[head, head, head, every, every],
            out_specs=[head, head, head],
        ),
        compiler_params=pltpu.CompilerParams(vmem_limit_bytes=VMEM_LIMIT),
        name="attend",
    )(plan, query, key, value, keys_all, values_all)


def attend_back_kernel(
    half,
    plan,
    query,
    key,
    value,
    keys_all,
    values_all,
    branch_low,
    w_out,
    attended,
    log_total,
    cosine,
    sine,
    d_query,
    d_keys_all,
    d_values_all,
    d_key_own,
    d_value_own,
    d_mixed,
    key_total,
    value_total,
):
    d_mixed[...] = dot(branch_low[...], w_out[...], 1, 1).astype(LOW)
    key_total[...] = jnp.zeros_like(key_total)
    value_total[...] = jnp.zeros_like(value_total)

    def part(start, count, steps, offset):
        span = pl.ds(start, count)
        queries, d_attended = query[span], d_mixed[span]
        log_sum = log_total[span][:, :1]
        center = jnp.sum(d_attended.astype(WIDE) * attended[span], axis=-1, keepdims=True)

        def back(scores, keys, values):
            probabilities = jnp.exp(scores - log_sum)
            d_scores = (probabilities * (dot(d_attended, values, 1, 1) - center)).astype(LOW)
            return (
                dot(d_scores, keys),
                dot(d_scores, queries, 0, 0),
                dot(probabilities.astype(LOW), d_attended, 0, 0),
            )

        allowed = lax.broadcasted_iota(jnp.int32, (count, count), 0) >= lax.broadcasted_iota(
            jnp.int32, (count, count), 1
        )
        scores = jnp.where(allowed, dot(queries, key[span], 1, 1) * SCALE, NEGATIVE)
        d_queries, d_own_keys, d_own_values = back(scores, key[span], value[span])

        def step(index, d_queries):
            place = plan[offset + index]
            keys, values = keys_all[place], values_all[place]
            more, d_keys, d_values = back(dot(queries, keys, 1, 1) * SCALE, keys, values)
            key_total[place] += d_keys
            value_total[place] += d_values
            return d_queries + more

        d_queries = lax.fori_loop(0, steps, step, d_queries) * SCALE
        d_query[span] = rotate(d_queries, cosine[span], -sine[span]).astype(LOW)
        return d_own_keys, d_own_values

    member = plan[1 + 2 * half]
    d_own_keys, d_own_values = part(0, PROMPT_DEV, plan[0], 1)
    key_total[member] += d_own_keys
    value_total[member] += d_own_values
    d_own_keys, d_own_values = part(PROMPT_DEV, query.shape[0] - PROMPT_DEV, half, 1 + half)
    late = pl.ds(PROMPT_DEV, query.shape[0] - PROMPT_DEV)
    d_key_own[...] = rotate(d_own_keys * SCALE, cosine[late], -sine[late]).astype(LOW)
    d_value_own[...] = d_own_values.astype(LOW)
    d_keys_all[...] = (key_total[...] * SCALE).astype(LOW)
    d_values_all[...] = value_total[...].astype(LOW)


def attend_back(
    plan, query, key, value, keys_all, values_all, branch_low, w_out, attended, log_total, cosine, sine
):
    rows, width = query.shape
    members = keys_all.shape[0]
    depth = branch_low.shape[1]
    late = rows - PROMPT_DEV
    head = pl.BlockSpec((rows, HEAD), lambda h, _: (0, h))
    every = pl.BlockSpec((members, PROMPT_DEV, HEAD), lambda h, _: (0, 0, h))
    own = pl.BlockSpec((late, HEAD), lambda h, _: (0, h))
    table = pl.BlockSpec((rows, HEAD), lambda h, _: (0, 0))
    return pl.pallas_call(
        functools.partial(attend_back_kernel, members // 2),
        out_shape=[
            shape((rows, width), LOW),
            shape((members, PROMPT_DEV, width), LOW),
            shape((members, PROMPT_DEV, width), LOW),
            shape((late, width), LOW),
            shape((late, width), LOW),
        ],
        grid_spec=pltpu.PrefetchScalarGridSpec(
            num_scalar_prefetch=1,
            grid=(width // HEAD,),
            in_specs=[
                head,
                head,
                head,
                every,
                every,
                pl.BlockSpec((rows, depth), lambda h, _: (0, 0)),
                pl.BlockSpec((HEAD, depth), lambda h, _: (h, 0)),
                head,
                head,
                table,
                table,
            ],
            out_specs=[head, every, every, own, own],
            scratch_shapes=[
                pltpu.VMEM((rows, HEAD), LOW),
                pltpu.VMEM((members, PROMPT_DEV, HEAD), WIDE),
                pltpu.VMEM((members, PROMPT_DEV, HEAD), WIDE),
            ],
        ),
        compiler_params=pltpu.CompilerParams(vmem_limit_bytes=VMEM_LIMIT),
        name="attend_back",
    )(
        plan, query, key, value, keys_all, values_all, branch_low, w_out, attended, log_total, cosine, sine
    )


def branch_kernel(count, mixed, w_out, states, act, resid, state_sem, *line_refs):
    line = Line(count, line_refs)
    rows = line.rows
    chunk_rows = pl.ds(pl.multiple_of(line.here * rows, rows), rows)
    fetch = pltpu.make_async_copy(states.at[chunk_rows], resid, state_sem)
    fetch.start()
    greet(line.peers())

    def part(chunk):
        return dot(mixed[pl.ds(pl.multiple_of(chunk * rows, rows), rows)], w_out[...])

    for slot in range(count - 1):
        line.scatter_slot(slot, part)
    line.scatter_end(part)
    fetch.wait()
    resid[...] += line.total[...]
    act[chunk_rows] = norm_rows(resid[...])[0].astype(LOW)
    for distance in range(count):
        line.gather_slot(act, distance)
    line.finish(act)


def branch(count, mixed, w_out, states):
    rows, depth = states.shape
    return pl.pallas_call(
        functools.partial(branch_kernel, count),
        out_shape=[shape((rows, depth), LOW), shape((rows // count, depth), WIDE)],
        in_specs=[VMEM, VMEM, ANY],
        out_specs=[VMEM, VMEM],
        scratch_shapes=[DMA] + Line.scratch(count, rows // count, depth),
        compiler_params=pltpu.CompilerParams(
            collective_id=2, has_side_effects=True, vmem_limit_bytes=VMEM_LIMIT
        ),
        name="branch",
    )(mixed, w_out, states)


def feed_kernel(
    act, out_low, w_gate, w_up, w_down, ffn, d_act, hidden, d_gate, d_up, ffn_total, d_total
):
    step = pl.program_id(0)
    gate = dot(act[...], w_gate[...])
    up = dot(act[...], w_up[...])
    d_hidden = dot(out_low[...], w_down[...], 1, 1)
    sigmoid = jax.nn.sigmoid(gate)
    swish = gate * sigmoid
    hidden[...] = (swish * up).astype(LOW)
    d_gate[...] = (d_hidden * up * sigmoid * (1.0 + gate * (1.0 - sigmoid))).astype(LOW)
    d_up[...] = (d_hidden * swish).astype(LOW)
    more = dot(hidden[...], w_down[...])
    d_more = dot(d_gate[...], w_gate[...], 1, 1) + dot(d_up[...], w_up[...], 1, 1)

    @pl.when(step == 0)
    def _():
        ffn_total[...] = more
        d_total[...] = d_more

    @pl.when(step > 0)
    def _():
        ffn_total[...] += more
        d_total[...] += d_more

    @pl.when(step == pl.num_programs(0) - 1)
    def _():
        ffn[...] = ffn_total[...].astype(LOW)
        d_act[...] = d_total[...].astype(LOW)


def feed(act, out_low, w_gate, w_up, w_down):
    rows, depth = act.shape
    units = w_gate.shape[1]
    tile = 512
    whole = pl.BlockSpec((rows, depth), lambda i: (0, 0))
    across = pl.BlockSpec((depth, tile), lambda i: (0, i))
    down = pl.BlockSpec((tile, depth), lambda i: (i, 0))
    inner = pl.BlockSpec((rows, tile), lambda i: (0, i))
    return pl.pallas_call(
        feed_kernel,
        out_shape=[shape((rows, depth), LOW)] * 2 + [shape((rows, units), LOW)] * 3,
        grid=(units // tile,),
        in_specs=[whole, whole, across, across, down],
        out_specs=[whole, whole, inner, inner, inner],
        scratch_shapes=[pltpu.VMEM((rows, depth), WIDE)] * 2,
        compiler_params=pltpu.CompilerParams(vmem_limit_bytes=VMEM_LIMIT),
        name="feed",
    )(act, out_low, w_gate, w_up, w_down)


def second_kernel(
    count,
    pairs,
    d_act,
    resid,
    cotangent,
    act,
    d_gate,
    d_up,
    branch_low,
    grad_resid,
    grad_gate,
    grad_up,
    cot_sem,
    *refs,
):
    line = Line(count, refs[: Line.scratch_count])
    refs = refs[Line.scratch_count :]
    order = bits_of(pairs)
    flows = [
        Weight(pairs, order, act, [d_gate], refs[: Weight.scratch_count]),
        Weight(pairs, order[::-1], act, [d_up], refs[Weight.scratch_count :]),
    ]
    rows = line.rows
    chunk_rows = pl.ds(pl.multiple_of(line.here * rows, rows), rows)
    fetch = pltpu.make_async_copy(cotangent.at[chunk_rows], grad_resid, cot_sem)
    fetch.start()
    greet(line.peers() + member_peers(2 * pairs))

    def part(chunk):
        return d_act[pl.ds(pl.multiple_of(chunk * rows, rows), rows)].astype(WIDE)

    for flow in flows:
        flow.start()
    line.scatter_slot(0, part)
    for flow in flows:
        flow.ready()
        flow.push(flow.halving.sends()[0])
    sends = max(1, len(flows[0].halving.sends()))
    first = [mask for mask in flows[0].halving.sends() if flows[0].halving.stage(mask) == 0]
    for index in range(1, len(first)):
        for flow in flows:
            flow.push(flow.halving.sends()[index])
    for slot in range(1, count - 1):
        line.scatter_slot(slot, part)
    line.scatter_end(part)
    fetch.wait()
    normed, inverse = norm_rows(resid[...])
    grad_resid[...] += norm_back(line.total[...], normed, inverse)
    branch_low[chunk_rows] = grad_resid[...].astype(LOW)
    line.gather_slot(branch_low, 0)
    for index in range(len(first), sends):
        for flow in flows:
            flow.push(flow.halving.sends()[index])
    for distance in range(1, count):
        line.gather_slot(branch_low, distance)
    flows[0].end(grad_gate)
    flows[1].end(grad_up)
    for flow in flows:
        flow.finish()
    line.finish(branch_low)


def second(count, members, d_act, resid, cotangent, act, d_gate, d_up):
    rows, depth = cotangent.shape
    units = d_gate.shape[1]
    pairs = members // 2
    block = depth // members
    return pl.pallas_call(
        functools.partial(second_kernel, count, pairs),
        out_shape=[
            shape((rows, depth), LOW),
            shape((rows // count, depth), WIDE),
            shape((block, units), LOW),
            shape((block, units), LOW),
        ],
        in_specs=[VMEM, VMEM, ANY, ANY, ANY, ANY],
        out_specs=[VMEM] * 4,
        scratch_shapes=[DMA]
        + Line.scratch(count, rows // count, depth)
        + Weight.scratch(pairs, rows, block, units, 1)
        + Weight.scratch(pairs, rows, block, units, 1),
        compiler_params=pltpu.CompilerParams(
            collective_id=3, has_side_effects=True, vmem_limit_bytes=VMEM_LIMIT
        ),
        name="second",
    )(d_act, resid, cotangent, in_blocks(act, members), d_gate, d_up)


def owner_kernel(
    pairs,
    d_keys_all,
    d_values_all,
    d_key_own,
    d_value_own,
    cosine,
    sine,
    d_key,
    d_value,
    *refs,
):
    member, tensor = lax.axis_index("dp"), lax.axis_index("tensor")
    parity = lax.rem(member, 2)
    partner = (flip(member, 1), tensor)
    order = bits_of(pairs)
    width = d_key.shape[1]
    flows = []
    for index, source in enumerate((d_keys_all, d_values_all)):
        mine, theirs, send, recv, send_sem, recv_sem, local_sem, core_send, core_recv = refs[
            9 * index : 9 * index + 9
        ]
        halving = Halving(pairs, order[::-1] if index else order, send, recv, send_sem, recv_sem)
        local = [
            pltpu.make_async_copy(source.at[2 * pair + parity], mine.at[pair], local_sem.at[pair])
            for pair in range(pairs)
        ]
        across = [
            remote(
                source.at[2 * pair + 1 - parity],
                theirs.at[pair],
                core_send.at[pair],
                core_recv.at[pair],
                partner,
            )
            for pair in range(pairs)
        ]

        def own(target, slots, recv, out, mine=mine, theirs=theirs):
            total = mine[target].astype(WIDE) + theirs[target].astype(WIDE)
            for slot in slots:
                total += recv[slot].astype(WIDE)
            out[...] = total.astype(out.dtype)

        flows.append((halving, local, across, own))
    greet(member_peers(2 * pairs))
    for _, local, across, _ in flows:
        for copy in across + local:
            copy.start()
    for halving, local, across, own in flows:
        for copy in local:
            copy.wait()
        for copy in across:
            copy.wait_recv()
        halving.push(halving.sends()[0], own)
    late = pl.ds(PROMPT_DEV, d_key.shape[0] - PROMPT_DEV)
    d_key[late] = d_key_own[...]
    d_value[late] = d_value_own[...]
    for index in range(1, pairs - 1):
        for halving, _, _, own in flows:
            halving.push(halving.sends()[index], own)
    early = pl.ds(0, PROMPT_DEV)
    total = refs[18]
    flows[0][0].end(flows[0][3], total)
    for start in range(0, width, HEAD):
        d_key[early, start : start + HEAD] = rotate(
            total[:, start : start + HEAD], cosine[early], -sine[early]
        ).astype(LOW)
    flows[1][0].end(flows[1][3], d_value.at[early])
    for halving, _, across, _ in flows:
        halving.finish()
        for copy in across:
            copy.wait_send()


def owner(members, d_keys_all, d_values_all, d_key_own, d_value_own, cosine, sine):
    width = d_key_own.shape[1]
    rows = cosine.shape[0]
    pairs = members // 2
    flow = [
        pltpu.VMEM((pairs, PROMPT_DEV, width), LOW),
        pltpu.VMEM((pairs, PROMPT_DEV, width), LOW),
        pltpu.VMEM((pairs - 1, PROMPT_DEV, width), LOW),
        pltpu.VMEM((pairs - 1, PROMPT_DEV, width), LOW),
        DMA((pairs - 1,)),
        DMA((pairs - 1,)),
        DMA((pairs,)),
        DMA((pairs,)),
        DMA((pairs,)),
    ]
    return pl.pallas_call(
        functools.partial(owner_kernel, pairs),
        out_shape=[shape((rows, width), LOW)] * 2,
        in_specs=[ANY, ANY] + [VMEM] * 4,
        out_specs=[VMEM] * 2,
        scratch_shapes=flow + flow + [pltpu.VMEM((PROMPT_DEV, width), WIDE)],
        compiler_params=pltpu.CompilerParams(
            collective_id=4, has_side_effects=True, vmem_limit_bytes=VMEM_LIMIT
        ),
        name="owner",
    )(d_keys_all, d_values_all, d_key_own, d_value_own, cosine, sine)


def first_kernel(
    count,
    pairs,
    d_query,
    d_key,
    d_value,
    w_query,
    w_key,
    w_value,
    grad_resid,
    states,
    act,
    mixed,
    branch_low,
    hidden,
    out_low,
    far_query,
    far_key,
    far_value,
    input_grad,
    grad_down,
    grad_out,
    grad_inner,
    state,
    state_sem,
    *refs,
):
    line = Line(count, refs[: Line.scratch_count])
    refs = refs[Line.scratch_count :]
    step = Weight.scratch_count
    order = bits_of(pairs)
    flows = [
        Weight(pairs, order, out_low, [hidden], refs[:step]),
        Weight(pairs, order[::-1], branch_low, [mixed], refs[step : 2 * step]),
        Weight(pairs, order[::-1], act, [far_query, far_key, far_value], refs[2 * step :]),
    ]
    rows = line.rows
    chunk_rows = pl.ds(pl.multiple_of(line.here * rows, rows), rows)
    fetch = pltpu.make_async_copy(states.at[chunk_rows], state, state_sem)
    fetch.start()
    greet(line.peers() + member_peers(2 * pairs))

    def part(chunk):
        span = pl.ds(pl.multiple_of(chunk * rows, rows), rows)
        return (
            dot(d_query[span], w_query[...], 1, 1)
            + dot(d_key[span], w_key[...], 1, 1)
            + dot(d_value[span], w_value[...], 1, 1)
        )

    for flow in flows:
        flow.start()
    line.scatter_slot(0, part)
    for flow in flows:
        flow.ready()
        flow.push(flow.halving.sends()[0])
    sends = len(flows[0].halving.sends())
    early = [mask for mask in flows[0].halving.sends() if flows[0].halving.stage(mask) == 0]
    for index in range(1, len(early)):
        for flow in flows:
            flow.push(flow.halving.sends()[index])
    for slot in range(1, count - 1):
        line.scatter_slot(slot, part)
    line.scatter_end(part)
    fetch.wait()
    normed, inverse = norm_rows(state[...])
    input_grad[chunk_rows] = (
        grad_resid[...] + norm_back(line.total[...], normed, inverse)
    ).astype(LOW)
    line.gather_slot(input_grad, 0)
    for index in range(len(early), sends):
        for flow in flows:
            flow.push(flow.halving.sends()[index])
    for distance in range(1, count):
        line.gather_slot(input_grad, distance)
    for flow, out in zip(flows, (grad_down, grad_out, grad_inner)):
        flow.end(out)
    for flow in flows:
        flow.finish()
    line.finish(input_grad)


def first(
    count,
    members,
    d_query,
    d_key,
    d_value,
    w_query,
    w_key,
    w_value,
    grad_resid,
    states,
    act,
    mixed,
    branch_low,
    hidden,
    out_low,
):
    rows, depth = states.shape
    width, units = d_query.shape[1], hidden.shape[1]
    pairs = members // 2
    block = depth // members
    return pl.pallas_call(
        functools.partial(first_kernel, count, pairs),
        out_shape=[
            shape((rows, depth), LOW),
            shape((block, units), LOW),
            shape((block, width), LOW),
            shape((block, 3 * width), LOW),
        ],
        in_specs=[VMEM] * 7 + [ANY] * 9,
        out_specs=[VMEM] * 4,
        scratch_shapes=[pltpu.VMEM((rows // count, depth), WIDE), DMA]
        + Line.scratch(count, rows // count, depth)
        + Weight.scratch(pairs, rows, block, units, 1)
        + Weight.scratch(pairs, rows, block, width, 1)
        + Weight.scratch(pairs, rows, block, 3 * width, 3),
        compiler_params=pltpu.CompilerParams(
            collective_id=5, has_side_effects=True, vmem_limit_bytes=VMEM_LIMIT
        ),
        name="first",
    )(
        d_query,
        d_key,
        d_value,
        w_query,
        w_key,
        w_value,
        grad_resid,
        states,
        in_blocks(act, members),
        mixed,
        in_blocks(branch_low, members),
        hidden,
        in_blocks(out_low, members),
        d_query,
        d_key,
        d_value,
    )


def body(
    states,
    w_query,
    w_key,
    w_value,
    w_out,
    w_gate,
    w_up,
    w_down,
    group_id,
    slice_start,
    cont_group,
    cotangent,
):
    rows = states.shape[0]
    members = lax.axis_size("dp")
    count = lax.axis_size("tensor")
    member = lax.axis_index("dp")
    half = members // 2
    index = jnp.arange(rows, dtype=jnp.int32)
    own_group = lax.dynamic_index_in_dim(group_id, member, 0, keepdims=False)
    own_start = lax.dynamic_index_in_dim(slice_start, member, 0, keepdims=False)
    positions = jnp.where(
        index < PROMPT_DEV, own_start + index, half * PROMPT_DEV + index - PROMPT_DEV
    )
    frequency = 10000.0 ** (-jnp.arange(HEAD // 2, dtype=WIDE) * 2.0 / HEAD)
    angles = positions.astype(WIDE)[:, None] * frequency[None, :]
    cosine = jnp.concatenate([jnp.cos(angles)] * 2, axis=1)
    sine = jnp.sin(angles)
    sine = jnp.concatenate([-sine, sine], axis=1)
    everyone = jnp.arange(members, dtype=jnp.int32)
    starts = jnp.arange(half, dtype=jnp.int32) * PROMPT_DEV

    def in_order(group):
        found = (group_id[None, :] == group) & (slice_start[None, :] == starts[:, None])
        return jnp.sum(jnp.where(found, everyone[None, :], 0), axis=1)

    plan = jnp.concatenate(
        [
            (own_start // PROMPT_DEV)[None],
            in_order(own_group),
            in_order(cont_group[0]),
            member[None],
        ]
    ).astype(jnp.int32)

    act_one, query, key, value, out_low, keys_all, values_all = project(
        members, states, w_query, w_key, w_value, cosine, sine, cotangent
    )
    mixed, attended, log_total = attend(plan, query, key, value, keys_all, values_all)
    act_two, resid = branch(count, mixed, w_out, states)
    ffn, d_act_two, hidden, d_gate, d_up = feed(act_two, out_low, w_gate, w_up, w_down)
    branch_low, grad_resid, grad_gate, grad_up = second(
        count, members, d_act_two, resid, cotangent, act_two, d_gate, d_up
    )
    ffn, branch_low = lax.optimization_barrier((ffn, branch_low))
    ffn = lax.psum_scatter(ffn, "tensor", scatter_dimension=0, tiled=True)
    d_query, d_keys_all, d_values_all, d_key_own, d_value_own = attend_back(
        plan, query, key, value, keys_all, values_all, branch_low, w_out, attended, log_total, cosine, sine
    )
    d_key, d_value = owner(
        members, d_keys_all, d_values_all, d_key_own, d_value_own, cosine, sine
    )
    ffn, d_key = lax.optimization_barrier((ffn, d_key))
    own_out = (resid + ffn.astype(WIDE)).astype(LOW)
    layer_out = lax.all_gather(own_out, "tensor", axis=0, tiled=True).astype(WIDE)
    input_grad, grad_down, grad_out, grad_inner = first(
        count,
        members,
        d_query,
        d_key,
        d_value,
        w_query,
        w_key,
        w_value,
        grad_resid,
        states,
        act_one,
        mixed,
        branch_low,
        hidden,
        out_low,
    )
    width = d_query.shape[1]
    return (
        layer_out,
        input_grad.astype(WIDE),
        grad_inner[:, :width].astype(WIDE),
        grad_inner[:, width : 2 * width].astype(WIDE),
        grad_inner[:, 2 * width :].astype(WIDE),
        grad_out.astype(WIDE).T,
        grad_gate.astype(WIDE),
        grad_up.astype(WIDE),
        grad_down.astype(WIDE).T,
    )


def solution(mesh):
    placed = (
        P("dp", None),
        P(None, "tensor"),
        P(None, "tensor"),
        P(None, "tensor"),
        P("tensor", None),
        P(None, "tensor"),
        P(None, "tensor"),
        P("tensor", None),
        P(),
        P(),
        P("dp"),
        P("dp", None),
    )
    return jax.shard_map(
        body,
        mesh=mesh,
        in_specs=placed,
        out_specs=(
            P("dp", None),
            P("dp", None),
            P("dp", "tensor"),
            P("dp", "tensor"),
            P("dp", "tensor"),
            P("tensor", "dp"),
            P("dp", "tensor"),
            P("dp", "tensor"),
            P("tensor", "dp"),
        ),
        check_vma=False,
    )
```

```python
import functools

import jax
import jax.numpy as jnp
import numpy as np
from jax import lax
from jax.experimental import pallas as pl
from jax.experimental.pallas import tpu as pltpu
from jax.sharding import PartitionSpec as P

HEAD = 128
PROMPT_DEV = 384
EPSILON = 1e-05
NEGATIVE = -1e30
SCALE = HEAD ** (-0.5)
LOW = jnp.bfloat16
WIDE = jnp.float32
MESH = pl.DeviceIdType.MESH
ANY = pl.BlockSpec(memory_space=pl.ANY)
VMEM = pl.BlockSpec(memory_space=pltpu.VMEM)
DMA = pltpu.SemaphoreType.DMA
VMEM_LIMIT = 60 * 2**20
GROUPS = 2
PIECE = 512


def dot(left, right, left_dim=1, right_dim=0):
    return lax.dot_general(
        left, right, (((left_dim,), (right_dim,)), ((), ())), preferred_element_type=WIDE
    )


def shape(dims, dtype):
    return jax.ShapeDtypeStruct(dims, dtype)


def norm_rows(values):
    row_mean = jnp.mean(values, axis=-1, keepdims=True)
    centred = values - row_mean
    inverse = lax.rsqrt(jnp.mean(centred * centred, axis=-1, keepdims=True) + EPSILON)
    return centred * inverse, inverse


def norm_back(gradient, normed, inverse):
    return inverse * (
        gradient
        - jnp.mean(gradient, axis=-1, keepdims=True)
        - normed * jnp.mean(gradient * normed, axis=-1, keepdims=True)
    )


def rotate(values, cosine, sine):
    return values * cosine + pltpu.roll(values, HEAD // 2, 1) * sine


def flip(index, mask):
    out, bit = index, 1
    while bit <= mask:
        if mask & bit:
            out = out + bit * (1 - 2 * lax.rem(lax.div(index, bit), 2))
        bit *= 2
    return out


def bits_of(count):
    return list(range(count.bit_length() - 1))


def greet(peers):
    barrier = pltpu.get_barrier_semaphore()
    for peer in peers:
        pl.semaphore_signal(barrier, inc=1, device_id=peer, device_id_type=MESH)
    pl.semaphore_wait(barrier, len(peers))


def remote(source, target, send_sem, recv_sem, device):
    return pltpu.make_async_remote_copy(
        src_ref=source,
        dst_ref=target,
        send_sem=send_sem,
        recv_sem=recv_sem,
        device_id=device,
        device_id_type=MESH,
    )


class Line:
    scratch_count = 10

    @staticmethod
    def scratch(count, groups, rows, width):
        rows = rows // groups
        return [
            pltpu.VMEM((rows, width), WIDE),
            pltpu.VMEM((groups, count, rows, width), LOW),
            pltpu.VMEM((groups, count, rows, width), LOW),
            pltpu.VMEM((groups, count, rows, width), LOW),
            DMA((groups, count)),
            DMA((groups, count)),
            DMA((groups, count)),
            DMA((groups, count)),
            DMA((groups, count)),
            DMA((groups, count)),
        ]

    def __init__(self, count, refs):
        self.count = count
        (
            self.total,
            self.outgoing,
            self.from_left,
            self.from_right,
            self.out_sem,
            self.left_sem,
            self.right_sem,
            self.to_right_sem,
            self.to_left_sem,
            self.got_sem,
        ) = refs
        self.groups = self.outgoing.shape[0]
        self.rows = self.total.shape[0]
        self.here = lax.axis_index("tensor")
        member = lax.axis_index("dp")
        self.right = (member, lax.rem(self.here + 1, count))
        self.left = (member, lax.rem(self.here + count - 1, count))

    def peers(self):
        return [self.left, self.right]

    def span(self, group, chunk):
        start = chunk * (self.rows * self.groups) + group * self.rows
        return pl.ds(pl.multiple_of(start, self.rows), self.rows)

    def rightward(self, group, chunk):
        return remote(
            self.outgoing.at[group, chunk],
            self.from_left.at[group, chunk],
            self.out_sem.at[group, chunk],
            self.left_sem.at[group, chunk],
            self.right,
        )

    def leftward(self, group, chunk):
        return remote(
            self.outgoing.at[group, chunk],
            self.from_right.at[group, chunk],
            self.out_sem.at[group, chunk],
            self.right_sem.at[group, chunk],
            self.left,
        )

    def scatter_slot(self, group, slot, part):
        here, count = self.here, self.count

        @pl.when(here <= slot)
        def _():
            chunk = count - 1 + here - slot
            self.total[...] = part[self.span(group, chunk)].astype(WIDE)

            @pl.when(here > 0)
            def _():
                self.rightward(group, chunk).wait_recv()
                self.total[...] += self.from_left[group, chunk].astype(WIDE)

            self.outgoing[group, chunk] = self.total[...].astype(LOW)
            self.rightward(group, chunk).start()

        @pl.when(count - 1 - here <= slot)
        def _():
            chunk = slot - (count - 1 - here)
            self.total[...] = part[self.span(group, chunk)].astype(WIDE)

            @pl.when(here < count - 1)
            def _():
                self.leftward(group, chunk).wait_recv()
                self.total[...] += self.from_right[group, chunk].astype(WIDE)

            self.outgoing[group, chunk] = self.total[...].astype(LOW)
            self.leftward(group, chunk).start()

    def scatter_end(self, group, part):
        here = self.here
        self.total[...] = part[self.span(group, here)].astype(WIDE)

        @pl.when(here > 0)
        def _():
            self.rightward(group, here).wait_recv()
            self.total[...] += self.from_left[group, here].astype(WIDE)

        @pl.when(here < self.count - 1)
        def _():
            self.leftward(group, here).wait_recv()
            self.total[...] += self.from_right[group, here].astype(WIDE)

    def passing(self, whole, group, chunk, right):
        ref = whole.at[self.span(group, chunk)]
        return remote(
            ref,
            ref,
            (self.to_right_sem if right else self.to_left_sem).at[group, chunk],
            self.got_sem.at[group, chunk],
            self.right if right else self.left,
        )

    def gather_slot(self, whole, group, distance):
        here, count = self.here, self.count

        @pl.when(here - distance >= 0)
        def _():
            if distance:
                self.passing(whole, group, here - distance, True).wait_recv()

            @pl.when(here < count - 1)
            def _():
                self.passing(whole, group, here - distance, True).start()

        @pl.when(here + distance <= count - 1)
        def _():
            if distance:
                self.passing(whole, group, here + distance, False).wait_recv()

            @pl.when(here > 0)
            def _():
                self.passing(whole, group, here + distance, False).start()

    def reduce(self, part, whole, finish, beside=()):
        beside = list(beside)
        last = self.count - 1
        self.scatter_slot(0, 0, part)
        for group in range(self.groups):
            for slot in range(1, last):
                if beside:
                    beside.pop(0)()
                self.scatter_slot(group, slot, part)
                if group:
                    self.gather_slot(whole, group - 1, slot)
            if group + 1 < self.groups:
                self.scatter_slot(group + 1, 0, part)
            if group:
                self.gather_slot(whole, group - 1, last)
            self.scatter_end(group, part)
            finish(group)
            self.gather_slot(whole, group, 0)
        for distance in range(1, self.count):
            if beside:
                beside.pop(0)()
            self.gather_slot(whole, self.groups - 1, distance)
        for act in beside:
            act()

    def sent(self, whole=None):
        here, count = self.here, self.count
        for group in range(self.groups):
            for chunk in range(count):

                @pl.when(here != chunk)
                def _(group=group, chunk=chunk):
                    self.rightward(group, chunk).wait_send()

                if whole is None:
                    continue

                @pl.when((chunk <= here) & (here < count - 1))
                def _(group=group, chunk=chunk):
                    self.passing(whole, group, chunk, True).wait_send()

                @pl.when((chunk >= here) & (here > 0))
                def _(group=group, chunk=chunk):
                    self.passing(whole, group, chunk, False).wait_send()


class Halving:
    @staticmethod
    def masks_of(pairs, order):
        def stage(mask):
            return min(order.index(bit) for bit in order if mask >> bit & 1)

        return sorted(range(1, pairs), key=lambda mask: (stage(mask), -mask.bit_count()))

    @staticmethod
    def scratch(pairs, block, width):
        count = pairs - 1
        pieces = max(1, width // PIECE)
        return [
            pltpu.VMEM((count, block, width), LOW),
            pltpu.VMEM((count, block, width), LOW),
            DMA((count, pieces)),
            DMA((count, pieces)),
        ]

    def __init__(self, pairs, order, own, refs, kept=None):
        self.order, self.own, self.kept = order, own, kept
        self.send, self.recv, self.send_sem, self.recv_sem = refs
        self.masks = Halving.masks_of(pairs, order)
        self.pieces = self.send_sem.shape[1]
        self.piece = self.send.shape[2] // self.pieces
        self.member = lax.axis_index("dp")
        self.tensor = lax.axis_index("tensor")
        self.high = lax.div(self.member, 2)

    def stage(self, mask):
        return min(
            [self.order.index(bit) for bit in self.order if mask >> bit & 1],
            default=len(self.order),
        )

    def steps(self, stage):
        return [mask for mask in self.masks if self.stage(mask) == stage]

    def columns(self, piece):
        return pl.ds(piece * self.piece, self.piece)

    def copy(self, mask, piece):
        index = self.masks.index(mask)
        bit = 1 << self.order[self.stage(mask)]
        return remote(
            self.send.at[index, :, self.columns(piece)],
            self.recv.at[index, :, self.columns(piece)],
            self.send_sem.at[index, piece],
            self.recv_sem.at[index, piece],
            (flip(self.member, bit * 2), self.tensor),
        )

    def settle(self):
        for piece in range(self.pieces):
            columns = self.columns(piece)
            self.kept[:, columns] = self.own(0, flip(self.high, 0), columns)

    def fill(self, mask, piece, out):
        columns = self.columns(piece)
        if self.kept is not None and not mask:
            total = self.kept[:, columns]
        else:
            total = self.own(mask, flip(self.high, mask), columns)
        for bit in self.order[: self.stage(mask)]:
            slot = mask | 1 << bit
            self.copy(slot, piece).wait_recv()
            total += self.recv[self.masks.index(slot), :, columns].astype(WIDE)
        out[:, columns] = total.astype(out.dtype)

    def push(self, mask, ready=None):
        for piece in range(self.pieces):
            if ready is not None:
                ready(piece)
            self.fill(mask, piece, self.send.at[self.masks.index(mask)])
            self.copy(mask, piece).start()

    def end(self, out):
        for piece in range(self.pieces):
            self.fill(0, piece, out)

    def sent(self):
        for mask in self.masks:
            for piece in range(self.pieces):
                self.copy(mask, piece).wait_send()


class Pairwise:
    def __init__(self, moves, refs):
        self.moves = moves
        self.local_sem, self.send_sem, self.recv_sem = refs
        member = lax.axis_index("dp")
        self.partner = (flip(member, 1), lax.axis_index("tensor"))

    @staticmethod
    def sems(count):
        return [DMA((count,)), DMA((count,)), DMA((count,))]

    def local(self, index):
        source, target, _, _ = self.moves[index]
        return pltpu.make_async_copy(source, target, self.local_sem.at[index])

    def across(self, index):
        _, _, source, target = self.moves[index]
        return remote(
            source, target, self.send_sem.at[index], self.recv_sem.at[index], self.partner
        )

    def start(self, index=None):
        for index in range(len(self.moves)) if index is None else [index]:
            self.across(index).start()
            self.local(index).start()

    def ready(self, index=None):
        for index in range(len(self.moves)) if index is None else [index]:
            self.local(index).wait()
            self.across(index).wait_recv()

    def sent(self):
        for index in range(len(self.moves)):
            self.across(index).wait_send()


class Lhs(Pairwise):
    @staticmethod
    def scratch(pairs, rows, block):
        return [pltpu.VMEM((pairs, 2 * rows, block), LOW)] + Pairwise.sems(pairs)

    def __init__(self, source, refs):
        self.held = refs[0]
        pairs, rows, block = self.held.shape
        rows = rows // 2
        parity = lax.rem(lax.axis_index("dp"), 2)

        def columns(index):
            if len(source.shape) == 3:
                return source.at[index]
            return source.at[:, pl.ds(pl.multiple_of(index * block, block), block)]

        super().__init__(
            [
                (
                    columns(2 * pair + parity),
                    self.held.at[pair, pl.ds(0, rows)],
                    columns(2 * pair + 1 - parity),
                    self.held.at[pair, pl.ds(rows, rows)],
                )
                for pair in range(pairs)
            ],
            refs[1:],
        )


class Rhs(Pairwise):
    @staticmethod
    def scratch(rows, width):
        return [pltpu.VMEM((2 * rows, width), LOW)] + Pairwise.sems(width // PIECE)

    def __init__(self, sources, refs):
        self.held = refs[0]
        rows = self.held.shape[0] // 2
        moves, at = [], 0
        for source in sources:
            for start in range(0, source.shape[1], PIECE):
                columns = pl.ds(at, PIECE)
                at += PIECE
                here = source.at[:, pl.ds(start, PIECE)]
                moves.append(
                    (
                        here,
                        self.held.at[pl.ds(0, rows), columns],
                        here,
                        self.held.at[pl.ds(rows, rows), columns],
                    )
                )
        super().__init__(moves, refs[1:])


def product_of(lhs, rhs):
    def own(mask, target, columns):
        return dot(lhs.held[target], rhs.held[:, columns], 0, 0)

    return own


def taker(refs):
    refs = list(refs)

    def take(count):
        out = refs[:count]
        del refs[:count]
        return out

    return take


def in_blocks(left, members):
    block = left.shape[1] // members
    if block % 128 == 0:
        return left
    return left.reshape(left.shape[0], members, block).transpose(1, 0, 2)


def member_peers(members):
    member, tensor = lax.axis_index("dp"), lax.axis_index("tensor")
    return [(flip(member, 1 << bit), tensor) for bit in bits_of(members)]


def project_kernel(
    members,
    states,
    w_query,
    w_key,
    w_value,
    cosine,
    sine,
    cotangent,
    act,
    query,
    key,
    value,
    out_low,
    keys_all,
    values_all,
    send_sem,
    recv_sem,
    local_sem,
):
    member, tensor = lax.axis_index("dp"), lax.axis_index("tensor")
    width = query.shape[1]
    greet(member_peers(members))
    rows = 64
    for start in range(0, states.shape[0], rows):
        span = pl.ds(start, rows)
        act[span] = norm_rows(states[span])[0].astype(LOW)

    def turned(weight, out):
        linear = dot(act[...], weight[...])
        for start in range(0, width, HEAD):
            out[:, start : start + HEAD] = rotate(
                linear[:, start : start + HEAD], cosine[...], sine[...]
            ).astype(LOW)

    high = [bit for bit in bits_of(members) if bit]
    orders = (high + [0], high[::-1] + [0])
    owns, alls = (key, value), (keys_all, values_all)

    def copy(flow, mask, bit):
        slot = mask | 1 << bit
        place = alls[flow].at[flip(member, mask)]
        return remote(
            place if mask else owns[flow].at[pl.ds(0, PROMPT_DEV)],
            place,
            send_sem.at[flow, slot],
            recv_sem.at[flow, slot],
            (flip(member, 1 << bit), tensor),
        )

    def forward(flow, mask):
        order = orders[flow]
        last = max([order.index(bit) for bit in order if mask >> bit & 1], default=-1)
        for bit in order[last + 1 :]:
            copy(flow, mask, bit).start()

    def came_by(flow, mask):
        order = orders[flow]
        bit = order[max(order.index(bit) for bit in order if mask >> bit & 1)]
        return copy(flow, mask ^ 1 << bit, bit)

    def keep(flow):
        return pltpu.make_async_copy(
            owns[flow].at[pl.ds(0, PROMPT_DEV)], alls[flow].at[member], local_sem.at[flow]
        )

    turned(w_key, key)
    forward(0, 0)
    value[...] = dot(act[...], w_value[...]).astype(LOW)
    forward(1, 0)
    keep(0).start()
    keep(1).start()
    turned(w_query, query)
    for start in range(0, states.shape[0], rows):
        span = pl.ds(start, rows)
        out_low[span] = cotangent[span].astype(LOW)
    masks = range(1, members)
    inner = sorted([mask for mask in masks if not mask & 1], key=lambda mask: mask.bit_count())
    for mask in inner:
        for flow in (0, 1):
            turn = flow if not mask & 2 else flow
            came_by(turn, mask).wait_recv()
            forward(turn, mask)
    for mask in masks:
        if mask & 1:
            for flow in (0, 1):
                came_by(flow, mask).wait_recv()
    for flow in (0, 1):
        keep(flow).wait()
        for mask in masks:
            came_by(flow, mask).wait_send()


def project(members, states, w_query, w_key, w_value, cosine, sine, cotangent):
    rows, depth = states.shape
    width = w_query.shape[1]
    return pl.pallas_call(
        functools.partial(project_kernel, members),
        out_shape=[
            shape((rows, depth), LOW),
            shape((rows, width), LOW),
            shape((rows, width), LOW),
            shape((rows, width), LOW),
            shape((rows, depth), LOW),
            shape((members, PROMPT_DEV, width), LOW),
            shape((members, PROMPT_DEV, width), LOW),
        ],
        in_specs=[VMEM] * 7,
        out_specs=[VMEM] * 5 + [ANY] * 2,
        scratch_shapes=[DMA((2, members)), DMA((2, members)), DMA((2,))],
        compiler_params=pltpu.CompilerParams(
            collective_id=1, has_side_effects=True, vmem_limit_bytes=VMEM_LIMIT
        ),
        name="project",
    )(states, w_query, w_key, w_value, cosine, sine, cotangent)


def make_plan(half, group_id, slice_start, cont_group, plan):
    member = lax.axis_index("dp")
    own, other = group_id[member], cont_group[0]
    plan[0] = lax.div(slice_start[member], PROMPT_DEV)

    def step(index, _):
        rank = lax.div(slice_start[index], PROMPT_DEV)

        @pl.when(group_id[index] == own)
        def _():
            plan[1 + rank] = index

        @pl.when(group_id[index] == other)
        def _():
            plan[1 + half + rank] = index

        return 0

    lax.fori_loop(0, 2 * half, step, 0)


def attend_kernel(
    half,
    group_id,
    slice_start,
    cont_group,
    query,
    key,
    value,
    keys_all,
    values_all,
    mixed,
    attended,
    log_total,
    plan,
):
    @pl.when(pl.program_id(0) == 0)
    def _():
        make_plan(half, group_id, slice_start, cont_group, plan)

    def part(start, count, steps, offset):
        span = pl.ds(start, count)
        queries = query[span]
        allowed = lax.broadcasted_iota(jnp.int32, (count, count), 0) >= lax.broadcasted_iota(
            jnp.int32, (count, count), 1
        )
        scores = jnp.where(allowed, dot(queries, key[span], 1, 1) * SCALE, NEGATIVE)
        top = jnp.max(scores, axis=-1, keepdims=True)
        weights = jnp.exp(scores - top)
        total = jnp.sum(weights, axis=-1, keepdims=True)
        result = dot(weights.astype(LOW), value[span])

        def step(index, carry):
            top, total, result = carry
            place = plan[offset + index]
            scores = dot(queries, keys_all[place], 1, 1) * SCALE
            higher = jnp.maximum(top, jnp.max(scores, axis=-1, keepdims=True))
            fade = jnp.exp(top - higher)
            weights = jnp.exp(scores - higher)
            total = total * fade + jnp.sum(weights, axis=-1, keepdims=True)
            result = result * fade + dot(weights.astype(LOW), values_all[place])
            return higher, total, result

        top, total, result = lax.fori_loop(0, steps, step, (top, total, result))
        result = result / total
        mixed[span] = result.astype(LOW)
        attended[span] = result
        log_total[span] = jnp.broadcast_to(top + jnp.log(total), (count, HEAD))

    part(0, PROMPT_DEV, plan[0], 1)
    part(PROMPT_DEV, query.shape[0] - PROMPT_DEV, half, 1 + half)


def attend(readers, query, key, value, keys_all, values_all):
    rows, width = query.shape
    members = keys_all.shape[0]
    head = pl.BlockSpec((rows, HEAD), lambda h, *_: (0, h))
    every = pl.BlockSpec((members, PROMPT_DEV, HEAD), lambda h, *_: (0, 0, h))
    return pl.pallas_call(
        functools.partial(attend_kernel, members // 2),
        out_shape=[
            shape((rows, width), LOW),
            shape((rows, width), WIDE),
            shape((rows, width), WIDE),
        ],
        grid_spec=pltpu.PrefetchScalarGridSpec(
            num_scalar_prefetch=3,
            grid=(width // HEAD,),
            in_specs=[head, head, head, every, every],
            out_specs=[head, head, head],
            scratch_shapes=[pltpu.SMEM((members + 1,), jnp.int32)],
        ),
        compiler_params=pltpu.CompilerParams(vmem_limit_bytes=VMEM_LIMIT),
        name="attend",
    )(*readers, query, key, value, keys_all, values_all)


def attend_back_kernel(
    half,
    group_id,
    slice_start,
    cont_group,
    query,
    key,
    value,
    keys_all,
    values_all,
    branch_low,
    w_out,
    attended,
    log_total,
    cosine,
    sine,
    d_query,
    d_keys_all,
    d_values_all,
    d_key_own,
    d_value_own,
    d_mixed,
    key_total,
    value_total,
    plan,
):
    @pl.when(pl.program_id(0) == 0)
    def _():
        make_plan(half, group_id, slice_start, cont_group, plan)

    d_mixed[...] = dot(branch_low[...], w_out[...], 1, 1).astype(LOW)
    key_total[...] = jnp.zeros_like(key_total)
    value_total[...] = jnp.zeros_like(value_total)

    def part(start, count, steps, offset):
        span = pl.ds(start, count)
        queries, d_attended = query[span], d_mixed[span]
        log_sum = log_total[span][:, :1]
        center = jnp.sum(d_attended.astype(WIDE) * attended[span], axis=-1, keepdims=True)

        def back(scores, keys, values):
            probabilities = jnp.exp(scores - log_sum)
            d_scores = (probabilities * (dot(d_attended, values, 1, 1) - center)).astype(LOW)
            return (
                dot(d_scores, keys),
                dot(d_scores, queries, 0, 0),
                dot(probabilities.astype(LOW), d_attended, 0, 0),
            )

        allowed = lax.broadcasted_iota(jnp.int32, (count, count), 0) >= lax.broadcasted_iota(
            jnp.int32, (count, count), 1
        )
        scores = jnp.where(allowed, dot(queries, key[span], 1, 1) * SCALE, NEGATIVE)
        d_queries, d_own_keys, d_own_values = back(scores, key[span], value[span])

        def step(index, d_queries):
            place = plan[offset + index]
            keys, values = keys_all[place], values_all[place]
            more, d_keys, d_values = back(dot(queries, keys, 1, 1) * SCALE, keys, values)
            key_total[place] += d_keys
            value_total[place] += d_values
            return d_queries + more

        d_queries = lax.fori_loop(0, steps, step, d_queries) * SCALE
        d_query[span] = rotate(d_queries, cosine[span], -sine[span]).astype(LOW)
        return d_own_keys, d_own_values

    member = lax.axis_index("dp")
    d_own_keys, d_own_values = part(0, PROMPT_DEV, plan[0], 1)
    key_total[member] += d_own_keys
    value_total[member] += d_own_values
    d_own_keys, d_own_values = part(PROMPT_DEV, query.shape[0] - PROMPT_DEV, half, 1 + half)
    late = pl.ds(PROMPT_DEV, query.shape[0] - PROMPT_DEV)
    d_key_own[...] = rotate(d_own_keys * SCALE, cosine[late], -sine[late]).astype(LOW)
    d_value_own[...] = d_own_values.astype(LOW)
    d_keys_all[...] = (key_total[...] * SCALE).astype(LOW)
    d_values_all[...] = value_total[...].astype(LOW)


def attend_back(
    readers,
    query,
    key,
    value,
    keys_all,
    values_all,
    branch_low,
    w_out,
    attended,
    log_total,
    cosine,
    sine,
):
    rows, width = query.shape
    members = keys_all.shape[0]
    depth = branch_low.shape[1]
    late = rows - PROMPT_DEV
    heads = width // HEAD
    head = pl.BlockSpec((rows, HEAD), lambda h, *_: (0, h))
    every = pl.BlockSpec((members, PROMPT_DEV, HEAD), lambda h, *_: (0, 0, h))
    own = pl.BlockSpec((late, HEAD), lambda h, *_: (0, h))
    table = pl.BlockSpec((rows, HEAD), lambda h, *_: (0, 0))
    return pl.pallas_call(
        functools.partial(attend_back_kernel, members // 2),
        out_shape=[
            shape((rows, width), LOW),
            shape((members, PROMPT_DEV, width), LOW),
            shape((members, PROMPT_DEV, width), LOW),
            shape((late, width), LOW),
            shape((late, width), LOW),
        ],
        grid_spec=pltpu.PrefetchScalarGridSpec(
            num_scalar_prefetch=3,
            grid=(heads,),
            in_specs=[
                head,
                head,
                head,
                every,
                every,
                pl.BlockSpec((rows, depth), lambda h, *_: (0, 0)),
                pl.BlockSpec((HEAD, depth), lambda h, *_: (h, 0)),
                head,
                head,
                table,
                table,
            ],
            out_specs=[head, every, every, own, own],
            scratch_shapes=[
                pltpu.VMEM((rows, HEAD), LOW),
                pltpu.VMEM((members, PROMPT_DEV, HEAD), WIDE),
                pltpu.VMEM((members, PROMPT_DEV, HEAD), WIDE),
                pltpu.SMEM((members + 1,), jnp.int32),
            ],
        ),
        compiler_params=pltpu.CompilerParams(vmem_limit_bytes=VMEM_LIMIT),
        name="attend_back",
    )(
        *readers,
        query,
        key,
        value,
        keys_all,
        values_all,
        branch_low,
        w_out,
        attended,
        log_total,
        cosine,
        sine,
    )


def place_of(group_id, slice_start, group, rank):
    place = 0
    for index in range(group_id.shape[0]):
        found = (group_id[index] == group) & (slice_start[index] == rank * PROMPT_DEV)
        place = jnp.maximum(place, jnp.where(found, index, 0))
    return place


def own_part(rows):
    return lax.broadcasted_iota(jnp.int32, (rows, rows), 0) >= lax.broadcasted_iota(
        jnp.int32, (rows, rows), 1
    )


def gather_attend_kernel(
    members,
    group_id,
    slice_start,
    cont_group,
    w_query_in,
    w_key_in,
    w_value_in,
    w_down_in,
    states_in,
    cotangent_in,
    cosine,
    sine,
    act,
    query,
    key,
    value,
    out_low,
    d_hidden,
    mixed,
    attended,
    log_total,
    keys_out,
    values_out,
    states,
    cotangent,
    weights,
    w_down,
    load_sem,
    weight_sem,
    down_sem,
    cot_sem,
    send_sem,
    recv_sem,
    keep_sem,
    out_sem,
    *every,
):
    member, tensor = lax.axis_index("dp"), lax.axis_index("tensor")
    heads = query.shape[0]
    keys_all, values_all = every[:heads], every[heads:]
    half = members // 2
    rows = states.shape[0]
    chunks = load_sem.shape[0]
    size = rows // chunks
    loads = []
    for index in range(chunks):
        span = pl.ds(index * size, size)
        loads.append(pltpu.make_async_copy(states_in.at[span], states.at[span], load_sem.at[index]))
    w_loads = [
        pltpu.make_async_copy(source, weights.at[index], weight_sem.at[index])
        for index, source in enumerate((w_key_in, w_value_in, w_query_in))
    ]
    cot_load = pltpu.make_async_copy(cotangent_in, cotangent, cot_sem)
    down_load = pltpu.make_async_copy(w_down_in, w_down, down_sem)
    for load in loads[:1] + w_loads[:2] + loads[1:] + w_loads[2:] + [cot_load, down_load]:
        load.start()
    step = 64
    for index in range(chunks):
        loads[index].wait()
        for start in range(index * size, index * size + size, step):
            span = pl.ds(start, step)
            act[span] = norm_rows(states[span])[0].astype(LOW)

    def turned(weight, out):
        linear = dot(act[...], weight)
        for head in range(heads):
            out[head] = rotate(
                linear[:, head * HEAD : head * HEAD + HEAD], cosine[...], sine[...]
            ).astype(LOW)

    high = [bit for bit in bits_of(members) if bit]
    orders = (high + [0], high[::-1] + [0])
    owns, alls = (key, value), (keys_all, values_all)
    early = pl.ds(0, PROMPT_DEV)

    def copy(flow, head, mask, bit):
        slot = mask | 1 << bit
        place = alls[flow][head].at[flip(member, mask)]
        return remote(
            place if mask else owns[flow].at[head, early],
            place,
            send_sem.at[flow, head, slot],
            recv_sem.at[flow, head, slot],
            (flip(member, 1 << bit), tensor),
        )

    def forward(flow, head, mask):
        order = orders[flow]
        last = max([order.index(bit) for bit in order if mask >> bit & 1], default=-1)
        for bit in order[last + 1 :]:
            copy(flow, head, mask, bit).start()

    def came_by(flow, head, mask):
        order = orders[flow]
        bit = order[max(order.index(bit) for bit in order if mask >> bit & 1)]
        return copy(flow, head, mask ^ 1 << bit, bit)

    def keep(flow, head):
        return pltpu.make_async_copy(
            owns[flow].at[head, early], alls[flow][head].at[member], keep_sem.at[flow, head]
        )

    def write(flow, head):
        return pltpu.make_async_copy(
            alls[flow][head], (keys_out, values_out)[flow].at[head], out_sem.at[flow, head]
        )

    masks = range(1, members)
    levels = len(high)

    def own_sends(head):
        if head < heads:
            for flow in (0, 1):
                forward(flow, head, 0)
            for flow in (0, 1):
                keep(flow, head).start()

    def level(head, count):
        if head < heads:
            for mask in masks:
                if not mask & 1 and mask.bit_count() == count:
                    for flow in (0, 1):
                        came_by(flow, head, mask).wait_recv()
                        forward(flow, head, mask)

    def complete(head):
        for flow in (0, 1):
            for mask in masks:
                if mask & 1:
                    came_by(flow, head, mask).wait_recv()
            keep(flow, head).wait()
            write(flow, head).start()

    own_group, other_group = group_id[member], cont_group[0]
    own_start = slice_start[member]
    own_places = [place_of(group_id, slice_start, own_group, rank) for rank in range(half)]
    other_places = [place_of(group_id, slice_start, other_group, rank) for rank in range(half)]
    block = 128

    def attend_rows(head, start, places, whole):
        span = pl.ds(start, block)
        queries = query[head, span]
        scores, values = [], []
        for rank, place in enumerate(places):
            score = dot(queries, keys_all[head][place], 1, 1) * SCALE
            if not whole:
                at = lax.broadcasted_iota(jnp.int32, score.shape, 0) + (own_start + start)
                to = lax.broadcasted_iota(jnp.int32, score.shape, 1) + rank * PROMPT_DEV
                score = jnp.where(to <= at, score, NEGATIVE)
            scores.append(score)
            values.append(values_all[head][place])
        if whole:
            score = dot(queries, key[head, span], 1, 1) * SCALE
            scores.append(jnp.where(own_part(block), score, NEGATIVE))
            values.append(value[head, span])
        top = functools.reduce(
            jnp.maximum, [jnp.max(score, axis=-1, keepdims=True) for score in scores]
        )
        total = jnp.zeros_like(top)
        result = jnp.zeros((block, HEAD), WIDE)
        for score, held in zip(scores, values):
            weight = jnp.exp(score - top)
            total += jnp.sum(weight, axis=-1, keepdims=True)
            result += dot(weight.astype(LOW), held)
        result = result / total
        mixed[span, head * HEAD : head * HEAD + HEAD] = result.astype(LOW)
        attended[head, span] = result
        log_total[head, span] = jnp.broadcast_to(top + jnp.log(total), (block, HEAD))

    w_loads[0].wait()
    turned(weights[0], key)
    w_loads[1].wait()
    linear = dot(act[...], weights[1])
    for head in range(heads):
        value[head] = linear[:, head * HEAD : head * HEAD + HEAD].astype(LOW)
    greet(member_peers(members))
    own_sends(0)
    own_sends(1)
    w_loads[2].wait()
    turned(weights[2], query)
    level(0, 1)
    own_sends(2)
    cot_load.wait()
    for start in range(0, rows, step):
        span = pl.ds(start, step)
        out_low[span] = cotangent[span].astype(LOW)
    for count in range(2, levels + 1):
        level(0, count)
    level(1, 1)
    own_sends(3)
    down_load.wait()
    units = d_hidden.shape[1]
    for start in range(0, units, 512):
        span = pl.ds(start, 512)
        d_hidden[:, span] = dot(out_low[...], w_down[span], 1, 1).astype(LOW)
    for head in range(heads):
        complete(head)

        @pl.loop(0, PROMPT_DEV // block)
        def _(index, head=head):
            attend_rows(head, pl.multiple_of(index * block, block), own_places, False)

        for count in range(2, levels + 1):
            level(head + 1, count)
        level(head + 2, 1)
        own_sends(head + 4)
        for start in range(PROMPT_DEV, rows, block):
            attend_rows(head, start, other_places, True)
    for head in range(heads):
        for flow in (0, 1):
            write(flow, head).wait()
            for mask in masks:
                came_by(flow, head, mask).wait_send()


def gather_attend(
    members, readers, w_query, w_key, w_value, w_down, states, cotangent, cosine, sine
):
    rows, depth = states.shape
    width, units = w_query.shape[1], w_down.shape[0]
    heads = width // HEAD
    smem = pl.BlockSpec(memory_space=pltpu.SMEM)
    row_heads = (heads, rows, HEAD)
    every = (heads, members, PROMPT_DEV, HEAD)
    return pl.pallas_call(
        functools.partial(gather_attend_kernel, members),
        out_shape=[
            shape((rows, depth), LOW),
            shape(row_heads, LOW),
            shape(row_heads, LOW),
            shape(row_heads, LOW),
            shape((rows, depth), LOW),
            shape((rows, units), LOW),
            shape((rows, width), LOW),
            shape(row_heads, WIDE),
            shape(row_heads, WIDE),
            shape(every, LOW),
            shape(every, LOW),
        ],
        in_specs=[smem] * 3 + [ANY] * 6 + [VMEM] * 2,
        out_specs=[VMEM] * 9 + [ANY] * 2,
        scratch_shapes=[
            pltpu.VMEM((rows, depth), WIDE),
            pltpu.VMEM((rows, depth), WIDE),
            pltpu.VMEM((3, depth, width), LOW),
            pltpu.VMEM((units, depth), LOW),
            DMA((4,)),
            DMA((3,)),
            DMA,
            DMA,
            DMA((2, heads, members)),
            DMA((2, heads, members)),
            DMA((2, heads)),
            DMA((2, heads)),
        ]
        + [pltpu.VMEM(every[1:], LOW)] * (2 * heads),
        compiler_params=pltpu.CompilerParams(
            collective_id=6, has_side_effects=True, vmem_limit_bytes=VMEM_LIMIT
        ),
        name="gather_attend",
    )(
        *readers,
        w_query,
        w_key,
        w_value,
        w_down,
        states,
        cotangent,
        cosine,
        sine,
    )


def back_owner_kernel(
    members,
    group_id,
    slice_start,
    cont_group,
    keys_in,
    values_in,
    query,
    key,
    value,
    branch_low,
    w_out,
    attended,
    log_total,
    cosine,
    sine,
    d_query,
    d_key,
    d_value,
    d_mixed,
    d_queries,
    own_keys,
    own_values,
    other_keys,
    other_values,
    load_sem,
    *refs,
):
    take = taker(refs)
    member = lax.axis_index("dp")
    heads, rows = query.shape[0], query.shape[1]
    keys_all, values_all = take(heads), take(heads)
    half = pairs = members // 2
    parity = lax.rem(member, 2)
    order = bits_of(pairs)
    moves, flows, sides = [], [], []
    for way in (order, order[::-1]):
        mine, leaving, theirs = take(3)
        local_free, send_sem, recv_sem = take(3)
        refs_of = take(4)
        sides.append((mine, leaving, theirs, send_sem, recv_sem))
        per_head = []
        for head in range(heads):

            def own(mask, target, columns, mine=mine, theirs=theirs, head=head):
                return mine[head, target, :, columns].astype(WIDE) + theirs[
                    head, target, :, columns
                ].astype(WIDE)

            per_head.append(Halving(pairs, way, own, [ref.at[head] for ref in refs_of]))
        flows.append(per_head)
    partner = (flip(member, 1), lax.axis_index("tensor"))

    def load(index, head):
        source, target = ((keys_in, keys_all), (values_in, values_all))[index]
        return pltpu.make_async_copy(source.at[head], target[head], load_sem.at[index, head])

    for head in range(heads):
        for index in (0, 1):
            load(index, head).start()

    def across(flow, head):
        _, leaving, theirs, send_sem, recv_sem = sides[flow]
        return remote(
            leaving.at[head], theirs.at[head], send_sem.at[head], recv_sem.at[head], partner
        )

    own_group, other_group = group_id[member], cont_group[0]
    own_start = slice_start[member]
    own_places = [place_of(group_id, slice_start, own_group, rank) for rank in range(half)]
    other_places = [place_of(group_id, slice_start, other_group, rank) for rank in range(half)]
    linear = dot(branch_low[...], w_out[...], 1, 1)
    for head in range(heads):
        d_mixed[head] = linear[:, head * HEAD : head * HEAD + HEAD].astype(LOW)
    greet(member_peers(members))
    late = rows - PROMPT_DEV

    def back(scores, queries, keys, values, d_attended, log_sum, center):
        probabilities = jnp.exp(scores - log_sum)
        d_scores = (probabilities * (dot(d_attended, values, 1, 1) - center)).astype(LOW)
        return (
            dot(d_scores, keys),
            dot(d_scores, queries, 0, 0),
            dot(probabilities.astype(LOW), d_attended, 0, 0),
        )

    def rows_of(head, start, count):
        span = pl.ds(start, count)
        d_attended = d_mixed[head, span]
        center = jnp.sum(d_attended.astype(WIDE) * attended[head, span], axis=-1, keepdims=True)
        return query[head, span], d_attended, log_total[head, span][:, :1], center

    def prompt_rank(head, rank):
        queries, d_attended, log_sum, center = rows_of(head, 0, PROMPT_DEV)
        place = own_places[rank]
        keys, values = keys_all[head][place], values_all[head][place]
        scores = dot(queries, keys, 1, 1) * SCALE
        at = lax.broadcasted_iota(jnp.int32, scores.shape, 0) + own_start
        to = lax.broadcasted_iota(jnp.int32, scores.shape, 1) + rank * PROMPT_DEV
        scores = jnp.where(to <= at, scores, NEGATIVE)
        more, d_keys, d_values = back(
            scores, queries, keys, values, d_attended, log_sum, center
        )
        early = pl.ds(0, PROMPT_DEV)
        if rank:
            d_queries[early] += more
        else:
            d_queries[early] = more
        own_keys[rank] = d_keys
        own_values[rank] = d_values

    def late_part(head):
        queries, d_attended, log_sum, center = rows_of(head, PROMPT_DEV, late)
        span = pl.ds(PROMPT_DEV, late)
        keys, values = key[head, span], value[head, span]
        scores = jnp.where(own_part(late), dot(queries, keys, 1, 1) * SCALE, NEGATIVE)
        total, d_keys, d_values = back(
            scores, queries, keys, values, d_attended, log_sum, center
        )
        columns = pl.ds(head * HEAD, HEAD)
        d_key[span, columns] = rotate(d_keys * SCALE, cosine[span], -sine[span]).astype(LOW)
        d_value[span, columns] = d_values.astype(LOW)
        for rank in range(half):
            place = other_places[rank]
            keys, values = keys_all[head][place], values_all[head][place]
            more, d_keys, d_values = back(
                dot(queries, keys, 1, 1) * SCALE, queries, keys, values, d_attended, log_sum, center
            )
            total += more
            other_keys[rank] = d_keys
            other_values[rank] = d_values
        d_queries[span] = total
        d_query[:, columns] = rotate(d_queries[...] * SCALE, cosine[...], -sine[...]).astype(LOW)

    def spread(head):
        for pair in range(pairs):
            for away in (0, 1):
                index = 2 * pair + (1 - parity if away else parity)
                rank = lax.div(slice_start[index], PROMPT_DEV)
                mine = jnp.where(group_id[index] == own_group, 1.0, 0.0)
                other = jnp.where(group_id[index] == other_group, 1.0, 0.0)
                for flow, (a, b, scale) in enumerate(
                    ((own_keys, other_keys, SCALE), (own_values, other_values, 1.0))
                ):
                    total = a[rank] * (mine * scale) + b[rank] * (other * scale)
                    sides[flow][away][head, pair] = total.astype(LOW)

    def begin(head):
        for flow in (0, 1):
            across(flow, head).start()

    def stage(head, index):
        if not 0 <= head < heads:
            return
        for flow in (0, 1):
            if not index:
                across(flow, head).wait_recv()
        for flow in (0, 1):
            for mask in flows[flow][head].steps(index):
                flows[flow][head].push(mask)

    def end(head):
        if not 0 <= head < heads:
            return
        early = pl.ds(0, PROMPT_DEV)
        columns = pl.ds(head * HEAD, HEAD)
        total = d_queries.at[early]
        flows[0][head].end(total)
        d_key[early, columns] = rotate(total[...], cosine[early], -sine[early]).astype(LOW)
        flows[1][head].end(d_value.at[early, columns])

    count = len(order)
    for head in range(heads):
        for index in (0, 1):
            load(index, head).wait()
        for rank in range(half):
            prompt_rank(head, rank)
            if rank == 0:
                stage(head - 1, 0)
            if rank == half - 1:
                for index in range(1, count):
                    stage(head - 1, index)
        late_part(head)
        spread(head)
        begin(head)
        end(head - 1)
    for index in range(count):
        stage(heads - 1, index)
    end(heads - 1)
    for flow in (0, 1):
        for head in range(heads):
            across(flow, head).wait_send()
            flows[flow][head].sent()


def back_owner(
    members,
    readers,
    keys_all,
    values_all,
    query,
    key,
    value,
    branch_low,
    w_out,
    attended,
    log_total,
    cosine,
    sine,
):
    heads, rows, _ = query.shape
    width = heads * HEAD
    pairs = members // 2
    smem = pl.BlockSpec(memory_space=pltpu.SMEM)
    every = pltpu.VMEM((members, PROMPT_DEV, HEAD), LOW)
    side = pltpu.VMEM((heads, pairs, PROMPT_DEV, HEAD), LOW)
    step = pltpu.VMEM((heads, pairs - 1, PROMPT_DEV, HEAD), LOW)
    flow = [side] * 3 + [DMA((heads,))] * 3 + [step] * 2 + [DMA((heads, pairs - 1, 1))] * 2
    total = pltpu.VMEM((pairs, PROMPT_DEV, HEAD), WIDE)
    return pl.pallas_call(
        functools.partial(back_owner_kernel, members),
        out_shape=[shape((rows, width), LOW)] * 3,
        in_specs=[smem] * 3 + [ANY] * 2 + [VMEM] * 9,
        out_specs=[VMEM] * 3,
        scratch_shapes=[
            pltpu.VMEM((heads, rows, HEAD), LOW),
            pltpu.VMEM((rows, HEAD), WIDE),
            total,
            total,
            total,
            total,
            DMA((2, heads)),
        ]
        + [every] * (2 * heads)
        + flow * 2,
        compiler_params=pltpu.CompilerParams(
            collective_id=7, has_side_effects=True, vmem_limit_bytes=VMEM_LIMIT
        ),
        name="back_owner",
    )(
        *readers,
        keys_all,
        values_all,
        query,
        key,
        value,
        branch_low,
        w_out,
        attended,
        log_total,
        cosine,
        sine,
    )


def branch_kernel(count, mixed, w_out, states, act, resid, part, state_sem, *refs):
    line = Line(count, refs)
    rows = resid.shape[0]
    fetch = pltpu.make_async_copy(
        states.at[pl.ds(pl.multiple_of(line.here * rows, rows), rows)], resid, state_sem
    )
    fetch.start()
    tile = 512
    for start in range(0, part.shape[1], tile):
        columns = pl.ds(start, tile)
        part[:, columns] = dot(mixed[...], w_out[:, columns])
    greet(line.peers())
    fetch.wait()

    def finish(group):
        span = pl.ds(group * line.rows, line.rows)
        resid[span] += line.total[...]
        act[line.span(group, line.here)] = norm_rows(resid[span])[0].astype(LOW)

    line.reduce(part, act, finish)
    line.sent(act)


def branch(count, mixed, w_out, states):
    rows, depth = states.shape
    return pl.pallas_call(
        functools.partial(branch_kernel, count),
        out_shape=[shape((rows, depth), LOW), shape((rows // count, depth), WIDE)],
        in_specs=[VMEM, VMEM, ANY],
        out_specs=[VMEM, VMEM],
        scratch_shapes=[pltpu.VMEM((rows, depth), WIDE), DMA]
        + Line.scratch(count, GROUPS, rows // count, depth),
        compiler_params=pltpu.CompilerParams(
            collective_id=2, has_side_effects=True, vmem_limit_bytes=VMEM_LIMIT
        ),
        name="branch",
    )(mixed, w_out, states)


def feed_kernel(
    act, resid, d_hidden, w_gate, w_up, w_down, ffn, d_act, hidden, d_gate, d_up, ffn_total, d_total
):
    step = pl.program_id(0)
    gate = dot(act[...], w_gate[...])
    up = dot(act[...], w_up[...])
    sigmoid = jax.nn.sigmoid(gate)
    swish = gate * sigmoid
    d_inner = d_hidden[...].astype(WIDE)
    hidden[...] = (swish * up).astype(LOW)
    d_gate[...] = (d_inner * up * sigmoid * (1.0 + gate * (1.0 - sigmoid))).astype(LOW)
    d_up[...] = (d_inner * swish).astype(LOW)

    def add(new):
        tile = 512
        for start in range(0, act.shape[1], tile):
            columns = pl.ds(start, tile)
            more = dot(hidden[...], w_down[:, columns])
            d_more = dot(d_gate[...], w_gate[columns], 1, 1) + dot(d_up[...], w_up[columns], 1, 1)
            if new:
                ffn_total[:, columns] = more
                d_total[:, columns] = d_more
            else:
                ffn_total[:, columns] += more
                d_total[:, columns] += d_more

    @pl.when(step == 0)
    def _():
        add(True)

    @pl.when(step > 0)
    def _():
        add(False)

    @pl.when(step == pl.num_programs(0) - 1)
    def _():
        rows = resid.shape[0]
        here = lax.axis_index("tensor")
        own = pl.ds(pl.multiple_of(here * rows, rows), rows)
        ffn_total[own] += resid[...]
        ffn[...] = ffn_total[...].astype(LOW)
        d_act[...] = d_total[...].astype(LOW)


def feed(act, resid, d_hidden, w_gate, w_up, w_down):
    rows, depth = act.shape
    units = w_gate.shape[1]
    tile = 256
    whole = pl.BlockSpec((rows, depth), lambda i: (0, 0))
    across = pl.BlockSpec((depth, tile), lambda i: (0, i))
    down = pl.BlockSpec((tile, depth), lambda i: (i, 0))
    inner = pl.BlockSpec((rows, tile), lambda i: (0, i))
    chunk = pl.BlockSpec(resid.shape, lambda i: (0, 0))
    return pl.pallas_call(
        feed_kernel,
        out_shape=[shape((rows, depth), LOW)] * 2 + [shape((rows, units), LOW)] * 3,
        grid=(units // tile,),
        in_specs=[whole, chunk, inner, across, across, down],
        out_specs=[whole, whole, inner, inner, inner],
        scratch_shapes=[pltpu.VMEM((rows, depth), WIDE)] * 2,
        compiler_params=pltpu.CompilerParams(vmem_limit_bytes=VMEM_LIMIT),
        name="feed",
    )(act, resid, d_hidden, w_gate, w_up, w_down)


def second_kernel(
    count,
    pairs,
    d_act,
    resid,
    cotangent,
    act,
    d_gate,
    d_up,
    branch_low,
    grad_resid,
    grad_gate,
    grad_up,
    cot_sem,
    *refs,
):
    take = taker(refs)
    line = Line(count, take(Line.scratch_count))
    lhs = Lhs(act, take(4))
    rights = [Rhs([source], take(4)) for source in (d_gate, d_up)]
    order = bits_of(pairs)
    flows = [
        Halving(pairs, way, product_of(lhs, right), take(4), *take(1))
        for way, right in zip((order, order[::-1]), rights)
    ]
    rows = resid.shape[0]
    fetch = pltpu.make_async_copy(
        cotangent.at[pl.ds(pl.multiple_of(line.here * rows, rows), rows)], grad_resid, cot_sem
    )
    fetch.start()
    greet(line.peers() + member_peers(2 * pairs))
    lhs.start()
    for piece in range(flows[0].pieces):
        for right in rights:
            right.start(piece)
    fetch.wait()

    def finish(group):
        span = pl.ds(group * line.rows, line.rows)
        normed, inverse = norm_rows(resid[span])
        grad_resid[span] += norm_back(line.total[...], normed, inverse)
        branch_low[line.span(group, line.here)] = grad_resid[span].astype(LOW)

    sides = [(lhs, right, flow) for right, flow in zip(rights, flows)]
    line.reduce(d_act, branch_low, finish, beside(order, sides))
    flows[0].end(grad_gate)
    flows[1].end(grad_up)
    for flow in flows:
        flow.sent()
    for move in [lhs] + rights:
        move.sent()
    line.sent(branch_low)


def beside(order, sides):
    def early():
        held = []
        for lhs, rhs, flow in sides:
            if lhs not in held:
                lhs.ready()
                held.append(lhs)
            flow.push(flow.steps(0)[0], rhs.ready)

    def others():
        for index in range(1, len(sides[0][2].steps(0))):
            for _, _, flow in sides:
                flow.push(flow.steps(0)[index])

    def settle():
        for _, _, flow in sides:
            flow.settle()

    def late():
        for stage in range(1, len(order)):
            for index in range(len(sides[0][2].steps(stage))):
                for _, _, flow in sides:
                    flow.push(flow.steps(stage)[index])

    return [early, others, settle, lambda: None, late]


def second(count, members, d_act, resid, cotangent, act, d_gate, d_up):
    rows, depth = cotangent.shape
    units = d_gate.shape[1]
    pairs = members // 2
    block = depth // members
    return pl.pallas_call(
        functools.partial(second_kernel, count, pairs),
        out_shape=[
            shape((rows, depth), LOW),
            shape((rows // count, depth), WIDE),
            shape((block, units), LOW),
            shape((block, units), LOW),
        ],
        in_specs=[VMEM] * 2 + [ANY] * 4,
        out_specs=[VMEM] * 4,
        scratch_shapes=[DMA]
        + Line.scratch(count, GROUPS, rows // count, depth)
        + Lhs.scratch(pairs, rows, block)
        + Rhs.scratch(rows, units) * 2
        + (Halving.scratch(pairs, block, units) + [pltpu.VMEM((block, units), WIDE)]) * 2,
        compiler_params=pltpu.CompilerParams(
            collective_id=3, has_side_effects=True, vmem_limit_bytes=VMEM_LIMIT
        ),
        name="second",
    )(d_act, resid, cotangent, in_blocks(act, members), d_gate, d_up)


def owner_kernel(
    pairs,
    d_keys_all,
    d_values_all,
    d_key_own,
    d_value_own,
    cosine,
    sine,
    d_key,
    d_value,
    *refs,
):
    take = taker(refs)
    parity = lax.rem(lax.axis_index("dp"), 2)
    order = bits_of(pairs)
    width = d_key.shape[1]
    moves, flows = [], []
    for way, source in zip((order, order[::-1]), (d_keys_all, d_values_all)):
        mine, theirs = take(2)
        moves.append(
            Pairwise(
                [
                    (
                        source.at[2 * pair + parity],
                        mine.at[pair],
                        source.at[2 * pair + 1 - parity],
                        theirs.at[pair],
                    )
                    for pair in range(pairs)
                ],
                take(3),
            )
        )

        def own(mask, target, columns, mine=mine, theirs=theirs):
            return mine[target, :, columns].astype(WIDE) + theirs[target, :, columns].astype(WIDE)

        flows.append(Halving(pairs, way, own, take(4)))
    (total,) = take(1)
    greet(member_peers(2 * pairs))
    for move in moves:
        move.start()
    for move, flow in zip(moves, flows):
        move.ready()
        flow.push(flow.masks[0])
    late = pl.ds(PROMPT_DEV, d_key.shape[0] - PROMPT_DEV)
    d_key[late] = d_key_own[...]
    d_value[late] = d_value_own[...]
    for index in range(1, pairs - 1):
        for flow in flows:
            flow.push(flow.masks[index])
    early = pl.ds(0, PROMPT_DEV)
    flows[0].end(total)
    for start in range(0, width, HEAD):
        d_key[early, start : start + HEAD] = rotate(
            total[:, start : start + HEAD], cosine[early], -sine[early]
        ).astype(LOW)
    flows[1].end(d_value.at[early])
    for move, flow in zip(moves, flows):
        flow.sent()
        move.sent()


def owner(members, d_keys_all, d_values_all, d_key_own, d_value_own, cosine, sine):
    width = d_key_own.shape[1]
    rows = cosine.shape[0]
    pairs = members // 2
    flow = (
        [pltpu.VMEM((pairs, PROMPT_DEV, width), LOW)] * 2
        + Pairwise.sems(pairs)
        + Halving.scratch(pairs, PROMPT_DEV, width)
    )
    return pl.pallas_call(
        functools.partial(owner_kernel, pairs),
        out_shape=[shape((rows, width), LOW)] * 2,
        in_specs=[ANY, ANY] + [VMEM] * 4,
        out_specs=[VMEM] * 2,
        scratch_shapes=flow * 2 + [pltpu.VMEM((PROMPT_DEV, width), WIDE)],
        compiler_params=pltpu.CompilerParams(
            collective_id=4, has_side_effects=True, vmem_limit_bytes=VMEM_LIMIT
        ),
        name="owner",
    )(d_keys_all, d_values_all, d_key_own, d_value_own, cosine, sine)


def first_kernel(
    count,
    pairs,
    grad_resid,
    d_query,
    d_key,
    d_value,
    w_query,
    w_key,
    w_value,
    states,
    act,
    mixed,
    branch_low,
    hidden,
    out_low,
    far_query,
    far_key,
    far_value,
    input_grad,
    grad_down,
    grad_out,
    grad_inner,
    part,
    state,
    weight,
    state_sem,
    weight_sem,
    *refs,
):
    take = taker(refs)
    line = Line(count, take(Line.scratch_count))
    order = bits_of(pairs)
    sides = []
    for left, rights, way in (
        (out_low, (hidden,), order),
        (act, (far_query, far_key, far_value), order[::-1]),
        (branch_low, (mixed,), order[::-1]),
    ):
        lhs, rhs = Lhs(left, take(4)), Rhs(rights, take(4))
        sides.append((lhs, rhs, Halving(pairs, way, product_of(lhs, rhs), take(4), *take(1))))
    rows = state.shape[0]
    fetch = pltpu.make_async_copy(
        states.at[pl.ds(pl.multiple_of(line.here * rows, rows), rows)], state, state_sem
    )
    loads = [
        pltpu.make_async_copy(source, weight.at[index], weight_sem.at[index])
        for index, source in enumerate((w_query, w_key, w_value))
    ]
    for load in loads:
        load.start()
    fetch.start()
    greet(line.peers() + member_peers(2 * pairs))
    for lhs, rhs, _ in sides:
        lhs.start()
        rhs.start()
    for load in loads:
        load.wait()
    tile = 512
    for start in range(0, part.shape[1], tile):
        columns = pl.ds(start, tile)
        part[:, columns] = (
            dot(d_query[...], weight[0, columns], 1, 1)
            + dot(d_key[...], weight[1, columns], 1, 1)
            + dot(d_value[...], weight[2, columns], 1, 1)
        )
    fetch.wait()

    def finish(group):
        span = pl.ds(group * line.rows, line.rows)
        normed, inverse = norm_rows(state[span])
        input_grad[line.span(group, line.here)] = (
            grad_resid[span] + norm_back(line.total[...], normed, inverse)
        ).astype(LOW)

    line.reduce(part, input_grad, finish, beside(order, sides))
    for (_, _, flow), target in zip(sides, (grad_down, grad_inner, grad_out)):
        flow.end(target)
    for lhs, rhs, flow in sides:
        flow.sent()
        lhs.sent()
        rhs.sent()
    line.sent(input_grad)


def first(
    count,
    members,
    grad_resid,
    weights,
    states,
    act,
    mixed,
    branch_low,
    hidden,
    out_low,
    d_query,
    d_key,
    d_value,
):
    rows, depth = states.shape
    width = d_query.shape[1]
    units = hidden.shape[1]
    pairs = members // 2
    block = depth // members
    scratch = []
    for wide in (units, 3 * width, width):
        scratch += Lhs.scratch(pairs, rows, block) + Rhs.scratch(rows, wide)
        scratch += Halving.scratch(pairs, block, wide) + [pltpu.VMEM((block, wide), WIDE)]
    return pl.pallas_call(
        functools.partial(first_kernel, count, pairs),
        out_shape=[
            shape((rows, depth), LOW),
            shape((block, units), LOW),
            shape((block, width), LOW),
            shape((block, 3 * width), LOW),
        ],
        in_specs=[VMEM] * 4 + [ANY] * 12,
        out_specs=[VMEM] * 4,
        scratch_shapes=[
            pltpu.VMEM((rows, depth), WIDE),
            pltpu.VMEM((rows // count, depth), WIDE),
            pltpu.VMEM((3, depth, width), LOW),
            DMA,
            DMA((3,)),
        ]
        + Line.scratch(count, GROUPS, rows // count, depth)
        + scratch,
        compiler_params=pltpu.CompilerParams(
            collective_id=5, has_side_effects=True, vmem_limit_bytes=VMEM_LIMIT
        ),
        name="first",
    )(
        grad_resid,
        d_query,
        d_key,
        d_value,
        *weights,
        states,
        in_blocks(act, members),
        mixed,
        in_blocks(branch_low, members),
        hidden,
        in_blocks(out_low, members),
        d_query,
        d_key,
        d_value,
    )


def body(
    states,
    w_query,
    w_key,
    w_value,
    w_out,
    w_gate,
    w_up,
    w_down,
    group_id,
    slice_start,
    cont_group,
    cotangent,
):
    rows = states.shape[0]
    members = lax.axis_size("dp")
    count = lax.axis_size("tensor")
    member = lax.axis_index("dp")
    index = jnp.arange(rows, dtype=jnp.int32)
    everyone = jnp.arange(members, dtype=jnp.int32)
    own_start = jnp.sum(jnp.where(everyone == member, slice_start, 0))
    prompt = members // 2 * PROMPT_DEV
    positions = jnp.where(index < PROMPT_DEV, own_start + index, prompt + index - PROMPT_DEV)
    frequency = 10000.0 ** (-np.arange(HEAD // 2) * 2.0 / HEAD)
    frequency = np.concatenate([frequency, frequency]).astype(np.float32)
    sign = np.repeat([-1.0, 1.0], HEAD // 2).astype(np.float32)
    angles = positions.astype(WIDE)[:, None] * frequency[None, :]
    cosine = jnp.cos(angles)
    sine = jnp.sin(angles) * sign[None, :]
    readers = (group_id, slice_start, cont_group)

    merged = members * PROMPT_DEV * w_query.shape[1] * 2 * 4 <= 16 * 2**20
    if merged:
        act_one, query, key, value, out_low, d_hidden, mixed, attended, log_total, *everyones = (
            gather_attend(
                members, readers, w_query, w_key, w_value, w_down, states, cotangent, cosine, sine
            )
        )
    else:
        act_one, query, key, value, out_low, *everyones = project(
            members, states, w_query, w_key, w_value, cosine, sine, cotangent
        )
        d_hidden = dot(out_low, w_down, 1, 1).astype(LOW)
        mixed, attended, log_total = attend(readers, query, key, value, *everyones)
    act_two, resid = branch(count, mixed, w_out, states)
    ffn, d_act_two, hidden, d_gate, d_up = feed(act_two, resid, d_hidden, w_gate, w_up, w_down)
    branch_low, grad_resid, grad_gate, grad_up = second(
        count, members, d_act_two, resid, cotangent, act_two, d_gate, d_up
    )
    ffn, branch_low = lax.optimization_barrier((ffn, branch_low))
    layer_out = lax.psum(ffn, "tensor").astype(WIDE)
    kept = (query, key, value, branch_low, w_out, attended, log_total, cosine, sine)
    if merged:
        d_query, d_key, d_value = back_owner(members, readers, *everyones, *kept)
    else:
        d_query, *d_everyones = attend_back(
            readers, query, key, value, *everyones, branch_low, w_out, attended, log_total, cosine, sine
        )
        d_key, d_value = owner(members, *d_everyones, cosine, sine)
    input_grad, grad_down, grad_out, grad_inner = first(
        count,
        members,
        grad_resid,
        (w_query, w_key, w_value),
        states,
        act_one,
        mixed,
        branch_low,
        hidden,
        out_low,
        d_query,
        d_key,
        d_value,
    )
    width = d_query.shape[1]
    return (
        layer_out,
        input_grad.astype(WIDE),
        grad_inner[:, :width].astype(WIDE),
        grad_inner[:, width : 2 * width].astype(WIDE),
        grad_inner[:, 2 * width :].astype(WIDE),
        grad_out.astype(WIDE).T,
        grad_gate.astype(WIDE),
        grad_up.astype(WIDE),
        grad_down.astype(WIDE).T,
    )


def solution(mesh):
    placed = (
        P("dp", None),
        P(None, "tensor"),
        P(None, "tensor"),
        P(None, "tensor"),
        P("tensor", None),
        P(None, "tensor"),
        P(None, "tensor"),
        P("tensor", None),
        P(),
        P(),
        P("dp"),
        P("dp", None),
    )
    return jax.shard_map(
        body,
        mesh=mesh,
        in_specs=placed,
        out_specs=(
            P("dp", None),
            P("dp", None),
            P("dp", "tensor"),
            P("dp", "tensor"),
            P("dp", "tensor"),
            P("tensor", "dp"),
            P("dp", "tensor"),
            P("dp", "tensor"),
            P("tensor", "dp"),
        ),
        check_vma=False,
    )
```

```python
import functools

import jax
import jax.numpy as jnp
import numpy as np
from jax import lax
from jax.experimental import pallas as pl
from jax.experimental.pallas import tpu as pltpu
from jax.sharding import PartitionSpec as P

HEAD = 128
PROMPT_DEV = 384
EPSILON = 1e-05
NEGATIVE = -1e30
SCALE = HEAD ** (-0.5)
SCALE_TWO = float(SCALE * np.log2(np.e))
LOW = jnp.bfloat16
WIDE = jnp.float32
MESH = pl.DeviceIdType.MESH
ANY = pl.BlockSpec(memory_space=pl.ANY)
VMEM = pl.BlockSpec(memory_space=pltpu.VMEM)
DMA = pltpu.SemaphoreType.DMA
VMEM_LIMIT = 62 * 2**20
GROUPS = 2
PIECE = 512


def dot(left, right, left_dim=1, right_dim=0):
    return lax.dot_general(
        left, right, (((left_dim,), (right_dim,)), ((), ())), preferred_element_type=WIDE
    )


def shape(dims, dtype):
    return jax.ShapeDtypeStruct(dims, dtype)


def norm_rows(values):
    row_mean = jnp.mean(values, axis=-1, keepdims=True)
    centred = values - row_mean
    inverse = lax.rsqrt(jnp.mean(centred * centred, axis=-1, keepdims=True) + EPSILON)
    return centred * inverse, inverse


def norm_back(gradient, normed, inverse):
    return inverse * (
        gradient
        - jnp.mean(gradient, axis=-1, keepdims=True)
        - normed * jnp.mean(gradient * normed, axis=-1, keepdims=True)
    )


def rotate(values, cosine, sine):
    return values * cosine + pltpu.roll(values, HEAD // 2, 1) * sine


def flip(index, mask):
    out, bit = index, 1
    while bit <= mask:
        if mask & bit:
            out = out + bit * (1 - 2 * lax.rem(lax.div(index, bit), 2))
        bit *= 2
    return out


def bits_of(count):
    return list(range(count.bit_length() - 1))


def greet(peers):
    barrier = pltpu.get_barrier_semaphore()
    for peer in peers:
        pl.semaphore_signal(barrier, inc=1, device_id=peer, device_id_type=MESH)
    pl.semaphore_wait(barrier, len(peers))


def remote(source, target, send_sem, recv_sem, device):
    return pltpu.make_async_remote_copy(
        src_ref=source,
        dst_ref=target,
        send_sem=send_sem,
        recv_sem=recv_sem,
        device_id=device,
        device_id_type=MESH,
    )


class Line:
    scratch_count = 10

    @staticmethod
    def scratch(count, groups, rows, width):
        rows = rows // groups
        return [
            pltpu.VMEM((rows, width), WIDE),
            pltpu.VMEM((groups, count, rows, width), LOW),
            pltpu.VMEM((groups, count, rows, width), LOW),
            pltpu.VMEM((groups, count, rows, width), LOW),
            DMA((groups, count)),
            DMA((groups, count)),
            DMA((groups, count)),
            DMA((groups, count)),
            DMA((groups, count)),
            DMA((groups, count)),
        ]

    def __init__(self, count, refs):
        self.count = count
        (
            self.total,
            self.outgoing,
            self.from_left,
            self.from_right,
            self.out_sem,
            self.left_sem,
            self.right_sem,
            self.to_right_sem,
            self.to_left_sem,
            self.got_sem,
        ) = refs
        self.groups = self.outgoing.shape[0]
        self.rows = self.total.shape[0]
        self.here = lax.axis_index("tensor")
        member = lax.axis_index("dp")
        self.right = (member, lax.rem(self.here + 1, count))
        self.left = (member, lax.rem(self.here + count - 1, count))

    def peers(self):
        return [self.left, self.right]

    def span(self, group, chunk):
        start = chunk * (self.rows * self.groups) + group * self.rows
        return pl.ds(pl.multiple_of(start, self.rows), self.rows)

    def rightward(self, group, chunk):
        return remote(
            self.outgoing.at[group, chunk],
            self.from_left.at[group, chunk],
            self.out_sem.at[group, chunk],
            self.left_sem.at[group, chunk],
            self.right,
        )

    def leftward(self, group, chunk):
        return remote(
            self.outgoing.at[group, chunk],
            self.from_right.at[group, chunk],
            self.out_sem.at[group, chunk],
            self.right_sem.at[group, chunk],
            self.left,
        )

    def add_and_pass(self, group, chunk, part, right, wait):
        copy, came = (self.rightward, self.from_left) if right else (self.leftward, self.from_right)
        total = part[self.span(group, chunk)].astype(WIDE)
        if wait:
            copy(group, chunk).wait_recv()
            total += came[group, chunk].astype(WIDE)
        self.outgoing[group, chunk] = total.astype(LOW)
        copy(group, chunk).start()

    def scatter_slot(self, group, slot, part):
        here, count = self.here, self.count
        ahead, back = count - 1 + here - slot, slot - (count - 1 - here)
        if slot == 0:

            @pl.when(here == 0)
            def _():
                self.add_and_pass(group, ahead, part, True, False)

            @pl.when(here == count - 1)
            def _():
                self.add_and_pass(group, back, part, False, False)

            return
        for wait in (False, True):

            @pl.when((here <= slot) & ((here > 0) if wait else (here == 0)))
            def _(wait=wait):
                self.add_and_pass(group, ahead, part, True, wait)

            @pl.when(
                (count - 1 - here <= slot) & ((here < count - 1) if wait else (here == count - 1))
            )
            def _(wait=wait):
                self.add_and_pass(group, back, part, False, wait)

    def scatter_end(self, group, part):
        here = self.here
        last = self.count - 1

        def left():
            self.rightward(group, here).wait_recv()
            return self.from_left[group, here].astype(WIDE)

        def right():
            self.leftward(group, here).wait_recv()
            return self.from_right[group, here].astype(WIDE)

        @pl.when(here == 0)
        def _():
            self.total[...] = part[self.span(group, here)].astype(WIDE) + right()

        @pl.when(here == last)
        def _():
            self.total[...] = part[self.span(group, here)].astype(WIDE) + left()

        @pl.when((here > 0) & (here < last))
        def _():
            self.total[...] = part[self.span(group, here)].astype(WIDE) + left() + right()

    def passing(self, whole, group, chunk, right):
        ref = whole.at[self.span(group, chunk)]
        return remote(
            ref,
            ref,
            (self.to_right_sem if right else self.to_left_sem).at[group, chunk],
            self.got_sem.at[group, chunk],
            self.right if right else self.left,
        )

    def gather_slot(self, whole, group, distance):
        here, count = self.here, self.count

        @pl.when(here - distance >= 0)
        def _():
            if distance:
                self.passing(whole, group, here - distance, True).wait_recv()

            @pl.when(here < count - 1)
            def _():
                self.passing(whole, group, here - distance, True).start()

        @pl.when(here + distance <= count - 1)
        def _():
            if distance:
                self.passing(whole, group, here + distance, False).wait_recv()

            @pl.when(here > 0)
            def _():
                self.passing(whole, group, here + distance, False).start()

    def reduce(self, part, whole, finish, beside=()):
        beside = list(beside)
        last = self.count - 1
        self.scatter_slot(0, 0, part)
        for group in range(self.groups):
            for slot in range(1, last):
                if beside:
                    beside.pop(0)()
                self.scatter_slot(group, slot, part)
                if group:
                    self.gather_slot(whole, group - 1, slot)
            if group + 1 < self.groups:
                self.scatter_slot(group + 1, 0, part)
            if group:
                self.gather_slot(whole, group - 1, last)
            self.scatter_end(group, part)
            finish(group)
            self.gather_slot(whole, group, 0)
        for distance in range(1, self.count):
            if beside:
                beside.pop(0)()
            self.gather_slot(whole, self.groups - 1, distance)
        for act in beside:
            act()

    def sent(self, whole=None):
        here, count = self.here, self.count
        for group in range(self.groups):
            for chunk in range(count):

                @pl.when(here != chunk)
                def _(group=group, chunk=chunk):
                    self.rightward(group, chunk).wait_send()

                if whole is None:
                    continue

                @pl.when((chunk <= here) & (here < count - 1))
                def _(group=group, chunk=chunk):
                    self.passing(whole, group, chunk, True).wait_send()

                @pl.when((chunk >= here) & (here > 0))
                def _(group=group, chunk=chunk):
                    self.passing(whole, group, chunk, False).wait_send()


class Halving:
    @staticmethod
    def masks_of(pairs, order):
        def stage(mask):
            return min(order.index(bit) for bit in order if mask >> bit & 1)

        return sorted(range(1, pairs), key=lambda mask: (stage(mask), -mask.bit_count()))

    @staticmethod
    def scratch(pairs, block, width):
        count = pairs - 1
        pieces = max(1, width // PIECE)
        return [
            pltpu.VMEM((count, block, width), LOW),
            pltpu.VMEM((count, block, width), LOW),
            DMA((count, pieces)),
            DMA((count, pieces)),
        ]

    def __init__(self, pairs, order, own, refs, kept=None):
        self.order, self.own, self.kept = order, own, kept
        self.send, self.recv, self.send_sem, self.recv_sem = refs
        self.masks = Halving.masks_of(pairs, order)
        self.pieces = self.send_sem.shape[1]
        self.piece = self.send.shape[2] // self.pieces
        self.member = lax.axis_index("dp")
        self.tensor = lax.axis_index("tensor")
        self.high = lax.div(self.member, 2)

    def stage(self, mask):
        return min(
            [self.order.index(bit) for bit in self.order if mask >> bit & 1],
            default=len(self.order),
        )

    def steps(self, stage):
        return [mask for mask in self.masks if self.stage(mask) == stage]

    def columns(self, piece):
        return pl.ds(piece * self.piece, self.piece)

    def copy(self, mask, piece):
        index = self.masks.index(mask)
        bit = 1 << self.order[self.stage(mask)]
        return remote(
            self.send.at[index, :, self.columns(piece)],
            self.recv.at[index, :, self.columns(piece)],
            self.send_sem.at[index, piece],
            self.recv_sem.at[index, piece],
            (flip(self.member, bit * 2), self.tensor),
        )

    def settle(self):
        for piece in range(self.pieces):
            columns = self.columns(piece)
            self.kept[:, columns] = self.own(0, flip(self.high, 0), columns)

    def fill(self, mask, piece, out):
        columns = self.columns(piece)
        if self.kept is not None and not mask:
            total = self.kept[:, columns]
        else:
            total = self.own(mask, flip(self.high, mask), columns)
        for bit in self.order[: self.stage(mask)]:
            slot = mask | 1 << bit
            self.copy(slot, piece).wait_recv()
            total += self.recv[self.masks.index(slot), :, columns].astype(WIDE)
        out[:, columns] = total.astype(out.dtype)

    def push(self, mask, ready=None):
        for piece in range(self.pieces):
            if ready is not None:
                ready(piece)
            self.fill(mask, piece, self.send.at[self.masks.index(mask)])
            self.copy(mask, piece).start()

    def end(self, out):
        for piece in range(self.pieces):
            self.fill(0, piece, out)

    def sent(self):
        for mask in self.masks:
            for piece in range(self.pieces):
                self.copy(mask, piece).wait_send()


class Pairwise:
    def __init__(self, moves, refs):
        self.moves = moves
        self.local_sem, self.send_sem, self.recv_sem = refs
        member = lax.axis_index("dp")
        self.partner = (flip(member, 1), lax.axis_index("tensor"))

    @staticmethod
    def sems(count):
        return [DMA((count,)), DMA((count,)), DMA((count,))]

    def local(self, index):
        source, target, _, _ = self.moves[index]
        return pltpu.make_async_copy(source, target, self.local_sem.at[index])

    def across(self, index):
        _, _, source, target = self.moves[index]
        return remote(
            source, target, self.send_sem.at[index], self.recv_sem.at[index], self.partner
        )

    def start(self, index=None):
        for index in range(len(self.moves)) if index is None else [index]:
            self.across(index).start()
            self.local(index).start()

    def ready(self, index=None):
        for index in range(len(self.moves)) if index is None else [index]:
            self.local(index).wait()
            self.across(index).wait_recv()

    def sent(self):
        for index in range(len(self.moves)):
            self.across(index).wait_send()


class Lhs(Pairwise):
    @staticmethod
    def scratch(pairs, rows, block):
        return [pltpu.VMEM((pairs, 2 * rows, block), LOW)] + Pairwise.sems(pairs)

    def __init__(self, source, refs):
        self.held = refs[0]
        pairs, rows, block = self.held.shape
        rows = rows // 2
        parity = lax.rem(lax.axis_index("dp"), 2)

        def columns(index):
            if len(source.shape) == 3:
                return source.at[index]
            return source.at[:, pl.ds(pl.multiple_of(index * block, block), block)]

        super().__init__(
            [
                (
                    columns(2 * pair + parity),
                    self.held.at[pair, pl.ds(0, rows)],
                    columns(2 * pair + 1 - parity),
                    self.held.at[pair, pl.ds(rows, rows)],
                )
                for pair in range(pairs)
            ],
            refs[1:],
        )


class Rhs(Pairwise):
    @staticmethod
    def scratch(rows, width):
        return [pltpu.VMEM((2 * rows, width), LOW)] + Pairwise.sems(width // PIECE)

    def __init__(self, sources, refs):
        self.held = refs[0]
        rows = self.held.shape[0] // 2
        moves, at = [], 0
        for source in sources:
            for start in range(0, source.shape[1], PIECE):
                columns = pl.ds(at, PIECE)
                at += PIECE
                here = source.at[:, pl.ds(start, PIECE)]
                moves.append(
                    (
                        here,
                        self.held.at[pl.ds(0, rows), columns],
                        here,
                        self.held.at[pl.ds(rows, rows), columns],
                    )
                )
        super().__init__(moves, refs[1:])


def product_of(lhs, rhs):
    def own(mask, target, columns):
        return dot(lhs.held[target], rhs.held[:, columns], 0, 0)

    return own


def taker(refs):
    refs = list(refs)

    def take(count):
        out = refs[:count]
        del refs[:count]
        return out

    return take


def in_blocks(left, members):
    block = left.shape[1] // members
    if block % 128 == 0:
        return left
    return left.reshape(left.shape[0], members, block).transpose(1, 0, 2)


def member_peers(members):
    member, tensor = lax.axis_index("dp"), lax.axis_index("tensor")
    return [(flip(member, 1 << bit), tensor) for bit in bits_of(members)]


def project_kernel(
    members,
    states,
    w_query,
    w_key,
    w_value,
    cosine,
    sine,
    cotangent,
    act,
    query,
    key,
    value,
    out_low,
    keys_all,
    values_all,
    send_sem,
    recv_sem,
    local_sem,
):
    member, tensor = lax.axis_index("dp"), lax.axis_index("tensor")
    width = query.shape[1]
    greet(member_peers(members))
    rows = 64
    for start in range(0, states.shape[0], rows):
        span = pl.ds(start, rows)
        act[span] = norm_rows(states[span])[0].astype(LOW)

    def turned(weight, out):
        linear = dot(act[...], weight[...])
        for start in range(0, width, HEAD):
            out[:, start : start + HEAD] = rotate(
                linear[:, start : start + HEAD], cosine[...], sine[...]
            ).astype(LOW)

    high = [bit for bit in bits_of(members) if bit]
    orders = (high + [0], high[::-1] + [0])
    owns, alls = (key, value), (keys_all, values_all)

    def copy(flow, mask, bit):
        slot = mask | 1 << bit
        place = alls[flow].at[flip(member, mask)]
        return remote(
            place if mask else owns[flow].at[pl.ds(0, PROMPT_DEV)],
            place,
            send_sem.at[flow, slot],
            recv_sem.at[flow, slot],
            (flip(member, 1 << bit), tensor),
        )

    def forward(flow, mask):
        order = orders[flow]
        last = max([order.index(bit) for bit in order if mask >> bit & 1], default=-1)
        for bit in order[last + 1 :]:
            copy(flow, mask, bit).start()

    def came_by(flow, mask):
        order = orders[flow]
        bit = order[max(order.index(bit) for bit in order if mask >> bit & 1)]
        return copy(flow, mask ^ 1 << bit, bit)

    def keep(flow):
        return pltpu.make_async_copy(
            owns[flow].at[pl.ds(0, PROMPT_DEV)], alls[flow].at[member], local_sem.at[flow]
        )

    turned(w_key, key)
    forward(0, 0)
    value[...] = dot(act[...], w_value[...]).astype(LOW)
    forward(1, 0)
    keep(0).start()
    keep(1).start()
    turned(w_query, query)
    for start in range(0, states.shape[0], rows):
        span = pl.ds(start, rows)
        out_low[span] = cotangent[span].astype(LOW)
    masks = range(1, members)
    inner = sorted([mask for mask in masks if not mask & 1], key=lambda mask: mask.bit_count())
    for mask in inner:
        for flow in (0, 1):
            turn = flow if not mask & 2 else flow
            came_by(turn, mask).wait_recv()
            forward(turn, mask)
    for mask in masks:
        if mask & 1:
            for flow in (0, 1):
                came_by(flow, mask).wait_recv()
    for flow in (0, 1):
        keep(flow).wait()
        for mask in masks:
            came_by(flow, mask).wait_send()


def project(members, states, w_query, w_key, w_value, cosine, sine, cotangent):
    rows, depth = states.shape
    width = w_query.shape[1]
    return pl.pallas_call(
        functools.partial(project_kernel, members),
        out_shape=[
            shape((rows, depth), LOW),
            shape((rows, width), LOW),
            shape((rows, width), LOW),
            shape((rows, width), LOW),
            shape((rows, depth), LOW),
            shape((members, PROMPT_DEV, width), LOW),
            shape((members, PROMPT_DEV, width), LOW),
        ],
        in_specs=[VMEM] * 7,
        out_specs=[VMEM] * 5 + [ANY] * 2,
        scratch_shapes=[DMA((2, members)), DMA((2, members)), DMA((2,))],
        compiler_params=pltpu.CompilerParams(
            collective_id=1, has_side_effects=True, vmem_limit_bytes=VMEM_LIMIT
        ),
        name="project",
    )(states, w_query, w_key, w_value, cosine, sine, cotangent)


def make_plan(half, group_id, slice_start, cont_group, plan):
    member = lax.axis_index("dp")
    own, other = group_id[member], cont_group[0]
    plan[0] = lax.div(slice_start[member], PROMPT_DEV)

    def step(index, _):
        rank = lax.div(slice_start[index], PROMPT_DEV)

        @pl.when(group_id[index] == own)
        def _():
            plan[1 + rank] = index

        @pl.when(group_id[index] == other)
        def _():
            plan[1 + half + rank] = index

        return 0

    lax.fori_loop(0, 2 * half, step, 0)


def attend_kernel(
    half,
    group_id,
    slice_start,
    cont_group,
    query,
    key,
    value,
    keys_all,
    values_all,
    mixed,
    attended,
    log_total,
    plan,
):
    @pl.when(pl.program_id(0) == 0)
    def _():
        make_plan(half, group_id, slice_start, cont_group, plan)

    def part(start, count, steps, offset):
        span = pl.ds(start, count)
        queries = query[span]
        allowed = lax.broadcasted_iota(jnp.int32, (count, count), 0) >= lax.broadcasted_iota(
            jnp.int32, (count, count), 1
        )
        scores = jnp.where(allowed, dot(queries, key[span], 1, 1) * SCALE, NEGATIVE)
        top = jnp.max(scores, axis=-1, keepdims=True)
        weights = jnp.exp(scores - top)
        total = jnp.sum(weights, axis=-1, keepdims=True)
        result = dot(weights.astype(LOW), value[span])

        def step(index, carry):
            top, total, result = carry
            place = plan[offset + index]
            scores = dot(queries, keys_all[place], 1, 1) * SCALE
            higher = jnp.maximum(top, jnp.max(scores, axis=-1, keepdims=True))
            fade = jnp.exp(top - higher)
            weights = jnp.exp(scores - higher)
            total = total * fade + jnp.sum(weights, axis=-1, keepdims=True)
            result = result * fade + dot(weights.astype(LOW), values_all[place])
            return higher, total, result

        top, total, result = lax.fori_loop(0, steps, step, (top, total, result))
        result = result / total
        mixed[span] = result.astype(LOW)
        attended[span] = result
        log_total[span] = jnp.broadcast_to(top + jnp.log(total), (count, HEAD))

    part(0, PROMPT_DEV, plan[0], 1)
    part(PROMPT_DEV, query.shape[0] - PROMPT_DEV, half, 1 + half)


def attend(readers, query, key, value, keys_all, values_all):
    rows, width = query.shape
    members = keys_all.shape[0]
    head = pl.BlockSpec((rows, HEAD), lambda h, *_: (0, h))
    every = pl.BlockSpec((members, PROMPT_DEV, HEAD), lambda h, *_: (0, 0, h))
    return pl.pallas_call(
        functools.partial(attend_kernel, members // 2),
        out_shape=[
            shape((rows, width), LOW),
            shape((rows, width), WIDE),
            shape((rows, width), WIDE),
        ],
        grid_spec=pltpu.PrefetchScalarGridSpec(
            num_scalar_prefetch=3,
            grid=(width // HEAD,),
            in_specs=[head, head, head, every, every],
            out_specs=[head, head, head],
            scratch_shapes=[pltpu.SMEM((members + 1,), jnp.int32)],
        ),
        compiler_params=pltpu.CompilerParams(vmem_limit_bytes=VMEM_LIMIT),
        name="attend",
    )(*readers, query, key, value, keys_all, values_all)


def attend_back_kernel(
    half,
    group_id,
    slice_start,
    cont_group,
    query,
    key,
    value,
    keys_all,
    values_all,
    branch_low,
    w_out,
    attended,
    log_total,
    cosine,
    sine,
    d_query,
    d_keys_all,
    d_values_all,
    d_key_own,
    d_value_own,
    d_mixed,
    key_total,
    value_total,
    plan,
):
    @pl.when(pl.program_id(0) == 0)
    def _():
        make_plan(half, group_id, slice_start, cont_group, plan)

    d_mixed[...] = dot(branch_low[...], w_out[...], 1, 1).astype(LOW)
    key_total[...] = jnp.zeros_like(key_total)
    value_total[...] = jnp.zeros_like(value_total)

    def part(start, count, steps, offset):
        span = pl.ds(start, count)
        queries, d_attended = query[span], d_mixed[span]
        log_sum = log_total[span][:, :1]
        center = jnp.sum(d_attended.astype(WIDE) * attended[span], axis=-1, keepdims=True)

        def back(scores, keys, values):
            probabilities = jnp.exp(scores - log_sum)
            d_scores = (probabilities * (dot(d_attended, values, 1, 1) - center)).astype(LOW)
            return (
                dot(d_scores, keys),
                dot(d_scores, queries, 0, 0),
                dot(probabilities.astype(LOW), d_attended, 0, 0),
            )

        allowed = lax.broadcasted_iota(jnp.int32, (count, count), 0) >= lax.broadcasted_iota(
            jnp.int32, (count, count), 1
        )
        scores = jnp.where(allowed, dot(queries, key[span], 1, 1) * SCALE, NEGATIVE)
        d_queries, d_own_keys, d_own_values = back(scores, key[span], value[span])

        def step(index, d_queries):
            place = plan[offset + index]
            keys, values = keys_all[place], values_all[place]
            more, d_keys, d_values = back(dot(queries, keys, 1, 1) * SCALE, keys, values)
            key_total[place] += d_keys
            value_total[place] += d_values
            return d_queries + more

        d_queries = lax.fori_loop(0, steps, step, d_queries) * SCALE
        d_query[span] = rotate(d_queries, cosine[span], -sine[span]).astype(LOW)
        return d_own_keys, d_own_values

    member = lax.axis_index("dp")
    d_own_keys, d_own_values = part(0, PROMPT_DEV, plan[0], 1)
    key_total[member] += d_own_keys
    value_total[member] += d_own_values
    d_own_keys, d_own_values = part(PROMPT_DEV, query.shape[0] - PROMPT_DEV, half, 1 + half)
    late = pl.ds(PROMPT_DEV, query.shape[0] - PROMPT_DEV)
    d_key_own[...] = rotate(d_own_keys * SCALE, cosine[late], -sine[late]).astype(LOW)
    d_value_own[...] = d_own_values.astype(LOW)
    d_keys_all[...] = (key_total[...] * SCALE).astype(LOW)
    d_values_all[...] = value_total[...].astype(LOW)


def attend_back(
    readers,
    query,
    key,
    value,
    keys_all,
    values_all,
    branch_low,
    w_out,
    attended,
    log_total,
    cosine,
    sine,
):
    rows, width = query.shape
    members = keys_all.shape[0]
    depth = branch_low.shape[1]
    late = rows - PROMPT_DEV
    heads = width // HEAD
    head = pl.BlockSpec((rows, HEAD), lambda h, *_: (0, h))
    every = pl.BlockSpec((members, PROMPT_DEV, HEAD), lambda h, *_: (0, 0, h))
    own = pl.BlockSpec((late, HEAD), lambda h, *_: (0, h))
    table = pl.BlockSpec((rows, HEAD), lambda h, *_: (0, 0))
    return pl.pallas_call(
        functools.partial(attend_back_kernel, members // 2),
        out_shape=[
            shape((rows, width), LOW),
            shape((members, PROMPT_DEV, width), LOW),
            shape((members, PROMPT_DEV, width), LOW),
            shape((late, width), LOW),
            shape((late, width), LOW),
        ],
        grid_spec=pltpu.PrefetchScalarGridSpec(
            num_scalar_prefetch=3,
            grid=(heads,),
            in_specs=[
                head,
                head,
                head,
                every,
                every,
                pl.BlockSpec((rows, depth), lambda h, *_: (0, 0)),
                pl.BlockSpec((HEAD, depth), lambda h, *_: (h, 0)),
                head,
                head,
                table,
                table,
            ],
            out_specs=[head, every, every, own, own],
            scratch_shapes=[
                pltpu.VMEM((rows, HEAD), LOW),
                pltpu.VMEM((members, PROMPT_DEV, HEAD), WIDE),
                pltpu.VMEM((members, PROMPT_DEV, HEAD), WIDE),
                pltpu.SMEM((members + 1,), jnp.int32),
            ],
        ),
        compiler_params=pltpu.CompilerParams(vmem_limit_bytes=VMEM_LIMIT),
        name="attend_back",
    )(
        *readers,
        query,
        key,
        value,
        keys_all,
        values_all,
        branch_low,
        w_out,
        attended,
        log_total,
        cosine,
        sine,
    )


def place_of(group_id, slice_start, group, rank):
    place = 0
    for index in range(group_id.shape[0]):
        found = (group_id[index] == group) & (slice_start[index] == rank * PROMPT_DEV)
        place = jnp.maximum(place, jnp.where(found, index, 0))
    return place


def own_part(rows):
    return lax.broadcasted_iota(jnp.int32, (rows, rows), 0) >= lax.broadcasted_iota(
        jnp.int32, (rows, rows), 1
    )


def gather_attend_kernel(
    members,
    group_id,
    slice_start,
    cont_group,
    w_query_in,
    w_key_in,
    w_value_in,
    w_down_in,
    states_in,
    cotangent_in,
    cosine,
    sine,
    act,
    query,
    key,
    value,
    out_low,
    d_hidden,
    mixed,
    attended,
    log_total,
    keys_out,
    values_out,
    states,
    cotangent,
    weights,
    w_down,
    load_sem,
    weight_sem,
    down_sem,
    cot_sem,
    send_sem,
    recv_sem,
    keep_sem,
    out_sem,
    *every,
):
    member, tensor = lax.axis_index("dp"), lax.axis_index("tensor")
    heads = query.shape[0]
    keys_all, values_all = every[:heads], every[heads:]
    half = members // 2
    rows = states.shape[0]
    chunks = load_sem.shape[0]
    size = rows // chunks
    loads = []
    for index in range(chunks):
        span = pl.ds(index * size, size)
        loads.append(pltpu.make_async_copy(states_in.at[span], states.at[span], load_sem.at[index]))
    w_loads = [
        pltpu.make_async_copy(source, weights.at[index], weight_sem.at[index])
        for index, source in enumerate((w_key_in, w_value_in, w_query_in))
    ]
    cot_load = pltpu.make_async_copy(cotangent_in, cotangent, cot_sem)
    down_load = pltpu.make_async_copy(w_down_in, w_down, down_sem)
    for load in loads[:1] + w_loads[:2] + loads[1:] + w_loads[2:] + [cot_load, down_load]:
        load.start()
    step = 64
    for index in range(chunks):
        loads[index].wait()
        for start in range(index * size, index * size + size, step):
            span = pl.ds(start, step)
            act[span] = norm_rows(states[span])[0].astype(LOW)

    def turned(weight, out):
        linear = dot(act[...], weight)
        for head in range(heads):
            out[head] = rotate(
                linear[:, head * HEAD : head * HEAD + HEAD], cosine[...], sine[...]
            ).astype(LOW)

    high = [bit for bit in bits_of(members) if bit]
    orders = (high + [0], high[::-1] + [0])
    owns, alls = (key, value), (keys_all, values_all)
    early = pl.ds(0, PROMPT_DEV)

    def copy(flow, head, mask, bit):
        slot = mask | 1 << bit
        place = alls[flow][head].at[flip(member, mask)]
        return remote(
            place if mask else owns[flow].at[head, early],
            place,
            send_sem.at[flow, head, slot],
            recv_sem.at[flow, head, slot],
            (flip(member, 1 << bit), tensor),
        )

    def forward(flow, head, mask):
        order = orders[flow]
        last = max([order.index(bit) for bit in order if mask >> bit & 1], default=-1)
        for bit in order[last + 1 :]:
            copy(flow, head, mask, bit).start()

    def came_by(flow, head, mask):
        order = orders[flow]
        bit = order[max(order.index(bit) for bit in order if mask >> bit & 1)]
        return copy(flow, head, mask ^ 1 << bit, bit)

    def keep(flow, head):
        return pltpu.make_async_copy(
            owns[flow].at[head, early], alls[flow][head].at[member], keep_sem.at[flow, head]
        )

    def write(flow, head):
        return pltpu.make_async_copy(
            alls[flow][head], (keys_out, values_out)[flow].at[head], out_sem.at[flow, head]
        )

    masks = range(1, members)
    levels = len(high)

    def own_sends(head):
        if head < heads:
            for flow in (0, 1):
                forward(flow, head, 0)
            for flow in (0, 1):
                keep(flow, head).start()

    def level(head, count):
        if head < heads:
            for mask in masks:
                if not mask & 1 and mask.bit_count() == count:
                    for flow in (0, 1):
                        came_by(flow, head, mask).wait_recv()
                        forward(flow, head, mask)

    def complete(head):
        for flow in (0, 1):
            for mask in masks:
                if mask & 1:
                    came_by(flow, head, mask).wait_recv()
            keep(flow, head).wait()
            write(flow, head).start()

    own_group, other_group = group_id[member], cont_group[0]
    own_start = slice_start[member]
    own_places = [place_of(group_id, slice_start, own_group, rank) for rank in range(half)]
    other_places = [place_of(group_id, slice_start, other_group, rank) for rank in range(half)]
    block = 128

    def attend_rows(head, start, places, whole):
        span = pl.ds(start, block)
        queries = query[head, span]
        scores, values = [], []
        for rank, place in enumerate(places):
            score = dot(queries, keys_all[head][place], 1, 1) * SCALE_TWO
            if not whole:
                at = lax.broadcasted_iota(jnp.int32, score.shape, 0) + (own_start + start)
                to = lax.broadcasted_iota(jnp.int32, score.shape, 1) + rank * PROMPT_DEV
                score = jnp.where(to <= at, score, NEGATIVE)
            scores.append(score)
            values.append(values_all[head][place])
        if whole:
            score = dot(queries, key[head, span], 1, 1) * SCALE_TWO
            scores.append(jnp.where(own_part(block), score, NEGATIVE))
            values.append(value[head, span])
        top = functools.reduce(
            jnp.maximum, [jnp.max(score, axis=-1, keepdims=True) for score in scores]
        )
        total = jnp.zeros_like(top)
        result = jnp.zeros((block, HEAD), WIDE)
        for score, held in zip(scores, values):
            weight = jnp.exp2(score - top)
            total += jnp.sum(weight, axis=-1, keepdims=True)
            result += dot(weight.astype(LOW), held)
        result = result / total
        mixed[span, head * HEAD : head * HEAD + HEAD] = result.astype(LOW)
        attended[head, span] = result
        log_total[head, span] = jnp.broadcast_to(top + jnp.log2(total), (block, HEAD))

    w_loads[0].wait()
    turned(weights[0], key)
    w_loads[1].wait()
    linear = dot(act[...], weights[1])
    for head in range(heads):
        value[head] = linear[:, head * HEAD : head * HEAD + HEAD].astype(LOW)
    greet(member_peers(members))
    own_sends(0)
    own_sends(1)
    w_loads[2].wait()
    turned(weights[2], query)
    level(0, 1)
    own_sends(2)
    cot_load.wait()
    for start in range(0, rows, step):
        span = pl.ds(start, step)
        out_low[span] = cotangent[span].astype(LOW)
    for count in range(2, levels + 1):
        level(0, count)
    level(1, 1)
    own_sends(3)
    down_load.wait()
    units = d_hidden.shape[1]
    for start in range(0, units, 512):
        span = pl.ds(start, 512)
        d_hidden[:, span] = dot(out_low[...], w_down[span], 1, 1).astype(LOW)
    for head in range(heads):
        complete(head)

        @pl.loop(0, PROMPT_DEV // block)
        def _(index, head=head):
            attend_rows(head, pl.multiple_of(index * block, block), own_places, False)

        for count in range(2, levels + 1):
            level(head + 1, count)
        level(head + 2, 1)
        own_sends(head + 4)
        for start in range(PROMPT_DEV, rows, block):
            attend_rows(head, start, other_places, True)
    for head in range(heads):
        for flow in (0, 1):
            write(flow, head).wait()
            for mask in masks:
                came_by(flow, head, mask).wait_send()


def gather_attend(
    members, readers, w_query, w_key, w_value, w_down, states, cotangent, cosine, sine
):
    rows, depth = states.shape
    width, units = w_query.shape[1], w_down.shape[0]
    heads = width // HEAD
    smem = pl.BlockSpec(memory_space=pltpu.SMEM)
    row_heads = (heads, rows, HEAD)
    every = (heads, members, PROMPT_DEV, HEAD)
    return pl.pallas_call(
        functools.partial(gather_attend_kernel, members),
        out_shape=[
            shape((rows, depth), LOW),
            shape(row_heads, LOW),
            shape(row_heads, LOW),
            shape(row_heads, LOW),
            shape((rows, depth), LOW),
            shape((rows, units), LOW),
            shape((rows, width), LOW),
            shape(row_heads, WIDE),
            shape(row_heads, WIDE),
            shape(every, LOW),
            shape(every, LOW),
        ],
        in_specs=[smem] * 3 + [ANY] * 6 + [VMEM] * 2,
        out_specs=[VMEM] * 9 + [ANY] * 2,
        scratch_shapes=[
            pltpu.VMEM((rows, depth), WIDE),
            pltpu.VMEM((rows, depth), WIDE),
            pltpu.VMEM((3, depth, width), LOW),
            pltpu.VMEM((units, depth), LOW),
            DMA((4,)),
            DMA((3,)),
            DMA,
            DMA,
            DMA((2, heads, members)),
            DMA((2, heads, members)),
            DMA((2, heads)),
            DMA((2, heads)),
        ]
        + [pltpu.VMEM(every[1:], LOW)] * (2 * heads),
        compiler_params=pltpu.CompilerParams(
            collective_id=6, has_side_effects=True, vmem_limit_bytes=VMEM_LIMIT
        ),
        name="gather_attend",
    )(
        *readers,
        w_query,
        w_key,
        w_value,
        w_down,
        states,
        cotangent,
        cosine,
        sine,
    )


def back_owner_kernel(
    members,
    count,
    group_id,
    slice_start,
    cont_group,
    keys_in,
    values_in,
    query,
    key,
    value,
    branch_low,
    w_out,
    attended,
    log_total,
    cosine,
    sine,
    own_out,
    d_query,
    d_key,
    d_value,
    early_out,
    d_mixed,
    d_queries,
    own_keys,
    own_values,
    other_keys,
    other_values,
    load_sem,
    *refs,
):
    take = taker(refs)
    member = lax.axis_index("dp")
    heads, rows = query.shape[0], query.shape[1]
    keys_all, values_all = take(heads), take(heads)
    out_send, out_recv = take(2)
    here = lax.axis_index("tensor")
    size = own_out.shape[0]
    own_rows = pl.ds(pl.multiple_of(here * size, size), size)

    def tell(distance):
        return remote(
            own_out,
            early_out.at[own_rows],
            out_send.at[distance - 1],
            out_recv.at[distance - 1],
            (member, lax.rem(here + distance, count)),
        )

    half = pairs = members // 2
    parity = lax.rem(member, 2)
    order = bits_of(pairs)
    moves, flows, sides = [], [], []
    for way in (order, order[::-1]):
        mine, leaving, theirs = take(3)
        local_free, send_sem, recv_sem = take(3)
        refs_of = take(4)
        sides.append((mine, leaving, theirs, send_sem, recv_sem))
        per_head = []
        for head in range(heads):

            def own(mask, target, columns, mine=mine, theirs=theirs, head=head):
                return mine[head, target, :, columns].astype(WIDE) + theirs[
                    head, target, :, columns
                ].astype(WIDE)

            per_head.append(Halving(pairs, way, own, [ref.at[head] for ref in refs_of]))
        flows.append(per_head)
    partner = (flip(member, 1), lax.axis_index("tensor"))

    def load(index, head):
        source, target = ((keys_in, keys_all), (values_in, values_all))[index]
        return pltpu.make_async_copy(source.at[head], target[head], load_sem.at[index, head])

    for head in range(heads):
        for index in (0, 1):
            load(index, head).start()

    def across(flow, head):
        _, leaving, theirs, send_sem, recv_sem = sides[flow]
        return remote(
            leaving.at[head], theirs.at[head], send_sem.at[head], recv_sem.at[head], partner
        )

    own_group, other_group = group_id[member], cont_group[0]
    own_start = slice_start[member]
    own_places = [place_of(group_id, slice_start, own_group, rank) for rank in range(half)]
    other_places = [place_of(group_id, slice_start, other_group, rank) for rank in range(half)]
    linear = dot(branch_low[...], w_out[...], 1, 1)
    for head in range(heads):
        d_mixed[head] = linear[:, head * HEAD : head * HEAD + HEAD].astype(LOW)
    across_line = [(member, lax.rem(here + distance, count)) for distance in range(1, count)]
    greet(member_peers(members) + across_line)
    for distance in range(1, count):
        tell(distance).start()
    early_out[own_rows] = own_out[...]
    late = rows - PROMPT_DEV

    def back(scores, queries, keys, values, d_attended, log_sum, center):
        probabilities = jnp.exp2(scores - log_sum)
        d_scores = (probabilities * (dot(d_attended, values, 1, 1) - center)).astype(LOW)
        return (
            dot(d_scores, keys),
            dot(d_scores, queries, 0, 0),
            dot(probabilities.astype(LOW), d_attended, 0, 0),
        )

    def rows_of(head, start, count):
        span = pl.ds(start, count)
        d_attended = d_mixed[head, span]
        center = jnp.sum(d_attended.astype(WIDE) * attended[head, span], axis=-1, keepdims=True)
        return query[head, span], d_attended, log_total[head, span][:, :1], center

    def prompt_rank(head, rank):
        queries, d_attended, log_sum, center = rows_of(head, 0, PROMPT_DEV)
        place = own_places[rank]
        keys, values = keys_all[head][place], values_all[head][place]
        scores = dot(queries, keys, 1, 1) * SCALE_TWO
        at = lax.broadcasted_iota(jnp.int32, scores.shape, 0) + own_start
        to = lax.broadcasted_iota(jnp.int32, scores.shape, 1) + rank * PROMPT_DEV
        scores = jnp.where(to <= at, scores, NEGATIVE)
        more, d_keys, d_values = back(
            scores, queries, keys, values, d_attended, log_sum, center
        )
        early = pl.ds(0, PROMPT_DEV)
        if rank:
            d_queries[early] += more
        else:
            d_queries[early] = more
        own_keys[rank] = d_keys
        own_values[rank] = d_values

    def late_part(head):
        queries, d_attended, log_sum, center = rows_of(head, PROMPT_DEV, late)
        span = pl.ds(PROMPT_DEV, late)
        keys, values = key[head, span], value[head, span]
        scores = jnp.where(own_part(late), dot(queries, keys, 1, 1) * SCALE_TWO, NEGATIVE)
        total, d_keys, d_values = back(
            scores, queries, keys, values, d_attended, log_sum, center
        )
        columns = pl.ds(head * HEAD, HEAD)
        d_key[span, columns] = rotate(d_keys * SCALE, cosine[span], -sine[span]).astype(LOW)
        d_value[span, columns] = d_values.astype(LOW)
        for rank in range(half):
            place = other_places[rank]
            keys, values = keys_all[head][place], values_all[head][place]
            more, d_keys, d_values = back(
                dot(queries, keys, 1, 1) * SCALE_TWO, queries, keys, values, d_attended, log_sum, center
            )
            total += more
            other_keys[rank] = d_keys
            other_values[rank] = d_values
        d_queries[span] = total
        d_query[:, columns] = rotate(d_queries[...] * SCALE, cosine[...], -sine[...]).astype(LOW)

    def spread(head):
        for pair in range(pairs):
            for away in (0, 1):
                index = 2 * pair + (1 - parity if away else parity)
                rank = lax.div(slice_start[index], PROMPT_DEV)
                mine = jnp.where(group_id[index] == own_group, 1.0, 0.0)
                other = jnp.where(group_id[index] == other_group, 1.0, 0.0)
                for flow, (a, b, scale) in enumerate(
                    ((own_keys, other_keys, SCALE), (own_values, other_values, 1.0))
                ):
                    total = a[rank] * (mine * scale) + b[rank] * (other * scale)
                    sides[flow][away][head, pair] = total.astype(LOW)

    def begin(head):
        for flow in (0, 1):
            across(flow, head).start()

    def stage(head, index):
        if not 0 <= head < heads:
            return
        for flow in (0, 1):
            if not index:
                across(flow, head).wait_recv()
        for flow in (0, 1):
            for mask in flows[flow][head].steps(index):
                flows[flow][head].push(mask)

    def end(head):
        if not 0 <= head < heads:
            return
        early = pl.ds(0, PROMPT_DEV)
        columns = pl.ds(head * HEAD, HEAD)
        total = d_queries.at[early]
        flows[0][head].end(total)
        d_key[early, columns] = rotate(total[...], cosine[early], -sine[early]).astype(LOW)
        flows[1][head].end(d_value.at[early, columns])

    depth = len(order)
    for head in range(heads):
        for index in (0, 1):
            load(index, head).wait()
        for rank in range(half):
            prompt_rank(head, rank)
            if rank == 0:
                stage(head - 1, 0)
            if rank == half - 1:
                for index in range(1, depth):
                    stage(head - 1, index)
        late_part(head)
        spread(head)
        begin(head)
        end(head - 1)
    for index in range(depth):
        stage(heads - 1, index)
    end(heads - 1)
    for flow in (0, 1):
        for head in range(heads):
            across(flow, head).wait_send()
            flows[flow][head].sent()
    for distance in range(1, count):
        tell(distance).wait()


def back_owner(
    members,
    count,
    readers,
    keys_all,
    values_all,
    query,
    key,
    value,
    branch_low,
    w_out,
    attended,
    log_total,
    cosine,
    sine,
    own_out,
):
    heads, rows, _ = query.shape
    width = heads * HEAD
    pairs = members // 2
    smem = pl.BlockSpec(memory_space=pltpu.SMEM)
    every = pltpu.VMEM((members, PROMPT_DEV, HEAD), LOW)
    side = pltpu.VMEM((heads, pairs, PROMPT_DEV, HEAD), LOW)
    step = pltpu.VMEM((heads, pairs - 1, PROMPT_DEV, HEAD), LOW)
    flow = [side] * 3 + [DMA((heads,))] * 3 + [step] * 2 + [DMA((heads, pairs - 1, 1))] * 2
    total = pltpu.VMEM((pairs, PROMPT_DEV, HEAD), WIDE)
    return pl.pallas_call(
        functools.partial(back_owner_kernel, members, count),
        out_shape=[shape((rows, width), LOW)] * 3
        + [shape((count * own_out.shape[0], own_out.shape[1]), LOW)],
        in_specs=[smem] * 3 + [ANY] * 2 + [VMEM] * 10,
        out_specs=[VMEM] * 4,
        scratch_shapes=[
            pltpu.VMEM((heads, rows, HEAD), LOW),
            pltpu.VMEM((rows, HEAD), WIDE),
            total,
            total,
            total,
            total,
            DMA((2, heads)),
        ]
        + [every] * (2 * heads)
        + [DMA((count - 1,))] * 2
        + flow * 2,
        compiler_params=pltpu.CompilerParams(
            collective_id=7, has_side_effects=True, vmem_limit_bytes=VMEM_LIMIT
        ),
        name="back_owner",
    )(
        *readers,
        keys_all,
        values_all,
        query,
        key,
        value,
        branch_low,
        w_out,
        attended,
        log_total,
        cosine,
        sine,
        own_out,
    )


def branch_kernel(count, mixed, w_out, states, act, resid, part, state_sem, *refs):
    line = Line(count, refs)
    rows = resid.shape[0]
    fetch = pltpu.make_async_copy(
        states.at[pl.ds(pl.multiple_of(line.here * rows, rows), rows)], resid, state_sem
    )
    fetch.start()
    tile = 512
    for start in range(0, part.shape[1], tile):
        columns = pl.ds(start, tile)
        part[:, columns] = dot(mixed[...], w_out[:, columns])
    greet(line.peers())
    fetch.wait()

    def finish(group):
        span = pl.ds(group * line.rows, line.rows)
        resid[span] += line.total[...]
        act[line.span(group, line.here)] = norm_rows(resid[span])[0].astype(LOW)

    line.reduce(part, act, finish)
    line.sent(act)


def branch(count, mixed, w_out, states):
    rows, depth = states.shape
    return pl.pallas_call(
        functools.partial(branch_kernel, count),
        out_shape=[shape((rows, depth), LOW), shape((rows // count, depth), WIDE)],
        in_specs=[VMEM, VMEM, ANY],
        out_specs=[VMEM, VMEM],
        scratch_shapes=[pltpu.VMEM((rows, depth), WIDE), DMA]
        + Line.scratch(count, GROUPS, rows // count, depth),
        compiler_params=pltpu.CompilerParams(
            collective_id=2, has_side_effects=True, vmem_limit_bytes=VMEM_LIMIT
        ),
        name="branch",
    )(mixed, w_out, states)


def feed_kernel(
    act, resid, d_hidden, w_gate, w_up, w_down, ffn_early, ffn_late, d_act, hidden, d_gate, d_up, ffn_total, d_total
):
    step = pl.program_id(0)
    gate = dot(act[...], w_gate[...])
    up = dot(act[...], w_up[...])
    sigmoid = jax.nn.sigmoid(gate)
    swish = gate * sigmoid
    d_inner = d_hidden[...].astype(WIDE)
    hidden[...] = (swish * up).astype(LOW)
    d_gate[...] = (d_inner * up * sigmoid * (1.0 + gate * (1.0 - sigmoid))).astype(LOW)
    d_up[...] = (d_inner * swish).astype(LOW)

    def add(new):
        tile = 512
        for start in range(0, act.shape[1], tile):
            columns = pl.ds(start, tile)
            more = dot(hidden[...], w_down[:, columns])
            d_more = dot(d_gate[...], w_gate[columns], 1, 1) + dot(d_up[...], w_up[columns], 1, 1)
            if new:
                ffn_total[:, columns] = more
                d_total[:, columns] = d_more
            else:
                ffn_total[:, columns] += more
                d_total[:, columns] += d_more

    @pl.when(step == 0)
    def _():
        add(True)

    @pl.when(step > 0)
    def _():
        add(False)

    @pl.when(step == pl.num_programs(0) - 1)
    def _():
        rows = resid.shape[0]
        here = lax.axis_index("tensor")
        own = pl.ds(pl.multiple_of(here * rows, rows), rows)
        ffn_total[own] += resid[...]
        for at, ffn in enumerate((ffn_early, ffn_late)):
            part = rows // 2
            for chunk in range(act.shape[0] // rows):
                ffn[pl.ds(chunk * part, part)] = ffn_total[
                    pl.ds(chunk * rows + at * part, part)
                ].astype(LOW)
        d_act[...] = d_total[...].astype(LOW)


def feed(act, resid, d_hidden, w_gate, w_up, w_down):
    rows, depth = act.shape
    units = w_gate.shape[1]
    tile = 256
    whole = pl.BlockSpec((rows, depth), lambda i: (0, 0))
    some = pl.BlockSpec((rows // 2, depth), lambda i: (0, 0))
    across = pl.BlockSpec((depth, tile), lambda i: (0, i))
    down = pl.BlockSpec((tile, depth), lambda i: (i, 0))
    inner = pl.BlockSpec((rows, tile), lambda i: (0, i))
    chunk = pl.BlockSpec(resid.shape, lambda i: (0, 0))
    return pl.pallas_call(
        feed_kernel,
        out_shape=[shape((rows // 2, depth), LOW)] * 2
        + [shape((rows, depth), LOW)]
        + [shape((rows, units), LOW)] * 3,
        grid=(units // tile,),
        in_specs=[whole, chunk, inner, across, across, down],
        out_specs=[some, some, whole, inner, inner, inner],
        scratch_shapes=[pltpu.VMEM((rows, depth), WIDE)] * 2,
        compiler_params=pltpu.CompilerParams(vmem_limit_bytes=VMEM_LIMIT),
        name="feed",
    )(act, resid, d_hidden, w_gate, w_up, w_down)


def second_kernel(
    count,
    pairs,
    d_act,
    ffn,
    resid,
    cotangent,
    act,
    d_gate,
    d_up,
    branch_low,
    grad_resid,
    own_out,
    grad_gate,
    grad_up,
    cot_sem,
    *refs,
):
    take = taker(refs)
    line = Line(count, take(Line.scratch_count))
    out_line = Line(count, take(Line.scratch_count))
    lhs = Lhs(act, take(4))
    rights = [Rhs([source], take(4)) for source in (d_gate, d_up)]
    order = bits_of(pairs)
    flows = [
        Halving(pairs, way, product_of(lhs, right), take(4), *take(1))
        for way, right in zip((order, order[::-1]), rights)
    ]
    rows = resid.shape[0]
    fetch = pltpu.make_async_copy(
        cotangent.at[pl.ds(pl.multiple_of(line.here * rows, rows), rows)], grad_resid, cot_sem
    )
    fetch.start()
    greet(line.peers() + member_peers(2 * pairs))
    lhs.start()
    for piece in range(flows[0].pieces):
        for right in rights:
            right.start(piece)
    fetch.wait()

    def finish(group):
        span = pl.ds(group * line.rows, line.rows)
        normed, inverse = norm_rows(resid[span])
        grad_resid[span] += norm_back(line.total[...], normed, inverse)
        branch_low[line.span(group, line.here)] = grad_resid[span].astype(LOW)

    sides = [(lhs, right, flow) for right, flow in zip(rights, flows)]
    early, others, settle, _, late = beside(order, sides)

    def out_slot(slot):
        return lambda: out_line.scatter_slot(0, slot, ffn)

    slots = [out_slot(slot) for slot in range(count - 1)]
    line.reduce(d_act, branch_low, finish, [early, others, settle, slots[0], late] + slots[1:])
    out_line.scatter_end(0, ffn)
    own_out[...] = out_line.total[...].astype(LOW)
    flows[0].end(grad_gate)
    flows[1].end(grad_up)
    for flow in flows:
        flow.sent()
    for move in [lhs] + rights:
        move.sent()
    line.sent(branch_low)
    out_line.sent()


def beside(order, sides):
    def early():
        held = []
        for lhs, rhs, flow in sides:
            if lhs not in held:
                lhs.ready()
                held.append(lhs)
            flow.push(flow.steps(0)[0], rhs.ready)

    def others():
        for index in range(1, len(sides[0][2].steps(0))):
            for _, _, flow in sides:
                flow.push(flow.steps(0)[index])

    def settle():
        for _, _, flow in sides:
            flow.settle()

    def late():
        for stage in range(1, len(order)):
            for index in range(len(sides[0][2].steps(stage))):
                for _, _, flow in sides:
                    flow.push(flow.steps(stage)[index])

    return [early, others, settle, lambda: None, late]


def second(count, members, d_act, ffn, resid, cotangent, act, d_gate, d_up):
    rows, depth = cotangent.shape
    units = d_gate.shape[1]
    pairs = members // 2
    block = depth // members
    return pl.pallas_call(
        functools.partial(second_kernel, count, pairs),
        out_shape=[
            shape((rows, depth), LOW),
            shape((rows // count, depth), WIDE),
            shape((ffn.shape[0] // count, depth), LOW),
            shape((block, units), LOW),
            shape((block, units), LOW),
        ],
        in_specs=[VMEM] * 3 + [ANY] * 4,
        out_specs=[VMEM] * 5,
        scratch_shapes=[DMA]
        + Line.scratch(count, GROUPS, rows // count, depth)
        + Line.scratch(count, 1, ffn.shape[0] // count, depth)
        + Lhs.scratch(pairs, rows, block)
        + Rhs.scratch(rows, units) * 2
        + (Halving.scratch(pairs, block, units) + [pltpu.VMEM((block, units), WIDE)]) * 2,
        compiler_params=pltpu.CompilerParams(
            collective_id=3, has_side_effects=True, vmem_limit_bytes=VMEM_LIMIT
        ),
        name="second",
    )(d_act, ffn, resid, cotangent, in_blocks(act, members), d_gate, d_up)


def owner_kernel(
    pairs,
    d_keys_all,
    d_values_all,
    d_key_own,
    d_value_own,
    cosine,
    sine,
    d_key,
    d_value,
    *refs,
):
    take = taker(refs)
    parity = lax.rem(lax.axis_index("dp"), 2)
    order = bits_of(pairs)
    width = d_key.shape[1]
    moves, flows = [], []
    for way, source in zip((order, order[::-1]), (d_keys_all, d_values_all)):
        mine, theirs = take(2)
        moves.append(
            Pairwise(
                [
                    (
                        source.at[2 * pair + parity],
                        mine.at[pair],
                        source.at[2 * pair + 1 - parity],
                        theirs.at[pair],
                    )
                    for pair in range(pairs)
                ],
                take(3),
            )
        )

        def own(mask, target, columns, mine=mine, theirs=theirs):
            return mine[target, :, columns].astype(WIDE) + theirs[target, :, columns].astype(WIDE)

        flows.append(Halving(pairs, way, own, take(4)))
    (total,) = take(1)
    greet(member_peers(2 * pairs))
    for move in moves:
        move.start()
    for move, flow in zip(moves, flows):
        move.ready()
        flow.push(flow.masks[0])
    late = pl.ds(PROMPT_DEV, d_key.shape[0] - PROMPT_DEV)
    d_key[late] = d_key_own[...]
    d_value[late] = d_value_own[...]
    for index in range(1, pairs - 1):
        for flow in flows:
            flow.push(flow.masks[index])
    early = pl.ds(0, PROMPT_DEV)
    flows[0].end(total)
    for start in range(0, width, HEAD):
        d_key[early, start : start + HEAD] = rotate(
            total[:, start : start + HEAD], cosine[early], -sine[early]
        ).astype(LOW)
    flows[1].end(d_value.at[early])
    for move, flow in zip(moves, flows):
        flow.sent()
        move.sent()


def owner(members, d_keys_all, d_values_all, d_key_own, d_value_own, cosine, sine):
    width = d_key_own.shape[1]
    rows = cosine.shape[0]
    pairs = members // 2
    flow = (
        [pltpu.VMEM((pairs, PROMPT_DEV, width), LOW)] * 2
        + Pairwise.sems(pairs)
        + Halving.scratch(pairs, PROMPT_DEV, width)
    )
    return pl.pallas_call(
        functools.partial(owner_kernel, pairs),
        out_shape=[shape((rows, width), LOW)] * 2,
        in_specs=[ANY, ANY] + [VMEM] * 4,
        out_specs=[VMEM] * 2,
        scratch_shapes=flow * 2 + [pltpu.VMEM((PROMPT_DEV, width), WIDE)],
        compiler_params=pltpu.CompilerParams(
            collective_id=4, has_side_effects=True, vmem_limit_bytes=VMEM_LIMIT
        ),
        name="owner",
    )(d_keys_all, d_values_all, d_key_own, d_value_own, cosine, sine)


def first_kernel(
    count,
    pairs,
    grad_resid,
    d_query,
    d_key,
    d_value,
    w_query,
    w_key,
    w_value,
    states,
    act,
    mixed,
    branch_low,
    hidden,
    out_low,
    far_query,
    far_key,
    far_value,
    input_grad,
    grad_down,
    grad_out,
    grad_query,
    grad_key,
    grad_value,
    inner_total,
    part,
    state,
    weight,
    state_sem,
    weight_sem,
    *refs,
):
    take = taker(refs)
    line = Line(count, take(Line.scratch_count))
    order = bits_of(pairs)
    sides = []
    for left, rights, way in (
        (out_low, (hidden,), order),
        (act, (far_query, far_key, far_value), order[::-1]),
        (branch_low, (mixed,), order[::-1]),
    ):
        lhs, rhs = Lhs(left, take(4)), Rhs(rights, take(4))
        sides.append((lhs, rhs, Halving(pairs, way, product_of(lhs, rhs), take(4), *take(1))))
    rows = state.shape[0]
    fetch = pltpu.make_async_copy(
        states.at[pl.ds(pl.multiple_of(line.here * rows, rows), rows)], state, state_sem
    )
    loads = [
        pltpu.make_async_copy(source, weight.at[index], weight_sem.at[index])
        for index, source in enumerate((w_query, w_key, w_value))
    ]
    for load in loads:
        load.start()
    fetch.start()
    greet(line.peers() + member_peers(2 * pairs))
    for lhs, rhs, _ in sides:
        lhs.start()
        rhs.start()
    for load in loads:
        load.wait()
    tile = 512
    for start in range(0, part.shape[1], tile):
        columns = pl.ds(start, tile)
        part[:, columns] = (
            dot(d_query[...], weight[0, columns], 1, 1)
            + dot(d_key[...], weight[1, columns], 1, 1)
            + dot(d_value[...], weight[2, columns], 1, 1)
        )
    fetch.wait()

    def finish(group):
        span = pl.ds(group * line.rows, line.rows)
        normed, inverse = norm_rows(state[span])
        input_grad[line.span(group, line.here)] = (
            grad_resid[span] + norm_back(line.total[...], normed, inverse)
        ).astype(LOW)

    line.reduce(part, input_grad, finish, beside(order, sides))
    for (_, _, flow), target in zip(sides, (grad_down, inner_total, grad_out)):
        flow.end(target)
    width = grad_query.shape[1]
    for index, target in enumerate((grad_query, grad_key, grad_value)):
        target[...] = inner_total[:, index * width : index * width + width]
    for lhs, rhs, flow in sides:
        flow.sent()
        lhs.sent()
        rhs.sent()
    line.sent(input_grad)


def first(
    count,
    members,
    grad_resid,
    weights,
    states,
    act,
    mixed,
    branch_low,
    hidden,
    out_low,
    d_query,
    d_key,
    d_value,
):
    rows, depth = states.shape
    width = d_query.shape[1]
    units = hidden.shape[1]
    pairs = members // 2
    block = depth // members
    scratch = []
    for wide in (units, 3 * width, width):
        scratch += Lhs.scratch(pairs, rows, block) + Rhs.scratch(rows, wide)
        scratch += Halving.scratch(pairs, block, wide) + [pltpu.VMEM((block, wide), WIDE)]
    return pl.pallas_call(
        functools.partial(first_kernel, count, pairs),
        out_shape=[
            shape((rows, depth), LOW),
            shape((block, units), LOW),
        ]
        + [shape((block, width), LOW)] * 4,
        in_specs=[VMEM] * 4 + [ANY] * 12,
        out_specs=[VMEM] * 6,
        scratch_shapes=[
            pltpu.VMEM((block, 3 * width), LOW),
            pltpu.VMEM((rows, depth), WIDE),
            pltpu.VMEM((rows // count, depth), WIDE),
            pltpu.VMEM((3, depth, width), LOW),
            DMA,
            DMA((3,)),
        ]
        + Line.scratch(count, GROUPS, rows // count, depth)
        + scratch,
        compiler_params=pltpu.CompilerParams(
            collective_id=5, has_side_effects=True, vmem_limit_bytes=VMEM_LIMIT
        ),
        name="first",
    )(
        grad_resid,
        d_query,
        d_key,
        d_value,
        *weights,
        states,
        in_blocks(act, members),
        mixed,
        in_blocks(branch_low, members),
        hidden,
        in_blocks(out_low, members),
        d_query,
        d_key,
        d_value,
    )


def widen_kernel(flat, early, late, *refs):
    count = len(refs) // 2
    sources, whole, targets = refs[:count], refs[count], refs[count + 1 :]
    half = early.shape[0]
    whole[pl.ds(0, half)] = early[...].astype(WIDE)
    whole[pl.ds(half, half)] = late[...].astype(WIDE)
    for index, (source, target) in enumerate(zip(sources, targets)):
        values = source[...].astype(WIDE)
        target[...] = values if index < flat else values.T


def widen(count, early, late, plain, turned):
    def rows(array):
        return pl.BlockSpec((array.shape[0] // count, array.shape[1]), lambda i: (i, 0))

    def columns(array):
        return pl.BlockSpec((array.shape[0], array.shape[1] // count), lambda i: (0, i))

    flipped = [shape(array.shape[::-1], WIDE) for array in turned]
    whole = shape((2 * early.shape[0], early.shape[1]), WIDE)
    return pl.pallas_call(
        functools.partial(widen_kernel, len(plain)),
        out_shape=[whole] + [shape(array.shape, WIDE) for array in plain] + flipped,
        grid=(count,),
        in_specs=[rows(array) for array in (early, late, *plain)]
        + [columns(array) for array in turned],
        out_specs=[rows(array) for array in (whole, *plain, *flipped)],
        compiler_params=pltpu.CompilerParams(vmem_limit_bytes=VMEM_LIMIT),
        name="widen",
    )(early, late, *plain, *turned)


def body(
    states,
    w_query,
    w_key,
    w_value,
    w_out,
    w_gate,
    w_up,
    w_down,
    group_id,
    slice_start,
    cont_group,
    cotangent,
):
    rows = states.shape[0]
    members = lax.axis_size("dp")
    count = lax.axis_size("tensor")
    member = lax.axis_index("dp")
    index = jnp.arange(rows, dtype=jnp.int32)
    everyone = jnp.arange(members, dtype=jnp.int32)
    own_start = jnp.sum(jnp.where(everyone == member, slice_start, 0))
    prompt = members // 2 * PROMPT_DEV
    positions = jnp.where(index < PROMPT_DEV, own_start + index, prompt + index - PROMPT_DEV)
    frequency = 10000.0 ** (-np.arange(HEAD // 2) * 2.0 / HEAD)
    frequency = np.concatenate([frequency, frequency]).astype(np.float32)
    sign = np.repeat([-1.0, 1.0], HEAD // 2).astype(np.float32)
    angles = positions.astype(WIDE)[:, None] * frequency[None, :]
    cosine = jnp.cos(angles)
    sine = jnp.sin(angles) * sign[None, :]
    readers = (group_id, slice_start, cont_group)

    merged = members * PROMPT_DEV * w_query.shape[1] * 2 * 4 <= 16 * 2**20
    if merged:
        act_one, query, key, value, out_low, d_hidden, mixed, attended, log_total, *everyones = (
            gather_attend(
                members, readers, w_query, w_key, w_value, w_down, states, cotangent, cosine, sine
            )
        )
    else:
        act_one, query, key, value, out_low, *everyones = project(
            members, states, w_query, w_key, w_value, cosine, sine, cotangent
        )
        d_hidden = dot(out_low, w_down, 1, 1).astype(LOW)
        mixed, attended, log_total = attend(readers, query, key, value, *everyones)
    act_two, resid = branch(count, mixed, w_out, states)
    ffn, ffn_late, d_act_two, hidden, d_gate, d_up = feed(act_two, resid, d_hidden, w_gate, w_up, w_down)
    branch_low, grad_resid, own_out, grad_gate, grad_up = second(
        count, members, d_act_two, ffn, resid, cotangent, act_two, d_gate, d_up
    )
    ffn_late, branch_low = lax.optimization_barrier((ffn_late, branch_low))
    late_out = lax.psum(ffn_late, "tensor")
    kept = (query, key, value, branch_low, w_out, attended, log_total, cosine, sine)
    if merged:
        d_query, d_key, d_value, early_out = back_owner(
            members, count, readers, *everyones, *kept, own_out
        )
    else:
        d_query, *d_everyones = attend_back(
            readers, query, key, value, *everyones, branch_low, w_out, attended, log_total, cosine, sine
        )
        d_key, d_value = owner(members, *d_everyones, cosine, sine)
        early_out = lax.all_gather(own_out, "tensor", axis=0, tiled=True)
    input_grad, grad_down, grad_out, *grad_inner = first(
        count,
        members,
        grad_resid,
        (w_query, w_key, w_value),
        states,
        act_one,
        mixed,
        branch_low,
        hidden,
        out_low,
        d_query,
        d_key,
        d_value,
    )
    *plain, grad_out, grad_down = widen(
        count,
        early_out,
        late_out,
        (input_grad, *grad_inner, grad_gate, grad_up),
        (grad_out, grad_down),
    )
    return (*plain[:5], grad_out, *plain[5:], grad_down)


def solution(mesh):
    placed = (
        P("dp", None),
        P(None, "tensor"),
        P(None, "tensor"),
        P(None, "tensor"),
        P("tensor", None),
        P(None, "tensor"),
        P(None, "tensor"),
        P("tensor", None),
        P(),
        P(),
        P("dp"),
        P("dp", None),
    )
    return jax.shard_map(
        body,
        mesh=mesh,
        in_specs=placed,
        out_specs=(
            P("dp", None),
            P("dp", None),
            P("dp", "tensor"),
            P("dp", "tensor"),
            P("dp", "tensor"),
            P("tensor", "dp"),
            P("dp", "tensor"),
            P("dp", "tensor"),
            P("tensor", "dp"),
        ),
        check_vma=False,
    )
```

```python
import functools

import jax
import jax.numpy as jnp
import numpy as np
from jax import lax
from jax.experimental import pallas as pl
from jax.experimental.pallas import tpu as pltpu
from jax.sharding import PartitionSpec as P

HEAD = 128
PROMPT_DEV = 384
EPSILON = 1e-05
NEGATIVE = -1e30
SCALE = HEAD ** (-0.5)
SCALE_TWO = float(SCALE * np.log2(np.e))
LOW = jnp.bfloat16
WIDE = jnp.float32
MESH = pl.DeviceIdType.MESH
ANY = pl.BlockSpec(memory_space=pl.ANY)
VMEM = pl.BlockSpec(memory_space=pltpu.VMEM)
DMA = pltpu.SemaphoreType.DMA
VMEM_LIMIT = 62 * 2**20
GROUPS = 2
PIECE = 512


def dot(left, right, left_dim=1, right_dim=0):
    return lax.dot_general(
        left, right, (((left_dim,), (right_dim,)), ((), ())), preferred_element_type=WIDE
    )


def shape(dims, dtype):
    return jax.ShapeDtypeStruct(dims, dtype)


def norm_rows(values):
    row_mean = jnp.mean(values, axis=-1, keepdims=True)
    centred = values - row_mean
    inverse = lax.rsqrt(jnp.mean(centred * centred, axis=-1, keepdims=True) + EPSILON)
    return centred * inverse, inverse


def norm_back(gradient, normed, inverse):
    return inverse * (
        gradient
        - jnp.mean(gradient, axis=-1, keepdims=True)
        - normed * jnp.mean(gradient * normed, axis=-1, keepdims=True)
    )


def rotate(values, cosine, sine):
    return values * cosine + pltpu.roll(values, HEAD // 2, 1) * sine


def flip(index, mask):
    out, bit = index, 1
    while bit <= mask:
        if mask & bit:
            out = out + bit * (1 - 2 * lax.rem(lax.div(index, bit), 2))
        bit *= 2
    return out


def bits_of(count):
    return list(range(count.bit_length() - 1))


def hail(peers):
    barrier = pltpu.get_barrier_semaphore()
    for peer in peers:
        pl.semaphore_signal(barrier, inc=1, device_id=peer, device_id_type=MESH)


def heed(peers):
    pl.semaphore_wait(pltpu.get_barrier_semaphore(), len(peers))


def greet(peers):
    hail(peers)
    heed(peers)


def remote(source, target, send_sem, recv_sem, device):
    return pltpu.make_async_remote_copy(
        src_ref=source,
        dst_ref=target,
        send_sem=send_sem,
        recv_sem=recv_sem,
        device_id=device,
        device_id_type=MESH,
    )


class Line:
    scratch_count = 10

    @staticmethod
    def scratch(count, groups, rows, width):
        rows = rows // groups
        return [
            pltpu.VMEM((rows, width), WIDE),
            pltpu.VMEM((groups, count, rows, width), LOW),
            pltpu.VMEM((groups, count, rows, width), LOW),
            pltpu.VMEM((groups, count, rows, width), LOW),
            DMA((groups, count)),
            DMA((groups, count)),
            DMA((groups, count)),
            DMA((groups, count)),
            DMA((groups, count)),
            DMA((groups, count)),
        ]

    def __init__(self, count, refs):
        self.count = count
        (
            self.total,
            self.outgoing,
            self.from_left,
            self.from_right,
            self.out_sem,
            self.left_sem,
            self.right_sem,
            self.to_right_sem,
            self.to_left_sem,
            self.got_sem,
        ) = refs
        self.groups = self.outgoing.shape[0]
        self.rows = self.total.shape[0]
        self.here = lax.axis_index("tensor")
        member = lax.axis_index("dp")
        self.right = (member, lax.rem(self.here + 1, count))
        self.left = (member, lax.rem(self.here + count - 1, count))

    def peers(self):
        return [self.left, self.right]

    def span(self, group, chunk):
        start = chunk * (self.rows * self.groups) + group * self.rows
        return pl.ds(pl.multiple_of(start, self.rows), self.rows)

    def rightward(self, group, chunk):
        return remote(
            self.outgoing.at[group, chunk],
            self.from_left.at[group, chunk],
            self.out_sem.at[group, chunk],
            self.left_sem.at[group, chunk],
            self.right,
        )

    def leftward(self, group, chunk):
        return remote(
            self.outgoing.at[group, chunk],
            self.from_right.at[group, chunk],
            self.out_sem.at[group, chunk],
            self.right_sem.at[group, chunk],
            self.left,
        )

    def add_and_pass(self, group, chunk, part, right, wait):
        copy, came = (self.rightward, self.from_left) if right else (self.leftward, self.from_right)
        total = part[self.span(group, chunk)].astype(WIDE)
        if wait:
            copy(group, chunk).wait_recv()
            total += came[group, chunk].astype(WIDE)
        self.outgoing[group, chunk] = total.astype(LOW)
        copy(group, chunk).start()

    def scatter_slot(self, group, slot, part):
        here, count = self.here, self.count
        ahead, back = count - 1 + here - slot, slot - (count - 1 - here)
        if slot == 0:

            @pl.when(here == 0)
            def _():
                self.add_and_pass(group, ahead, part, True, False)

            @pl.when(here == count - 1)
            def _():
                self.add_and_pass(group, back, part, False, False)

            return
        for wait in (False, True):

            @pl.when((here <= slot) & ((here > 0) if wait else (here == 0)))
            def _(wait=wait):
                self.add_and_pass(group, ahead, part, True, wait)

            @pl.when(
                (count - 1 - here <= slot) & ((here < count - 1) if wait else (here == count - 1))
            )
            def _(wait=wait):
                self.add_and_pass(group, back, part, False, wait)

    def scatter_end(self, group, part):
        here = self.here
        last = self.count - 1

        def left():
            self.rightward(group, here).wait_recv()
            return self.from_left[group, here].astype(WIDE)

        def right():
            self.leftward(group, here).wait_recv()
            return self.from_right[group, here].astype(WIDE)

        @pl.when(here == 0)
        def _():
            self.total[...] = part[self.span(group, here)].astype(WIDE) + right()

        @pl.when(here == last)
        def _():
            self.total[...] = part[self.span(group, here)].astype(WIDE) + left()

        @pl.when((here > 0) & (here < last))
        def _():
            self.total[...] = part[self.span(group, here)].astype(WIDE) + left() + right()

    def passing(self, whole, group, chunk, right):
        ref = whole.at[self.span(group, chunk)]
        return remote(
            ref,
            ref,
            (self.to_right_sem if right else self.to_left_sem).at[group, chunk],
            self.got_sem.at[group, chunk],
            self.right if right else self.left,
        )

    def gather_slot(self, whole, group, distance):
        here, count = self.here, self.count

        @pl.when(here - distance >= 0)
        def _():
            if distance:
                self.passing(whole, group, here - distance, True).wait_recv()

            @pl.when(here < count - 1)
            def _():
                self.passing(whole, group, here - distance, True).start()

        @pl.when(here + distance <= count - 1)
        def _():
            if distance:
                self.passing(whole, group, here + distance, False).wait_recv()

            @pl.when(here > 0)
            def _():
                self.passing(whole, group, here + distance, False).start()

    def reduce(self, part, whole, finish, beside=()):
        beside = list(beside)
        last = self.count - 1
        self.scatter_slot(0, 0, part)
        for group in range(self.groups):
            for slot in range(1, last):
                if beside:
                    beside.pop(0)()
                self.scatter_slot(group, slot, part)
                if group:
                    self.gather_slot(whole, group - 1, slot)
            if group + 1 < self.groups:
                self.scatter_slot(group + 1, 0, part)
            if group:
                self.gather_slot(whole, group - 1, last)
            self.scatter_end(group, part)
            finish(group)
            self.gather_slot(whole, group, 0)
        for distance in range(1, self.count):
            if beside:
                beside.pop(0)()
            self.gather_slot(whole, self.groups - 1, distance)
        for act in beside:
            act()

    def sent(self, whole=None):
        here, count = self.here, self.count
        for group in range(self.groups):
            for chunk in range(count):

                @pl.when(here != chunk)
                def _(group=group, chunk=chunk):
                    self.rightward(group, chunk).wait_send()

                if whole is None:
                    continue

                @pl.when((chunk <= here) & (here < count - 1))
                def _(group=group, chunk=chunk):
                    self.passing(whole, group, chunk, True).wait_send()

                @pl.when((chunk >= here) & (here > 0))
                def _(group=group, chunk=chunk):
                    self.passing(whole, group, chunk, False).wait_send()


class Halving:
    @staticmethod
    def masks_of(pairs, order):
        def stage(mask):
            return min(order.index(bit) for bit in order if mask >> bit & 1)

        return sorted(range(1, pairs), key=lambda mask: (stage(mask), -mask.bit_count()))

    @staticmethod
    def scratch(pairs, block, width):
        count = pairs - 1
        pieces = max(1, width // PIECE)
        return [
            pltpu.VMEM((count, block, width), LOW),
            pltpu.VMEM((count, block, width), LOW),
            DMA((count, pieces)),
            DMA((count, pieces)),
        ]

    def __init__(self, pairs, order, own, refs, kept=None):
        self.order, self.own, self.kept = order, own, kept
        self.send, self.recv, self.send_sem, self.recv_sem = refs
        self.masks = Halving.masks_of(pairs, order)
        self.pieces = self.send_sem.shape[1]
        self.piece = self.send.shape[2] // self.pieces
        self.member = lax.axis_index("dp")
        self.tensor = lax.axis_index("tensor")
        self.high = lax.div(self.member, 2)

    def stage(self, mask):
        return min(
            [self.order.index(bit) for bit in self.order if mask >> bit & 1],
            default=len(self.order),
        )

    def steps(self, stage):
        return [mask for mask in self.masks if self.stage(mask) == stage]

    def columns(self, piece):
        return pl.ds(piece * self.piece, self.piece)

    def copy(self, mask, piece):
        index = self.masks.index(mask)
        bit = 1 << self.order[self.stage(mask)]
        return remote(
            self.send.at[index, :, self.columns(piece)],
            self.recv.at[index, :, self.columns(piece)],
            self.send_sem.at[index, piece],
            self.recv_sem.at[index, piece],
            (flip(self.member, bit * 2), self.tensor),
        )

    def settle(self):
        for piece in range(self.pieces):
            columns = self.columns(piece)
            self.kept[:, columns] = self.own(0, flip(self.high, 0), columns)

    def fill(self, mask, piece, out):
        columns = self.columns(piece)
        if self.kept is not None and not mask:
            total = self.kept[:, columns]
        else:
            total = self.own(mask, flip(self.high, mask), columns)
        for bit in self.order[: self.stage(mask)]:
            slot = mask | 1 << bit
            self.copy(slot, piece).wait_recv()
            total += self.recv[self.masks.index(slot), :, columns].astype(WIDE)
        out[:, columns] = total.astype(out.dtype)

    def push_piece(self, mask, piece):
        self.fill(mask, piece, self.send.at[self.masks.index(mask)])
        self.copy(mask, piece).start()

    def push(self, mask):
        for piece in range(self.pieces):
            self.push_piece(mask, piece)

    def end(self, out):
        for piece in range(self.pieces):
            self.fill(0, piece, out)

    def sent(self):
        for mask in self.masks:
            for piece in range(self.pieces):
                self.copy(mask, piece).wait_send()


class Pairwise:
    def __init__(self, moves, refs):
        self.moves, self.done = moves, False
        self.local_sem, self.send_sem, self.recv_sem = refs
        member = lax.axis_index("dp")
        self.partner = (flip(member, 1), lax.axis_index("tensor"))

    @staticmethod
    def sems(count):
        return [DMA((count,)), DMA((count,)), DMA((count,))]

    def local(self, index):
        source, target, _, _ = self.moves[index]
        return pltpu.make_async_copy(source, target, self.local_sem.at[index])

    def across(self, index):
        _, _, source, target = self.moves[index]
        return remote(
            source, target, self.send_sem.at[index], self.recv_sem.at[index], self.partner
        )

    def start(self, index=None):
        for index in range(len(self.moves)) if index is None else [index]:
            self.across(index).start()
            self.local(index).start()

    def ready(self, index=None):
        if index is None and self.done:
            return
        self.done = index is None
        for index in range(len(self.moves)) if index is None else [index]:
            self.local(index).wait()
            self.across(index).wait_recv()

    def sent(self):
        for index in range(len(self.moves)):
            self.across(index).wait_send()


class Lhs(Pairwise):
    @staticmethod
    def scratch(pairs, rows, block):
        return [pltpu.VMEM((pairs, 2 * rows, block), LOW)] + Pairwise.sems(pairs)

    def __init__(self, source, refs):
        self.held = refs[0]
        pairs, rows, block = self.held.shape
        rows = rows // 2
        parity = lax.rem(lax.axis_index("dp"), 2)

        def columns(index):
            if len(source.shape) == 3:
                return source.at[index]
            return source.at[:, pl.ds(pl.multiple_of(index * block, block), block)]

        super().__init__(
            [
                (
                    columns(2 * pair + parity),
                    self.held.at[pair, pl.ds(0, rows)],
                    columns(2 * pair + 1 - parity),
                    self.held.at[pair, pl.ds(rows, rows)],
                )
                for pair in range(pairs)
            ],
            refs[1:],
        )


class Rhs(Pairwise):
    @staticmethod
    def scratch(rows, width):
        return [pltpu.VMEM((2 * rows, width), LOW)] + Pairwise.sems(width // PIECE)

    def __init__(self, sources, refs):
        self.held = refs[0]
        rows = self.held.shape[0] // 2
        moves, at = [], 0
        for source in sources:
            for start in range(0, source.shape[1], PIECE):
                columns = pl.ds(at, PIECE)
                at += PIECE
                here = source.at[:, pl.ds(start, PIECE)]
                moves.append(
                    (
                        here,
                        self.held.at[pl.ds(0, rows), columns],
                        here,
                        self.held.at[pl.ds(rows, rows), columns],
                    )
                )
        super().__init__(moves, refs[1:])


def product_of(lhs, rhs):
    def own(mask, target, columns):
        return dot(lhs.held[target], rhs.held[:, columns], 0, 0)

    return own


def taker(refs):
    refs = list(refs)

    def take(count):
        out = refs[:count]
        del refs[:count]
        return out

    return take


def in_blocks(left, members):
    block = left.shape[1] // members
    if block % 128 == 0:
        return left
    return left.reshape(left.shape[0], members, block).transpose(1, 0, 2)


def member_peers(members):
    member, tensor = lax.axis_index("dp"), lax.axis_index("tensor")
    return [(flip(member, 1 << bit), tensor) for bit in bits_of(members)]


def project_kernel(
    members,
    states,
    w_query,
    w_key,
    w_value,
    cosine,
    sine,
    act,
    query,
    key,
    value,
    keys_all,
    values_all,
    send_sem,
    recv_sem,
    local_sem,
):
    member, tensor = lax.axis_index("dp"), lax.axis_index("tensor")
    width = query.shape[1]
    greet(member_peers(members))
    rows = 64
    for start in range(0, states.shape[0], rows):
        span = pl.ds(start, rows)
        act[span] = norm_rows(states[span])[0].astype(LOW)

    def turned(weight, out):
        linear = dot(act[...], weight[...])
        for start in range(0, width, HEAD):
            out[:, start : start + HEAD] = rotate(
                linear[:, start : start + HEAD], cosine[...], sine[...]
            ).astype(LOW)

    high = [bit for bit in bits_of(members) if bit]
    orders = (high + [0], high[::-1] + [0])
    owns, alls = (key, value), (keys_all, values_all)

    def copy(flow, mask, bit):
        slot = mask | 1 << bit
        place = alls[flow].at[flip(member, mask)]
        return remote(
            place if mask else owns[flow].at[pl.ds(0, PROMPT_DEV)],
            place,
            send_sem.at[flow, slot],
            recv_sem.at[flow, slot],
            (flip(member, 1 << bit), tensor),
        )

    def forward(flow, mask):
        order = orders[flow]
        last = max([order.index(bit) for bit in order if mask >> bit & 1], default=-1)
        for bit in order[last + 1 :]:
            copy(flow, mask, bit).start()

    def came_by(flow, mask):
        order = orders[flow]
        bit = order[max(order.index(bit) for bit in order if mask >> bit & 1)]
        return copy(flow, mask ^ 1 << bit, bit)

    def keep(flow):
        return pltpu.make_async_copy(
            owns[flow].at[pl.ds(0, PROMPT_DEV)], alls[flow].at[member], local_sem.at[flow]
        )

    turned(w_key, key)
    forward(0, 0)
    value[...] = dot(act[...], w_value[...]).astype(LOW)
    forward(1, 0)
    keep(0).start()
    keep(1).start()
    turned(w_query, query)
    masks = range(1, members)
    inner = sorted([mask for mask in masks if not mask & 1], key=lambda mask: mask.bit_count())
    for mask in inner:
        for flow in (0, 1):
            turn = flow if not mask & 2 else flow
            came_by(turn, mask).wait_recv()
            forward(turn, mask)
    for mask in masks:
        if mask & 1:
            for flow in (0, 1):
                came_by(flow, mask).wait_recv()
    for flow in (0, 1):
        keep(flow).wait()
        for mask in masks:
            came_by(flow, mask).wait_send()


def project(members, states, w_query, w_key, w_value, cosine, sine):
    rows, depth = states.shape
    width = w_query.shape[1]
    return pl.pallas_call(
        functools.partial(project_kernel, members),
        out_shape=[
            shape((rows, depth), LOW),
            shape((rows, width), LOW),
            shape((rows, width), LOW),
            shape((rows, width), LOW),
            shape((members, PROMPT_DEV, width), LOW),
            shape((members, PROMPT_DEV, width), LOW),
        ],
        in_specs=[VMEM] * 6,
        out_specs=[VMEM] * 4 + [ANY] * 2,
        scratch_shapes=[DMA((2, members)), DMA((2, members)), DMA((2,))],
        compiler_params=pltpu.CompilerParams(
            collective_id=1, has_side_effects=True, vmem_limit_bytes=VMEM_LIMIT
        ),
        name="project",
    )(states, w_query, w_key, w_value, cosine, sine)


def make_plan(half, group_id, slice_start, cont_group, plan):
    member = lax.axis_index("dp")
    own, other = group_id[member], cont_group[0]
    plan[0] = lax.div(slice_start[member], PROMPT_DEV)

    def step(index, _):
        rank = lax.div(slice_start[index], PROMPT_DEV)

        @pl.when(group_id[index] == own)
        def _():
            plan[1 + rank] = index

        @pl.when(group_id[index] == other)
        def _():
            plan[1 + half + rank] = index

        return 0

    lax.fori_loop(0, 2 * half, step, 0)


def attend_kernel(
    half,
    group_id,
    slice_start,
    cont_group,
    query,
    key,
    value,
    keys_all,
    values_all,
    mixed,
    attended,
    log_total,
    plan,
):
    @pl.when(pl.program_id(0) == 0)
    def _():
        make_plan(half, group_id, slice_start, cont_group, plan)

    def part(start, count, steps, offset):
        span = pl.ds(start, count)
        queries = query[span]
        allowed = lax.broadcasted_iota(jnp.int32, (count, count), 0) >= lax.broadcasted_iota(
            jnp.int32, (count, count), 1
        )
        scores = jnp.where(allowed, dot(queries, key[span], 1, 1) * SCALE, NEGATIVE)
        top = jnp.max(scores, axis=-1, keepdims=True)
        weights = jnp.exp(scores - top)
        total = jnp.sum(weights, axis=-1, keepdims=True)
        result = dot(weights.astype(LOW), value[span])

        def step(index, carry):
            top, total, result = carry
            place = plan[offset + index]
            scores = dot(queries, keys_all[place], 1, 1) * SCALE
            higher = jnp.maximum(top, jnp.max(scores, axis=-1, keepdims=True))
            fade = jnp.exp(top - higher)
            weights = jnp.exp(scores - higher)
            total = total * fade + jnp.sum(weights, axis=-1, keepdims=True)
            result = result * fade + dot(weights.astype(LOW), values_all[place])
            return higher, total, result

        top, total, result = lax.fori_loop(0, steps, step, (top, total, result))
        result = result / total
        mixed[span] = result.astype(LOW)
        attended[span] = result
        log_total[span] = jnp.broadcast_to(top + jnp.log(total), (count, HEAD))

    part(0, PROMPT_DEV, plan[0], 1)
    part(PROMPT_DEV, query.shape[0] - PROMPT_DEV, half, 1 + half)


def attend(readers, query, key, value, keys_all, values_all):
    rows, width = query.shape
    members = keys_all.shape[0]
    head = pl.BlockSpec((rows, HEAD), lambda h, *_: (0, h))
    every = pl.BlockSpec((members, PROMPT_DEV, HEAD), lambda h, *_: (0, 0, h))
    return pl.pallas_call(
        functools.partial(attend_kernel, members // 2),
        out_shape=[
            shape((rows, width), LOW),
            shape((rows, width), WIDE),
            shape((rows, width), WIDE),
        ],
        grid_spec=pltpu.PrefetchScalarGridSpec(
            num_scalar_prefetch=3,
            grid=(width // HEAD,),
            in_specs=[head, head, head, every, every],
            out_specs=[head, head, head],
            scratch_shapes=[pltpu.SMEM((members + 1,), jnp.int32)],
        ),
        compiler_params=pltpu.CompilerParams(vmem_limit_bytes=VMEM_LIMIT),
        name="attend",
    )(*readers, query, key, value, keys_all, values_all)


def attend_back_kernel(
    half,
    group_id,
    slice_start,
    cont_group,
    query,
    key,
    value,
    keys_all,
    values_all,
    branch_low,
    w_out,
    attended,
    log_total,
    cosine,
    sine,
    d_query,
    d_keys_all,
    d_values_all,
    d_key_own,
    d_value_own,
    d_mixed,
    key_total,
    value_total,
    plan,
):
    @pl.when(pl.program_id(0) == 0)
    def _():
        make_plan(half, group_id, slice_start, cont_group, plan)

    d_mixed[...] = dot(branch_low[...], w_out[...], 1, 1).astype(LOW)
    key_total[...] = jnp.zeros_like(key_total)
    value_total[...] = jnp.zeros_like(value_total)

    def part(start, count, steps, offset):
        span = pl.ds(start, count)
        queries, d_attended = query[span], d_mixed[span]
        log_sum = log_total[span][:, :1]
        center = jnp.sum(d_attended.astype(WIDE) * attended[span], axis=-1, keepdims=True)

        def back(scores, keys, values):
            probabilities = jnp.exp(scores - log_sum)
            d_scores = (probabilities * (dot(d_attended, values, 1, 1) - center)).astype(LOW)
            return (
                dot(d_scores, keys),
                dot(d_scores, queries, 0, 0),
                dot(probabilities.astype(LOW), d_attended, 0, 0),
            )

        allowed = lax.broadcasted_iota(jnp.int32, (count, count), 0) >= lax.broadcasted_iota(
            jnp.int32, (count, count), 1
        )
        scores = jnp.where(allowed, dot(queries, key[span], 1, 1) * SCALE, NEGATIVE)
        d_queries, d_own_keys, d_own_values = back(scores, key[span], value[span])

        def step(index, d_queries):
            place = plan[offset + index]
            keys, values = keys_all[place], values_all[place]
            more, d_keys, d_values = back(dot(queries, keys, 1, 1) * SCALE, keys, values)
            key_total[place] += d_keys
            value_total[place] += d_values
            return d_queries + more

        d_queries = lax.fori_loop(0, steps, step, d_queries) * SCALE
        d_query[span] = rotate(d_queries, cosine[span], -sine[span]).astype(LOW)
        return d_own_keys, d_own_values

    member = lax.axis_index("dp")
    d_own_keys, d_own_values = part(0, PROMPT_DEV, plan[0], 1)
    key_total[member] += d_own_keys
    value_total[member] += d_own_values
    d_own_keys, d_own_values = part(PROMPT_DEV, query.shape[0] - PROMPT_DEV, half, 1 + half)
    late = pl.ds(PROMPT_DEV, query.shape[0] - PROMPT_DEV)
    d_key_own[...] = rotate(d_own_keys * SCALE, cosine[late], -sine[late]).astype(LOW)
    d_value_own[...] = d_own_values.astype(LOW)
    d_keys_all[...] = (key_total[...] * SCALE).astype(LOW)
    d_values_all[...] = value_total[...].astype(LOW)


def attend_back(
    readers,
    query,
    key,
    value,
    keys_all,
    values_all,
    branch_low,
    w_out,
    attended,
    log_total,
    cosine,
    sine,
):
    rows, width = query.shape
    members = keys_all.shape[0]
    depth = branch_low.shape[1]
    late = rows - PROMPT_DEV
    heads = width // HEAD
    head = pl.BlockSpec((rows, HEAD), lambda h, *_: (0, h))
    every = pl.BlockSpec((members, PROMPT_DEV, HEAD), lambda h, *_: (0, 0, h))
    own = pl.BlockSpec((late, HEAD), lambda h, *_: (0, h))
    table = pl.BlockSpec((rows, HEAD), lambda h, *_: (0, 0))
    return pl.pallas_call(
        functools.partial(attend_back_kernel, members // 2),
        out_shape=[
            shape((rows, width), LOW),
            shape((members, PROMPT_DEV, width), LOW),
            shape((members, PROMPT_DEV, width), LOW),
            shape((late, width), LOW),
            shape((late, width), LOW),
        ],
        grid_spec=pltpu.PrefetchScalarGridSpec(
            num_scalar_prefetch=3,
            grid=(heads,),
            in_specs=[
                head,
                head,
                head,
                every,
                every,
                pl.BlockSpec((rows, depth), lambda h, *_: (0, 0)),
                pl.BlockSpec((HEAD, depth), lambda h, *_: (h, 0)),
                head,
                head,
                table,
                table,
            ],
            out_specs=[head, every, every, own, own],
            scratch_shapes=[
                pltpu.VMEM((rows, HEAD), LOW),
                pltpu.VMEM((members, PROMPT_DEV, HEAD), WIDE),
                pltpu.VMEM((members, PROMPT_DEV, HEAD), WIDE),
                pltpu.SMEM((members + 1,), jnp.int32),
            ],
        ),
        compiler_params=pltpu.CompilerParams(vmem_limit_bytes=VMEM_LIMIT),
        name="attend_back",
    )(
        *readers,
        query,
        key,
        value,
        keys_all,
        values_all,
        branch_low,
        w_out,
        attended,
        log_total,
        cosine,
        sine,
    )


def place_of(group_id, slice_start, group, rank):
    place = 0
    for index in range(group_id.shape[0]):
        found = (group_id[index] == group) & (slice_start[index] == rank * PROMPT_DEV)
        place = jnp.maximum(place, jnp.where(found, index, 0))
    return place


def own_part(rows):
    return lax.broadcasted_iota(jnp.int32, (rows, rows), 0) >= lax.broadcasted_iota(
        jnp.int32, (rows, rows), 1
    )


def gather_attend_kernel(
    members,
    group_id,
    slice_start,
    cont_group,
    w_query_in,
    w_key_in,
    w_value_in,
    states_in,
    table,
    act,
    query,
    key,
    value,
    cosine,
    sine,
    mixed,
    attended,
    log_total,
    keys_out,
    values_out,
    states,
    weights,
    load_sem,
    weight_sem,
    send_sem,
    recv_sem,
    keep_sem,
    out_sem,
    *every,
):
    member, tensor = lax.axis_index("dp"), lax.axis_index("tensor")
    heads = query.shape[0]
    keys_all, values_all = every[:heads], every[heads:]
    half = members // 2
    rows = states.shape[0]
    chunks = load_sem.shape[0]
    size = rows // chunks
    loads = []
    for index in range(chunks):
        span = pl.ds(index * size, size)
        loads.append(pltpu.make_async_copy(states_in.at[span], states.at[span], load_sem.at[index]))
    w_loads = [
        pltpu.make_async_copy(source, weights.at[index], weight_sem.at[index])
        for index, source in enumerate((w_key_in, w_value_in, w_query_in))
    ]
    for load in loads[:1] + w_loads[:1] + loads[1:] + w_loads[1:]:
        load.start()
    hail(member_peers(members))
    index = lax.broadcasted_iota(jnp.int32, cosine.shape, 0)
    prompt = half * PROMPT_DEV - PROMPT_DEV
    positions = index + jnp.where(index < PROMPT_DEV, slice_start[member], prompt)
    angles = positions.astype(WIDE) * table[:1]
    cosine[...] = jnp.cos(angles)
    sine[...] = jnp.sin(angles) * table[1:2]
    step = 64
    for index in range(chunks):
        loads[index].wait()
        for start in range(index * size, index * size + size, step):
            span = pl.ds(start, step)
            act[span] = norm_rows(states[span])[0].astype(LOW)

    def turned(weight, out):
        linear = dot(act[...], weight)
        for head in range(heads):
            out[head] = rotate(
                linear[:, head * HEAD : head * HEAD + HEAD], cosine[...], sine[...]
            ).astype(LOW)

    high = [bit for bit in bits_of(members) if bit]
    orders = (high + [0], high[::-1] + [0])
    owns, alls = (key, value), (keys_all, values_all)
    early = pl.ds(0, PROMPT_DEV)

    def copy(flow, head, mask, bit):
        slot = mask | 1 << bit
        place = alls[flow][head].at[flip(member, mask)]
        return remote(
            place if mask else owns[flow].at[head, early],
            place,
            send_sem.at[flow, head, slot],
            recv_sem.at[flow, head, slot],
            (flip(member, 1 << bit), tensor),
        )

    def forward(flow, head, mask):
        order = orders[flow]
        last = max([order.index(bit) for bit in order if mask >> bit & 1], default=-1)
        for bit in order[last + 1 :]:
            copy(flow, head, mask, bit).start()

    def came_by(flow, head, mask):
        order = orders[flow]
        bit = order[max(order.index(bit) for bit in order if mask >> bit & 1)]
        return copy(flow, head, mask ^ 1 << bit, bit)

    def keep(flow, head):
        return pltpu.make_async_copy(
            owns[flow].at[head, early], alls[flow][head].at[member], keep_sem.at[flow, head]
        )

    def write(flow, head):
        return pltpu.make_async_copy(
            alls[flow][head], (keys_out, values_out)[flow].at[head], out_sem.at[flow, head]
        )

    masks = range(1, members)
    levels = len(high)

    def own_sends(head):
        if head < heads:
            for flow in (0, 1):
                forward(flow, head, 0)
            for flow in (0, 1):
                keep(flow, head).start()

    def level(head, count):
        if head < heads:
            for mask in masks:
                if not mask & 1 and mask.bit_count() == count:
                    for flow in (0, 1):
                        came_by(flow, head, mask).wait_recv()
                        forward(flow, head, mask)

    def complete(head):
        for flow in (0, 1):
            for mask in masks:
                if mask & 1:
                    came_by(flow, head, mask).wait_recv()
            keep(flow, head).wait()
            write(flow, head).start()

    own_group, other_group = group_id[member], cont_group[0]
    own_start = slice_start[member]
    own_places = [place_of(group_id, slice_start, own_group, rank) for rank in range(half)]
    other_places = [place_of(group_id, slice_start, other_group, rank) for rank in range(half)]
    block = 128

    def attend_rows(head, start, places, whole):
        span = pl.ds(start, block)
        queries = query[head, span]
        scores, values = [], []
        for rank, place in enumerate(places):
            score = dot(queries, keys_all[head][place], 1, 1) * SCALE_TWO
            if not whole:
                at = lax.broadcasted_iota(jnp.int32, score.shape, 0) + (own_start + start)
                to = lax.broadcasted_iota(jnp.int32, score.shape, 1) + rank * PROMPT_DEV
                score = jnp.where(to <= at, score, NEGATIVE)
            scores.append(score)
            values.append(values_all[head][place])
        if whole:
            score = dot(queries, key[head, span], 1, 1) * SCALE_TWO
            scores.append(jnp.where(own_part(block), score, NEGATIVE))
            values.append(value[head, span])
        top = functools.reduce(
            jnp.maximum, [jnp.max(score, axis=-1, keepdims=True) for score in scores]
        )
        total = jnp.zeros_like(top)
        result = jnp.zeros((block, HEAD), WIDE)
        for score, held in zip(scores, values):
            weight = jnp.exp2(score - top)
            total += jnp.sum(weight, axis=-1, keepdims=True)
            result += dot(weight.astype(LOW), held)
        result = result / total
        mixed[span, head * HEAD : head * HEAD + HEAD] = result.astype(LOW)
        attended[head, span] = result
        log_total[head, span] = jnp.broadcast_to(top + jnp.log2(total), (block, HEAD))

    w_loads[0].wait()
    turned(weights[0], key)
    heed(member_peers(members))
    w_loads[1].wait()
    linear = dot(act[...], weights[1])
    for head in range(heads):
        value[head] = linear[:, head * HEAD : head * HEAD + HEAD].astype(LOW)
    own_sends(0)
    own_sends(1)
    w_loads[2].wait()
    turned(weights[2], query)
    level(0, 1)
    own_sends(2)
    for count in range(2, levels + 1):
        level(0, count)
    level(1, 1)
    own_sends(3)
    for head in range(heads):
        complete(head)

        @pl.loop(0, PROMPT_DEV // block)
        def _(index, head=head):
            attend_rows(head, pl.multiple_of(index * block, block), own_places, False)

        for count in range(2, levels + 1):
            level(head + 1, count)
        level(head + 2, 1)
        own_sends(head + 4)
        for start in range(PROMPT_DEV, rows, block):
            attend_rows(head, start, other_places, True)
    for head in range(heads):
        for flow in (0, 1):
            write(flow, head).wait()
            for mask in masks:
                came_by(flow, head, mask).wait_send()


def gather_attend(members, readers, w_query, w_key, w_value, states, table):
    rows, depth = states.shape
    width = w_query.shape[1]
    heads = width // HEAD
    smem = pl.BlockSpec(memory_space=pltpu.SMEM)
    row_heads = (heads, rows, HEAD)
    every = (heads, members, PROMPT_DEV, HEAD)
    return pl.pallas_call(
        functools.partial(gather_attend_kernel, members),
        out_shape=[
            shape((rows, depth), LOW),
            shape(row_heads, LOW),
            shape(row_heads, LOW),
            shape(row_heads, LOW),
            shape((rows, HEAD), WIDE),
            shape((rows, HEAD), WIDE),
            shape((rows, width), LOW),
            shape(row_heads, WIDE),
            shape(row_heads, WIDE),
            shape(every, LOW),
            shape(every, LOW),
        ],
        in_specs=[smem] * 3 + [ANY] * 4 + [VMEM],
        out_specs=[VMEM] * 9 + [ANY] * 2,
        scratch_shapes=[
            pltpu.VMEM((rows, depth), WIDE),
            pltpu.VMEM((3, depth, width), LOW),
            DMA((4,)),
            DMA((3,)),
            DMA((2, heads, members)),
            DMA((2, heads, members)),
            DMA((2, heads)),
            DMA((2, heads)),
        ]
        + [pltpu.VMEM(every[1:], LOW)] * (2 * heads),
        compiler_params=pltpu.CompilerParams(
            collective_id=6, has_side_effects=True, vmem_limit_bytes=VMEM_LIMIT
        ),
        name="gather_attend",
    )(
        *readers,
        w_query,
        w_key,
        w_value,
        states,
        table,
    )


def back_owner_kernel(
    members,
    count,
    group_id,
    slice_start,
    cont_group,
    keys_in,
    values_in,
    query_in,
    key_in,
    value_in,
    attended_in,
    log_total_in,
    branch_low,
    w_out,
    cosine,
    sine,
    own_out,
    d_query,
    d_key,
    d_value,
    early_out,
    query,
    key,
    value,
    attended,
    log_total,
    d_mixed,
    d_queries,
    own_keys,
    own_values,
    other_keys,
    other_values,
    load_sem,
    *refs,
):
    take = taker(refs)
    member = lax.axis_index("dp")
    heads, rows = query.shape[0], query.shape[1]
    keys_all, values_all = take(heads), take(heads)
    out_send, out_recv = take(2)
    here = lax.axis_index("tensor")
    size = own_out.shape[0]
    own_rows = pl.ds(pl.multiple_of(here * size, size), size)

    def tell(distance):
        return remote(
            own_out,
            early_out.at[own_rows],
            out_send.at[distance - 1],
            out_recv.at[distance - 1],
            (member, lax.rem(here + distance, count)),
        )

    half = pairs = members // 2
    parity = lax.rem(member, 2)
    order = bits_of(pairs)
    moves, flows, sides = [], [], []
    for way in (order, order[::-1]):
        mine, leaving, theirs = take(3)
        local_free, send_sem, recv_sem = take(3)
        refs_of = take(4)
        sides.append((mine, leaving, theirs, send_sem, recv_sem))
        per_head = []
        for head in range(heads):

            def own(mask, target, columns, mine=mine, theirs=theirs, head=head):
                return mine[head, target, :, columns].astype(WIDE) + theirs[
                    head, target, :, columns
                ].astype(WIDE)

            per_head.append(Halving(pairs, way, own, [ref.at[head] for ref in refs_of]))
        flows.append(per_head)
    partner = (flip(member, 1), lax.axis_index("tensor"))

    sources = (keys_in, values_in, query_in, key_in, value_in, attended_in, log_total_in)

    def load(index, head):
        if index < 2:
            target = (keys_all, values_all)[index][head]
        else:
            target = (query, key, value, attended, log_total)[index - 2].at[head]
        return pltpu.make_async_copy(
            sources[index].at[head], target, load_sem.at[index, head]
        )

    for head in range(heads):
        for index in range(len(sources)):
            load(index, head).start()

    def across(flow, head):
        _, leaving, theirs, send_sem, recv_sem = sides[flow]
        return remote(
            leaving.at[head], theirs.at[head], send_sem.at[head], recv_sem.at[head], partner
        )

    own_group, other_group = group_id[member], cont_group[0]
    own_start = slice_start[member]
    own_places = [place_of(group_id, slice_start, own_group, rank) for rank in range(half)]
    other_places = [place_of(group_id, slice_start, other_group, rank) for rank in range(half)]
    across_line = [(member, lax.rem(here + distance, count)) for distance in range(1, count)]
    hail(member_peers(members) + across_line)
    linear = dot(branch_low[...], w_out[...], 1, 1)
    for head in range(heads):
        d_mixed[head] = linear[:, head * HEAD : head * HEAD + HEAD].astype(LOW)
    heed(member_peers(members) + across_line)
    for distance in range(1, count):
        tell(distance).start()
    early_out[own_rows] = own_out[...]
    late = rows - PROMPT_DEV

    def back(scores, queries, keys, values, d_attended, log_sum, center):
        probabilities = jnp.exp2(scores - log_sum)
        d_scores = (probabilities * (dot(d_attended, values, 1, 1) - center)).astype(LOW)
        return (
            dot(d_scores, keys),
            dot(d_scores, queries, 0, 0),
            dot(probabilities.astype(LOW), d_attended, 0, 0),
        )

    def rows_of(head, start, count):
        span = pl.ds(start, count)
        d_attended = d_mixed[head, span]
        center = jnp.sum(d_attended.astype(WIDE) * attended[head, span], axis=-1, keepdims=True)
        return query[head, span], d_attended, log_total[head, span][:, :1], center

    def prompt_rank(head, rank):
        queries, d_attended, log_sum, center = rows_of(head, 0, PROMPT_DEV)
        place = own_places[rank]
        keys, values = keys_all[head][place], values_all[head][place]
        scores = dot(queries, keys, 1, 1) * SCALE_TWO
        at = lax.broadcasted_iota(jnp.int32, scores.shape, 0) + own_start
        to = lax.broadcasted_iota(jnp.int32, scores.shape, 1) + rank * PROMPT_DEV
        scores = jnp.where(to <= at, scores, NEGATIVE)
        more, d_keys, d_values = back(
            scores, queries, keys, values, d_attended, log_sum, center
        )
        early = pl.ds(0, PROMPT_DEV)
        if rank:
            d_queries[early] += more
        else:
            d_queries[early] = more
        own_keys[rank] = d_keys
        own_values[rank] = d_values

    def late_part(head):
        queries, d_attended, log_sum, center = rows_of(head, PROMPT_DEV, late)
        span = pl.ds(PROMPT_DEV, late)
        keys, values = key[head, span], value[head, span]
        scores = jnp.where(own_part(late), dot(queries, keys, 1, 1) * SCALE_TWO, NEGATIVE)
        total, d_keys, d_values = back(
            scores, queries, keys, values, d_attended, log_sum, center
        )
        columns = pl.ds(head * HEAD, HEAD)
        d_key[span, columns] = rotate(d_keys * SCALE, cosine[span], -sine[span]).astype(LOW)
        d_value[span, columns] = d_values.astype(LOW)
        for rank in range(half):
            place = other_places[rank]
            keys, values = keys_all[head][place], values_all[head][place]
            more, d_keys, d_values = back(
                dot(queries, keys, 1, 1) * SCALE_TWO, queries, keys, values, d_attended, log_sum, center
            )
            total += more
            other_keys[rank] = d_keys
            other_values[rank] = d_values
        d_queries[span] = total
        d_query[:, columns] = rotate(d_queries[...] * SCALE, cosine[...], -sine[...]).astype(LOW)

    def spread(head):
        for pair in range(pairs):
            for away in (0, 1):
                index = 2 * pair + (1 - parity if away else parity)
                rank = lax.div(slice_start[index], PROMPT_DEV)
                mine = jnp.where(group_id[index] == own_group, 1.0, 0.0)
                other = jnp.where(group_id[index] == other_group, 1.0, 0.0)
                for flow, (a, b, scale) in enumerate(
                    ((own_keys, other_keys, SCALE), (own_values, other_values, 1.0))
                ):
                    total = a[rank] * (mine * scale) + b[rank] * (other * scale)
                    sides[flow][away][head, pair] = total.astype(LOW)

    def begin(head):
        for flow in (0, 1):
            across(flow, head).start()

    def stage(head, index):
        if not 0 <= head < heads:
            return
        for flow in (0, 1):
            if not index:
                across(flow, head).wait_recv()
        for flow in (0, 1):
            for mask in flows[flow][head].steps(index):
                flows[flow][head].push(mask)

    def end(head):
        if not 0 <= head < heads:
            return
        early = pl.ds(0, PROMPT_DEV)
        columns = pl.ds(head * HEAD, HEAD)
        total = d_queries.at[early]
        flows[0][head].end(total)
        d_key[early, columns] = rotate(total[...], cosine[early], -sine[early]).astype(LOW)
        flows[1][head].end(d_value.at[early, columns])

    depth = len(order)
    for head in range(heads):
        for index in range(len(sources)):
            load(index, head).wait()
        for rank in range(half):
            prompt_rank(head, rank)
            if rank == 0:
                stage(head - 1, 0)
            if rank == half - 1:
                for index in range(1, depth):
                    stage(head - 1, index)
        late_part(head)
        spread(head)
        begin(head)
        end(head - 1)
    for index in range(depth):
        stage(heads - 1, index)
    end(heads - 1)
    for flow in (0, 1):
        for head in range(heads):
            across(flow, head).wait_send()
            flows[flow][head].sent()
    for distance in range(1, count):
        tell(distance).wait()


def back_owner(
    members,
    count,
    readers,
    keys_all,
    values_all,
    query,
    key,
    value,
    branch_low,
    w_out,
    attended,
    log_total,
    cosine,
    sine,
    own_out,
):
    heads, rows, _ = query.shape
    width = heads * HEAD
    pairs = members // 2
    smem = pl.BlockSpec(memory_space=pltpu.SMEM)
    every = pltpu.VMEM((members, PROMPT_DEV, HEAD), LOW)
    side = pltpu.VMEM((heads, pairs, PROMPT_DEV, HEAD), LOW)
    step = pltpu.VMEM((heads, pairs - 1, PROMPT_DEV, HEAD), LOW)
    flow = [side] * 3 + [DMA((heads,))] * 3 + [step] * 2 + [DMA((heads, pairs - 1, 1))] * 2
    total = pltpu.VMEM((pairs, PROMPT_DEV, HEAD), WIDE)
    return pl.pallas_call(
        functools.partial(back_owner_kernel, members, count),
        out_shape=[shape((rows, width), LOW)] * 3
        + [shape((count * own_out.shape[0], own_out.shape[1]), LOW)],
        in_specs=[smem] * 3 + [ANY] * 7 + [VMEM] * 5,
        out_specs=[VMEM] * 4,
        scratch_shapes=[
            pltpu.VMEM((heads, rows, HEAD), LOW),
            pltpu.VMEM((heads, rows, HEAD), LOW),
            pltpu.VMEM((heads, rows, HEAD), LOW),
            pltpu.VMEM((heads, rows, HEAD), WIDE),
            pltpu.VMEM((heads, rows, HEAD), WIDE),
            pltpu.VMEM((heads, rows, HEAD), LOW),
            pltpu.VMEM((rows, HEAD), WIDE),
            total,
            total,
            total,
            total,
            DMA((7, heads)),
        ]
        + [every] * (2 * heads)
        + [DMA((count - 1,))] * 2
        + flow * 2,
        compiler_params=pltpu.CompilerParams(
            collective_id=7, has_side_effects=True, vmem_limit_bytes=VMEM_LIMIT
        ),
        name="back_owner",
    )(
        *readers,
        keys_all,
        values_all,
        query,
        key,
        value,
        attended,
        log_total,
        branch_low,
        w_out,
        cosine,
        sine,
        own_out,
    )


def branch_kernel(
    count,
    mixed,
    w_out,
    states,
    cotangent_in,
    w_down_in,
    act,
    resid,
    out_low,
    d_hidden,
    part,
    cotangent,
    w_down,
    state_sem,
    cot_sem,
    down_sem,
    *refs,
):
    line = Line(count, refs)
    rows = resid.shape[0]
    fetch = pltpu.make_async_copy(
        states.at[pl.ds(pl.multiple_of(line.here * rows, rows), rows)], resid, state_sem
    )
    cot_load = pltpu.make_async_copy(cotangent_in, cotangent, cot_sem)
    down_load = pltpu.make_async_copy(w_down_in, w_down, down_sem)
    for load in (fetch, cot_load, down_load):
        load.start()
    hail(line.peers())
    tile = 512
    for start in range(0, part.shape[1], tile):
        columns = pl.ds(start, tile)
        part[:, columns] = dot(mixed[...], w_out[:, columns])
    heed(line.peers())
    fetch.wait()

    def finish(group):
        span = pl.ds(group * line.rows, line.rows)
        resid[span] += line.total[...]
        act[line.span(group, line.here)] = norm_rows(resid[span])[0].astype(LOW)

    def cast():
        cot_load.wait()
        step = 64
        for start in range(0, out_low.shape[0], step):
            span = pl.ds(start, step)
            out_low[span] = cotangent[span].astype(LOW)
        down_load.wait()

    def inner(start):
        def act():
            span = pl.ds(start, tile)
            d_hidden[:, span] = dot(out_low[...], w_down[span], 1, 1).astype(LOW)

        return act

    inners = [inner(start) for start in range(0, d_hidden.shape[1], tile)]
    line.reduce(part, act, finish, [cast] + inners)
    line.sent(act)


def branch(count, mixed, w_out, states, cotangent, w_down):
    rows, depth = states.shape
    units = w_down.shape[0]
    return pl.pallas_call(
        functools.partial(branch_kernel, count),
        out_shape=[
            shape((rows, depth), LOW),
            shape((rows // count, depth), WIDE),
            shape((rows, depth), LOW),
            shape((rows, units), LOW),
        ],
        in_specs=[VMEM, VMEM, ANY, ANY, ANY],
        out_specs=[VMEM] * 4,
        scratch_shapes=[
            pltpu.VMEM((rows, depth), WIDE),
            pltpu.VMEM((rows, depth), WIDE),
            pltpu.VMEM((units, depth), LOW),
            DMA,
            DMA,
            DMA,
        ]
        + Line.scratch(count, GROUPS, rows // count, depth),
        compiler_params=pltpu.CompilerParams(
            collective_id=2, has_side_effects=True, vmem_limit_bytes=VMEM_LIMIT
        ),
        name="branch",
    )(mixed, w_out, states, cotangent, w_down)


def feed_kernel(
    act, resid, d_hidden, w_gate, w_up, w_down, ffn_early, ffn_late, d_act, hidden, d_gate, d_up, ffn_total, d_total
):
    step = pl.program_id(0)
    gate = dot(act[...], w_gate[...])
    up = dot(act[...], w_up[...])
    sigmoid = jax.nn.sigmoid(gate)
    swish = gate * sigmoid
    d_inner = d_hidden[...].astype(WIDE)
    hidden[...] = (swish * up).astype(LOW)
    d_gate[...] = (d_inner * up * sigmoid * (1.0 + gate * (1.0 - sigmoid))).astype(LOW)
    d_up[...] = (d_inner * swish).astype(LOW)

    def add(new):
        tile = 512
        for start in range(0, act.shape[1], tile):
            columns = pl.ds(start, tile)
            more = dot(hidden[...], w_down[:, columns])
            d_more = dot(d_gate[...], w_gate[columns], 1, 1) + dot(d_up[...], w_up[columns], 1, 1)
            if new:
                ffn_total[:, columns] = more
                d_total[:, columns] = d_more
            else:
                ffn_total[:, columns] += more
                d_total[:, columns] += d_more

    @pl.when(step == 0)
    def _():
        add(True)

    @pl.when(step > 0)
    def _():
        add(False)

    @pl.when(step == pl.num_programs(0) - 1)
    def _():
        rows = resid.shape[0]
        here = lax.axis_index("tensor")
        own = pl.ds(pl.multiple_of(here * rows, rows), rows)
        ffn_total[own] += resid[...]
        for at, ffn in enumerate((ffn_early, ffn_late)):
            part = rows // 2
            for chunk in range(act.shape[0] // rows):
                ffn[pl.ds(chunk * part, part)] = ffn_total[
                    pl.ds(chunk * rows + at * part, part)
                ].astype(LOW)
        d_act[...] = d_total[...].astype(LOW)


def feed(act, resid, d_hidden, w_gate, w_up, w_down):
    rows, depth = act.shape
    units = w_gate.shape[1]
    tile = 256
    whole = pl.BlockSpec((rows, depth), lambda i: (0, 0))
    some = pl.BlockSpec((rows // 2, depth), lambda i: (0, 0))
    across = pl.BlockSpec((depth, tile), lambda i: (0, i))
    down = pl.BlockSpec((tile, depth), lambda i: (i, 0))
    inner = pl.BlockSpec((rows, tile), lambda i: (0, i))
    chunk = pl.BlockSpec(resid.shape, lambda i: (0, 0))
    return pl.pallas_call(
        feed_kernel,
        out_shape=[shape((rows // 2, depth), LOW)] * 2
        + [shape((rows, depth), LOW)]
        + [shape((rows, units), LOW)] * 3,
        grid=(units // tile,),
        in_specs=[whole, chunk, inner, across, across, down],
        out_specs=[some, some, whole, inner, inner, inner],
        scratch_shapes=[pltpu.VMEM((rows, depth), WIDE)] * 2,
        compiler_params=pltpu.CompilerParams(vmem_limit_bytes=VMEM_LIMIT),
        name="feed",
    )(act, resid, d_hidden, w_gate, w_up, w_down)


def second_kernel(
    count,
    pairs,
    d_act,
    ffn,
    resid,
    cotangent,
    act,
    d_gate,
    d_up,
    branch_low,
    grad_resid,
    own_out,
    grad_gate,
    grad_up,
    cot_sem,
    *refs,
):
    take = taker(refs)
    line = Line(count, take(Line.scratch_count))
    out_line = Line(count, take(Line.scratch_count))
    lhs = Lhs(act, take(4))
    rights = [Rhs([source], take(4)) for source in (d_gate, d_up)]
    order = bits_of(pairs)
    flows = [
        Halving(pairs, way, product_of(lhs, right), take(4), *take(1))
        for way, right in zip((order, order[::-1]), rights)
    ]
    rows = resid.shape[0]
    fetch = pltpu.make_async_copy(
        cotangent.at[pl.ds(pl.multiple_of(line.here * rows, rows), rows)], grad_resid, cot_sem
    )
    fetch.start()
    greet(line.peers() + member_peers(2 * pairs))
    lhs.start()
    for piece in range(flows[0].pieces):
        for right in rights:
            right.start(piece)
    fetch.wait()

    def finish(group):
        span = pl.ds(group * line.rows, line.rows)
        normed, inverse = norm_rows(resid[span])
        grad_resid[span] += norm_back(line.total[...], normed, inverse)
        branch_low[line.span(group, line.here)] = grad_resid[span].astype(LOW)

    sides = [(lhs, right, flow) for right, flow in zip(rights, flows)]
    ahead, early, others, settle, late = beside(order, sides)

    def out_slot(slot):
        return lambda: out_line.scatter_slot(0, slot, ffn)

    slots = [out_slot(slot) for slot in range(count - 1)]

    def fourth():
        settle()
        slots[0]()

    line.reduce(d_act, branch_low, finish, [ahead, early, others, fourth, late] + slots[1:])
    out_line.scatter_end(0, ffn)
    own_out[...] = out_line.total[...].astype(LOW)
    flows[0].end(grad_gate)
    flows[1].end(grad_up)
    for flow in flows:
        flow.sent()
    for move in [lhs] + rights:
        move.sent()
    line.sent(branch_low)
    out_line.sent()


def beside(order, sides):
    masks = [flow.steps(0) for _, _, flow in sides]

    def ahead():
        for (lhs, rhs, flow), (mask, *_) in zip(sides[:2], masks):
            lhs.ready()
            rhs.ready(0)
            flow.push_piece(mask, 0)

    def early():
        for at, ((lhs, rhs, flow), (mask, *_)) in enumerate(zip(sides, masks)):
            if at > 1:
                lhs.ready()
            for piece in range(0 if at > 1 else 1, flow.pieces):
                rhs.ready(piece)
                flow.push_piece(mask, piece)

    def others():
        for index in range(1, len(masks[0])):
            for (_, _, flow), steps in zip(sides, masks):
                flow.push(steps[index])

    def settle():
        for _, _, flow in sides:
            flow.settle()

    def late():
        for stage in range(1, len(order)):
            for index in range(len(sides[0][2].steps(stage))):
                for _, _, flow in sides:
                    flow.push(flow.steps(stage)[index])

    return [ahead, early, others, settle, late]


def second(count, members, d_act, ffn, resid, cotangent, act, d_gate, d_up):
    rows, depth = cotangent.shape
    units = d_gate.shape[1]
    pairs = members // 2
    block = depth // members
    return pl.pallas_call(
        functools.partial(second_kernel, count, pairs),
        out_shape=[
            shape((rows, depth), LOW),
            shape((rows // count, depth), WIDE),
            shape((ffn.shape[0] // count, depth), LOW),
            shape((block, units), LOW),
            shape((block, units), LOW),
        ],
        in_specs=[VMEM] * 3 + [ANY] * 4,
        out_specs=[VMEM] * 5,
        scratch_shapes=[DMA]
        + Line.scratch(count, GROUPS, rows // count, depth)
        + Line.scratch(count, 1, ffn.shape[0] // count, depth)
        + Lhs.scratch(pairs, rows, block)
        + Rhs.scratch(rows, units) * 2
        + (Halving.scratch(pairs, block, units) + [pltpu.VMEM((block, units), WIDE)]) * 2,
        compiler_params=pltpu.CompilerParams(
            collective_id=3, has_side_effects=True, vmem_limit_bytes=VMEM_LIMIT
        ),
        name="second",
    )(d_act, ffn, resid, cotangent, in_blocks(act, members), d_gate, d_up)


def owner_kernel(
    pairs,
    d_keys_all,
    d_values_all,
    d_key_own,
    d_value_own,
    cosine,
    sine,
    d_key,
    d_value,
    *refs,
):
    take = taker(refs)
    parity = lax.rem(lax.axis_index("dp"), 2)
    order = bits_of(pairs)
    width = d_key.shape[1]
    moves, flows = [], []
    for way, source in zip((order, order[::-1]), (d_keys_all, d_values_all)):
        mine, theirs = take(2)
        moves.append(
            Pairwise(
                [
                    (
                        source.at[2 * pair + parity],
                        mine.at[pair],
                        source.at[2 * pair + 1 - parity],
                        theirs.at[pair],
                    )
                    for pair in range(pairs)
                ],
                take(3),
            )
        )

        def own(mask, target, columns, mine=mine, theirs=theirs):
            return mine[target, :, columns].astype(WIDE) + theirs[target, :, columns].astype(WIDE)

        flows.append(Halving(pairs, way, own, take(4)))
    (total,) = take(1)
    greet(member_peers(2 * pairs))
    for move in moves:
        move.start()
    for move, flow in zip(moves, flows):
        move.ready()
        flow.push(flow.masks[0])
    late = pl.ds(PROMPT_DEV, d_key.shape[0] - PROMPT_DEV)
    d_key[late] = d_key_own[...]
    d_value[late] = d_value_own[...]
    for index in range(1, pairs - 1):
        for flow in flows:
            flow.push(flow.masks[index])
    early = pl.ds(0, PROMPT_DEV)
    flows[0].end(total)
    for start in range(0, width, HEAD):
        d_key[early, start : start + HEAD] = rotate(
            total[:, start : start + HEAD], cosine[early], -sine[early]
        ).astype(LOW)
    flows[1].end(d_value.at[early])
    for move, flow in zip(moves, flows):
        flow.sent()
        move.sent()


def owner(members, d_keys_all, d_values_all, d_key_own, d_value_own, cosine, sine):
    width = d_key_own.shape[1]
    rows = cosine.shape[0]
    pairs = members // 2
    flow = (
        [pltpu.VMEM((pairs, PROMPT_DEV, width), LOW)] * 2
        + Pairwise.sems(pairs)
        + Halving.scratch(pairs, PROMPT_DEV, width)
    )
    return pl.pallas_call(
        functools.partial(owner_kernel, pairs),
        out_shape=[shape((rows, width), LOW)] * 2,
        in_specs=[ANY, ANY] + [VMEM] * 4,
        out_specs=[VMEM] * 2,
        scratch_shapes=flow * 2 + [pltpu.VMEM((PROMPT_DEV, width), WIDE)],
        compiler_params=pltpu.CompilerParams(
            collective_id=4, has_side_effects=True, vmem_limit_bytes=VMEM_LIMIT
        ),
        name="owner",
    )(d_keys_all, d_values_all, d_key_own, d_value_own, cosine, sine)


def first_kernel(
    count,
    pairs,
    grad_resid,
    d_query,
    d_key,
    d_value,
    w_query,
    w_key,
    w_value,
    states,
    act,
    mixed,
    branch_low,
    hidden,
    out_low,
    far_query,
    far_key,
    far_value,
    input_grad,
    grad_down,
    grad_out,
    grad_query,
    grad_key,
    grad_value,
    inner_total,
    part,
    state,
    weight,
    state_sem,
    weight_sem,
    *refs,
):
    take = taker(refs)
    line = Line(count, take(Line.scratch_count))
    order = bits_of(pairs)
    sides = []
    for left, rights, way in (
        (out_low, (hidden,), order),
        (act, (far_query, far_key, far_value), order[::-1]),
        (branch_low, (mixed,), order[::-1]),
    ):
        lhs, rhs = Lhs(left, take(4)), Rhs(rights, take(4))
        sides.append((lhs, rhs, Halving(pairs, way, product_of(lhs, rhs), take(4), *take(1))))
    rows = state.shape[0]
    fetch = pltpu.make_async_copy(
        states.at[pl.ds(pl.multiple_of(line.here * rows, rows), rows)], state, state_sem
    )
    loads = [
        pltpu.make_async_copy(source, weight.at[index], weight_sem.at[index])
        for index, source in enumerate((w_query, w_key, w_value))
    ]
    for load in loads:
        load.start()
    fetch.start()
    greet(line.peers() + member_peers(2 * pairs))
    for lhs, rhs, _ in sides[:2]:
        lhs.start()
        rhs.start(0)
    for at, (lhs, rhs, flow) in enumerate(sides):
        if at > 1:
            lhs.start()
        for piece in range(0 if at > 1 else 1, flow.pieces):
            rhs.start(piece)
    for load in loads:
        load.wait()
    tile = 512
    for start in range(0, part.shape[1], tile):
        columns = pl.ds(start, tile)
        part[:, columns] = (
            dot(d_query[...], weight[0, columns], 1, 1)
            + dot(d_key[...], weight[1, columns], 1, 1)
            + dot(d_value[...], weight[2, columns], 1, 1)
        )
    fetch.wait()

    def finish(group):
        span = pl.ds(group * line.rows, line.rows)
        normed, inverse = norm_rows(state[span])
        input_grad[line.span(group, line.here)] = (
            grad_resid[span] + norm_back(line.total[...], normed, inverse)
        ).astype(LOW)

    line.reduce(part, input_grad, finish, beside(order, sides))
    for (_, _, flow), target in zip(sides, (grad_down, inner_total, grad_out)):
        flow.end(target)
    width = grad_query.shape[1]
    for index, target in enumerate((grad_query, grad_key, grad_value)):
        target[...] = inner_total[:, index * width : index * width + width]
    for lhs, rhs, flow in sides:
        flow.sent()
        lhs.sent()
        rhs.sent()
    line.sent(input_grad)


def first(
    count,
    members,
    grad_resid,
    weights,
    states,
    act,
    mixed,
    branch_low,
    hidden,
    out_low,
    d_query,
    d_key,
    d_value,
):
    rows, depth = states.shape
    width = d_query.shape[1]
    units = hidden.shape[1]
    pairs = members // 2
    block = depth // members
    scratch = []
    for wide in (units, 3 * width, width):
        scratch += Lhs.scratch(pairs, rows, block) + Rhs.scratch(rows, wide)
        scratch += Halving.scratch(pairs, block, wide) + [pltpu.VMEM((block, wide), WIDE)]
    return pl.pallas_call(
        functools.partial(first_kernel, count, pairs),
        out_shape=[
            shape((rows, depth), LOW),
            shape((block, units), LOW),
        ]
        + [shape((block, width), LOW)] * 4,
        in_specs=[VMEM] * 4 + [ANY] * 12,
        out_specs=[VMEM] * 6,
        scratch_shapes=[
            pltpu.VMEM((block, 3 * width), LOW),
            pltpu.VMEM((rows, depth), WIDE),
            pltpu.VMEM((rows // count, depth), WIDE),
            pltpu.VMEM((3, depth, width), LOW),
            DMA,
            DMA((3,)),
        ]
        + Line.scratch(count, GROUPS, rows // count, depth)
        + scratch,
        compiler_params=pltpu.CompilerParams(
            collective_id=5, has_side_effects=True, vmem_limit_bytes=VMEM_LIMIT
        ),
        name="first",
    )(
        grad_resid,
        d_query,
        d_key,
        d_value,
        *weights,
        states,
        in_blocks(act, members),
        mixed,
        in_blocks(branch_low, members),
        hidden,
        in_blocks(out_low, members),
        d_query,
        d_key,
        d_value,
    )


def widen_kernel(flat, early, late, *refs):
    count = len(refs) // 2
    sources, whole, targets = refs[:count], refs[count], refs[count + 1 :]
    half = early.shape[0]
    whole[pl.ds(0, half)] = early[...].astype(WIDE)
    whole[pl.ds(half, half)] = late[...].astype(WIDE)
    for index, (source, target) in enumerate(zip(sources, targets)):
        values = source[...].astype(WIDE)
        target[...] = values if index < flat else values.T


def widen(count, early, late, plain, turned):
    def rows(array):
        return pl.BlockSpec((array.shape[0] // count, array.shape[1]), lambda i: (i, 0))

    def columns(array):
        return pl.BlockSpec((array.shape[0], array.shape[1] // count), lambda i: (0, i))

    flipped = [shape(array.shape[::-1], WIDE) for array in turned]
    whole = shape((2 * early.shape[0], early.shape[1]), WIDE)
    return pl.pallas_call(
        functools.partial(widen_kernel, len(plain)),
        out_shape=[whole] + [shape(array.shape, WIDE) for array in plain] + flipped,
        grid=(count,),
        in_specs=[rows(array) for array in (early, late, *plain)]
        + [columns(array) for array in turned],
        out_specs=[rows(array) for array in (whole, *plain, *flipped)],
        compiler_params=pltpu.CompilerParams(vmem_limit_bytes=VMEM_LIMIT),
        name="widen",
    )(early, late, *plain, *turned)


def body(
    states,
    w_query,
    w_key,
    w_value,
    w_out,
    w_gate,
    w_up,
    w_down,
    group_id,
    slice_start,
    cont_group,
    cotangent,
):
    rows = states.shape[0]
    members = lax.axis_size("dp")
    count = lax.axis_size("tensor")
    frequency = 10000.0 ** (-np.arange(HEAD // 2) * 2.0 / HEAD)
    frequency = np.concatenate([frequency, frequency]).astype(np.float32)
    sign = np.repeat([-1.0, 1.0], HEAD // 2).astype(np.float32)
    readers = (group_id, slice_start, cont_group)
    merged = members * PROMPT_DEV * w_query.shape[1] * 2 * 4 <= 16 * 2**20
    if merged:
        table = jnp.stack([frequency, sign])
        act_one, query, key, value, cosine, sine, mixed, attended, log_total, *everyones = (
            gather_attend(members, readers, w_query, w_key, w_value, states, table)
        )
    else:
        index = jnp.arange(rows, dtype=jnp.int32)
        everyone = jnp.arange(members, dtype=jnp.int32)
        own_start = jnp.sum(jnp.where(everyone == lax.axis_index("dp"), slice_start, 0))
        prompt = members // 2 * PROMPT_DEV
        positions = jnp.where(index < PROMPT_DEV, own_start + index, prompt + index - PROMPT_DEV)
        angles = positions.astype(WIDE)[:, None] * frequency[None, :]
        cosine = jnp.cos(angles)
        sine = jnp.sin(angles) * sign[None, :]
        act_one, query, key, value, *everyones = project(
            members, states, w_query, w_key, w_value, cosine, sine
        )
        mixed, attended, log_total = attend(readers, query, key, value, *everyones)
    act_two, resid, out_low, d_hidden = branch(count, mixed, w_out, states, cotangent, w_down)
    ffn, ffn_late, d_act_two, hidden, d_gate, d_up = feed(act_two, resid, d_hidden, w_gate, w_up, w_down)
    branch_low, grad_resid, own_out, grad_gate, grad_up = second(
        count, members, d_act_two, ffn, resid, cotangent, act_two, d_gate, d_up
    )
    ffn_late, branch_low = lax.optimization_barrier((ffn_late, branch_low))
    late_out = lax.psum(ffn_late, "tensor")
    kept = (query, key, value, branch_low, w_out, attended, log_total, cosine, sine)
    if merged:
        d_query, d_key, d_value, early_out = back_owner(
            members, count, readers, *everyones, *kept, own_out
        )
    else:
        d_query, *d_everyones = attend_back(
            readers, query, key, value, *everyones, branch_low, w_out, attended, log_total, cosine, sine
        )
        d_key, d_value = owner(members, *d_everyones, cosine, sine)
        early_out = lax.all_gather(own_out, "tensor", axis=0, tiled=True)
    input_grad, grad_down, grad_out, *grad_inner = first(
        count,
        members,
        grad_resid,
        (w_query, w_key, w_value),
        states,
        act_one,
        mixed,
        branch_low,
        hidden,
        out_low,
        d_query,
        d_key,
        d_value,
    )
    *plain, grad_out, grad_down = widen(
        count,
        early_out,
        late_out,
        (input_grad, *grad_inner, grad_gate, grad_up),
        (grad_out, grad_down),
    )
    return (*plain[:5], grad_out, *plain[5:], grad_down)


def solution(mesh):
    placed = (
        P("dp", None),
        P(None, "tensor"),
        P(None, "tensor"),
        P(None, "tensor"),
        P("tensor", None),
        P(None, "tensor"),
        P(None, "tensor"),
        P("tensor", None),
        P(),
        P(),
        P("dp"),
        P("dp", None),
    )
    return jax.shard_map(
        body,
        mesh=mesh,
        in_specs=placed,
        out_specs=(
            P("dp", None),
            P("dp", None),
            P("dp", "tensor"),
            P("dp", "tensor"),
            P("dp", "tensor"),
            P("tensor", "dp"),
            P("dp", "tensor"),
            P("dp", "tensor"),
            P("tensor", "dp"),
        ),
        check_vma=False,
    )
```

```python
import functools

import jax
import jax.numpy as jnp
import numpy as np
from jax import lax
from jax.experimental import pallas as pl
from jax.experimental.pallas import tpu as pltpu
from jax.sharding import PartitionSpec as P

HEAD = 128
PROMPT_DEV = 384
EPSILON = 1e-05
NEGATIVE = -1e30
SCALE = HEAD ** (-0.5)
SCALE_TWO = float(SCALE * np.log2(np.e))
LOW = jnp.bfloat16
WIDE = jnp.float32
MESH = pl.DeviceIdType.MESH
ANY = pl.BlockSpec(memory_space=pl.ANY)
VMEM = pl.BlockSpec(memory_space=pltpu.VMEM)
DMA = pltpu.SemaphoreType.DMA
VMEM_LIMIT = 62 * 2**20
GROUPS = 2
PIECE = 512


def dot(left, right, left_dim=1, right_dim=0):
    return lax.dot_general(
        left, right, (((left_dim,), (right_dim,)), ((), ())), preferred_element_type=WIDE
    )


def shape(dims, dtype):
    return jax.ShapeDtypeStruct(dims, dtype)


def norm_rows(values):
    row_mean = jnp.mean(values, axis=-1, keepdims=True)
    centred = values - row_mean
    inverse = lax.rsqrt(jnp.mean(centred * centred, axis=-1, keepdims=True) + EPSILON)
    return centred * inverse, inverse


def norm_back(gradient, normed, inverse):
    return inverse * (
        gradient
        - jnp.mean(gradient, axis=-1, keepdims=True)
        - normed * jnp.mean(gradient * normed, axis=-1, keepdims=True)
    )


def rotate(values, cosine, sine):
    return values * cosine + pltpu.roll(values, HEAD // 2, 1) * sine


def flip(index, mask):
    out, bit = index, 1
    while bit <= mask:
        if mask & bit:
            out = out + bit * (1 - 2 * lax.rem(lax.div(index, bit), 2))
        bit *= 2
    return out


def bits_of(count):
    return list(range(count.bit_length() - 1))


def hail(peers):
    barrier = pltpu.get_barrier_semaphore()
    for peer in peers:
        pl.semaphore_signal(barrier, inc=1, device_id=peer, device_id_type=MESH)


def heed(peers):
    pl.semaphore_wait(pltpu.get_barrier_semaphore(), len(peers))


def greet(peers):
    hail(peers)
    heed(peers)


def remote(source, target, send_sem, recv_sem, device):
    return pltpu.make_async_remote_copy(
        src_ref=source,
        dst_ref=target,
        send_sem=send_sem,
        recv_sem=recv_sem,
        device_id=device,
        device_id_type=MESH,
    )


class Line:
    scratch_count = 10

    @staticmethod
    def scratch(count, groups, rows, width):
        rows = rows // groups
        return [
            pltpu.VMEM((rows, width), WIDE),
            pltpu.VMEM((groups, count, rows, width), LOW),
            pltpu.VMEM((groups, count, rows, width), LOW),
            pltpu.VMEM((groups, count, rows, width), LOW),
            DMA((groups, count)),
            DMA((groups, count)),
            DMA((groups, count)),
            DMA((groups, count)),
            DMA((groups, count)),
            DMA((groups, count)),
        ]

    def __init__(self, count, refs):
        self.count = count
        (
            self.total,
            self.outgoing,
            self.from_left,
            self.from_right,
            self.out_sem,
            self.left_sem,
            self.right_sem,
            self.to_right_sem,
            self.to_left_sem,
            self.got_sem,
        ) = refs
        self.groups = self.outgoing.shape[0]
        self.rows = self.total.shape[0]
        self.here = lax.axis_index("tensor")
        member = lax.axis_index("dp")
        self.right = (member, lax.rem(self.here + 1, count))
        self.left = (member, lax.rem(self.here + count - 1, count))

    def peers(self):
        return [self.left, self.right]

    def span(self, group, chunk):
        start = chunk * (self.rows * self.groups) + group * self.rows
        return pl.ds(pl.multiple_of(start, self.rows), self.rows)

    def rightward(self, group, chunk):
        return remote(
            self.outgoing.at[group, chunk],
            self.from_left.at[group, chunk],
            self.out_sem.at[group, chunk],
            self.left_sem.at[group, chunk],
            self.right,
        )

    def leftward(self, group, chunk):
        return remote(
            self.outgoing.at[group, chunk],
            self.from_right.at[group, chunk],
            self.out_sem.at[group, chunk],
            self.right_sem.at[group, chunk],
            self.left,
        )

    def add_and_pass(self, group, chunk, part, right, wait):
        copy, came = (self.rightward, self.from_left) if right else (self.leftward, self.from_right)
        total = part[self.span(group, chunk)].astype(WIDE)
        if wait:
            copy(group, chunk).wait_recv()
            total += came[group, chunk].astype(WIDE)
        self.outgoing[group, chunk] = total.astype(LOW)
        copy(group, chunk).start()

    def scatter_slot(self, group, slot, part):
        here, count = self.here, self.count
        ahead, back = count - 1 + here - slot, slot - (count - 1 - here)
        if slot == 0:

            @pl.when(here == 0)
            def _():
                self.add_and_pass(group, ahead, part, True, False)

            @pl.when(here == count - 1)
            def _():
                self.add_and_pass(group, back, part, False, False)

            return
        for wait in (False, True):

            @pl.when((here <= slot) & ((here > 0) if wait else (here == 0)))
            def _(wait=wait):
                self.add_and_pass(group, ahead, part, True, wait)

            @pl.when(
                (count - 1 - here <= slot) & ((here < count - 1) if wait else (here == count - 1))
            )
            def _(wait=wait):
                self.add_and_pass(group, back, part, False, wait)

    def scatter_end(self, group, part):
        here = self.here
        last = self.count - 1

        def left():
            self.rightward(group, here).wait_recv()
            return self.from_left[group, here].astype(WIDE)

        def right():
            self.leftward(group, here).wait_recv()
            return self.from_right[group, here].astype(WIDE)

        @pl.when(here == 0)
        def _():
            self.total[...] = part[self.span(group, here)].astype(WIDE) + right()

        @pl.when(here == last)
        def _():
            self.total[...] = part[self.span(group, here)].astype(WIDE) + left()

        @pl.when((here > 0) & (here < last))
        def _():
            self.total[...] = part[self.span(group, here)].astype(WIDE) + left() + right()

    def passing(self, whole, group, chunk, right):
        ref = whole.at[self.span(group, chunk)]
        return remote(
            ref,
            ref,
            (self.to_right_sem if right else self.to_left_sem).at[group, chunk],
            self.got_sem.at[group, chunk],
            self.right if right else self.left,
        )

    def gather_slot(self, whole, group, distance):
        here, count = self.here, self.count

        @pl.when(here - distance >= 0)
        def _():
            if distance:
                self.passing(whole, group, here - distance, True).wait_recv()

            @pl.when(here < count - 1)
            def _():
                self.passing(whole, group, here - distance, True).start()

        @pl.when(here + distance <= count - 1)
        def _():
            if distance:
                self.passing(whole, group, here + distance, False).wait_recv()

            @pl.when(here > 0)
            def _():
                self.passing(whole, group, here + distance, False).start()

    def reduce(self, part, whole, finish, beside=()):
        beside = list(beside)
        last = self.count - 1
        self.scatter_slot(0, 0, part)
        for group in range(self.groups):
            for slot in range(1, last):
                if beside:
                    beside.pop(0)()
                self.scatter_slot(group, slot, part)
                if group:
                    self.gather_slot(whole, group - 1, slot)
            if group + 1 < self.groups:
                self.scatter_slot(group + 1, 0, part)
            if group:
                self.gather_slot(whole, group - 1, last)
            self.scatter_end(group, part)
            finish(group)
            self.gather_slot(whole, group, 0)
        for distance in range(1, self.count):
            if beside:
                beside.pop(0)()
            self.gather_slot(whole, self.groups - 1, distance)
        for act in beside:
            act()

    def sent(self, whole=None):
        here, count = self.here, self.count
        for group in range(self.groups):
            for chunk in range(count):

                @pl.when(here != chunk)
                def _(group=group, chunk=chunk):
                    self.rightward(group, chunk).wait_send()

                if whole is None:
                    continue

                @pl.when((chunk <= here) & (here < count - 1))
                def _(group=group, chunk=chunk):
                    self.passing(whole, group, chunk, True).wait_send()

                @pl.when((chunk >= here) & (here > 0))
                def _(group=group, chunk=chunk):
                    self.passing(whole, group, chunk, False).wait_send()


class Halving:
    @staticmethod
    def masks_of(pairs, order):
        def stage(mask):
            return min(order.index(bit) for bit in order if mask >> bit & 1)

        return sorted(range(1, pairs), key=lambda mask: (stage(mask), -mask.bit_count()))

    @staticmethod
    def scratch(pairs, block, width):
        count = pairs - 1
        pieces = max(1, width // PIECE)
        return [
            pltpu.VMEM((count, block, width), LOW),
            pltpu.VMEM((count, block, width), LOW),
            DMA((count, pieces)),
            DMA((count, pieces)),
        ]

    def __init__(self, pairs, order, own, refs, kept=None):
        self.order, self.own, self.kept = order, own, kept
        self.send, self.recv, self.send_sem, self.recv_sem = refs
        self.masks = Halving.masks_of(pairs, order)
        self.pieces = self.send_sem.shape[1]
        self.piece = self.send.shape[2] // self.pieces
        self.member = lax.axis_index("dp")
        self.tensor = lax.axis_index("tensor")
        self.high = lax.div(self.member, 2)

    def stage(self, mask):
        return min(
            [self.order.index(bit) for bit in self.order if mask >> bit & 1],
            default=len(self.order),
        )

    def steps(self, stage):
        return [mask for mask in self.masks if self.stage(mask) == stage]

    def columns(self, piece):
        return pl.ds(piece * self.piece, self.piece)

    def copy(self, mask, piece):
        index = self.masks.index(mask)
        bit = 1 << self.order[self.stage(mask)]
        return remote(
            self.send.at[index, :, self.columns(piece)],
            self.recv.at[index, :, self.columns(piece)],
            self.send_sem.at[index, piece],
            self.recv_sem.at[index, piece],
            (flip(self.member, bit * 2), self.tensor),
        )

    def settle(self):
        for piece in range(self.pieces):
            columns = self.columns(piece)
            self.kept[:, columns] = self.own(0, flip(self.high, 0), columns)

    def fill(self, mask, piece, out):
        columns = self.columns(piece)
        if self.kept is not None and not mask:
            total = self.kept[:, columns]
        else:
            total = self.own(mask, flip(self.high, mask), columns)
        for bit in self.order[: self.stage(mask)]:
            slot = mask | 1 << bit
            self.copy(slot, piece).wait_recv()
            total += self.recv[self.masks.index(slot), :, columns].astype(WIDE)
        out[:, columns] = total.astype(out.dtype)

    def push_piece(self, mask, piece):
        self.fill(mask, piece, self.send.at[self.masks.index(mask)])
        self.copy(mask, piece).start()

    def push(self, mask):
        for piece in range(self.pieces):
            self.push_piece(mask, piece)

    def end(self, out):
        for piece in range(self.pieces):
            self.fill(0, piece, out)

    def sent(self):
        for mask in self.masks:
            for piece in range(self.pieces):
                self.copy(mask, piece).wait_send()


class Pairwise:
    def __init__(self, moves, refs):
        self.moves, self.done = moves, False
        self.local_sem, self.send_sem, self.recv_sem = refs
        member = lax.axis_index("dp")
        self.partner = (flip(member, 1), lax.axis_index("tensor"))

    @staticmethod
    def sems(count):
        return [DMA((count,)), DMA((count,)), DMA((count,))]

    def local(self, index):
        source, target, _, _ = self.moves[index]
        return pltpu.make_async_copy(source, target, self.local_sem.at[index])

    def across(self, index):
        _, _, source, target = self.moves[index]
        return remote(
            source, target, self.send_sem.at[index], self.recv_sem.at[index], self.partner
        )

    def start(self, index=None):
        for index in range(len(self.moves)) if index is None else [index]:
            self.across(index).start()
            self.local(index).start()

    def ready(self, index=None):
        if index is None and self.done:
            return
        self.done = index is None
        for index in range(len(self.moves)) if index is None else [index]:
            self.local(index).wait()
            self.across(index).wait_recv()

    def sent(self):
        for index in range(len(self.moves)):
            self.across(index).wait_send()


class Lhs(Pairwise):
    @staticmethod
    def scratch(pairs, rows, block):
        return [pltpu.VMEM((pairs, 2 * rows, block), LOW)] + Pairwise.sems(pairs)

    def __init__(self, source, refs):
        self.held = refs[0]
        pairs, rows, block = self.held.shape
        rows = rows // 2
        parity = lax.rem(lax.axis_index("dp"), 2)

        def columns(index):
            if len(source.shape) == 3:
                return source.at[index]
            return source.at[:, pl.ds(pl.multiple_of(index * block, block), block)]

        super().__init__(
            [
                (
                    columns(2 * pair + parity),
                    self.held.at[pair, pl.ds(0, rows)],
                    columns(2 * pair + 1 - parity),
                    self.held.at[pair, pl.ds(rows, rows)],
                )
                for pair in range(pairs)
            ],
            refs[1:],
        )


class Rhs(Pairwise):
    @staticmethod
    def scratch(rows, width):
        return [pltpu.VMEM((2 * rows, width), LOW)] + Pairwise.sems(width // PIECE)

    def __init__(self, sources, refs):
        self.held = refs[0]
        rows = self.held.shape[0] // 2
        moves, at = [], 0
        for source in sources:
            for start in range(0, source.shape[1], PIECE):
                columns = pl.ds(at, PIECE)
                at += PIECE
                here = source.at[:, pl.ds(start, PIECE)]
                moves.append(
                    (
                        here,
                        self.held.at[pl.ds(0, rows), columns],
                        here,
                        self.held.at[pl.ds(rows, rows), columns],
                    )
                )
        super().__init__(moves, refs[1:])


def product_of(lhs, rhs):
    def own(mask, target, columns):
        return dot(lhs.held[target], rhs.held[:, columns], 0, 0)

    return own


def taker(refs):
    refs = list(refs)

    def take(count):
        out = refs[:count]
        del refs[:count]
        return out

    return take


def in_blocks(left, members):
    block = left.shape[1] // members
    if block % 128 == 0:
        return left
    return left.reshape(left.shape[0], members, block).transpose(1, 0, 2)


def member_peers(members):
    member, tensor = lax.axis_index("dp"), lax.axis_index("tensor")
    return [(flip(member, 1 << bit), tensor) for bit in bits_of(members)]


def project_kernel(
    members,
    states,
    w_query,
    w_key,
    w_value,
    cosine,
    sine,
    act,
    query,
    key,
    value,
    keys_all,
    values_all,
    send_sem,
    recv_sem,
    local_sem,
):
    member, tensor = lax.axis_index("dp"), lax.axis_index("tensor")
    width = query.shape[1]
    greet(member_peers(members))
    rows = 64
    for start in range(0, states.shape[0], rows):
        span = pl.ds(start, rows)
        act[span] = norm_rows(states[span])[0].astype(LOW)

    def turned(weight, out):
        linear = dot(act[...], weight[...])
        for start in range(0, width, HEAD):
            out[:, start : start + HEAD] = rotate(
                linear[:, start : start + HEAD], cosine[...], sine[...]
            ).astype(LOW)

    high = [bit for bit in bits_of(members) if bit]
    orders = (high + [0], high[::-1] + [0])
    owns, alls = (key, value), (keys_all, values_all)

    def copy(flow, mask, bit):
        slot = mask | 1 << bit
        place = alls[flow].at[flip(member, mask)]
        return remote(
            place if mask else owns[flow].at[pl.ds(0, PROMPT_DEV)],
            place,
            send_sem.at[flow, slot],
            recv_sem.at[flow, slot],
            (flip(member, 1 << bit), tensor),
        )

    def forward(flow, mask):
        order = orders[flow]
        last = max([order.index(bit) for bit in order if mask >> bit & 1], default=-1)
        for bit in order[last + 1 :]:
            copy(flow, mask, bit).start()

    def came_by(flow, mask):
        order = orders[flow]
        bit = order[max(order.index(bit) for bit in order if mask >> bit & 1)]
        return copy(flow, mask ^ 1 << bit, bit)

    def keep(flow):
        return pltpu.make_async_copy(
            owns[flow].at[pl.ds(0, PROMPT_DEV)], alls[flow].at[member], local_sem.at[flow]
        )

    turned(w_key, key)
    forward(0, 0)
    value[...] = dot(act[...], w_value[...]).astype(LOW)
    forward(1, 0)
    keep(0).start()
    keep(1).start()
    turned(w_query, query)
    masks = range(1, members)
    inner = sorted([mask for mask in masks if not mask & 1], key=lambda mask: mask.bit_count())
    for mask in inner:
        for flow in (0, 1):
            turn = flow if not mask & 2 else flow
            came_by(turn, mask).wait_recv()
            forward(turn, mask)
    for mask in masks:
        if mask & 1:
            for flow in (0, 1):
                came_by(flow, mask).wait_recv()
    for flow in (0, 1):
        keep(flow).wait()
        for mask in masks:
            came_by(flow, mask).wait_send()


def project(members, states, w_query, w_key, w_value, cosine, sine):
    rows, depth = states.shape
    width = w_query.shape[1]
    return pl.pallas_call(
        functools.partial(project_kernel, members),
        out_shape=[
            shape((rows, depth), LOW),
            shape((rows, width), LOW),
            shape((rows, width), LOW),
            shape((rows, width), LOW),
            shape((members, PROMPT_DEV, width), LOW),
            shape((members, PROMPT_DEV, width), LOW),
        ],
        in_specs=[VMEM] * 6,
        out_specs=[VMEM] * 4 + [ANY] * 2,
        scratch_shapes=[DMA((2, members)), DMA((2, members)), DMA((2,))],
        compiler_params=pltpu.CompilerParams(
            collective_id=1, has_side_effects=True, vmem_limit_bytes=VMEM_LIMIT
        ),
        name="project",
    )(states, w_query, w_key, w_value, cosine, sine)


def make_plan(half, group_id, slice_start, cont_group, plan):
    member = lax.axis_index("dp")
    own, other = group_id[member], cont_group[0]
    plan[0] = lax.div(slice_start[member], PROMPT_DEV)

    def step(index, _):
        rank = lax.div(slice_start[index], PROMPT_DEV)

        @pl.when(group_id[index] == own)
        def _():
            plan[1 + rank] = index

        @pl.when(group_id[index] == other)
        def _():
            plan[1 + half + rank] = index

        return 0

    lax.fori_loop(0, 2 * half, step, 0)


def attend_kernel(
    half,
    group_id,
    slice_start,
    cont_group,
    query,
    key,
    value,
    keys_all,
    values_all,
    mixed,
    attended,
    log_total,
    plan,
):
    @pl.when(pl.program_id(0) == 0)
    def _():
        make_plan(half, group_id, slice_start, cont_group, plan)

    def part(start, count, steps, offset):
        span = pl.ds(start, count)
        queries = query[span]
        allowed = lax.broadcasted_iota(jnp.int32, (count, count), 0) >= lax.broadcasted_iota(
            jnp.int32, (count, count), 1
        )
        scores = jnp.where(allowed, dot(queries, key[span], 1, 1) * SCALE, NEGATIVE)
        top = jnp.max(scores, axis=-1, keepdims=True)
        weights = jnp.exp(scores - top)
        total = jnp.sum(weights, axis=-1, keepdims=True)
        result = dot(weights.astype(LOW), value[span])

        def step(index, carry):
            top, total, result = carry
            place = plan[offset + index]
            scores = dot(queries, keys_all[place], 1, 1) * SCALE
            higher = jnp.maximum(top, jnp.max(scores, axis=-1, keepdims=True))
            fade = jnp.exp(top - higher)
            weights = jnp.exp(scores - higher)
            total = total * fade + jnp.sum(weights, axis=-1, keepdims=True)
            result = result * fade + dot(weights.astype(LOW), values_all[place])
            return higher, total, result

        top, total, result = lax.fori_loop(0, steps, step, (top, total, result))
        result = result / total
        mixed[span] = result.astype(LOW)
        attended[span] = result
        log_total[span] = jnp.broadcast_to(top + jnp.log(total), (count, HEAD))

    part(0, PROMPT_DEV, plan[0], 1)
    part(PROMPT_DEV, query.shape[0] - PROMPT_DEV, half, 1 + half)


def attend(readers, query, key, value, keys_all, values_all):
    rows, width = query.shape
    members = keys_all.shape[0]
    head = pl.BlockSpec((rows, HEAD), lambda h, *_: (0, h))
    every = pl.BlockSpec((members, PROMPT_DEV, HEAD), lambda h, *_: (0, 0, h))
    return pl.pallas_call(
        functools.partial(attend_kernel, members // 2),
        out_shape=[
            shape((rows, width), LOW),
            shape((rows, width), WIDE),
            shape((rows, width), WIDE),
        ],
        grid_spec=pltpu.PrefetchScalarGridSpec(
            num_scalar_prefetch=3,
            grid=(width // HEAD,),
            in_specs=[head, head, head, every, every],
            out_specs=[head, head, head],
            scratch_shapes=[pltpu.SMEM((members + 1,), jnp.int32)],
        ),
        compiler_params=pltpu.CompilerParams(vmem_limit_bytes=VMEM_LIMIT),
        name="attend",
    )(*readers, query, key, value, keys_all, values_all)


def attend_back_kernel(
    half,
    group_id,
    slice_start,
    cont_group,
    query,
    key,
    value,
    keys_all,
    values_all,
    branch_low,
    w_out,
    attended,
    log_total,
    cosine,
    sine,
    d_query,
    d_keys_all,
    d_values_all,
    d_key_own,
    d_value_own,
    d_mixed,
    key_total,
    value_total,
    plan,
):
    @pl.when(pl.program_id(0) == 0)
    def _():
        make_plan(half, group_id, slice_start, cont_group, plan)

    d_mixed[...] = dot(branch_low[...], w_out[...], 1, 1).astype(LOW)
    key_total[...] = jnp.zeros_like(key_total)
    value_total[...] = jnp.zeros_like(value_total)

    def part(start, count, steps, offset):
        span = pl.ds(start, count)
        queries, d_attended = query[span], d_mixed[span]
        log_sum = log_total[span][:, :1]
        center = jnp.sum(d_attended.astype(WIDE) * attended[span], axis=-1, keepdims=True)

        def back(scores, keys, values):
            probabilities = jnp.exp(scores - log_sum)
            d_scores = (probabilities * (dot(d_attended, values, 1, 1) - center)).astype(LOW)
            return (
                dot(d_scores, keys),
                dot(d_scores, queries, 0, 0),
                dot(probabilities.astype(LOW), d_attended, 0, 0),
            )

        allowed = lax.broadcasted_iota(jnp.int32, (count, count), 0) >= lax.broadcasted_iota(
            jnp.int32, (count, count), 1
        )
        scores = jnp.where(allowed, dot(queries, key[span], 1, 1) * SCALE, NEGATIVE)
        d_queries, d_own_keys, d_own_values = back(scores, key[span], value[span])

        def step(index, d_queries):
            place = plan[offset + index]
            keys, values = keys_all[place], values_all[place]
            more, d_keys, d_values = back(dot(queries, keys, 1, 1) * SCALE, keys, values)
            key_total[place] += d_keys
            value_total[place] += d_values
            return d_queries + more

        d_queries = lax.fori_loop(0, steps, step, d_queries) * SCALE
        d_query[span] = rotate(d_queries, cosine[span], -sine[span]).astype(LOW)
        return d_own_keys, d_own_values

    member = lax.axis_index("dp")
    d_own_keys, d_own_values = part(0, PROMPT_DEV, plan[0], 1)
    key_total[member] += d_own_keys
    value_total[member] += d_own_values
    d_own_keys, d_own_values = part(PROMPT_DEV, query.shape[0] - PROMPT_DEV, half, 1 + half)
    late = pl.ds(PROMPT_DEV, query.shape[0] - PROMPT_DEV)
    d_key_own[...] = rotate(d_own_keys * SCALE, cosine[late], -sine[late]).astype(LOW)
    d_value_own[...] = d_own_values.astype(LOW)
    d_keys_all[...] = (key_total[...] * SCALE).astype(LOW)
    d_values_all[...] = value_total[...].astype(LOW)


def attend_back(
    readers,
    query,
    key,
    value,
    keys_all,
    values_all,
    branch_low,
    w_out,
    attended,
    log_total,
    cosine,
    sine,
):
    rows, width = query.shape
    members = keys_all.shape[0]
    depth = branch_low.shape[1]
    late = rows - PROMPT_DEV
    heads = width // HEAD
    head = pl.BlockSpec((rows, HEAD), lambda h, *_: (0, h))
    every = pl.BlockSpec((members, PROMPT_DEV, HEAD), lambda h, *_: (0, 0, h))
    own = pl.BlockSpec((late, HEAD), lambda h, *_: (0, h))
    table = pl.BlockSpec((rows, HEAD), lambda h, *_: (0, 0))
    return pl.pallas_call(
        functools.partial(attend_back_kernel, members // 2),
        out_shape=[
            shape((rows, width), LOW),
            shape((members, PROMPT_DEV, width), LOW),
            shape((members, PROMPT_DEV, width), LOW),
            shape((late, width), LOW),
            shape((late, width), LOW),
        ],
        grid_spec=pltpu.PrefetchScalarGridSpec(
            num_scalar_prefetch=3,
            grid=(heads,),
            in_specs=[
                head,
                head,
                head,
                every,
                every,
                pl.BlockSpec((rows, depth), lambda h, *_: (0, 0)),
                pl.BlockSpec((HEAD, depth), lambda h, *_: (h, 0)),
                head,
                head,
                table,
                table,
            ],
            out_specs=[head, every, every, own, own],
            scratch_shapes=[
                pltpu.VMEM((rows, HEAD), LOW),
                pltpu.VMEM((members, PROMPT_DEV, HEAD), WIDE),
                pltpu.VMEM((members, PROMPT_DEV, HEAD), WIDE),
                pltpu.SMEM((members + 1,), jnp.int32),
            ],
        ),
        compiler_params=pltpu.CompilerParams(vmem_limit_bytes=VMEM_LIMIT),
        name="attend_back",
    )(
        *readers,
        query,
        key,
        value,
        keys_all,
        values_all,
        branch_low,
        w_out,
        attended,
        log_total,
        cosine,
        sine,
    )


def place_of(group_id, slice_start, group, rank):
    place = 0
    for index in range(group_id.shape[0]):
        found = (group_id[index] == group) & (slice_start[index] == rank * PROMPT_DEV)
        place = jnp.maximum(place, jnp.where(found, index, 0))
    return place


def own_part(rows):
    return lax.broadcasted_iota(jnp.int32, (rows, rows), 0) >= lax.broadcasted_iota(
        jnp.int32, (rows, rows), 1
    )


def gather_attend_kernel(
    members,
    group_id,
    slice_start,
    cont_group,
    w_query_in,
    w_key_in,
    w_value_in,
    states_in,
    table,
    act,
    query,
    key,
    value,
    cosine,
    sine,
    mixed,
    attended,
    log_total,
    keys_out,
    values_out,
    states,
    weights,
    load_sem,
    weight_sem,
    send_sem,
    recv_sem,
    keep_sem,
    out_sem,
    *every,
):
    member, tensor = lax.axis_index("dp"), lax.axis_index("tensor")
    heads = query.shape[0]
    keys_all, values_all = every[:heads], every[heads:]
    half = members // 2
    rows = states.shape[0]
    chunks = load_sem.shape[0]
    size = rows // chunks
    loads = []
    for index in range(chunks):
        span = pl.ds(index * size, size)
        loads.append(pltpu.make_async_copy(states_in.at[span], states.at[span], load_sem.at[index]))
    w_loads = [
        pltpu.make_async_copy(source, weights.at[index], weight_sem.at[index])
        for index, source in enumerate((w_key_in, w_value_in, w_query_in))
    ]
    for load in loads[:1] + w_loads[:1] + loads[1:] + w_loads[1:]:
        load.start()
    hail(member_peers(members))
    index = lax.broadcasted_iota(jnp.int32, cosine.shape, 0)
    prompt = half * PROMPT_DEV - PROMPT_DEV
    positions = index + jnp.where(index < PROMPT_DEV, slice_start[member], prompt)
    angles = positions.astype(WIDE) * table[:1]
    cosine[...] = jnp.cos(angles)
    sine[...] = jnp.sin(angles) * table[1:2]
    step = 64
    for index in range(chunks):
        loads[index].wait()
        for start in range(index * size, index * size + size, step):
            span = pl.ds(start, step)
            act[span] = norm_rows(states[span])[0].astype(LOW)

    def turned(weight, out):
        linear = dot(act[...], weight)
        for head in range(heads):
            out[head] = rotate(
                linear[:, head * HEAD : head * HEAD + HEAD], cosine[...], sine[...]
            ).astype(LOW)

    high = [bit for bit in bits_of(members) if bit]
    orders = (high + [0], high[::-1] + [0])
    owns, alls = (key, value), (keys_all, values_all)
    early = pl.ds(0, PROMPT_DEV)

    def copy(flow, head, mask, bit):
        slot = mask | 1 << bit
        place = alls[flow][head].at[flip(member, mask)]
        return remote(
            place if mask else owns[flow].at[head, early],
            place,
            send_sem.at[flow, head, slot],
            recv_sem.at[flow, head, slot],
            (flip(member, 1 << bit), tensor),
        )

    def forward(flow, head, mask):
        order = orders[flow]
        last = max([order.index(bit) for bit in order if mask >> bit & 1], default=-1)
        for bit in order[last + 1 :]:
            copy(flow, head, mask, bit).start()

    def came_by(flow, head, mask):
        order = orders[flow]
        bit = order[max(order.index(bit) for bit in order if mask >> bit & 1)]
        return copy(flow, head, mask ^ 1 << bit, bit)

    def keep(flow, head):
        return pltpu.make_async_copy(
            owns[flow].at[head, early], alls[flow][head].at[member], keep_sem.at[flow, head]
        )

    def write(flow, head):
        return pltpu.make_async_copy(
            alls[flow][head], (keys_out, values_out)[flow].at[head], out_sem.at[flow, head]
        )

    masks = range(1, members)
    levels = len(high)

    def own_sends(head):
        if head < heads:
            for flow in (0, 1):
                forward(flow, head, 0)
            for flow in (0, 1):
                keep(flow, head).start()

    def level(head, count):
        if head < heads:
            for mask in masks:
                if not mask & 1 and mask.bit_count() == count:
                    for flow in (0, 1):
                        came_by(flow, head, mask).wait_recv()
                        forward(flow, head, mask)

    def complete(head):
        for flow in (0, 1):
            for mask in masks:
                if mask & 1:
                    came_by(flow, head, mask).wait_recv()
            keep(flow, head).wait()
            write(flow, head).start()

    own_group, other_group = group_id[member], cont_group[0]
    own_start = slice_start[member]
    own_places = [place_of(group_id, slice_start, own_group, rank) for rank in range(half)]
    other_places = [place_of(group_id, slice_start, other_group, rank) for rank in range(half)]
    block = 128

    def attend_rows(head, start, places, whole):
        span = pl.ds(start, block)
        queries = query[head, span]
        scores, values = [], []
        for rank, place in enumerate(places):
            score = dot(queries, keys_all[head][place], 1, 1) * SCALE_TWO
            if not whole:
                at = lax.broadcasted_iota(jnp.int32, score.shape, 0) + (own_start + start)
                to = lax.broadcasted_iota(jnp.int32, score.shape, 1) + rank * PROMPT_DEV
                score = jnp.where(to <= at, score, NEGATIVE)
            scores.append(score)
            values.append(values_all[head][place])
        if whole:
            score = dot(queries, key[head, span], 1, 1) * SCALE_TWO
            scores.append(jnp.where(own_part(block), score, NEGATIVE))
            values.append(value[head, span])
        top = functools.reduce(
            jnp.maximum, [jnp.max(score, axis=-1, keepdims=True) for score in scores]
        )
        total = jnp.zeros_like(top)
        result = jnp.zeros((block, HEAD), WIDE)
        for score, held in zip(scores, values):
            weight = jnp.exp2(score - top)
            total += jnp.sum(weight, axis=-1, keepdims=True)
            result += dot(weight.astype(LOW), held)
        result = result / total
        mixed[span, head * HEAD : head * HEAD + HEAD] = result.astype(LOW)
        attended[head, span] = result
        log_total[head, span] = jnp.broadcast_to(top + jnp.log2(total), (block, HEAD))

    w_loads[0].wait()
    turned(weights[0], key)
    heed(member_peers(members))
    w_loads[1].wait()
    linear = dot(act[...], weights[1])
    for head in range(heads):
        value[head] = linear[:, head * HEAD : head * HEAD + HEAD].astype(LOW)
    own_sends(0)
    own_sends(1)
    w_loads[2].wait()
    turned(weights[2], query)
    level(0, 1)
    own_sends(2)
    for count in range(2, levels + 1):
        level(0, count)
    level(1, 1)
    own_sends(3)
    for head in range(heads):
        complete(head)

        @pl.loop(0, PROMPT_DEV // block)
        def _(index, head=head):
            attend_rows(head, pl.multiple_of(index * block, block), own_places, False)

        for count in range(2, levels + 1):
            level(head + 1, count)
        level(head + 2, 1)
        own_sends(head + 4)
        for start in range(PROMPT_DEV, rows, block):
            attend_rows(head, start, other_places, True)
    for head in range(heads):
        for flow in (0, 1):
            write(flow, head).wait()
            for mask in masks:
                came_by(flow, head, mask).wait_send()


def gather_attend(members, readers, w_query, w_key, w_value, states, table):
    rows, depth = states.shape
    width = w_query.shape[1]
    heads = width // HEAD
    smem = pl.BlockSpec(memory_space=pltpu.SMEM)
    row_heads = (heads, rows, HEAD)
    every = (heads, members, PROMPT_DEV, HEAD)
    return pl.pallas_call(
        functools.partial(gather_attend_kernel, members),
        out_shape=[
            shape((rows, depth), LOW),
            shape(row_heads, LOW),
            shape(row_heads, LOW),
            shape(row_heads, LOW),
            shape((rows, HEAD), WIDE),
            shape((rows, HEAD), WIDE),
            shape((rows, width), LOW),
            shape(row_heads, WIDE),
            shape(row_heads, WIDE),
            shape(every, LOW),
            shape(every, LOW),
        ],
        in_specs=[smem] * 3 + [ANY] * 4 + [VMEM],
        out_specs=[VMEM] * 9 + [ANY] * 2,
        scratch_shapes=[
            pltpu.VMEM((rows, depth), WIDE),
            pltpu.VMEM((3, depth, width), LOW),
            DMA((4,)),
            DMA((3,)),
            DMA((2, heads, members)),
            DMA((2, heads, members)),
            DMA((2, heads)),
            DMA((2, heads)),
        ]
        + [pltpu.VMEM(every[1:], LOW)] * (2 * heads),
        compiler_params=pltpu.CompilerParams(
            collective_id=6, has_side_effects=True, vmem_limit_bytes=VMEM_LIMIT
        ),
        name="gather_attend",
    )(
        *readers,
        w_query,
        w_key,
        w_value,
        states,
        table,
    )


def back_owner_kernel(
    members,
    count,
    group_id,
    slice_start,
    cont_group,
    keys_in,
    values_in,
    query_in,
    key_in,
    value_in,
    attended_in,
    log_total_in,
    branch_low,
    w_out,
    cosine,
    sine,
    own_out,
    d_query,
    d_key,
    d_value,
    early_out,
    query,
    key,
    value,
    attended,
    log_total,
    d_mixed,
    d_queries,
    own_keys,
    own_values,
    other_keys,
    other_values,
    load_sem,
    *refs,
):
    take = taker(refs)
    member = lax.axis_index("dp")
    heads, rows = query.shape[0], query.shape[1]
    keys_all, values_all = take(heads), take(heads)
    out_send, out_recv = take(2)
    here = lax.axis_index("tensor")
    size = own_out.shape[0]
    own_rows = pl.ds(pl.multiple_of(here * size, size), size)

    def tell(distance):
        return remote(
            own_out,
            early_out.at[own_rows],
            out_send.at[distance - 1],
            out_recv.at[distance - 1],
            (member, lax.rem(here + distance, count)),
        )

    half = pairs = members // 2
    parity = lax.rem(member, 2)
    order = bits_of(pairs)
    moves, flows, sides = [], [], []
    for way in (order, order[::-1]):
        mine, leaving, theirs = take(3)
        local_free, send_sem, recv_sem = take(3)
        refs_of = take(4)
        sides.append((mine, leaving, theirs, send_sem, recv_sem))
        per_head = []
        for head in range(heads):

            def own(mask, target, columns, mine=mine, theirs=theirs, head=head):
                return mine[head, target, :, columns].astype(WIDE) + theirs[
                    head, target, :, columns
                ].astype(WIDE)

            per_head.append(Halving(pairs, way, own, [ref.at[head] for ref in refs_of]))
        flows.append(per_head)
    partner = (flip(member, 1), lax.axis_index("tensor"))

    sources = (keys_in, values_in, query_in, key_in, value_in, attended_in, log_total_in)

    def load(index, head):
        if index < 2:
            target = (keys_all, values_all)[index][head]
        else:
            target = (query, key, value, attended, log_total)[index - 2].at[head]
        return pltpu.make_async_copy(
            sources[index].at[head], target, load_sem.at[index, head]
        )

    for head in range(heads):
        for index in range(len(sources)):
            load(index, head).start()

    def across(flow, head):
        _, leaving, theirs, send_sem, recv_sem = sides[flow]
        return remote(
            leaving.at[head], theirs.at[head], send_sem.at[head], recv_sem.at[head], partner
        )

    own_group, other_group = group_id[member], cont_group[0]
    own_start = slice_start[member]
    own_places = [place_of(group_id, slice_start, own_group, rank) for rank in range(half)]
    other_places = [place_of(group_id, slice_start, other_group, rank) for rank in range(half)]
    across_line = [(member, lax.rem(here + distance, count)) for distance in range(1, count)]
    hail(member_peers(members) + across_line)
    linear = dot(branch_low[...], w_out[...], 1, 1)
    for head in range(heads):
        d_mixed[head] = linear[:, head * HEAD : head * HEAD + HEAD].astype(LOW)
    heed(member_peers(members) + across_line)
    for distance in range(1, count):
        tell(distance).start()
    early_out[own_rows] = own_out[...]
    late = rows - PROMPT_DEV

    def back(scores, queries, keys, values, d_attended, log_sum, center):
        probabilities = jnp.exp2(scores - log_sum)
        d_scores = (probabilities * (dot(d_attended, values, 1, 1) - center)).astype(LOW)
        return (
            dot(d_scores, keys),
            dot(d_scores, queries, 0, 0),
            dot(probabilities.astype(LOW), d_attended, 0, 0),
        )

    def rows_of(head, start, count):
        span = pl.ds(start, count)
        d_attended = d_mixed[head, span]
        center = jnp.sum(d_attended.astype(WIDE) * attended[head, span], axis=-1, keepdims=True)
        return query[head, span], d_attended, log_total[head, span][:, :1], center

    def prompt_rank(head, rank):
        queries, d_attended, log_sum, center = rows_of(head, 0, PROMPT_DEV)
        place = own_places[rank]
        keys, values = keys_all[head][place], values_all[head][place]
        scores = dot(queries, keys, 1, 1) * SCALE_TWO
        at = lax.broadcasted_iota(jnp.int32, scores.shape, 0) + own_start
        to = lax.broadcasted_iota(jnp.int32, scores.shape, 1) + rank * PROMPT_DEV
        scores = jnp.where(to <= at, scores, NEGATIVE)
        more, d_keys, d_values = back(
            scores, queries, keys, values, d_attended, log_sum, center
        )
        early = pl.ds(0, PROMPT_DEV)
        if rank:
            d_queries[early] += more
        else:
            d_queries[early] = more
        own_keys[rank] = d_keys
        own_values[rank] = d_values

    def late_part(head):
        queries, d_attended, log_sum, center = rows_of(head, PROMPT_DEV, late)
        span = pl.ds(PROMPT_DEV, late)
        keys, values = key[head, span], value[head, span]
        scores = jnp.where(own_part(late), dot(queries, keys, 1, 1) * SCALE_TWO, NEGATIVE)
        total, d_keys, d_values = back(
            scores, queries, keys, values, d_attended, log_sum, center
        )
        columns = pl.ds(head * HEAD, HEAD)
        d_key[span, columns] = rotate(d_keys * SCALE, cosine[span], -sine[span]).astype(LOW)
        d_value[span, columns] = d_values.astype(LOW)
        for rank in range(half):
            place = other_places[rank]
            keys, values = keys_all[head][place], values_all[head][place]
            more, d_keys, d_values = back(
                dot(queries, keys, 1, 1) * SCALE_TWO, queries, keys, values, d_attended, log_sum, center
            )
            total += more
            other_keys[rank] = d_keys
            other_values[rank] = d_values
        d_queries[span] = total
        d_query[:, columns] = rotate(d_queries[...] * SCALE, cosine[...], -sine[...]).astype(LOW)

    def spread(head):
        for pair in range(pairs):
            for away in (0, 1):
                index = 2 * pair + (1 - parity if away else parity)
                rank = lax.div(slice_start[index], PROMPT_DEV)
                mine = jnp.where(group_id[index] == own_group, 1.0, 0.0)
                other = jnp.where(group_id[index] == other_group, 1.0, 0.0)
                for flow, (a, b, scale) in enumerate(
                    ((own_keys, other_keys, SCALE), (own_values, other_values, 1.0))
                ):
                    total = a[rank] * (mine * scale) + b[rank] * (other * scale)
                    sides[flow][away][head, pair] = total.astype(LOW)

    def begin(head):
        for flow in (0, 1):
            across(flow, head).start()

    def stage(head, index):
        if not 0 <= head < heads:
            return
        for flow in (0, 1):
            if not index:
                across(flow, head).wait_recv()
        for flow in (0, 1):
            for mask in flows[flow][head].steps(index):
                flows[flow][head].push(mask)

    def end(head):
        if not 0 <= head < heads:
            return
        early = pl.ds(0, PROMPT_DEV)
        columns = pl.ds(head * HEAD, HEAD)
        total = d_queries.at[early]
        flows[0][head].end(total)
        d_key[early, columns] = rotate(total[...], cosine[early], -sine[early]).astype(LOW)
        flows[1][head].end(d_value.at[early, columns])

    depth = len(order)
    for head in range(heads):
        for index in range(len(sources)):
            load(index, head).wait()
        for rank in range(half):
            prompt_rank(head, rank)
            if rank == 0:
                stage(head - 1, 0)
            if rank == half - 1:
                for index in range(1, depth):
                    stage(head - 1, index)
        late_part(head)
        spread(head)
        begin(head)
        end(head - 1)
    for index in range(depth):
        stage(heads - 1, index)
    end(heads - 1)
    for flow in (0, 1):
        for head in range(heads):
            across(flow, head).wait_send()
            flows[flow][head].sent()
    for distance in range(1, count):
        tell(distance).wait()


def back_owner(
    members,
    count,
    readers,
    keys_all,
    values_all,
    query,
    key,
    value,
    branch_low,
    w_out,
    attended,
    log_total,
    cosine,
    sine,
    own_out,
):
    heads, rows, _ = query.shape
    width = heads * HEAD
    pairs = members // 2
    smem = pl.BlockSpec(memory_space=pltpu.SMEM)
    every = pltpu.VMEM((members, PROMPT_DEV, HEAD), LOW)
    side = pltpu.VMEM((heads, pairs, PROMPT_DEV, HEAD), LOW)
    step = pltpu.VMEM((heads, pairs - 1, PROMPT_DEV, HEAD), LOW)
    flow = [side] * 3 + [DMA((heads,))] * 3 + [step] * 2 + [DMA((heads, pairs - 1, 1))] * 2
    total = pltpu.VMEM((pairs, PROMPT_DEV, HEAD), WIDE)
    return pl.pallas_call(
        functools.partial(back_owner_kernel, members, count),
        out_shape=[shape((rows, width), LOW)] * 3
        + [shape((count * own_out.shape[0], own_out.shape[1]), LOW)],
        in_specs=[smem] * 3 + [ANY] * 7 + [VMEM] * 5,
        out_specs=[VMEM] * 4,
        scratch_shapes=[
            pltpu.VMEM((heads, rows, HEAD), LOW),
            pltpu.VMEM((heads, rows, HEAD), LOW),
            pltpu.VMEM((heads, rows, HEAD), LOW),
            pltpu.VMEM((heads, rows, HEAD), WIDE),
            pltpu.VMEM((heads, rows, HEAD), WIDE),
            pltpu.VMEM((heads, rows, HEAD), LOW),
            pltpu.VMEM((rows, HEAD), WIDE),
            total,
            total,
            total,
            total,
            DMA((7, heads)),
        ]
        + [every] * (2 * heads)
        + [DMA((count - 1,))] * 2
        + flow * 2,
        compiler_params=pltpu.CompilerParams(
            collective_id=7, has_side_effects=True, vmem_limit_bytes=VMEM_LIMIT
        ),
        name="back_owner",
    )(
        *readers,
        keys_all,
        values_all,
        query,
        key,
        value,
        attended,
        log_total,
        branch_low,
        w_out,
        cosine,
        sine,
        own_out,
    )


def middle_kernel(
    count,
    mixed,
    w_out,
    states,
    cotangent_in,
    w_gate_in,
    w_up_in,
    w_down_in,
    act,
    resid,
    out_low_out,
    ffn_early,
    ffn_late,
    d_act_out,
    hidden_out,
    d_gate_out,
    d_up_out,
    part,
    cotangent,
    out_low,
    d_hidden,
    w_gate,
    w_up,
    w_down,
    rows_in,
    ffn_total,
    d_total,
    ffn,
    d_act,
    hidden,
    d_gate,
    d_up,
    state_sem,
    cot_sem,
    weight_sem,
    out_sem,
    *refs,
):
    line = Line(count, refs)
    rows, size = resid.shape[0], line.rows
    fetch = pltpu.make_async_copy(
        states.at[pl.ds(pl.multiple_of(line.here * rows, rows), rows)], resid, state_sem
    )
    slots, step, _ = cotangent.shape

    def cot_load(index):
        return pltpu.make_async_copy(
            cotangent_in.at[pl.ds(index * step, step)],
            cotangent.at[index % slots],
            cot_sem.at[index % slots],
        )

    down_load, gate_load, up_load = [
        pltpu.make_async_copy(source, target, weight_sem.at[index])
        for index, (source, target) in enumerate(
            ((w_down_in, w_down), (w_gate_in, w_gate), (w_up_in, w_up))
        )
    ]
    fetch.start()
    for index in range(slots):
        cot_load(index).start()
    for load in (down_load, gate_load, up_load):
        load.start()
    hail(line.peers())
    tile = 512
    for start in range(0, part.shape[1], tile):
        columns = pl.ds(start, tile)
        part[:, columns] = dot(mixed[...], w_out[:, columns]).astype(LOW)
    heed(line.peers())
    fetch.wait()

    def finish(group):
        span = pl.ds(group * size, size)
        resid[span] += line.total[...]
        act[line.span(group, line.here)] = norm_rows(resid[span])[0].astype(LOW)

    leaving = []

    def leave(source, target):
        copy = pltpu.make_async_copy(source, target, out_sem.at[len(leaving)])
        copy.start()
        leaving.append(copy)

    def cast():
        steps = out_low.shape[0] // step
        for index in range(steps):
            cot_load(index).wait()
            out_low[pl.ds(index * step, step)] = cotangent[index % slots].astype(LOW)
            if index + slots < steps:
                cot_load(index + slots).start()
        leave(out_low, out_low_out)
        down_load.wait()

    def inner(start):
        span = pl.ds(start, tile)
        d_hidden[:, span] = dot(out_low[...], w_down[span], 1, 1).astype(LOW)

    units, block = d_hidden.shape[1], 256
    starts = list(range(0, units, tile))

    def inners(some):
        def run():
            for start in some:
                inner(start)

        return run

    def begin(group):
        if not group:
            gate_load.wait()
            up_load.wait()
        for chunk in range(count):
            rows_in[pl.ds(chunk * size, size)] = act[line.span(group, chunk)]
        ffn_total[...] = jnp.zeros_like(ffn_total)
        d_total[...] = jnp.zeros_like(d_total)

    def feed(group, first, last):
        @pl.loop(first, last)
        def _(index):
            columns = pl.ds(pl.multiple_of(index * block, block), block)
            gate = dot(rows_in[...], w_gate[:, columns])
            up = dot(rows_in[...], w_up[:, columns])
            sigmoid = jax.nn.sigmoid(gate)
            swish = gate * sigmoid
            d_inner = jnp.concatenate(
                [d_hidden[line.span(group, chunk), columns] for chunk in range(count)]
            ).astype(WIDE)
            new_hidden = (swish * up).astype(LOW)
            new_gate = (d_inner * up * sigmoid * (1.0 + gate * (1.0 - sigmoid))).astype(LOW)
            new_up = (d_inner * swish).astype(LOW)
            for chunk in range(count):
                own = slice(chunk * size, chunk * size + size)
                hidden[chunk, group, :, columns] = new_hidden[own]
                d_gate[chunk, group, :, columns] = new_gate[own]
                d_up[chunk, group, :, columns] = new_up[own]
            for start in range(0, part.shape[1], tile):
                out = pl.ds(start, tile)
                ffn_total[:, out] += dot(new_hidden, w_down[columns, out])
                d_total[:, out] += dot(new_gate, w_gate[out, columns], 1, 1) + dot(
                    new_up, w_up[out, columns], 1, 1
                )

    def end(group):
        own = pl.ds(pl.multiple_of(line.here * size, size), size)
        ffn_total[own] += resid[pl.ds(group * size, size)]
        ffn[group] = ffn_total[...].astype(LOW)
        leave(ffn.at[group], (ffn_early, ffn_late)[group])
        for chunk in range(count):
            d_act[chunk, group] = d_total[pl.ds(chunk * size, size)].astype(LOW)
        for source, target in (
            (d_act, d_act_out),
            (hidden, hidden_out),
            (d_gate, d_gate_out),
            (d_up, d_up_out),
        ):
            leave(source.at[:, group], target.at[:, group])

    blocks = units // block
    third = -(-blocks // 3)

    def opening():
        begin(0)
        feed(0, 0, third)

    def closing():
        feed(0, 2 * third, blocks)
        end(0)

    line.reduce(
        part,
        act,
        finish,
        [
            cast,
            inners(starts[:1]),
            inners(starts[1:2]),
            inners(starts[2:]),
            opening,
            lambda: feed(0, third, 2 * third),
            closing,
        ],
    )
    begin(1)
    feed(1, 0, blocks)
    end(1)
    for copy in leaving:
        copy.wait()
    line.sent(act)


def middle(count, mixed, w_out, states, cotangent, w_gate, w_up, w_down):
    rows, depth = states.shape
    units = w_down.shape[0]
    size = rows // count // GROUPS
    split = (count, GROUPS, size)
    wide, inside = (*split, depth), (*split, units)
    some = (GROUPS, rows // GROUPS, depth)
    outs = pl.pallas_call(
        functools.partial(middle_kernel, count),
        out_shape=[
            shape((rows, depth), LOW),
            shape((rows // count, depth), WIDE),
            shape((rows, depth), LOW),
            shape(some[1:], LOW),
            shape(some[1:], LOW),
            shape(wide, LOW),
            shape(inside, LOW),
            shape(inside, LOW),
            shape(inside, LOW),
        ],
        in_specs=[VMEM] * 2 + [ANY] * 5,
        out_specs=[VMEM] * 2 + [ANY] * 7,
        scratch_shapes=[
            pltpu.VMEM((rows, depth), LOW),
            pltpu.VMEM((2, 64, depth), WIDE),
            pltpu.VMEM((rows, depth), LOW),
            pltpu.VMEM((rows, units), LOW),
            pltpu.VMEM((depth, units), LOW),
            pltpu.VMEM((depth, units), LOW),
            pltpu.VMEM((units, depth), LOW),
            pltpu.VMEM(some[1:], LOW),
            pltpu.VMEM(some[1:], WIDE),
            pltpu.VMEM(some[1:], WIDE),
            pltpu.VMEM(some, LOW),
            pltpu.VMEM(wide, LOW),
            pltpu.VMEM(inside, LOW),
            pltpu.VMEM(inside, LOW),
            pltpu.VMEM(inside, LOW),
            DMA,
            DMA((2,)),
            DMA((3,)),
            DMA((1 + 5 * GROUPS,)),
        ]
        + Line.scratch(count, GROUPS, rows // count, depth),
        compiler_params=pltpu.CompilerParams(
            collective_id=2, has_side_effects=True, vmem_limit_bytes=VMEM_LIMIT
        ),
        name="middle",
    )(mixed, w_out, states, cotangent, w_gate, w_up, w_down)
    return [*outs[:5], *(out.reshape(rows, -1) for out in outs[5:])]


def second_kernel(
    count,
    pairs,
    d_act,
    ffn,
    resid,
    cotangent,
    act,
    d_gate,
    d_up,
    branch_low,
    grad_resid,
    own_out,
    grad_gate,
    grad_up,
    cot_sem,
    *refs,
):
    take = taker(refs)
    line = Line(count, take(Line.scratch_count))
    out_line = Line(count, take(Line.scratch_count))
    lhs = Lhs(act, take(4))
    rights = [Rhs([source], take(4)) for source in (d_gate, d_up)]
    order = bits_of(pairs)
    flows = [
        Halving(pairs, way, product_of(lhs, right), take(4), *take(1))
        for way, right in zip((order, order[::-1]), rights)
    ]
    rows = resid.shape[0]
    fetch = pltpu.make_async_copy(
        cotangent.at[pl.ds(pl.multiple_of(line.here * rows, rows), rows)], grad_resid, cot_sem
    )
    fetch.start()
    greet(line.peers() + member_peers(2 * pairs))
    lhs.start()
    for piece in range(flows[0].pieces):
        for right in rights:
            right.start(piece)
    fetch.wait()

    def finish(group):
        span = pl.ds(group * line.rows, line.rows)
        normed, inverse = norm_rows(resid[span])
        grad_resid[span] += norm_back(line.total[...], normed, inverse)
        branch_low[line.span(group, line.here)] = grad_resid[span].astype(LOW)

    sides = [(lhs, right, flow) for right, flow in zip(rights, flows)]
    ahead, early, others, settle, late = beside(order, sides)

    def out_slot(slot):
        return lambda: out_line.scatter_slot(0, slot, ffn)

    slots = [out_slot(slot) for slot in range(count - 1)]

    def fourth():
        settle()
        slots[0]()

    line.reduce(d_act, branch_low, finish, [ahead, early, others, fourth, late] + slots[1:])
    out_line.scatter_end(0, ffn)
    own_out[...] = out_line.total[...].astype(LOW)
    flows[0].end(grad_gate)
    flows[1].end(grad_up)
    for flow in flows:
        flow.sent()
    for move in [lhs] + rights:
        move.sent()
    line.sent(branch_low)
    out_line.sent()


def beside(order, sides):
    masks = [flow.steps(0) for _, _, flow in sides]

    def ahead():
        for (lhs, rhs, flow), (mask, *_) in zip(sides[:2], masks):
            lhs.ready()
            rhs.ready(0)
            flow.push_piece(mask, 0)

    def early():
        for at, ((lhs, rhs, flow), (mask, *_)) in enumerate(zip(sides, masks)):
            if at > 1:
                lhs.ready()
            for piece in range(0 if at > 1 else 1, flow.pieces):
                rhs.ready(piece)
                flow.push_piece(mask, piece)

    def others():
        for index in range(1, len(masks[0])):
            for (_, _, flow), steps in zip(sides, masks):
                flow.push(steps[index])

    def settle():
        for _, _, flow in sides:
            flow.settle()

    def late():
        for stage in range(1, len(order)):
            for index in range(len(sides[0][2].steps(stage))):
                for _, _, flow in sides:
                    flow.push(flow.steps(stage)[index])

    return [ahead, early, others, settle, late]


def second(count, members, d_act, ffn, resid, cotangent, act, d_gate, d_up):
    rows, depth = cotangent.shape
    units = d_gate.shape[1]
    pairs = members // 2
    block = depth // members
    return pl.pallas_call(
        functools.partial(second_kernel, count, pairs),
        out_shape=[
            shape((rows, depth), LOW),
            shape((rows // count, depth), WIDE),
            shape((ffn.shape[0] // count, depth), LOW),
            shape((block, units), LOW),
            shape((block, units), LOW),
        ],
        in_specs=[VMEM] * 3 + [ANY] * 4,
        out_specs=[VMEM] * 5,
        scratch_shapes=[DMA]
        + Line.scratch(count, GROUPS, rows // count, depth)
        + Line.scratch(count, 1, ffn.shape[0] // count, depth)
        + Lhs.scratch(pairs, rows, block)
        + Rhs.scratch(rows, units) * 2
        + (Halving.scratch(pairs, block, units) + [pltpu.VMEM((block, units), WIDE)]) * 2,
        compiler_params=pltpu.CompilerParams(
            collective_id=3, has_side_effects=True, vmem_limit_bytes=VMEM_LIMIT
        ),
        name="second",
    )(d_act, ffn, resid, cotangent, in_blocks(act, members), d_gate, d_up)


def owner_kernel(
    pairs,
    d_keys_all,
    d_values_all,
    d_key_own,
    d_value_own,
    cosine,
    sine,
    d_key,
    d_value,
    *refs,
):
    take = taker(refs)
    parity = lax.rem(lax.axis_index("dp"), 2)
    order = bits_of(pairs)
    width = d_key.shape[1]
    moves, flows = [], []
    for way, source in zip((order, order[::-1]), (d_keys_all, d_values_all)):
        mine, theirs = take(2)
        moves.append(
            Pairwise(
                [
                    (
                        source.at[2 * pair + parity],
                        mine.at[pair],
                        source.at[2 * pair + 1 - parity],
                        theirs.at[pair],
                    )
                    for pair in range(pairs)
                ],
                take(3),
            )
        )

        def own(mask, target, columns, mine=mine, theirs=theirs):
            return mine[target, :, columns].astype(WIDE) + theirs[target, :, columns].astype(WIDE)

        flows.append(Halving(pairs, way, own, take(4)))
    (total,) = take(1)
    greet(member_peers(2 * pairs))
    for move in moves:
        move.start()
    for move, flow in zip(moves, flows):
        move.ready()
        flow.push(flow.masks[0])
    late = pl.ds(PROMPT_DEV, d_key.shape[0] - PROMPT_DEV)
    d_key[late] = d_key_own[...]
    d_value[late] = d_value_own[...]
    for index in range(1, pairs - 1):
        for flow in flows:
            flow.push(flow.masks[index])
    early = pl.ds(0, PROMPT_DEV)
    flows[0].end(total)
    for start in range(0, width, HEAD):
        d_key[early, start : start + HEAD] = rotate(
            total[:, start : start + HEAD], cosine[early], -sine[early]
        ).astype(LOW)
    flows[1].end(d_value.at[early])
    for move, flow in zip(moves, flows):
        flow.sent()
        move.sent()


def owner(members, d_keys_all, d_values_all, d_key_own, d_value_own, cosine, sine):
    width = d_key_own.shape[1]
    rows = cosine.shape[0]
    pairs = members // 2
    flow = (
        [pltpu.VMEM((pairs, PROMPT_DEV, width), LOW)] * 2
        + Pairwise.sems(pairs)
        + Halving.scratch(pairs, PROMPT_DEV, width)
    )
    return pl.pallas_call(
        functools.partial(owner_kernel, pairs),
        out_shape=[shape((rows, width), LOW)] * 2,
        in_specs=[ANY, ANY] + [VMEM] * 4,
        out_specs=[VMEM] * 2,
        scratch_shapes=flow * 2 + [pltpu.VMEM((PROMPT_DEV, width), WIDE)],
        compiler_params=pltpu.CompilerParams(
            collective_id=4, has_side_effects=True, vmem_limit_bytes=VMEM_LIMIT
        ),
        name="owner",
    )(d_keys_all, d_values_all, d_key_own, d_value_own, cosine, sine)


def first_kernel(
    count,
    pairs,
    grad_resid,
    d_query,
    d_key,
    d_value,
    w_query,
    w_key,
    w_value,
    states,
    act,
    mixed,
    branch_low,
    hidden,
    out_low,
    far_query,
    far_key,
    far_value,
    input_grad,
    grad_down,
    grad_out,
    grad_query,
    grad_key,
    grad_value,
    inner_total,
    part,
    state,
    weight,
    state_sem,
    weight_sem,
    *refs,
):
    take = taker(refs)
    line = Line(count, take(Line.scratch_count))
    order = bits_of(pairs)
    sides = []
    for left, rights, way in (
        (out_low, (hidden,), order),
        (act, (far_query, far_key, far_value), order[::-1]),
        (branch_low, (mixed,), order[::-1]),
    ):
        lhs, rhs = Lhs(left, take(4)), Rhs(rights, take(4))
        sides.append((lhs, rhs, Halving(pairs, way, product_of(lhs, rhs), take(4), *take(1))))
    rows = state.shape[0]
    fetch = pltpu.make_async_copy(
        states.at[pl.ds(pl.multiple_of(line.here * rows, rows), rows)], state, state_sem
    )
    loads = [
        pltpu.make_async_copy(source, weight.at[index], weight_sem.at[index])
        for index, source in enumerate((w_query, w_key, w_value))
    ]
    for load in loads:
        load.start()
    fetch.start()
    greet(line.peers() + member_peers(2 * pairs))
    for lhs, rhs, _ in sides[:2]:
        lhs.start()
        rhs.start(0)
    for at, (lhs, rhs, flow) in enumerate(sides):
        if at > 1:
            lhs.start()
        for piece in range(0 if at > 1 else 1, flow.pieces):
            rhs.start(piece)
    for load in loads:
        load.wait()
    tile = 512
    for start in range(0, part.shape[1], tile):
        columns = pl.ds(start, tile)
        part[:, columns] = (
            dot(d_query[...], weight[0, columns], 1, 1)
            + dot(d_key[...], weight[1, columns], 1, 1)
            + dot(d_value[...], weight[2, columns], 1, 1)
        )
    fetch.wait()

    def finish(group):
        span = pl.ds(group * line.rows, line.rows)
        normed, inverse = norm_rows(state[span])
        input_grad[line.span(group, line.here)] = (
            grad_resid[span] + norm_back(line.total[...], normed, inverse)
        ).astype(LOW)

    line.reduce(part, input_grad, finish, beside(order, sides))
    for (_, _, flow), target in zip(sides, (grad_down, inner_total, grad_out)):
        flow.end(target)
    width = grad_query.shape[1]
    for index, target in enumerate((grad_query, grad_key, grad_value)):
        target[...] = inner_total[:, index * width : index * width + width]
    for lhs, rhs, flow in sides:
        flow.sent()
        lhs.sent()
        rhs.sent()
    line.sent(input_grad)


def first(
    count,
    members,
    grad_resid,
    weights,
    states,
    act,
    mixed,
    branch_low,
    hidden,
    out_low,
    d_query,
    d_key,
    d_value,
):
    rows, depth = states.shape
    width = d_query.shape[1]
    units = hidden.shape[1]
    pairs = members // 2
    block = depth // members
    scratch = []
    for wide in (units, 3 * width, width):
        scratch += Lhs.scratch(pairs, rows, block) + Rhs.scratch(rows, wide)
        scratch += Halving.scratch(pairs, block, wide) + [pltpu.VMEM((block, wide), WIDE)]
    return pl.pallas_call(
        functools.partial(first_kernel, count, pairs),
        out_shape=[
            shape((rows, depth), LOW),
            shape((block, units), LOW),
        ]
        + [shape((block, width), LOW)] * 4,
        in_specs=[VMEM] * 4 + [ANY] * 12,
        out_specs=[VMEM] * 6,
        scratch_shapes=[
            pltpu.VMEM((block, 3 * width), LOW),
            pltpu.VMEM((rows, depth), WIDE),
            pltpu.VMEM((rows // count, depth), WIDE),
            pltpu.VMEM((3, depth, width), LOW),
            DMA,
            DMA((3,)),
        ]
        + Line.scratch(count, GROUPS, rows // count, depth)
        + scratch,
        compiler_params=pltpu.CompilerParams(
            collective_id=5, has_side_effects=True, vmem_limit_bytes=VMEM_LIMIT
        ),
        name="first",
    )(
        grad_resid,
        d_query,
        d_key,
        d_value,
        *weights,
        states,
        in_blocks(act, members),
        mixed,
        in_blocks(branch_low, members),
        hidden,
        in_blocks(out_low, members),
        d_query,
        d_key,
        d_value,
    )


def widen_kernel(flat, early, late, *refs):
    count = len(refs) // 2
    sources, whole, targets = refs[:count], refs[count], refs[count + 1 :]
    half = early.shape[0]
    whole[pl.ds(0, half)] = early[...].astype(WIDE)
    whole[pl.ds(half, half)] = late[...].astype(WIDE)
    for index, (source, target) in enumerate(zip(sources, targets)):
        values = source[...].astype(WIDE)
        target[...] = values if index < flat else values.T


def widen(count, early, late, plain, turned):
    def rows(array):
        return pl.BlockSpec((array.shape[0] // count, array.shape[1]), lambda i: (i, 0))

    def columns(array):
        return pl.BlockSpec((array.shape[0], array.shape[1] // count), lambda i: (0, i))

    flipped = [shape(array.shape[::-1], WIDE) for array in turned]
    whole = shape((2 * early.shape[0], early.shape[1]), WIDE)
    return pl.pallas_call(
        functools.partial(widen_kernel, len(plain)),
        out_shape=[whole] + [shape(array.shape, WIDE) for array in plain] + flipped,
        grid=(count,),
        in_specs=[rows(array) for array in (early, late, *plain)]
        + [columns(array) for array in turned],
        out_specs=[rows(array) for array in (whole, *plain, *flipped)],
        compiler_params=pltpu.CompilerParams(vmem_limit_bytes=VMEM_LIMIT),
        name="widen",
    )(early, late, *plain, *turned)


def body(
    states,
    w_query,
    w_key,
    w_value,
    w_out,
    w_gate,
    w_up,
    w_down,
    group_id,
    slice_start,
    cont_group,
    cotangent,
):
    rows = states.shape[0]
    members = lax.axis_size("dp")
    count = lax.axis_size("tensor")
    frequency = 10000.0 ** (-np.arange(HEAD // 2) * 2.0 / HEAD)
    frequency = np.concatenate([frequency, frequency]).astype(np.float32)
    sign = np.repeat([-1.0, 1.0], HEAD // 2).astype(np.float32)
    readers = (group_id, slice_start, cont_group)
    merged = members * PROMPT_DEV * w_query.shape[1] * 2 * 4 <= 16 * 2**20
    if merged:
        table = jnp.stack([frequency, sign])
        act_one, query, key, value, cosine, sine, mixed, attended, log_total, *everyones = (
            gather_attend(members, readers, w_query, w_key, w_value, states, table)
        )
    else:
        index = jnp.arange(rows, dtype=jnp.int32)
        everyone = jnp.arange(members, dtype=jnp.int32)
        own_start = jnp.sum(jnp.where(everyone == lax.axis_index("dp"), slice_start, 0))
        prompt = members // 2 * PROMPT_DEV
        positions = jnp.where(index < PROMPT_DEV, own_start + index, prompt + index - PROMPT_DEV)
        angles = positions.astype(WIDE)[:, None] * frequency[None, :]
        cosine = jnp.cos(angles)
        sine = jnp.sin(angles) * sign[None, :]
        act_one, query, key, value, *everyones = project(
            members, states, w_query, w_key, w_value, cosine, sine
        )
        mixed, attended, log_total = attend(readers, query, key, value, *everyones)
    act_two, resid, out_low, ffn, ffn_late, d_act_two, hidden, d_gate, d_up = middle(
        count, mixed, w_out, states, cotangent, w_gate, w_up, w_down
    )
    branch_low, grad_resid, own_out, grad_gate, grad_up = second(
        count, members, d_act_two, ffn, resid, cotangent, act_two, d_gate, d_up
    )
    ffn_late, branch_low = lax.optimization_barrier((ffn_late, branch_low))
    late_out = lax.psum(ffn_late, "tensor")
    kept = (query, key, value, branch_low, w_out, attended, log_total, cosine, sine)
    if merged:
        d_query, d_key, d_value, early_out = back_owner(
            members, count, readers, *everyones, *kept, own_out
        )
    else:
        d_query, *d_everyones = attend_back(
            readers, query, key, value, *everyones, branch_low, w_out, attended, log_total, cosine, sine
        )
        d_key, d_value = owner(members, *d_everyones, cosine, sine)
        early_out = lax.all_gather(own_out, "tensor", axis=0, tiled=True)
    input_grad, grad_down, grad_out, *grad_inner = first(
        count,
        members,
        grad_resid,
        (w_query, w_key, w_value),
        states,
        act_one,
        mixed,
        branch_low,
        hidden,
        out_low,
        d_query,
        d_key,
        d_value,
    )
    *plain, grad_out, grad_down = widen(
        count,
        early_out,
        late_out,
        (input_grad, *grad_inner, grad_gate, grad_up),
        (grad_out, grad_down),
    )
    return (*plain[:5], grad_out, *plain[5:], grad_down)


def solution(mesh):
    placed = (
        P("dp", None),
        P(None, "tensor"),
        P(None, "tensor"),
        P(None, "tensor"),
        P("tensor", None),
        P(None, "tensor"),
        P(None, "tensor"),
        P("tensor", None),
        P(),
        P(),
        P("dp"),
        P("dp", None),
    )
    return jax.shard_map(
        body,
        mesh=mesh,
        in_specs=placed,
        out_specs=(
            P("dp", None),
            P("dp", None),
            P("dp", "tensor"),
            P("dp", "tensor"),
            P("dp", "tensor"),
            P("tensor", "dp"),
            P("dp", "tensor"),
            P("dp", "tensor"),
            P("tensor", "dp"),
        ),
        check_vma=False,
    )
```

```python
import functools

import jax
import jax.numpy as jnp
import numpy as np
from jax import lax
from jax.experimental import pallas as pl
from jax.experimental.pallas import tpu as pltpu
from jax.sharding import PartitionSpec as P

HEAD = 128
PROMPT_DEV = 384
EPSILON = 1e-05
NEGATIVE = -1e30
SCALE = HEAD ** (-0.5)
SCALE_TWO = float(SCALE * np.log2(np.e))
LOW = jnp.bfloat16
WIDE = jnp.float32
MESH = pl.DeviceIdType.MESH
ANY = pl.BlockSpec(memory_space=pl.ANY)
VMEM = pl.BlockSpec(memory_space=pltpu.VMEM)
DMA = pltpu.SemaphoreType.DMA
VMEM_LIMIT = 62 * 2**20
GROUPS = 2
PIECE = 512


def dot(left, right, left_dim=1, right_dim=0):
    return lax.dot_general(
        left, right, (((left_dim,), (right_dim,)), ((), ())), preferred_element_type=WIDE
    )


def shape(dims, dtype):
    return jax.ShapeDtypeStruct(dims, dtype)


def norm_rows(values):
    row_mean = jnp.mean(values, axis=-1, keepdims=True)
    centred = values - row_mean
    inverse = lax.rsqrt(jnp.mean(centred * centred, axis=-1, keepdims=True) + EPSILON)
    return centred * inverse, inverse


def norm_back(gradient, normed, inverse):
    return inverse * (
        gradient
        - jnp.mean(gradient, axis=-1, keepdims=True)
        - normed * jnp.mean(gradient * normed, axis=-1, keepdims=True)
    )


def rotate(values, cosine, sine):
    return values * cosine + pltpu.roll(values, HEAD // 2, 1) * sine


def flip(index, mask):
    out, bit = index, 1
    while bit <= mask:
        if mask & bit:
            out = out + bit * (1 - 2 * lax.rem(lax.div(index, bit), 2))
        bit *= 2
    return out


def bits_of(count):
    return list(range(count.bit_length() - 1))


def hail(peers):
    barrier = pltpu.get_barrier_semaphore()
    for peer in peers:
        pl.semaphore_signal(barrier, inc=1, device_id=peer, device_id_type=MESH)


def heed(peers):
    pl.semaphore_wait(pltpu.get_barrier_semaphore(), len(peers))


def greet(peers):
    hail(peers)
    heed(peers)


def remote(source, target, send_sem, recv_sem, device):
    return pltpu.make_async_remote_copy(
        src_ref=source,
        dst_ref=target,
        send_sem=send_sem,
        recv_sem=recv_sem,
        device_id=device,
        device_id_type=MESH,
    )


class Line:
    scratch_count = 10

    @staticmethod
    def scratch(count, groups, rows, width):
        rows = rows // groups
        return [
            pltpu.VMEM((rows, width), WIDE),
            pltpu.VMEM((groups, count, rows, width), LOW),
            pltpu.VMEM((groups, count, rows, width), LOW),
            pltpu.VMEM((groups, count, rows, width), LOW),
            DMA((groups, count)),
            DMA((groups, count)),
            DMA((groups, count)),
            DMA((groups, count)),
            DMA((groups, count)),
            DMA((groups, count)),
        ]

    def __init__(self, count, refs):
        self.count = count
        (
            self.total,
            self.outgoing,
            self.from_left,
            self.from_right,
            self.out_sem,
            self.left_sem,
            self.right_sem,
            self.to_right_sem,
            self.to_left_sem,
            self.got_sem,
        ) = refs
        self.groups = self.outgoing.shape[0]
        self.rows = self.total.shape[0]
        self.here = lax.axis_index("tensor")
        member = lax.axis_index("dp")
        self.right = (member, lax.rem(self.here + 1, count))
        self.left = (member, lax.rem(self.here + count - 1, count))

    def peers(self):
        return [self.left, self.right]

    def span(self, group, chunk):
        start = chunk * (self.rows * self.groups) + group * self.rows
        return pl.ds(pl.multiple_of(start, self.rows), self.rows)

    def rightward(self, group, chunk):
        return remote(
            self.outgoing.at[group, chunk],
            self.from_left.at[group, chunk],
            self.out_sem.at[group, chunk],
            self.left_sem.at[group, chunk],
            self.right,
        )

    def leftward(self, group, chunk):
        return remote(
            self.outgoing.at[group, chunk],
            self.from_right.at[group, chunk],
            self.out_sem.at[group, chunk],
            self.right_sem.at[group, chunk],
            self.left,
        )

    def add_and_pass(self, group, chunk, part, right, wait):
        copy, came = (self.rightward, self.from_left) if right else (self.leftward, self.from_right)
        total = part[self.span(group, chunk)].astype(WIDE)
        if wait:
            copy(group, chunk).wait_recv()
            total += came[group, chunk].astype(WIDE)
        self.outgoing[group, chunk] = total.astype(LOW)
        copy(group, chunk).start()

    def scatter_slot(self, group, slot, part):
        here, count = self.here, self.count
        ahead, back = count - 1 + here - slot, slot - (count - 1 - here)
        if slot == 0:

            @pl.when(here == 0)
            def _():
                self.add_and_pass(group, ahead, part, True, False)

            @pl.when(here == count - 1)
            def _():
                self.add_and_pass(group, back, part, False, False)

            return
        for wait in (False, True):

            @pl.when((here <= slot) & ((here > 0) if wait else (here == 0)))
            def _(wait=wait):
                self.add_and_pass(group, ahead, part, True, wait)

            @pl.when(
                (count - 1 - here <= slot) & ((here < count - 1) if wait else (here == count - 1))
            )
            def _(wait=wait):
                self.add_and_pass(group, back, part, False, wait)

    def scatter_end(self, group, part):
        here = self.here
        last = self.count - 1

        def left():
            self.rightward(group, here).wait_recv()
            return self.from_left[group, here].astype(WIDE)

        def right():
            self.leftward(group, here).wait_recv()
            return self.from_right[group, here].astype(WIDE)

        @pl.when(here == 0)
        def _():
            self.total[...] = part[self.span(group, here)].astype(WIDE) + right()

        @pl.when(here == last)
        def _():
            self.total[...] = part[self.span(group, here)].astype(WIDE) + left()

        @pl.when((here > 0) & (here < last))
        def _():
            self.total[...] = part[self.span(group, here)].astype(WIDE) + left() + right()

    def passing(self, whole, group, chunk, right):
        ref = whole.at[self.span(group, chunk)]
        return remote(
            ref,
            ref,
            (self.to_right_sem if right else self.to_left_sem).at[group, chunk],
            self.got_sem.at[group, chunk],
            self.right if right else self.left,
        )

    def gather_slot(self, whole, group, distance):
        here, count = self.here, self.count

        @pl.when(here - distance >= 0)
        def _():
            if distance:
                self.passing(whole, group, here - distance, True).wait_recv()

            @pl.when(here < count - 1)
            def _():
                self.passing(whole, group, here - distance, True).start()

        @pl.when(here + distance <= count - 1)
        def _():
            if distance:
                self.passing(whole, group, here + distance, False).wait_recv()

            @pl.when(here > 0)
            def _():
                self.passing(whole, group, here + distance, False).start()

    def reduce(self, part, whole, finish, beside=()):
        beside = list(beside)
        last = self.count - 1
        self.scatter_slot(0, 0, part)
        for group in range(self.groups):
            for slot in range(1, last):
                if beside:
                    beside.pop(0)()
                self.scatter_slot(group, slot, part)
                if group:
                    self.gather_slot(whole, group - 1, slot)
            if group + 1 < self.groups:
                self.scatter_slot(group + 1, 0, part)
            if group:
                self.gather_slot(whole, group - 1, last)
            self.scatter_end(group, part)
            finish(group)
            self.gather_slot(whole, group, 0)
        for distance in range(1, self.count):
            if beside:
                beside.pop(0)()
            self.gather_slot(whole, self.groups - 1, distance)
        for act in beside:
            act()

    def sent(self, whole=None):
        here, count = self.here, self.count
        for group in range(self.groups):
            for chunk in range(count):

                @pl.when(here != chunk)
                def _(group=group, chunk=chunk):
                    self.rightward(group, chunk).wait_send()

                if whole is None:
                    continue

                @pl.when((chunk <= here) & (here < count - 1))
                def _(group=group, chunk=chunk):
                    self.passing(whole, group, chunk, True).wait_send()

                @pl.when((chunk >= here) & (here > 0))
                def _(group=group, chunk=chunk):
                    self.passing(whole, group, chunk, False).wait_send()


class Halving:
    @staticmethod
    def masks_of(pairs, order):
        def stage(mask):
            return min(order.index(bit) for bit in order if mask >> bit & 1)

        return sorted(range(1, pairs), key=lambda mask: (stage(mask), -mask.bit_count()))

    @staticmethod
    def scratch(pairs, block, width):
        count = pairs - 1
        pieces = max(1, width // PIECE)
        return [
            pltpu.VMEM((count, block, width), LOW),
            pltpu.VMEM((count, block, width), LOW),
            DMA((count, pieces)),
            DMA((count, pieces)),
        ]

    def __init__(self, pairs, order, own, refs, kept=None):
        self.order, self.own, self.kept = order, own, kept
        self.send, self.recv, self.send_sem, self.recv_sem = refs
        self.masks = Halving.masks_of(pairs, order)
        self.pieces = self.send_sem.shape[1]
        self.piece = self.send.shape[2] // self.pieces
        self.member = lax.axis_index("dp")
        self.tensor = lax.axis_index("tensor")
        self.high = lax.div(self.member, 2)

    def stage(self, mask):
        return min(
            [self.order.index(bit) for bit in self.order if mask >> bit & 1],
            default=len(self.order),
        )

    def steps(self, stage):
        return [mask for mask in self.masks if self.stage(mask) == stage]

    def columns(self, piece):
        return pl.ds(piece * self.piece, self.piece)

    def copy(self, mask, piece):
        index = self.masks.index(mask)
        bit = 1 << self.order[self.stage(mask)]
        return remote(
            self.send.at[index, :, self.columns(piece)],
            self.recv.at[index, :, self.columns(piece)],
            self.send_sem.at[index, piece],
            self.recv_sem.at[index, piece],
            (flip(self.member, bit * 2), self.tensor),
        )

    def settle(self):
        for piece in range(self.pieces):
            columns = self.columns(piece)
            self.kept[:, columns] = self.own(0, flip(self.high, 0), columns)

    def fill(self, mask, piece, out):
        columns = self.columns(piece)
        if self.kept is not None and not mask:
            total = self.kept[:, columns]
        else:
            total = self.own(mask, flip(self.high, mask), columns)
        for bit in self.order[: self.stage(mask)]:
            slot = mask | 1 << bit
            self.copy(slot, piece).wait_recv()
            total += self.recv[self.masks.index(slot), :, columns].astype(WIDE)
        out[:, columns] = total.astype(out.dtype)

    def push_piece(self, mask, piece):
        self.fill(mask, piece, self.send.at[self.masks.index(mask)])
        self.copy(mask, piece).start()

    def push(self, mask):
        for piece in range(self.pieces):
            self.push_piece(mask, piece)

    def end(self, out):
        for piece in range(self.pieces):
            self.fill(0, piece, out)

    def sent(self):
        for mask in self.masks:
            for piece in range(self.pieces):
                self.copy(mask, piece).wait_send()


class Pairwise:
    def __init__(self, moves, refs):
        self.moves, self.done = moves, False
        self.local_sem, self.send_sem, self.recv_sem = refs
        member = lax.axis_index("dp")
        self.partner = (flip(member, 1), lax.axis_index("tensor"))

    @staticmethod
    def sems(count):
        return [DMA((count,)), DMA((count,)), DMA((count,))]

    def local(self, index):
        source, target, _, _ = self.moves[index]
        return pltpu.make_async_copy(source, target, self.local_sem.at[index])

    def across(self, index):
        _, _, source, target = self.moves[index]
        return remote(
            source, target, self.send_sem.at[index], self.recv_sem.at[index], self.partner
        )

    def start(self, index=None):
        for index in range(len(self.moves)) if index is None else [index]:
            self.across(index).start()
            self.local(index).start()

    def ready(self, index=None):
        if index is None and self.done:
            return
        self.done = index is None
        for index in range(len(self.moves)) if index is None else [index]:
            self.local(index).wait()
            self.across(index).wait_recv()

    def sent(self):
        for index in range(len(self.moves)):
            self.across(index).wait_send()


class Lhs(Pairwise):
    @staticmethod
    def scratch(pairs, rows, block):
        return [pltpu.VMEM((pairs, 2 * rows, block), LOW)] + Pairwise.sems(pairs)

    def __init__(self, source, refs):
        self.held = refs[0]
        pairs, rows, block = self.held.shape
        rows = rows // 2
        parity = lax.rem(lax.axis_index("dp"), 2)

        def columns(index):
            if len(source.shape) == 3:
                return source.at[index]
            return source.at[:, pl.ds(pl.multiple_of(index * block, block), block)]

        super().__init__(
            [
                (
                    columns(2 * pair + parity),
                    self.held.at[pair, pl.ds(0, rows)],
                    columns(2 * pair + 1 - parity),
                    self.held.at[pair, pl.ds(rows, rows)],
                )
                for pair in range(pairs)
            ],
            refs[1:],
        )


class Rhs(Pairwise):
    @staticmethod
    def scratch(rows, width):
        return [pltpu.VMEM((2 * rows, width), LOW)] + Pairwise.sems(width // PIECE)

    def __init__(self, sources, refs):
        self.held = refs[0]
        rows = self.held.shape[0] // 2
        moves, at = [], 0
        for source in sources:
            for start in range(0, source.shape[1], PIECE):
                columns = pl.ds(at, PIECE)
                at += PIECE
                here = source.at[:, pl.ds(start, PIECE)]
                moves.append(
                    (
                        here,
                        self.held.at[pl.ds(0, rows), columns],
                        here,
                        self.held.at[pl.ds(rows, rows), columns],
                    )
                )
        super().__init__(moves, refs[1:])


def product_of(lhs, rhs):
    def own(mask, target, columns):
        return dot(lhs.held[target], rhs.held[:, columns], 0, 0)

    return own


def taker(refs):
    refs = list(refs)

    def take(count):
        out = refs[:count]
        del refs[:count]
        return out

    return take


def in_blocks(left, members):
    block = left.shape[1] // members
    if block % 128 == 0:
        return left
    return left.reshape(left.shape[0], members, block).transpose(1, 0, 2)


def member_peers(members):
    member, tensor = lax.axis_index("dp"), lax.axis_index("tensor")
    return [(flip(member, 1 << bit), tensor) for bit in bits_of(members)]


def project_kernel(
    members,
    states,
    w_query,
    w_key,
    w_value,
    cosine,
    sine,
    act,
    query,
    key,
    value,
    keys_all,
    values_all,
    send_sem,
    recv_sem,
    local_sem,
):
    member, tensor = lax.axis_index("dp"), lax.axis_index("tensor")
    width = query.shape[1]
    greet(member_peers(members))
    rows = 64
    for start in range(0, states.shape[0], rows):
        span = pl.ds(start, rows)
        act[span] = norm_rows(states[span])[0].astype(LOW)

    def turned(weight, out):
        linear = dot(act[...], weight[...])
        for start in range(0, width, HEAD):
            out[:, start : start + HEAD] = rotate(
                linear[:, start : start + HEAD], cosine[...], sine[...]
            ).astype(LOW)

    high = [bit for bit in bits_of(members) if bit]
    orders = (high + [0], high[::-1] + [0])
    owns, alls = (key, value), (keys_all, values_all)

    def copy(flow, mask, bit):
        slot = mask | 1 << bit
        place = alls[flow].at[flip(member, mask)]
        return remote(
            place if mask else owns[flow].at[pl.ds(0, PROMPT_DEV)],
            place,
            send_sem.at[flow, slot],
            recv_sem.at[flow, slot],
            (flip(member, 1 << bit), tensor),
        )

    def forward(flow, mask):
        order = orders[flow]
        last = max([order.index(bit) for bit in order if mask >> bit & 1], default=-1)
        for bit in order[last + 1 :]:
            copy(flow, mask, bit).start()

    def came_by(flow, mask):
        order = orders[flow]
        bit = order[max(order.index(bit) for bit in order if mask >> bit & 1)]
        return copy(flow, mask ^ 1 << bit, bit)

    def keep(flow):
        return pltpu.make_async_copy(
            owns[flow].at[pl.ds(0, PROMPT_DEV)], alls[flow].at[member], local_sem.at[flow]
        )

    turned(w_key, key)
    forward(0, 0)
    value[...] = dot(act[...], w_value[...]).astype(LOW)
    forward(1, 0)
    keep(0).start()
    keep(1).start()
    turned(w_query, query)
    masks = range(1, members)
    inner = sorted([mask for mask in masks if not mask & 1], key=lambda mask: mask.bit_count())
    for mask in inner:
        for flow in (0, 1):
            turn = flow if not mask & 2 else flow
            came_by(turn, mask).wait_recv()
            forward(turn, mask)
    for mask in masks:
        if mask & 1:
            for flow in (0, 1):
                came_by(flow, mask).wait_recv()
    for flow in (0, 1):
        keep(flow).wait()
        for mask in masks:
            came_by(flow, mask).wait_send()


def project(members, states, w_query, w_key, w_value, cosine, sine):
    rows, depth = states.shape
    width = w_query.shape[1]
    return pl.pallas_call(
        functools.partial(project_kernel, members),
        out_shape=[
            shape((rows, depth), LOW),
            shape((rows, width), LOW),
            shape((rows, width), LOW),
            shape((rows, width), LOW),
            shape((members, PROMPT_DEV, width), LOW),
            shape((members, PROMPT_DEV, width), LOW),
        ],
        in_specs=[VMEM] * 6,
        out_specs=[VMEM] * 4 + [ANY] * 2,
        scratch_shapes=[DMA((2, members)), DMA((2, members)), DMA((2,))],
        compiler_params=pltpu.CompilerParams(
            collective_id=1, has_side_effects=True, vmem_limit_bytes=VMEM_LIMIT
        ),
        name="project",
    )(states, w_query, w_key, w_value, cosine, sine)


def make_plan(half, group_id, slice_start, cont_group, plan):
    member = lax.axis_index("dp")
    own, other = group_id[member], cont_group[0]
    plan[0] = lax.div(slice_start[member], PROMPT_DEV)

    def step(index, _):
        rank = lax.div(slice_start[index], PROMPT_DEV)

        @pl.when(group_id[index] == own)
        def _():
            plan[1 + rank] = index

        @pl.when(group_id[index] == other)
        def _():
            plan[1 + half + rank] = index

        return 0

    lax.fori_loop(0, 2 * half, step, 0)


def attend_kernel(
    half,
    group_id,
    slice_start,
    cont_group,
    query,
    key,
    value,
    keys_all,
    values_all,
    mixed,
    attended,
    log_total,
    plan,
):
    @pl.when(pl.program_id(0) == 0)
    def _():
        make_plan(half, group_id, slice_start, cont_group, plan)

    def part(start, count, steps, offset):
        span = pl.ds(start, count)
        queries = query[span]
        allowed = lax.broadcasted_iota(jnp.int32, (count, count), 0) >= lax.broadcasted_iota(
            jnp.int32, (count, count), 1
        )
        scores = jnp.where(allowed, dot(queries, key[span], 1, 1) * SCALE, NEGATIVE)
        top = jnp.max(scores, axis=-1, keepdims=True)
        weights = jnp.exp(scores - top)
        total = jnp.sum(weights, axis=-1, keepdims=True)
        result = dot(weights.astype(LOW), value[span])

        def step(index, carry):
            top, total, result = carry
            place = plan[offset + index]
            scores = dot(queries, keys_all[place], 1, 1) * SCALE
            higher = jnp.maximum(top, jnp.max(scores, axis=-1, keepdims=True))
            fade = jnp.exp(top - higher)
            weights = jnp.exp(scores - higher)
            total = total * fade + jnp.sum(weights, axis=-1, keepdims=True)
            result = result * fade + dot(weights.astype(LOW), values_all[place])
            return higher, total, result

        top, total, result = lax.fori_loop(0, steps, step, (top, total, result))
        result = result / total
        mixed[span] = result.astype(LOW)
        attended[span] = result
        log_total[span] = jnp.broadcast_to(top + jnp.log(total), (count, HEAD))

    part(0, PROMPT_DEV, plan[0], 1)
    part(PROMPT_DEV, query.shape[0] - PROMPT_DEV, half, 1 + half)


def attend(readers, query, key, value, keys_all, values_all):
    rows, width = query.shape
    members = keys_all.shape[0]
    head = pl.BlockSpec((rows, HEAD), lambda h, *_: (0, h))
    every = pl.BlockSpec((members, PROMPT_DEV, HEAD), lambda h, *_: (0, 0, h))
    return pl.pallas_call(
        functools.partial(attend_kernel, members // 2),
        out_shape=[
            shape((rows, width), LOW),
            shape((rows, width), WIDE),
            shape((rows, width), WIDE),
        ],
        grid_spec=pltpu.PrefetchScalarGridSpec(
            num_scalar_prefetch=3,
            grid=(width // HEAD,),
            in_specs=[head, head, head, every, every],
            out_specs=[head, head, head],
            scratch_shapes=[pltpu.SMEM((members + 1,), jnp.int32)],
        ),
        compiler_params=pltpu.CompilerParams(vmem_limit_bytes=VMEM_LIMIT),
        name="attend",
    )(*readers, query, key, value, keys_all, values_all)


def attend_back_kernel(
    half,
    group_id,
    slice_start,
    cont_group,
    query,
    key,
    value,
    keys_all,
    values_all,
    branch_low,
    w_out,
    attended,
    log_total,
    cosine,
    sine,
    d_query,
    d_keys_all,
    d_values_all,
    d_key_own,
    d_value_own,
    d_mixed,
    key_total,
    value_total,
    plan,
):
    @pl.when(pl.program_id(0) == 0)
    def _():
        make_plan(half, group_id, slice_start, cont_group, plan)

    d_mixed[...] = dot(branch_low[...], w_out[...], 1, 1).astype(LOW)
    key_total[...] = jnp.zeros_like(key_total)
    value_total[...] = jnp.zeros_like(value_total)

    def part(start, count, steps, offset):
        span = pl.ds(start, count)
        queries, d_attended = query[span], d_mixed[span]
        log_sum = log_total[span][:, :1]
        center = jnp.sum(d_attended.astype(WIDE) * attended[span], axis=-1, keepdims=True)

        def back(scores, keys, values):
            probabilities = jnp.exp(scores - log_sum)
            d_scores = (probabilities * (dot(d_attended, values, 1, 1) - center)).astype(LOW)
            return (
                dot(d_scores, keys),
                dot(d_scores, queries, 0, 0),
                dot(probabilities.astype(LOW), d_attended, 0, 0),
            )

        allowed = lax.broadcasted_iota(jnp.int32, (count, count), 0) >= lax.broadcasted_iota(
            jnp.int32, (count, count), 1
        )
        scores = jnp.where(allowed, dot(queries, key[span], 1, 1) * SCALE, NEGATIVE)
        d_queries, d_own_keys, d_own_values = back(scores, key[span], value[span])

        def step(index, d_queries):
            place = plan[offset + index]
            keys, values = keys_all[place], values_all[place]
            more, d_keys, d_values = back(dot(queries, keys, 1, 1) * SCALE, keys, values)
            key_total[place] += d_keys
            value_total[place] += d_values
            return d_queries + more

        d_queries = lax.fori_loop(0, steps, step, d_queries) * SCALE
        d_query[span] = rotate(d_queries, cosine[span], -sine[span]).astype(LOW)
        return d_own_keys, d_own_values

    member = lax.axis_index("dp")
    d_own_keys, d_own_values = part(0, PROMPT_DEV, plan[0], 1)
    key_total[member] += d_own_keys
    value_total[member] += d_own_values
    d_own_keys, d_own_values = part(PROMPT_DEV, query.shape[0] - PROMPT_DEV, half, 1 + half)
    late = pl.ds(PROMPT_DEV, query.shape[0] - PROMPT_DEV)
    d_key_own[...] = rotate(d_own_keys * SCALE, cosine[late], -sine[late]).astype(LOW)
    d_value_own[...] = d_own_values.astype(LOW)
    d_keys_all[...] = (key_total[...] * SCALE).astype(LOW)
    d_values_all[...] = value_total[...].astype(LOW)


def attend_back(
    readers,
    query,
    key,
    value,
    keys_all,
    values_all,
    branch_low,
    w_out,
    attended,
    log_total,
    cosine,
    sine,
):
    rows, width = query.shape
    members = keys_all.shape[0]
    depth = branch_low.shape[1]
    late = rows - PROMPT_DEV
    heads = width // HEAD
    head = pl.BlockSpec((rows, HEAD), lambda h, *_: (0, h))
    every = pl.BlockSpec((members, PROMPT_DEV, HEAD), lambda h, *_: (0, 0, h))
    own = pl.BlockSpec((late, HEAD), lambda h, *_: (0, h))
    table = pl.BlockSpec((rows, HEAD), lambda h, *_: (0, 0))
    return pl.pallas_call(
        functools.partial(attend_back_kernel, members // 2),
        out_shape=[
            shape((rows, width), LOW),
            shape((members, PROMPT_DEV, width), LOW),
            shape((members, PROMPT_DEV, width), LOW),
            shape((late, width), LOW),
            shape((late, width), LOW),
        ],
        grid_spec=pltpu.PrefetchScalarGridSpec(
            num_scalar_prefetch=3,
            grid=(heads,),
            in_specs=[
                head,
                head,
                head,
                every,
                every,
                pl.BlockSpec((rows, depth), lambda h, *_: (0, 0)),
                pl.BlockSpec((HEAD, depth), lambda h, *_: (h, 0)),
                head,
                head,
                table,
                table,
            ],
            out_specs=[head, every, every, own, own],
            scratch_shapes=[
                pltpu.VMEM((rows, HEAD), LOW),
                pltpu.VMEM((members, PROMPT_DEV, HEAD), WIDE),
                pltpu.VMEM((members, PROMPT_DEV, HEAD), WIDE),
                pltpu.SMEM((members + 1,), jnp.int32),
            ],
        ),
        compiler_params=pltpu.CompilerParams(vmem_limit_bytes=VMEM_LIMIT),
        name="attend_back",
    )(
        *readers,
        query,
        key,
        value,
        keys_all,
        values_all,
        branch_low,
        w_out,
        attended,
        log_total,
        cosine,
        sine,
    )


def place_of(group_id, slice_start, group, rank):
    place = 0
    for index in range(group_id.shape[0]):
        found = (group_id[index] == group) & (slice_start[index] == rank * PROMPT_DEV)
        place = jnp.maximum(place, jnp.where(found, index, 0))
    return place


def own_part(rows):
    return lax.broadcasted_iota(jnp.int32, (rows, rows), 0) >= lax.broadcasted_iota(
        jnp.int32, (rows, rows), 1
    )


def gather_attend_kernel(
    members,
    group_id,
    slice_start,
    cont_group,
    w_query_in,
    w_key_in,
    w_value_in,
    states_in,
    table,
    act,
    query,
    key,
    value,
    cosine,
    sine,
    mixed,
    attended,
    log_total,
    keys_out,
    values_out,
    states,
    weights,
    load_sem,
    weight_sem,
    send_sem,
    recv_sem,
    keep_sem,
    out_sem,
    *every,
):
    member, tensor = lax.axis_index("dp"), lax.axis_index("tensor")
    heads = query.shape[0]
    keys_all, values_all = every[:heads], every[heads:]
    half = members // 2
    rows = states.shape[0]
    chunks = load_sem.shape[0]
    size = rows // chunks
    loads = []
    for index in range(chunks):
        span = pl.ds(index * size, size)
        loads.append(pltpu.make_async_copy(states_in.at[span], states.at[span], load_sem.at[index]))
    w_loads = [
        pltpu.make_async_copy(source, weights.at[index], weight_sem.at[index])
        for index, source in enumerate((w_key_in, w_value_in, w_query_in))
    ]
    for load in loads[:1] + w_loads[:1] + loads[1:] + w_loads[1:]:
        load.start()
    hail(member_peers(members))
    index = lax.broadcasted_iota(jnp.int32, cosine.shape, 0)
    prompt = half * PROMPT_DEV - PROMPT_DEV
    positions = index + jnp.where(index < PROMPT_DEV, slice_start[member], prompt)
    angles = positions.astype(WIDE) * table[:1]
    cosine[...] = jnp.cos(angles)
    sine[...] = jnp.sin(angles) * table[1:2]
    step = 64
    for index in range(chunks):
        loads[index].wait()
        for start in range(index * size, index * size + size, step):
            span = pl.ds(start, step)
            act[span] = norm_rows(states[span])[0].astype(LOW)

    def turned(weight, out):
        linear = dot(act[...], weight)
        for head in range(heads):
            out[head] = rotate(
                linear[:, head * HEAD : head * HEAD + HEAD], cosine[...], sine[...]
            ).astype(LOW)

    high = [bit for bit in bits_of(members) if bit]
    orders = (high + [0], high[::-1] + [0])
    owns, alls = (key, value), (keys_all, values_all)
    early = pl.ds(0, PROMPT_DEV)

    def copy(flow, head, mask, bit):
        slot = mask | 1 << bit
        place = alls[flow][head].at[flip(member, mask)]
        return remote(
            place if mask else owns[flow].at[head, early],
            place,
            send_sem.at[flow, head, slot],
            recv_sem.at[flow, head, slot],
            (flip(member, 1 << bit), tensor),
        )

    def forward(flow, head, mask):
        order = orders[flow]
        last = max([order.index(bit) for bit in order if mask >> bit & 1], default=-1)
        for bit in order[last + 1 :]:
            copy(flow, head, mask, bit).start()

    def came_by(flow, head, mask):
        order = orders[flow]
        bit = order[max(order.index(bit) for bit in order if mask >> bit & 1)]
        return copy(flow, head, mask ^ 1 << bit, bit)

    def keep(flow, head):
        return pltpu.make_async_copy(
            owns[flow].at[head, early], alls[flow][head].at[member], keep_sem.at[flow, head]
        )

    def write(flow, head):
        return pltpu.make_async_copy(
            alls[flow][head], (keys_out, values_out)[flow].at[head], out_sem.at[flow, head]
        )

    masks = range(1, members)
    levels = len(high)

    def own_sends(head):
        if head < heads:
            for flow in (0, 1):
                forward(flow, head, 0)
            for flow in (0, 1):
                keep(flow, head).start()

    def level(head, count):
        if head < heads:
            for mask in masks:
                if not mask & 1 and mask.bit_count() == count:
                    for flow in (0, 1):
                        came_by(flow, head, mask).wait_recv()
                        forward(flow, head, mask)

    def complete(head):
        for flow in (0, 1):
            for mask in masks:
                if mask & 1:
                    came_by(flow, head, mask).wait_recv()
            keep(flow, head).wait()
            write(flow, head).start()

    own_group, other_group = group_id[member], cont_group[0]
    own_start = slice_start[member]
    own_places = [place_of(group_id, slice_start, own_group, rank) for rank in range(half)]
    other_places = [place_of(group_id, slice_start, other_group, rank) for rank in range(half)]
    block = 128

    def attend_rows(head, start, places, whole):
        span = pl.ds(start, block)
        queries = query[head, span]
        scores, values = [], []
        for rank, place in enumerate(places):
            score = dot(queries, keys_all[head][place], 1, 1) * SCALE_TWO
            if not whole:
                at = lax.broadcasted_iota(jnp.int32, score.shape, 0) + (own_start + start)
                to = lax.broadcasted_iota(jnp.int32, score.shape, 1) + rank * PROMPT_DEV
                score = jnp.where(to <= at, score, NEGATIVE)
            scores.append(score)
            values.append(values_all[head][place])
        if whole:
            score = dot(queries, key[head, span], 1, 1) * SCALE_TWO
            scores.append(jnp.where(own_part(block), score, NEGATIVE))
            values.append(value[head, span])
        top = functools.reduce(
            jnp.maximum, [jnp.max(score, axis=-1, keepdims=True) for score in scores]
        )
        total = jnp.zeros_like(top)
        result = jnp.zeros((block, HEAD), WIDE)
        for score, held in zip(scores, values):
            weight = jnp.exp2(score - top)
            total += jnp.sum(weight, axis=-1, keepdims=True)
            result += dot(weight.astype(LOW), held)
        result = result / total
        mixed[span, head * HEAD : head * HEAD + HEAD] = result.astype(LOW)
        attended[head, span] = result
        log_total[head, span] = jnp.broadcast_to(top + jnp.log2(total), (block, HEAD))

    w_loads[0].wait()
    turned(weights[0], key)
    heed(member_peers(members))
    forward(0, 0, 0)
    w_loads[1].wait()
    linear = dot(act[...], weights[1])
    for head in range(heads):
        value[head] = linear[:, head * HEAD : head * HEAD + HEAD].astype(LOW)
    forward(1, 0, 0)
    for flow in (0, 1):
        keep(flow, 0).start()
    own_sends(1)
    w_loads[2].wait()
    turned(weights[2], query)
    level(0, 1)
    own_sends(2)
    for count in range(2, levels + 1):
        level(0, count)
    level(1, 1)
    own_sends(3)
    for head in range(heads):
        complete(head)

        @pl.loop(0, PROMPT_DEV // block)
        def _(index, head=head):
            attend_rows(head, pl.multiple_of(index * block, block), own_places, False)

        for count in range(2, levels + 1):
            level(head + 1, count)
        level(head + 2, 1)
        own_sends(head + 4)
        for start in range(PROMPT_DEV, rows, block):
            attend_rows(head, start, other_places, True)
    for head in range(heads):
        for flow in (0, 1):
            write(flow, head).wait()
            for mask in masks:
                came_by(flow, head, mask).wait_send()


def gather_attend(members, readers, w_query, w_key, w_value, states, table):
    rows, depth = states.shape
    width = w_query.shape[1]
    heads = width // HEAD
    smem = pl.BlockSpec(memory_space=pltpu.SMEM)
    row_heads = (heads, rows, HEAD)
    every = (heads, members, PROMPT_DEV, HEAD)
    return pl.pallas_call(
        functools.partial(gather_attend_kernel, members),
        out_shape=[
            shape((rows, depth), LOW),
            shape(row_heads, LOW),
            shape(row_heads, LOW),
            shape(row_heads, LOW),
            shape((rows, HEAD), WIDE),
            shape((rows, HEAD), WIDE),
            shape((rows, width), LOW),
            shape(row_heads, WIDE),
            shape(row_heads, WIDE),
            shape(every, LOW),
            shape(every, LOW),
        ],
        in_specs=[smem] * 3 + [ANY] * 4 + [VMEM],
        out_specs=[VMEM] * 9 + [ANY] * 2,
        scratch_shapes=[
            pltpu.VMEM((rows, depth), WIDE),
            pltpu.VMEM((3, depth, width), LOW),
            DMA((4,)),
            DMA((3,)),
            DMA((2, heads, members)),
            DMA((2, heads, members)),
            DMA((2, heads)),
            DMA((2, heads)),
        ]
        + [pltpu.VMEM(every[1:], LOW)] * (2 * heads),
        compiler_params=pltpu.CompilerParams(
            collective_id=6, has_side_effects=True, vmem_limit_bytes=VMEM_LIMIT
        ),
        name="gather_attend",
    )(
        *readers,
        w_query,
        w_key,
        w_value,
        states,
        table,
    )


def back_owner_kernel(
    members,
    count,
    group_id,
    slice_start,
    cont_group,
    keys_in,
    values_in,
    query_in,
    key_in,
    value_in,
    attended_in,
    log_total_in,
    branch_low,
    w_out,
    cosine,
    sine,
    own_early,
    own_late,
    d_query,
    d_key,
    d_value,
    early_out,
    late_out,
    query,
    key,
    value,
    attended,
    log_total,
    d_mixed,
    d_queries,
    own_keys,
    own_values,
    other_keys,
    other_values,
    load_sem,
    *refs,
):
    take = taker(refs)
    member = lax.axis_index("dp")
    heads, rows = query.shape[0], query.shape[1]
    keys_all, values_all = take(heads), take(heads)
    out_send, out_recv = take(2)
    here = lax.axis_index("tensor")
    size = own_early.shape[0]
    own_rows = pl.ds(pl.multiple_of(here * size, size), size)
    told = ((own_early, early_out), (own_late, late_out))

    def tell(which, distance):
        source, target = told[which]
        return remote(
            source,
            target.at[own_rows],
            out_send.at[which, distance - 1],
            out_recv.at[which, distance - 1],
            (member, lax.rem(here + distance, count)),
        )

    half = pairs = members // 2
    parity = lax.rem(member, 2)
    order = bits_of(pairs)
    moves, flows, sides = [], [], []
    for way in (order, order[::-1]):
        mine, leaving, theirs = take(3)
        local_free, send_sem, recv_sem = take(3)
        refs_of = take(4)
        sides.append((mine, leaving, theirs, send_sem, recv_sem))
        per_head = []
        for head in range(heads):

            def own(mask, target, columns, mine=mine, theirs=theirs, head=head):
                return mine[head, target, :, columns].astype(WIDE) + theirs[
                    head, target, :, columns
                ].astype(WIDE)

            per_head.append(Halving(pairs, way, own, [ref.at[head] for ref in refs_of]))
        flows.append(per_head)
    partner = (flip(member, 1), lax.axis_index("tensor"))

    sources = (keys_in, values_in, query_in, key_in, value_in, attended_in, log_total_in)

    def load(index, head):
        if index < 2:
            target = (keys_all, values_all)[index][head]
        else:
            target = (query, key, value, attended, log_total)[index - 2].at[head]
        return pltpu.make_async_copy(
            sources[index].at[head], target, load_sem.at[index, head]
        )

    for head in range(heads):
        for index in range(len(sources)):
            load(index, head).start()

    def across(flow, head):
        _, leaving, theirs, send_sem, recv_sem = sides[flow]
        return remote(
            leaving.at[head], theirs.at[head], send_sem.at[head], recv_sem.at[head], partner
        )

    own_group, other_group = group_id[member], cont_group[0]
    own_start = slice_start[member]
    own_places = [place_of(group_id, slice_start, own_group, rank) for rank in range(half)]
    other_places = [place_of(group_id, slice_start, other_group, rank) for rank in range(half)]
    across_line = [(member, lax.rem(here + distance, count)) for distance in range(1, count)]
    hail(member_peers(members) + across_line)
    linear = dot(branch_low[...], w_out[...], 1, 1)
    for head in range(heads):
        d_mixed[head] = linear[:, head * HEAD : head * HEAD + HEAD].astype(LOW)
    heed(member_peers(members) + across_line)
    for which, (source, target) in enumerate(told):
        for distance in range(1, count):
            tell(which, distance).start()
        target[own_rows] = source[...]
    late = rows - PROMPT_DEV

    def back(scores, queries, keys, values, d_attended, log_sum, center):
        probabilities = jnp.exp2(scores - log_sum)
        d_scores = (probabilities * (dot(d_attended, values, 1, 1) - center)).astype(LOW)
        return (
            dot(d_scores, keys),
            dot(d_scores, queries, 0, 0),
            dot(probabilities.astype(LOW), d_attended, 0, 0),
        )

    def rows_of(head, start, count):
        span = pl.ds(start, count)
        d_attended = d_mixed[head, span]
        center = jnp.sum(d_attended.astype(WIDE) * attended[head, span], axis=-1, keepdims=True)
        return query[head, span], d_attended, log_total[head, span][:, :1], center

    def prompt_rank(head, rank):
        queries, d_attended, log_sum, center = rows_of(head, 0, PROMPT_DEV)
        place = own_places[rank]
        keys, values = keys_all[head][place], values_all[head][place]
        scores = dot(queries, keys, 1, 1) * SCALE_TWO
        at = lax.broadcasted_iota(jnp.int32, scores.shape, 0) + own_start
        to = lax.broadcasted_iota(jnp.int32, scores.shape, 1) + rank * PROMPT_DEV
        scores = jnp.where(to <= at, scores, NEGATIVE)
        more, d_keys, d_values = back(
            scores, queries, keys, values, d_attended, log_sum, center
        )
        early = pl.ds(0, PROMPT_DEV)
        if rank:
            d_queries[early] += more
        else:
            d_queries[early] = more
        own_keys[rank] = d_keys
        own_values[rank] = d_values

    def late_part(head):
        queries, d_attended, log_sum, center = rows_of(head, PROMPT_DEV, late)
        span = pl.ds(PROMPT_DEV, late)
        keys, values = key[head, span], value[head, span]
        scores = jnp.where(own_part(late), dot(queries, keys, 1, 1) * SCALE_TWO, NEGATIVE)
        total, d_keys, d_values = back(
            scores, queries, keys, values, d_attended, log_sum, center
        )
        columns = pl.ds(head * HEAD, HEAD)
        d_key[span, columns] = rotate(d_keys * SCALE, cosine[span], -sine[span]).astype(LOW)
        d_value[span, columns] = d_values.astype(LOW)
        for rank in range(half):
            place = other_places[rank]
            keys, values = keys_all[head][place], values_all[head][place]
            more, d_keys, d_values = back(
                dot(queries, keys, 1, 1) * SCALE_TWO, queries, keys, values, d_attended, log_sum, center
            )
            total += more
            other_keys[rank] = d_keys
            other_values[rank] = d_values
        d_queries[span] = total
        d_query[:, columns] = rotate(d_queries[...] * SCALE, cosine[...], -sine[...]).astype(LOW)

    def spread(head):
        for pair in range(pairs):
            for away in (0, 1):
                index = 2 * pair + (1 - parity if away else parity)
                rank = lax.div(slice_start[index], PROMPT_DEV)
                mine = jnp.where(group_id[index] == own_group, 1.0, 0.0)
                other = jnp.where(group_id[index] == other_group, 1.0, 0.0)
                for flow, (a, b, scale) in enumerate(
                    ((own_keys, other_keys, SCALE), (own_values, other_values, 1.0))
                ):
                    total = a[rank] * (mine * scale) + b[rank] * (other * scale)
                    sides[flow][away][head, pair] = total.astype(LOW)

    def begin(head):
        for flow in (0, 1):
            across(flow, head).start()

    def stage(head, index):
        if not 0 <= head < heads:
            return
        for flow in (0, 1):
            if not index:
                across(flow, head).wait_recv()
        for flow in (0, 1):
            for mask in flows[flow][head].steps(index):
                flows[flow][head].push(mask)

    def end(head):
        if not 0 <= head < heads:
            return
        early = pl.ds(0, PROMPT_DEV)
        columns = pl.ds(head * HEAD, HEAD)
        total = d_queries.at[early]
        flows[0][head].end(total)
        d_key[early, columns] = rotate(total[...], cosine[early], -sine[early]).astype(LOW)
        flows[1][head].end(d_value.at[early, columns])

    depth = len(order)
    for head in range(heads):
        for index in range(len(sources)):
            load(index, head).wait()
        for rank in range(half):
            prompt_rank(head, rank)
            if rank == 0:
                stage(head - 1, 0)
            if rank == half - 1:
                for index in range(1, depth):
                    stage(head - 1, index)
        late_part(head)
        spread(head)
        begin(head)
        end(head - 1)
    for index in range(depth):
        stage(heads - 1, index)
    end(heads - 1)
    for flow in (0, 1):
        for head in range(heads):
            across(flow, head).wait_send()
            flows[flow][head].sent()
    for which in range(len(told)):
        for distance in range(1, count):
            tell(which, distance).wait()


def back_owner(
    members,
    count,
    readers,
    keys_all,
    values_all,
    query,
    key,
    value,
    branch_low,
    w_out,
    attended,
    log_total,
    cosine,
    sine,
    own_early,
    own_late,
):
    heads, rows, _ = query.shape
    width = heads * HEAD
    pairs = members // 2
    smem = pl.BlockSpec(memory_space=pltpu.SMEM)
    every = pltpu.VMEM((members, PROMPT_DEV, HEAD), LOW)
    side = pltpu.VMEM((heads, pairs, PROMPT_DEV, HEAD), LOW)
    step = pltpu.VMEM((heads, pairs - 1, PROMPT_DEV, HEAD), LOW)
    flow = [side] * 3 + [DMA((heads,))] * 3 + [step] * 2 + [DMA((heads, pairs - 1, 1))] * 2
    total = pltpu.VMEM((pairs, PROMPT_DEV, HEAD), WIDE)
    return pl.pallas_call(
        functools.partial(back_owner_kernel, members, count),
        out_shape=[shape((rows, width), LOW)] * 3
        + [shape((count * own_early.shape[0], own_early.shape[1]), LOW)] * 2,
        in_specs=[smem] * 3 + [ANY] * 7 + [VMEM] * 6,
        out_specs=[VMEM] * 5,
        scratch_shapes=[
            pltpu.VMEM((heads, rows, HEAD), LOW),
            pltpu.VMEM((heads, rows, HEAD), LOW),
            pltpu.VMEM((heads, rows, HEAD), LOW),
            pltpu.VMEM((heads, rows, HEAD), WIDE),
            pltpu.VMEM((heads, rows, HEAD), WIDE),
            pltpu.VMEM((heads, rows, HEAD), LOW),
            pltpu.VMEM((rows, HEAD), WIDE),
            total,
            total,
            total,
            total,
            DMA((7, heads)),
        ]
        + [every] * (2 * heads)
        + [DMA((2, count - 1))] * 2
        + flow * 2,
        compiler_params=pltpu.CompilerParams(
            collective_id=7, has_side_effects=True, vmem_limit_bytes=VMEM_LIMIT
        ),
        name="back_owner",
    )(
        *readers,
        keys_all,
        values_all,
        query,
        key,
        value,
        attended,
        log_total,
        branch_low,
        w_out,
        cosine,
        sine,
        own_early,
        own_late,
    )


def middle_kernel(
    count,
    mixed,
    w_out,
    states,
    cotangent_in,
    w_gate_in,
    w_up_in,
    w_down_in,
    act,
    resid,
    own_early,
    out_low_out,
    ffn_late,
    d_act_out,
    hidden_out,
    d_gate_out,
    d_up_out,
    part,
    cotangent,
    out_low,
    d_hidden,
    w_gate,
    w_up,
    w_down,
    rows_in,
    ffn_total,
    d_total,
    ffn,
    hidden,
    d_gate,
    d_up,
    state_sem,
    cot_sem,
    weight_sem,
    out_sem,
    *refs,
):
    line = Line(count, refs[: Line.scratch_count])
    out_line = Line(count, refs[Line.scratch_count :])
    rows, size = resid.shape[0], line.rows
    fetch = pltpu.make_async_copy(
        states.at[pl.ds(pl.multiple_of(line.here * rows, rows), rows)], resid, state_sem
    )
    slots, step, _ = cotangent.shape

    def cot_load(index):
        return pltpu.make_async_copy(
            cotangent_in.at[pl.ds(index * step, step)],
            cotangent.at[index % slots],
            cot_sem.at[index % slots],
        )

    down_load, gate_load, up_load = [
        pltpu.make_async_copy(source, target, weight_sem.at[index])
        for index, (source, target) in enumerate(
            ((w_down_in, w_down), (w_gate_in, w_gate), (w_up_in, w_up))
        )
    ]
    fetch.start()
    for index in range(slots):
        cot_load(index).start()
    for load in (down_load, gate_load, up_load):
        load.start()
    hail(line.peers())
    tile = 512
    for start in range(0, part.shape[1], tile):
        columns = pl.ds(start, tile)
        part[:, columns] = dot(mixed[...], w_out[:, columns]).astype(LOW)
    heed(line.peers())
    fetch.wait()

    def finish(group):
        span = pl.ds(group * size, size)
        resid[span] += line.total[...]
        act[line.span(group, line.here)] = norm_rows(resid[span])[0].astype(LOW)

    leaving = []

    def leave(source, target):
        copy = pltpu.make_async_copy(source, target, out_sem.at[len(leaving)])
        copy.start()
        leaving.append(copy)

    def cast():
        steps = out_low.shape[0] // step
        for index in range(steps):
            cot_load(index).wait()
            out_low[pl.ds(index * step, step)] = cotangent[index % slots].astype(LOW)
            if index + slots < steps:
                cot_load(index + slots).start()
        leave(out_low, out_low_out)
        down_load.wait()

    def inner(start):
        span = pl.ds(start, tile)
        d_hidden[:, span] = dot(out_low[...], w_down[span], 1, 1).astype(LOW)

    units, block = d_hidden.shape[1], 256
    starts = list(range(0, units, tile))

    def inners(some):
        def run():
            for start in some:
                inner(start)

        return run

    def begin(group):
        if not group:
            gate_load.wait()
            up_load.wait()
        for chunk in range(count):
            rows_in[pl.ds(chunk * size, size)] = act[line.span(group, chunk)]
        ffn_total[...] = jnp.zeros_like(ffn_total)
        d_total[...] = jnp.zeros_like(d_total)

    def feed(group, first, last):
        @pl.loop(first, last)
        def _(index):
            columns = pl.ds(pl.multiple_of(index * block, block), block)
            gate = dot(rows_in[...], w_gate[:, columns])
            up = dot(rows_in[...], w_up[:, columns])
            sigmoid = jax.nn.sigmoid(gate)
            swish = gate * sigmoid
            d_inner = jnp.concatenate(
                [d_hidden[line.span(group, chunk), columns] for chunk in range(count)]
            ).astype(WIDE)
            new_hidden = (swish * up).astype(LOW)
            new_gate = (d_inner * up * sigmoid * (1.0 + gate * (1.0 - sigmoid))).astype(LOW)
            new_up = (d_inner * swish).astype(LOW)
            for chunk in range(count):
                own = slice(chunk * size, chunk * size + size)
                hidden[chunk, group, :, columns] = new_hidden[own]
                d_gate[chunk, group, :, columns] = new_gate[own]
                d_up[chunk, group, :, columns] = new_up[own]
            for start in range(0, part.shape[1], tile):
                out = pl.ds(start, tile)
                ffn_total[:, out] += dot(new_hidden, w_down[columns, out])
                d_total[:, out] += dot(new_gate, w_gate[out, columns], 1, 1) + dot(
                    new_up, w_up[out, columns], 1, 1
                )

    def end(group):
        own = pl.ds(pl.multiple_of(line.here * size, size), size)
        ffn_total[own] += resid[pl.ds(group * size, size)]
        ffn[group] = ffn_total[...].astype(LOW)
        if group:
            leave(ffn.at[group], ffn_late)
        for chunk in range(count):
            span = line.span(group, chunk)
            part[span] = d_total[pl.ds(chunk * size, size)].astype(LOW)
            leave(part.at[span], d_act_out.at[span])
        for source, target in (
            (hidden, hidden_out),
            (d_gate, d_gate_out),
            (d_up, d_up_out),
        ):
            leave(source.at[:, group], target.at[:, group])

    blocks = units // block
    third = -(-blocks // 3)

    def opening():
        begin(0)
        feed(0, 0, third)

    def closing():
        feed(0, 2 * third, blocks)
        end(0)

    line.reduce(
        part,
        act,
        finish,
        [
            cast,
            inners(starts[:1]),
            inners(starts[1:2]),
            inners(starts[2:]),
            opening,
            lambda: feed(0, third, 2 * third),
            closing,
        ],
    )
    early = ffn.at[0]
    out_line.scatter_slot(0, 0, early)
    begin(1)
    feed(1, 0, third)
    out_line.scatter_slot(0, 1, early)
    feed(1, third, 2 * third)
    for slot in range(2, count - 1):
        out_line.scatter_slot(0, slot, early)
    feed(1, 2 * third, blocks)
    end(1)
    out_line.scatter_end(0, early)
    own_early[...] = out_line.total[...].astype(LOW)
    for copy in leaving:
        copy.wait()
    line.sent(act)
    out_line.sent()


def middle(count, mixed, w_out, states, cotangent, w_gate, w_up, w_down):
    rows, depth = states.shape
    units = w_down.shape[0]
    size = rows // count // GROUPS
    split = (count, GROUPS, size)
    inside = (*split, units)
    some = (GROUPS, rows // GROUPS, depth)
    outs = pl.pallas_call(
        functools.partial(middle_kernel, count),
        out_shape=[
            shape((rows, depth), LOW),
            shape((rows // count, depth), WIDE),
            shape((size, depth), LOW),
            shape((rows, depth), LOW),
            shape(some[1:], LOW),
            shape((rows, depth), LOW),
            shape(inside, LOW),
            shape(inside, LOW),
            shape(inside, LOW),
        ],
        in_specs=[VMEM] * 2 + [ANY] * 5,
        out_specs=[VMEM] * 3 + [ANY] * 6,
        scratch_shapes=[
            pltpu.VMEM((rows, depth), LOW),
            pltpu.VMEM((2, 64, depth), WIDE),
            pltpu.VMEM((rows, depth), LOW),
            pltpu.VMEM((rows, units), LOW),
            pltpu.VMEM((depth, units), LOW),
            pltpu.VMEM((depth, units), LOW),
            pltpu.VMEM((units, depth), LOW),
            pltpu.VMEM(some[1:], LOW),
            pltpu.VMEM(some[1:], WIDE),
            pltpu.VMEM(some[1:], WIDE),
            pltpu.VMEM(some, LOW),
            pltpu.VMEM(inside, LOW),
            pltpu.VMEM(inside, LOW),
            pltpu.VMEM(inside, LOW),
            DMA,
            DMA((2,)),
            DMA((3,)),
            DMA(((4 + count) * GROUPS,)),
        ]
        + Line.scratch(count, GROUPS, rows // count, depth)
        + Line.scratch(count, 1, size, depth),
        compiler_params=pltpu.CompilerParams(
            collective_id=2, has_side_effects=True, vmem_limit_bytes=VMEM_LIMIT
        ),
        name="middle",
    )(mixed, w_out, states, cotangent, w_gate, w_up, w_down)
    return [*outs[:6], *(out.reshape(rows, -1) for out in outs[6:])]


def second_kernel(
    count,
    pairs,
    d_act_in,
    ffn_in,
    resid_in,
    cotangent,
    act,
    d_gate,
    d_up,
    branch_low,
    grad_resid,
    own_out,
    grad_gate,
    grad_up,
    d_act,
    ffn,
    resid,
    cot_sem,
    load_sem,
    *refs,
):
    take = taker(refs)
    line = Line(count, take(Line.scratch_count))
    out_line = Line(count, take(Line.scratch_count))
    lhs = Lhs(act, take(4))
    rights = [Rhs([source], take(4)) for source in (d_gate, d_up)]
    order = bits_of(pairs)
    flows = [
        Halving(pairs, way, product_of(lhs, right), take(4), *take(1))
        for way, right in zip((order, order[::-1]), rights)
    ]
    rows = resid.shape[0]
    fetch = pltpu.make_async_copy(
        cotangent.at[pl.ds(pl.multiple_of(line.here * rows, rows), rows)], grad_resid, cot_sem
    )
    peers = line.peers() + member_peers(2 * pairs)
    hail(peers)
    loads = [
        pltpu.make_async_copy(source, target, load_sem.at[index])
        for index, (source, target) in enumerate(
            ((d_act_in, d_act), (ffn_in, ffn), (resid_in, resid))
        )
    ]
    fetch.start()
    for load in loads:
        load.start()
    heed(peers)
    lhs.start()
    for piece in range(flows[0].pieces):
        for right in rights:
            right.start(piece)
    fetch.wait()
    for load in loads:
        load.wait()

    def finish(group):
        span = pl.ds(group * line.rows, line.rows)
        normed, inverse = norm_rows(resid[span])
        grad_resid[span] += norm_back(line.total[...], normed, inverse)
        branch_low[line.span(group, line.here)] = grad_resid[span].astype(LOW)

    sides = [(lhs, right, flow) for right, flow in zip(rights, flows)]
    ahead, early, others, settle, late = beside(order, sides)

    def out_slot(slot):
        return lambda: out_line.scatter_slot(0, slot, ffn)

    slots = [out_slot(slot) for slot in range(count - 1)]

    def fourth():
        settle()
        slots[0]()

    line.reduce(d_act, branch_low, finish, [ahead, early, others, fourth, late] + slots[1:])
    out_line.scatter_end(0, ffn)
    own_out[...] = out_line.total[...].astype(LOW)
    flows[0].end(grad_gate)
    flows[1].end(grad_up)
    for flow in flows:
        flow.sent()
    for move in [lhs] + rights:
        move.sent()
    line.sent(branch_low)
    out_line.sent()


def beside(order, sides):
    masks = [flow.steps(0) for _, _, flow in sides]

    def ahead():
        for (lhs, rhs, flow), (mask, *_) in zip(sides[:2], masks):
            lhs.ready()
            rhs.ready(0)
            flow.push_piece(mask, 0)

    def early():
        for at, ((lhs, rhs, flow), (mask, *_)) in enumerate(zip(sides, masks)):
            if at > 1:
                lhs.ready()
            for piece in range(0 if at > 1 else 1, flow.pieces):
                rhs.ready(piece)
                flow.push_piece(mask, piece)

    def others():
        for index in range(1, len(masks[0])):
            for (_, _, flow), steps in zip(sides, masks):
                flow.push(steps[index])

    def settle():
        for _, _, flow in sides:
            flow.settle()

    def late():
        for stage in range(1, len(order)):
            for index in range(len(sides[0][2].steps(stage))):
                for _, _, flow in sides:
                    flow.push(flow.steps(stage)[index])

    return [ahead, early, others, settle, late]


def second(count, members, d_act, ffn, resid, cotangent, act, d_gate, d_up):
    rows, depth = cotangent.shape
    units = d_gate.shape[1]
    pairs = members // 2
    block = depth // members
    return pl.pallas_call(
        functools.partial(second_kernel, count, pairs),
        out_shape=[
            shape((rows, depth), LOW),
            shape((rows // count, depth), WIDE),
            shape((ffn.shape[0] // count, depth), LOW),
            shape((block, units), LOW),
            shape((block, units), LOW),
        ],
        in_specs=[ANY] * 7,
        out_specs=[VMEM] * 5,
        scratch_shapes=[
            pltpu.VMEM(d_act.shape, LOW),
            pltpu.VMEM(ffn.shape, LOW),
            pltpu.VMEM(resid.shape, WIDE),
            DMA,
            DMA((3,)),
        ]
        + Line.scratch(count, GROUPS, rows // count, depth)
        + Line.scratch(count, 1, ffn.shape[0] // count, depth)
        + Lhs.scratch(pairs, rows, block)
        + Rhs.scratch(rows, units) * 2
        + (Halving.scratch(pairs, block, units) + [pltpu.VMEM((block, units), WIDE)]) * 2,
        compiler_params=pltpu.CompilerParams(
            collective_id=3, has_side_effects=True, vmem_limit_bytes=VMEM_LIMIT
        ),
        name="second",
    )(d_act, ffn, resid, cotangent, in_blocks(act, members), d_gate, d_up)


def owner_kernel(
    pairs,
    d_keys_all,
    d_values_all,
    d_key_own,
    d_value_own,
    cosine,
    sine,
    d_key,
    d_value,
    *refs,
):
    take = taker(refs)
    parity = lax.rem(lax.axis_index("dp"), 2)
    order = bits_of(pairs)
    width = d_key.shape[1]
    moves, flows = [], []
    for way, source in zip((order, order[::-1]), (d_keys_all, d_values_all)):
        mine, theirs = take(2)
        moves.append(
            Pairwise(
                [
                    (
                        source.at[2 * pair + parity],
                        mine.at[pair],
                        source.at[2 * pair + 1 - parity],
                        theirs.at[pair],
                    )
                    for pair in range(pairs)
                ],
                take(3),
            )
        )

        def own(mask, target, columns, mine=mine, theirs=theirs):
            return mine[target, :, columns].astype(WIDE) + theirs[target, :, columns].astype(WIDE)

        flows.append(Halving(pairs, way, own, take(4)))
    (total,) = take(1)
    greet(member_peers(2 * pairs))
    for move in moves:
        move.start()
    for move, flow in zip(moves, flows):
        move.ready()
        flow.push(flow.masks[0])
    late = pl.ds(PROMPT_DEV, d_key.shape[0] - PROMPT_DEV)
    d_key[late] = d_key_own[...]
    d_value[late] = d_value_own[...]
    for index in range(1, pairs - 1):
        for flow in flows:
            flow.push(flow.masks[index])
    early = pl.ds(0, PROMPT_DEV)
    flows[0].end(total)
    for start in range(0, width, HEAD):
        d_key[early, start : start + HEAD] = rotate(
            total[:, start : start + HEAD], cosine[early], -sine[early]
        ).astype(LOW)
    flows[1].end(d_value.at[early])
    for move, flow in zip(moves, flows):
        flow.sent()
        move.sent()


def owner(members, d_keys_all, d_values_all, d_key_own, d_value_own, cosine, sine):
    width = d_key_own.shape[1]
    rows = cosine.shape[0]
    pairs = members // 2
    flow = (
        [pltpu.VMEM((pairs, PROMPT_DEV, width), LOW)] * 2
        + Pairwise.sems(pairs)
        + Halving.scratch(pairs, PROMPT_DEV, width)
    )
    return pl.pallas_call(
        functools.partial(owner_kernel, pairs),
        out_shape=[shape((rows, width), LOW)] * 2,
        in_specs=[ANY, ANY] + [VMEM] * 4,
        out_specs=[VMEM] * 2,
        scratch_shapes=flow * 2 + [pltpu.VMEM((PROMPT_DEV, width), WIDE)],
        compiler_params=pltpu.CompilerParams(
            collective_id=4, has_side_effects=True, vmem_limit_bytes=VMEM_LIMIT
        ),
        name="owner",
    )(d_keys_all, d_values_all, d_key_own, d_value_own, cosine, sine)


def first_kernel(
    count,
    pairs,
    grad_resid,
    d_query,
    d_key,
    d_value,
    w_query,
    w_key,
    w_value,
    states,
    act,
    mixed,
    branch_low,
    hidden,
    out_low,
    far_query,
    far_key,
    far_value,
    input_grad,
    grad_down,
    grad_out,
    grad_query,
    grad_key,
    grad_value,
    inner_total,
    part,
    state,
    weight,
    state_sem,
    weight_sem,
    *refs,
):
    take = taker(refs)
    line = Line(count, take(Line.scratch_count))
    order = bits_of(pairs)
    sides = []
    for left, rights, way in (
        (out_low, (hidden,), order),
        (act, (far_query, far_key, far_value), order[::-1]),
        (branch_low, (mixed,), order[::-1]),
    ):
        lhs, rhs = Lhs(left, take(4)), Rhs(rights, take(4))
        sides.append((lhs, rhs, Halving(pairs, way, product_of(lhs, rhs), take(4), *take(1))))
    rows = state.shape[0]
    fetch = pltpu.make_async_copy(
        states.at[pl.ds(pl.multiple_of(line.here * rows, rows), rows)], state, state_sem
    )
    loads = [
        pltpu.make_async_copy(source, weight.at[index], weight_sem.at[index])
        for index, source in enumerate((w_query, w_key, w_value))
    ]
    for load in loads:
        load.start()
    fetch.start()
    greet(line.peers() + member_peers(2 * pairs))
    for lhs, rhs, _ in sides[:2]:
        lhs.start()
        rhs.start(0)
    for at, (lhs, rhs, flow) in enumerate(sides):
        if at > 1:
            lhs.start()
        for piece in range(0 if at > 1 else 1, flow.pieces):
            rhs.start(piece)
    for load in loads:
        load.wait()
    tile = 512
    for start in range(0, part.shape[1], tile):
        columns = pl.ds(start, tile)
        part[:, columns] = (
            dot(d_query[...], weight[0, columns], 1, 1)
            + dot(d_key[...], weight[1, columns], 1, 1)
            + dot(d_value[...], weight[2, columns], 1, 1)
        )
    fetch.wait()

    def finish(group):
        span = pl.ds(group * line.rows, line.rows)
        normed, inverse = norm_rows(state[span])
        input_grad[line.span(group, line.here)] = (
            grad_resid[span] + norm_back(line.total[...], normed, inverse)
        ).astype(LOW)

    line.reduce(part, input_grad, finish, beside(order, sides))
    for (_, _, flow), target in zip(sides, (grad_down, inner_total, grad_out)):
        flow.end(target)
    width = grad_query.shape[1]
    for index, target in enumerate((grad_query, grad_key, grad_value)):
        target[...] = inner_total[:, index * width : index * width + width]
    for lhs, rhs, flow in sides:
        flow.sent()
        lhs.sent()
        rhs.sent()
    line.sent(input_grad)


def first(
    count,
    members,
    grad_resid,
    weights,
    states,
    act,
    mixed,
    branch_low,
    hidden,
    out_low,
    d_query,
    d_key,
    d_value,
):
    rows, depth = states.shape
    width = d_query.shape[1]
    units = hidden.shape[1]
    pairs = members // 2
    block = depth // members
    scratch = []
    for wide in (units, 3 * width, width):
        scratch += Lhs.scratch(pairs, rows, block) + Rhs.scratch(rows, wide)
        scratch += Halving.scratch(pairs, block, wide) + [pltpu.VMEM((block, wide), WIDE)]
    return pl.pallas_call(
        functools.partial(first_kernel, count, pairs),
        out_shape=[
            shape((rows, depth), LOW),
            shape((block, units), LOW),
        ]
        + [shape((block, width), LOW)] * 4,
        in_specs=[VMEM] * 4 + [ANY] * 12,
        out_specs=[VMEM] * 6,
        scratch_shapes=[
            pltpu.VMEM((block, 3 * width), LOW),
            pltpu.VMEM((rows, depth), WIDE),
            pltpu.VMEM((rows // count, depth), WIDE),
            pltpu.VMEM((3, depth, width), LOW),
            DMA,
            DMA((3,)),
        ]
        + Line.scratch(count, GROUPS, rows // count, depth)
        + scratch,
        compiler_params=pltpu.CompilerParams(
            collective_id=5, has_side_effects=True, vmem_limit_bytes=VMEM_LIMIT
        ),
        name="first",
    )(
        grad_resid,
        d_query,
        d_key,
        d_value,
        *weights,
        states,
        in_blocks(act, members),
        mixed,
        in_blocks(branch_low, members),
        hidden,
        in_blocks(out_low, members),
        d_query,
        d_key,
        d_value,
    )


def widen_kernel(flat, early, late, *refs):
    count = len(refs) // 2
    sources, whole, targets = refs[:count], refs[count], refs[count + 1 :]
    half = early.shape[0]
    whole[pl.ds(0, half)] = early[...].astype(WIDE)
    whole[pl.ds(half, half)] = late[...].astype(WIDE)
    for index, (source, target) in enumerate(zip(sources, targets)):
        values = source[...].astype(WIDE)
        target[...] = values if index < flat else values.T


def widen(count, early, late, plain, turned):
    def rows(array):
        return pl.BlockSpec((array.shape[0] // count, array.shape[1]), lambda i: (i, 0))

    def columns(array):
        return pl.BlockSpec((array.shape[0], array.shape[1] // count), lambda i: (0, i))

    flipped = [shape(array.shape[::-1], WIDE) for array in turned]
    whole = shape((2 * early.shape[0], early.shape[1]), WIDE)
    return pl.pallas_call(
        functools.partial(widen_kernel, len(plain)),
        out_shape=[whole] + [shape(array.shape, WIDE) for array in plain] + flipped,
        grid=(count,),
        in_specs=[rows(array) for array in (early, late, *plain)]
        + [columns(array) for array in turned],
        out_specs=[rows(array) for array in (whole, *plain, *flipped)],
        compiler_params=pltpu.CompilerParams(vmem_limit_bytes=VMEM_LIMIT),
        name="widen",
    )(early, late, *plain, *turned)


def body(
    states,
    w_query,
    w_key,
    w_value,
    w_out,
    w_gate,
    w_up,
    w_down,
    group_id,
    slice_start,
    cont_group,
    cotangent,
):
    rows = states.shape[0]
    members = lax.axis_size("dp")
    count = lax.axis_size("tensor")
    frequency = 10000.0 ** (-np.arange(HEAD // 2) * 2.0 / HEAD)
    frequency = np.concatenate([frequency, frequency]).astype(np.float32)
    sign = np.repeat([-1.0, 1.0], HEAD // 2).astype(np.float32)
    readers = (group_id, slice_start, cont_group)
    merged = members * PROMPT_DEV * w_query.shape[1] * 2 * 4 <= 16 * 2**20
    if merged:
        table = jnp.stack([frequency, sign])
        act_one, query, key, value, cosine, sine, mixed, attended, log_total, *everyones = (
            gather_attend(members, readers, w_query, w_key, w_value, states, table)
        )
    else:
        index = jnp.arange(rows, dtype=jnp.int32)
        everyone = jnp.arange(members, dtype=jnp.int32)
        own_start = jnp.sum(jnp.where(everyone == lax.axis_index("dp"), slice_start, 0))
        prompt = members // 2 * PROMPT_DEV
        positions = jnp.where(index < PROMPT_DEV, own_start + index, prompt + index - PROMPT_DEV)
        angles = positions.astype(WIDE)[:, None] * frequency[None, :]
        cosine = jnp.cos(angles)
        sine = jnp.sin(angles) * sign[None, :]
        act_one, query, key, value, *everyones = project(
            members, states, w_query, w_key, w_value, cosine, sine
        )
        mixed, attended, log_total = attend(readers, query, key, value, *everyones)
    act_two, resid, own_early, out_low, ffn_late, d_act_two, hidden, d_gate, d_up = middle(
        count, mixed, w_out, states, cotangent, w_gate, w_up, w_down
    )
    branch_low, grad_resid, own_late, grad_gate, grad_up = second(
        count, members, d_act_two, ffn_late, resid, cotangent, act_two, d_gate, d_up
    )
    kept = (query, key, value, branch_low, w_out, attended, log_total, cosine, sine)
    if merged:
        d_query, d_key, d_value, early_out, late_out = back_owner(
            members, count, readers, *everyones, *kept, own_early, own_late
        )
    else:
        d_query, *d_everyones = attend_back(
            readers, query, key, value, *everyones, branch_low, w_out, attended, log_total, cosine, sine
        )
        d_key, d_value = owner(members, *d_everyones, cosine, sine)
        early_out, late_out = [
            lax.all_gather(own, "tensor", axis=0, tiled=True) for own in (own_early, own_late)
        ]
    input_grad, grad_down, grad_out, *grad_inner = first(
        count,
        members,
        grad_resid,
        (w_query, w_key, w_value),
        states,
        act_one,
        mixed,
        branch_low,
        hidden,
        out_low,
        d_query,
        d_key,
        d_value,
    )
    *plain, grad_out, grad_down = widen(
        count,
        early_out,
        late_out,
        (input_grad, *grad_inner, grad_gate, grad_up),
        (grad_out, grad_down),
    )
    return (*plain[:5], grad_out, *plain[5:], grad_down)


def solution(mesh):
    placed = (
        P("dp", None),
        P(None, "tensor"),
        P(None, "tensor"),
        P(None, "tensor"),
        P("tensor", None),
        P(None, "tensor"),
        P(None, "tensor"),
        P("tensor", None),
        P(),
        P(),
        P("dp"),
        P("dp", None),
    )
    return jax.shard_map(
        body,
        mesh=mesh,
        in_specs=placed,
        out_specs=(
            P("dp", None),
            P("dp", None),
            P("dp", "tensor"),
            P("dp", "tensor"),
            P("dp", "tensor"),
            P("tensor", "dp"),
            P("dp", "tensor"),
            P("dp", "tensor"),
            P("tensor", "dp"),
        ),
        check_vma=False,
    )
```

```python
import functools

import jax
import jax.numpy as jnp
import numpy as np
from jax import lax
from jax.experimental import pallas as pl
from jax.experimental.pallas import tpu as pltpu
from jax.sharding import PartitionSpec as P

HEAD = 128
PROMPT_DEV = 384
EPSILON = 1e-05
NEGATIVE = -1e30
SCALE = HEAD ** (-0.5)
SCALE_TWO = float(SCALE * np.log2(np.e))
LOW = jnp.bfloat16
WIDE = jnp.float32
MESH = pl.DeviceIdType.MESH
ANY = pl.BlockSpec(memory_space=pl.ANY)
VMEM = pl.BlockSpec(memory_space=pltpu.VMEM)
DMA = pltpu.SemaphoreType.DMA
VMEM_LIMIT = 63 * 2**20
GROUPS = 2
PIECE = 512


def dot(left, right, left_dim=1, right_dim=0):
    return lax.dot_general(
        left, right, (((left_dim,), (right_dim,)), ((), ())), preferred_element_type=WIDE
    )


def shape(dims, dtype):
    return jax.ShapeDtypeStruct(dims, dtype)


def norm_rows(values):
    row_mean = jnp.mean(values, axis=-1, keepdims=True)
    centred = values - row_mean
    inverse = lax.rsqrt(jnp.mean(centred * centred, axis=-1, keepdims=True) + EPSILON)
    return centred * inverse, inverse


def norm_back(gradient, normed, inverse):
    return inverse * (
        gradient
        - jnp.mean(gradient, axis=-1, keepdims=True)
        - normed * jnp.mean(gradient * normed, axis=-1, keepdims=True)
    )


def rotate(values, cosine, sine):
    return values * cosine + pltpu.roll(values, HEAD // 2, 1) * sine


def flip(index, mask):
    out, bit = index, 1
    while bit <= mask:
        if mask & bit:
            out = out + bit * (1 - 2 * lax.rem(lax.div(index, bit), 2))
        bit *= 2
    return out


def bits_of(count):
    return list(range(count.bit_length() - 1))


def hail(peers):
    barrier = pltpu.get_barrier_semaphore()
    for peer in peers:
        pl.semaphore_signal(barrier, inc=1, device_id=peer, device_id_type=MESH)


def heed(peers):
    pl.semaphore_wait(pltpu.get_barrier_semaphore(), len(peers))


def greet(peers):
    hail(peers)
    heed(peers)


def remote(source, target, send_sem, recv_sem, device):
    return pltpu.make_async_remote_copy(
        src_ref=source,
        dst_ref=target,
        send_sem=send_sem,
        recv_sem=recv_sem,
        device_id=device,
        device_id_type=MESH,
    )


class Line:
    scratch_count = 10

    @staticmethod
    def scratch(count, groups, rows, width):
        rows = rows // groups
        return [
            pltpu.VMEM((rows, width), WIDE),
            pltpu.VMEM((groups, count, rows, width), LOW),
            pltpu.VMEM((groups, count, rows, width), LOW),
            pltpu.VMEM((groups, count, rows, width), LOW),
            DMA((groups, count)),
            DMA((groups, count)),
            DMA((groups, count)),
            DMA((groups, count)),
            DMA((groups, count)),
            DMA((groups, count)),
        ]

    def __init__(self, count, refs):
        self.count = count
        (
            self.total,
            self.outgoing,
            self.from_left,
            self.from_right,
            self.out_sem,
            self.left_sem,
            self.right_sem,
            self.to_right_sem,
            self.to_left_sem,
            self.got_sem,
        ) = refs
        self.groups = self.outgoing.shape[0]
        self.rows = self.total.shape[0]
        self.here = lax.axis_index("tensor")
        member = lax.axis_index("dp")
        self.right = (member, lax.rem(self.here + 1, count))
        self.left = (member, lax.rem(self.here + count - 1, count))

    def peers(self):
        return [self.left, self.right]

    def span(self, group, chunk):
        start = chunk * (self.rows * self.groups) + group * self.rows
        return pl.ds(pl.multiple_of(start, self.rows), self.rows)

    def rightward(self, group, chunk):
        return remote(
            self.outgoing.at[group, chunk],
            self.from_left.at[group, chunk],
            self.out_sem.at[group, chunk],
            self.left_sem.at[group, chunk],
            self.right,
        )

    def leftward(self, group, chunk):
        return remote(
            self.outgoing.at[group, chunk],
            self.from_right.at[group, chunk],
            self.out_sem.at[group, chunk],
            self.right_sem.at[group, chunk],
            self.left,
        )

    def add_and_pass(self, group, chunk, part, right, wait):
        copy, came = (self.rightward, self.from_left) if right else (self.leftward, self.from_right)
        total = part[self.span(group, chunk)].astype(WIDE)
        if wait:
            copy(group, chunk).wait_recv()
            total += came[group, chunk].astype(WIDE)
        self.outgoing[group, chunk] = total.astype(LOW)
        copy(group, chunk).start()

    def scatter_slot(self, group, slot, part):
        here, count = self.here, self.count
        ahead, back = count - 1 + here - slot, slot - (count - 1 - here)
        if slot == 0:

            @pl.when(here == 0)
            def _():
                self.add_and_pass(group, ahead, part, True, False)

            @pl.when(here == count - 1)
            def _():
                self.add_and_pass(group, back, part, False, False)

            return
        for wait in (False, True):

            @pl.when((here <= slot) & ((here > 0) if wait else (here == 0)))
            def _(wait=wait):
                self.add_and_pass(group, ahead, part, True, wait)

            @pl.when(
                (count - 1 - here <= slot) & ((here < count - 1) if wait else (here == count - 1))
            )
            def _(wait=wait):
                self.add_and_pass(group, back, part, False, wait)

    def scatter_end(self, group, part):
        here = self.here
        last = self.count - 1

        def left():
            self.rightward(group, here).wait_recv()
            return self.from_left[group, here].astype(WIDE)

        def right():
            self.leftward(group, here).wait_recv()
            return self.from_right[group, here].astype(WIDE)

        @pl.when(here == 0)
        def _():
            self.total[...] = part[self.span(group, here)].astype(WIDE) + right()

        @pl.when(here == last)
        def _():
            self.total[...] = part[self.span(group, here)].astype(WIDE) + left()

        @pl.when((here > 0) & (here < last))
        def _():
            self.total[...] = part[self.span(group, here)].astype(WIDE) + left() + right()

    def passing(self, whole, group, chunk, right):
        ref = whole.at[self.span(group, chunk)]
        return remote(
            ref,
            ref,
            (self.to_right_sem if right else self.to_left_sem).at[group, chunk],
            self.got_sem.at[group, chunk],
            self.right if right else self.left,
        )

    def gather_slot(self, whole, group, distance):
        here, count = self.here, self.count

        @pl.when(here - distance >= 0)
        def _():
            if distance:
                self.passing(whole, group, here - distance, True).wait_recv()

            @pl.when(here < count - 1)
            def _():
                self.passing(whole, group, here - distance, True).start()

        @pl.when(here + distance <= count - 1)
        def _():
            if distance:
                self.passing(whole, group, here + distance, False).wait_recv()

            @pl.when(here > 0)
            def _():
                self.passing(whole, group, here + distance, False).start()

    def reduce(self, part, whole, finish, beside=()):
        beside = list(beside)
        last = self.count - 1
        self.scatter_slot(0, 0, part)
        for group in range(self.groups):
            for slot in range(1, last):
                if beside:
                    beside.pop(0)()
                self.scatter_slot(group, slot, part)
                if group:
                    self.gather_slot(whole, group - 1, slot)
            if group + 1 < self.groups:
                self.scatter_slot(group + 1, 0, part)
            if group:
                self.gather_slot(whole, group - 1, last)
            self.scatter_end(group, part)
            finish(group)
            self.gather_slot(whole, group, 0)
        for distance in range(1, self.count):
            if beside:
                beside.pop(0)()
            self.gather_slot(whole, self.groups - 1, distance)
        for act in beside:
            act()

    def sent(self, whole=None):
        here, count = self.here, self.count
        for group in range(self.groups):
            for chunk in range(count):

                @pl.when(here != chunk)
                def _(group=group, chunk=chunk):
                    self.rightward(group, chunk).wait_send()

                if whole is None:
                    continue

                @pl.when((chunk <= here) & (here < count - 1))
                def _(group=group, chunk=chunk):
                    self.passing(whole, group, chunk, True).wait_send()

                @pl.when((chunk >= here) & (here > 0))
                def _(group=group, chunk=chunk):
                    self.passing(whole, group, chunk, False).wait_send()


class Halving:
    @staticmethod
    def masks_of(pairs, order):
        def stage(mask):
            return min(order.index(bit) for bit in order if mask >> bit & 1)

        return sorted(range(1, pairs), key=lambda mask: (stage(mask), -mask.bit_count()))

    @staticmethod
    def scratch(pairs, block, width):
        count = pairs - 1
        pieces = max(1, width // PIECE)
        return [
            pltpu.VMEM((count, block, width), LOW),
            pltpu.VMEM((count, block, width), LOW),
            DMA((count, pieces)),
            DMA((count, pieces)),
        ]

    def __init__(self, pairs, order, own, refs, kept=None):
        self.order, self.own, self.kept = order, own, kept
        self.send, self.recv, self.send_sem, self.recv_sem = refs
        self.masks = Halving.masks_of(pairs, order)
        self.pieces = self.send_sem.shape[1]
        self.piece = self.send.shape[2] // self.pieces
        self.member = lax.axis_index("dp")
        self.tensor = lax.axis_index("tensor")
        self.high = lax.div(self.member, 2)

    def stage(self, mask):
        return min(
            [self.order.index(bit) for bit in self.order if mask >> bit & 1],
            default=len(self.order),
        )

    def steps(self, stage):
        return [mask for mask in self.masks if self.stage(mask) == stage]

    def columns(self, piece):
        return pl.ds(piece * self.piece, self.piece)

    def copy(self, mask, piece):
        index = self.masks.index(mask)
        bit = 1 << self.order[self.stage(mask)]
        return remote(
            self.send.at[index, :, self.columns(piece)],
            self.recv.at[index, :, self.columns(piece)],
            self.send_sem.at[index, piece],
            self.recv_sem.at[index, piece],
            (flip(self.member, bit * 2), self.tensor),
        )

    def settle(self):
        for piece in range(self.pieces):
            columns = self.columns(piece)
            self.kept[:, columns] = self.own(0, flip(self.high, 0), columns)

    def fill(self, mask, piece, out):
        columns = self.columns(piece)
        if self.kept is not None and not mask:
            total = self.kept[:, columns]
        else:
            total = self.own(mask, flip(self.high, mask), columns)
        for bit in self.order[: self.stage(mask)]:
            slot = mask | 1 << bit
            self.copy(slot, piece).wait_recv()
            total += self.recv[self.masks.index(slot), :, columns].astype(WIDE)
        out[:, columns] = total.astype(out.dtype)

    def push_piece(self, mask, piece):
        self.fill(mask, piece, self.send.at[self.masks.index(mask)])
        self.copy(mask, piece).start()

    def push(self, mask):
        for piece in range(self.pieces):
            self.push_piece(mask, piece)

    def end(self, out):
        for piece in range(self.pieces):
            self.fill(0, piece, out)

    def sent(self):
        for mask in self.masks:
            for piece in range(self.pieces):
                self.copy(mask, piece).wait_send()


class Pairwise:
    def __init__(self, moves, refs):
        self.moves, self.done = moves, False
        self.local_sem, self.send_sem, self.recv_sem = refs
        member = lax.axis_index("dp")
        self.partner = (flip(member, 1), lax.axis_index("tensor"))

    @staticmethod
    def sems(count):
        return [DMA((count,)), DMA((count,)), DMA((count,))]

    def local(self, index):
        source, target, _, _ = self.moves[index]
        return pltpu.make_async_copy(source, target, self.local_sem.at[index])

    def across(self, index):
        _, _, source, target = self.moves[index]
        return remote(
            source, target, self.send_sem.at[index], self.recv_sem.at[index], self.partner
        )

    def start(self, index=None):
        for index in range(len(self.moves)) if index is None else [index]:
            self.across(index).start()
            self.local(index).start()

    def ready(self, index=None):
        if index is None and self.done:
            return
        self.done = index is None
        for index in range(len(self.moves)) if index is None else [index]:
            self.local(index).wait()
            self.across(index).wait_recv()

    def sent(self):
        for index in range(len(self.moves)):
            self.across(index).wait_send()


class Lhs(Pairwise):
    @staticmethod
    def scratch(pairs, rows, block):
        return [pltpu.VMEM((pairs, 2 * rows, block), LOW)] + Pairwise.sems(pairs)

    def __init__(self, source, refs):
        self.held = refs[0]
        pairs, rows, block = self.held.shape
        rows = rows // 2
        parity = lax.rem(lax.axis_index("dp"), 2)

        def columns(index):
            if len(source.shape) == 3:
                return source.at[index]
            return source.at[:, pl.ds(pl.multiple_of(index * block, block), block)]

        super().__init__(
            [
                (
                    columns(2 * pair + parity),
                    self.held.at[pair, pl.ds(0, rows)],
                    columns(2 * pair + 1 - parity),
                    self.held.at[pair, pl.ds(rows, rows)],
                )
                for pair in range(pairs)
            ],
            refs[1:],
        )


class Rhs(Pairwise):
    @staticmethod
    def scratch(rows, width):
        return [pltpu.VMEM((2 * rows, width), LOW)] + Pairwise.sems(width // PIECE)

    def __init__(self, sources, refs):
        self.held = refs[0]
        rows = self.held.shape[0] // 2
        moves, at = [], 0
        for source in sources:
            for start in range(0, source.shape[1], PIECE):
                columns = pl.ds(at, PIECE)
                at += PIECE
                here = source.at[:, pl.ds(start, PIECE)]
                moves.append(
                    (
                        here,
                        self.held.at[pl.ds(0, rows), columns],
                        here,
                        self.held.at[pl.ds(rows, rows), columns],
                    )
                )
        super().__init__(moves, refs[1:])


def product_of(lhs, rhs):
    def own(mask, target, columns):
        return dot(lhs.held[target], rhs.held[:, columns], 0, 0)

    return own


def taker(refs):
    refs = list(refs)

    def take(count):
        out = refs[:count]
        del refs[:count]
        return out

    return take


def in_blocks(left, members):
    block = left.shape[1] // members
    if block % 128 == 0:
        return left
    return left.reshape(left.shape[0], members, block).transpose(1, 0, 2)


def member_peers(members):
    member, tensor = lax.axis_index("dp"), lax.axis_index("tensor")
    return [(flip(member, 1 << bit), tensor) for bit in bits_of(members)]


def project_kernel(
    members,
    states,
    w_query,
    w_key,
    w_value,
    cosine,
    sine,
    act,
    query,
    key,
    value,
    keys_all,
    values_all,
    send_sem,
    recv_sem,
    local_sem,
):
    member, tensor = lax.axis_index("dp"), lax.axis_index("tensor")
    width = query.shape[1]
    greet(member_peers(members))
    rows = 64
    for start in range(0, states.shape[0], rows):
        span = pl.ds(start, rows)
        act[span] = norm_rows(states[span])[0].astype(LOW)

    def turned(weight, out):
        linear = dot(act[...], weight[...])
        for start in range(0, width, HEAD):
            out[:, start : start + HEAD] = rotate(
                linear[:, start : start + HEAD], cosine[...], sine[...]
            ).astype(LOW)

    high = [bit for bit in bits_of(members) if bit]
    orders = (high + [0], high[::-1] + [0])
    owns, alls = (key, value), (keys_all, values_all)

    def copy(flow, mask, bit):
        slot = mask | 1 << bit
        place = alls[flow].at[flip(member, mask)]
        return remote(
            place if mask else owns[flow].at[pl.ds(0, PROMPT_DEV)],
            place,
            send_sem.at[flow, slot],
            recv_sem.at[flow, slot],
            (flip(member, 1 << bit), tensor),
        )

    def forward(flow, mask):
        order = orders[flow]
        last = max([order.index(bit) for bit in order if mask >> bit & 1], default=-1)
        for bit in order[last + 1 :]:
            copy(flow, mask, bit).start()

    def came_by(flow, mask):
        order = orders[flow]
        bit = order[max(order.index(bit) for bit in order if mask >> bit & 1)]
        return copy(flow, mask ^ 1 << bit, bit)

    def keep(flow):
        return pltpu.make_async_copy(
            owns[flow].at[pl.ds(0, PROMPT_DEV)], alls[flow].at[member], local_sem.at[flow]
        )

    turned(w_key, key)
    forward(0, 0)
    value[...] = dot(act[...], w_value[...]).astype(LOW)
    forward(1, 0)
    keep(0).start()
    keep(1).start()
    turned(w_query, query)
    masks = range(1, members)
    inner = sorted([mask for mask in masks if not mask & 1], key=lambda mask: mask.bit_count())
    for mask in inner:
        for flow in (0, 1):
            turn = flow if not mask & 2 else flow
            came_by(turn, mask).wait_recv()
            forward(turn, mask)
    for mask in masks:
        if mask & 1:
            for flow in (0, 1):
                came_by(flow, mask).wait_recv()
    for flow in (0, 1):
        keep(flow).wait()
        for mask in masks:
            came_by(flow, mask).wait_send()


def project(members, states, w_query, w_key, w_value, cosine, sine):
    rows, depth = states.shape
    width = w_query.shape[1]
    return pl.pallas_call(
        functools.partial(project_kernel, members),
        out_shape=[
            shape((rows, depth), LOW),
            shape((rows, width), LOW),
            shape((rows, width), LOW),
            shape((rows, width), LOW),
            shape((members, PROMPT_DEV, width), LOW),
            shape((members, PROMPT_DEV, width), LOW),
        ],
        in_specs=[VMEM] * 6,
        out_specs=[VMEM] * 4 + [ANY] * 2,
        scratch_shapes=[DMA((2, members)), DMA((2, members)), DMA((2,))],
        compiler_params=pltpu.CompilerParams(
            collective_id=1, has_side_effects=True, vmem_limit_bytes=VMEM_LIMIT
        ),
        name="project",
    )(states, w_query, w_key, w_value, cosine, sine)


def make_plan(half, group_id, slice_start, cont_group, plan):
    member = lax.axis_index("dp")
    own, other = group_id[member], cont_group[0]
    plan[0] = lax.div(slice_start[member], PROMPT_DEV)

    def step(index, _):
        rank = lax.div(slice_start[index], PROMPT_DEV)

        @pl.when(group_id[index] == own)
        def _():
            plan[1 + rank] = index

        @pl.when(group_id[index] == other)
        def _():
            plan[1 + half + rank] = index

        return 0

    lax.fori_loop(0, 2 * half, step, 0)


def attend_kernel(
    half,
    group_id,
    slice_start,
    cont_group,
    query,
    key,
    value,
    keys_all,
    values_all,
    mixed,
    attended,
    log_total,
    plan,
):
    @pl.when(pl.program_id(0) == 0)
    def _():
        make_plan(half, group_id, slice_start, cont_group, plan)

    def part(start, count, steps, offset):
        span = pl.ds(start, count)
        queries = query[span]
        allowed = lax.broadcasted_iota(jnp.int32, (count, count), 0) >= lax.broadcasted_iota(
            jnp.int32, (count, count), 1
        )
        scores = jnp.where(allowed, dot(queries, key[span], 1, 1) * SCALE, NEGATIVE)
        top = jnp.max(scores, axis=-1, keepdims=True)
        weights = jnp.exp(scores - top)
        total = jnp.sum(weights, axis=-1, keepdims=True)
        result = dot(weights.astype(LOW), value[span])

        def step(index, carry):
            top, total, result = carry
            place = plan[offset + index]
            scores = dot(queries, keys_all[place], 1, 1) * SCALE
            higher = jnp.maximum(top, jnp.max(scores, axis=-1, keepdims=True))
            fade = jnp.exp(top - higher)
            weights = jnp.exp(scores - higher)
            total = total * fade + jnp.sum(weights, axis=-1, keepdims=True)
            result = result * fade + dot(weights.astype(LOW), values_all[place])
            return higher, total, result

        top, total, result = lax.fori_loop(0, steps, step, (top, total, result))
        result = result / total
        mixed[span] = result.astype(LOW)
        attended[span] = result
        log_total[span] = jnp.broadcast_to(top + jnp.log(total), (count, HEAD))

    part(0, PROMPT_DEV, plan[0], 1)
    part(PROMPT_DEV, query.shape[0] - PROMPT_DEV, half, 1 + half)


def attend(readers, query, key, value, keys_all, values_all):
    rows, width = query.shape
    members = keys_all.shape[0]
    head = pl.BlockSpec((rows, HEAD), lambda h, *_: (0, h))
    every = pl.BlockSpec((members, PROMPT_DEV, HEAD), lambda h, *_: (0, 0, h))
    return pl.pallas_call(
        functools.partial(attend_kernel, members // 2),
        out_shape=[
            shape((rows, width), LOW),
            shape((rows, width), WIDE),
            shape((rows, width), WIDE),
        ],
        grid_spec=pltpu.PrefetchScalarGridSpec(
            num_scalar_prefetch=3,
            grid=(width // HEAD,),
            in_specs=[head, head, head, every, every],
            out_specs=[head, head, head],
            scratch_shapes=[pltpu.SMEM((members + 1,), jnp.int32)],
        ),
        compiler_params=pltpu.CompilerParams(vmem_limit_bytes=VMEM_LIMIT),
        name="attend",
    )(*readers, query, key, value, keys_all, values_all)


def attend_back_kernel(
    half,
    group_id,
    slice_start,
    cont_group,
    query,
    key,
    value,
    keys_all,
    values_all,
    branch_low,
    w_out,
    attended,
    log_total,
    cosine,
    sine,
    d_query,
    d_keys_all,
    d_values_all,
    d_key_own,
    d_value_own,
    d_mixed,
    key_total,
    value_total,
    plan,
):
    @pl.when(pl.program_id(0) == 0)
    def _():
        make_plan(half, group_id, slice_start, cont_group, plan)

    d_mixed[...] = dot(branch_low[...], w_out[...], 1, 1).astype(LOW)
    key_total[...] = jnp.zeros_like(key_total)
    value_total[...] = jnp.zeros_like(value_total)

    def part(start, count, steps, offset):
        span = pl.ds(start, count)
        queries, d_attended = query[span], d_mixed[span]
        log_sum = log_total[span][:, :1]
        center = jnp.sum(d_attended.astype(WIDE) * attended[span], axis=-1, keepdims=True)

        def back(scores, keys, values):
            probabilities = jnp.exp(scores - log_sum)
            d_scores = (probabilities * (dot(d_attended, values, 1, 1) - center)).astype(LOW)
            return (
                dot(d_scores, keys),
                dot(d_scores, queries, 0, 0),
                dot(probabilities.astype(LOW), d_attended, 0, 0),
            )

        allowed = lax.broadcasted_iota(jnp.int32, (count, count), 0) >= lax.broadcasted_iota(
            jnp.int32, (count, count), 1
        )
        scores = jnp.where(allowed, dot(queries, key[span], 1, 1) * SCALE, NEGATIVE)
        d_queries, d_own_keys, d_own_values = back(scores, key[span], value[span])

        def step(index, d_queries):
            place = plan[offset + index]
            keys, values = keys_all[place], values_all[place]
            more, d_keys, d_values = back(dot(queries, keys, 1, 1) * SCALE, keys, values)
            key_total[place] += d_keys
            value_total[place] += d_values
            return d_queries + more

        d_queries = lax.fori_loop(0, steps, step, d_queries) * SCALE
        d_query[span] = rotate(d_queries, cosine[span], -sine[span]).astype(LOW)
        return d_own_keys, d_own_values

    member = lax.axis_index("dp")
    d_own_keys, d_own_values = part(0, PROMPT_DEV, plan[0], 1)
    key_total[member] += d_own_keys
    value_total[member] += d_own_values
    d_own_keys, d_own_values = part(PROMPT_DEV, query.shape[0] - PROMPT_DEV, half, 1 + half)
    late = pl.ds(PROMPT_DEV, query.shape[0] - PROMPT_DEV)
    d_key_own[...] = rotate(d_own_keys * SCALE, cosine[late], -sine[late]).astype(LOW)
    d_value_own[...] = d_own_values.astype(LOW)
    d_keys_all[...] = (key_total[...] * SCALE).astype(LOW)
    d_values_all[...] = value_total[...].astype(LOW)


def attend_back(
    readers,
    query,
    key,
    value,
    keys_all,
    values_all,
    branch_low,
    w_out,
    attended,
    log_total,
    cosine,
    sine,
):
    rows, width = query.shape
    members = keys_all.shape[0]
    depth = branch_low.shape[1]
    late = rows - PROMPT_DEV
    heads = width // HEAD
    head = pl.BlockSpec((rows, HEAD), lambda h, *_: (0, h))
    every = pl.BlockSpec((members, PROMPT_DEV, HEAD), lambda h, *_: (0, 0, h))
    own = pl.BlockSpec((late, HEAD), lambda h, *_: (0, h))
    table = pl.BlockSpec((rows, HEAD), lambda h, *_: (0, 0))
    return pl.pallas_call(
        functools.partial(attend_back_kernel, members // 2),
        out_shape=[
            shape((rows, width), LOW),
            shape((members, PROMPT_DEV, width), LOW),
            shape((members, PROMPT_DEV, width), LOW),
            shape((late, width), LOW),
            shape((late, width), LOW),
        ],
        grid_spec=pltpu.PrefetchScalarGridSpec(
            num_scalar_prefetch=3,
            grid=(heads,),
            in_specs=[
                head,
                head,
                head,
                every,
                every,
                pl.BlockSpec((rows, depth), lambda h, *_: (0, 0)),
                pl.BlockSpec((HEAD, depth), lambda h, *_: (h, 0)),
                head,
                head,
                table,
                table,
            ],
            out_specs=[head, every, every, own, own],
            scratch_shapes=[
                pltpu.VMEM((rows, HEAD), LOW),
                pltpu.VMEM((members, PROMPT_DEV, HEAD), WIDE),
                pltpu.VMEM((members, PROMPT_DEV, HEAD), WIDE),
                pltpu.SMEM((members + 1,), jnp.int32),
            ],
        ),
        compiler_params=pltpu.CompilerParams(vmem_limit_bytes=VMEM_LIMIT),
        name="attend_back",
    )(
        *readers,
        query,
        key,
        value,
        keys_all,
        values_all,
        branch_low,
        w_out,
        attended,
        log_total,
        cosine,
        sine,
    )


def place_of(group_id, slice_start, group, rank):
    place = 0
    for index in range(group_id.shape[0]):
        found = (group_id[index] == group) & (slice_start[index] == rank * PROMPT_DEV)
        place = jnp.maximum(place, jnp.where(found, index, 0))
    return place


def own_part(rows):
    return lax.broadcasted_iota(jnp.int32, (rows, rows), 0) >= lax.broadcasted_iota(
        jnp.int32, (rows, rows), 1
    )


def gather_attend_kernel(
    members,
    group_id,
    slice_start,
    cont_group,
    w_query_in,
    w_key_in,
    w_value_in,
    states_in,
    table,
    act,
    query,
    key,
    value,
    cosine,
    sine,
    mixed,
    attended,
    log_total,
    keys_out,
    values_out,
    states,
    weights,
    load_sem,
    weight_sem,
    send_sem,
    recv_sem,
    keep_sem,
    out_sem,
    *every,
):
    member, tensor = lax.axis_index("dp"), lax.axis_index("tensor")
    heads = query.shape[0]
    keys_all, values_all = every[:heads], every[heads:]
    half = members // 2
    rows = states.shape[0]
    chunks = load_sem.shape[0]
    size = rows // chunks
    loads = []
    for index in range(chunks):
        span = pl.ds(index * size, size)
        loads.append(pltpu.make_async_copy(states_in.at[span], states.at[span], load_sem.at[index]))
    w_loads = [
        pltpu.make_async_copy(source, weights.at[index], weight_sem.at[index])
        for index, source in enumerate((w_key_in, w_value_in, w_query_in))
    ]
    for load in loads[:1] + w_loads[:1] + loads[1:] + w_loads[1:]:
        load.start()
    hail(member_peers(members))
    index = lax.broadcasted_iota(jnp.int32, cosine.shape, 0)
    prompt = half * PROMPT_DEV - PROMPT_DEV
    positions = index + jnp.where(index < PROMPT_DEV, slice_start[member], prompt)
    angles = positions.astype(WIDE) * table[:1]
    cosine[...] = jnp.cos(angles)
    sine[...] = jnp.sin(angles) * table[1:2]
    step = 64
    for index in range(chunks):
        loads[index].wait()
        for start in range(index * size, index * size + size, step):
            span = pl.ds(start, step)
            act[span] = norm_rows(states[span])[0].astype(LOW)

    def turned(weight, out):
        linear = dot(act[...], weight)
        for head in range(heads):
            out[head] = rotate(
                linear[:, head * HEAD : head * HEAD + HEAD], cosine[...], sine[...]
            ).astype(LOW)

    high = [bit for bit in bits_of(members) if bit]
    orders = (high + [0], high[::-1] + [0])
    owns, alls = (key, value), (keys_all, values_all)
    early = pl.ds(0, PROMPT_DEV)

    def copy(flow, head, mask, bit):
        slot = mask | 1 << bit
        place = alls[flow][head].at[flip(member, mask)]
        return remote(
            place if mask else owns[flow].at[head, early],
            place,
            send_sem.at[flow, head, slot],
            recv_sem.at[flow, head, slot],
            (flip(member, 1 << bit), tensor),
        )

    def forward(flow, head, mask):
        order = orders[flow]
        last = max([order.index(bit) for bit in order if mask >> bit & 1], default=-1)
        for bit in order[last + 1 :]:
            copy(flow, head, mask, bit).start()

    def came_by(flow, head, mask):
        order = orders[flow]
        bit = order[max(order.index(bit) for bit in order if mask >> bit & 1)]
        return copy(flow, head, mask ^ 1 << bit, bit)

    def keep(flow, head):
        return pltpu.make_async_copy(
            owns[flow].at[head, early], alls[flow][head].at[member], keep_sem.at[flow, head]
        )

    def write(flow, head):
        return pltpu.make_async_copy(
            alls[flow][head], (keys_out, values_out)[flow].at[head], out_sem.at[flow, head]
        )

    masks = range(1, members)
    levels = len(high)

    def own_sends(head):
        if head < heads:
            for flow in (0, 1):
                forward(flow, head, 0)
            for flow in (0, 1):
                keep(flow, head).start()

    def level(head, count):
        if head < heads:
            for mask in masks:
                if not mask & 1 and mask.bit_count() == count:
                    for flow in (0, 1):
                        came_by(flow, head, mask).wait_recv()
                        forward(flow, head, mask)

    def complete(head):
        for flow in (0, 1):
            for mask in masks:
                if mask & 1:
                    came_by(flow, head, mask).wait_recv()
            keep(flow, head).wait()
            write(flow, head).start()

    own_group, other_group = group_id[member], cont_group[0]
    own_start = slice_start[member]
    own_places = [place_of(group_id, slice_start, own_group, rank) for rank in range(half)]
    other_places = [place_of(group_id, slice_start, other_group, rank) for rank in range(half)]
    block = 128

    def attend_rows(head, start, places, whole):
        span = pl.ds(start, block)
        queries = query[head, span]
        scores, values = [], []
        for rank, place in enumerate(places):
            score = dot(queries, keys_all[head][place], 1, 1) * SCALE_TWO
            if not whole:
                at = lax.broadcasted_iota(jnp.int32, score.shape, 0) + (own_start + start)
                to = lax.broadcasted_iota(jnp.int32, score.shape, 1) + rank * PROMPT_DEV
                score = jnp.where(to <= at, score, NEGATIVE)
            scores.append(score)
            values.append(values_all[head][place])
        if whole:
            score = dot(queries, key[head, span], 1, 1) * SCALE_TWO
            scores.append(jnp.where(own_part(block), score, NEGATIVE))
            values.append(value[head, span])
        top = functools.reduce(
            jnp.maximum, [jnp.max(score, axis=-1, keepdims=True) for score in scores]
        )
        total = jnp.zeros_like(top)
        result = jnp.zeros((block, HEAD), WIDE)
        for score, held in zip(scores, values):
            weight = jnp.exp2(score - top)
            total += jnp.sum(weight, axis=-1, keepdims=True)
            result += dot(weight.astype(LOW), held)
        result = result / total
        mixed[span, head * HEAD : head * HEAD + HEAD] = result.astype(LOW)
        attended[head, span] = result
        log_total[head, span] = jnp.broadcast_to(top + jnp.log2(total), (block, HEAD))

    w_loads[0].wait()
    turned(weights[0], key)
    heed(member_peers(members))
    forward(0, 0, 0)
    w_loads[1].wait()
    linear = dot(act[...], weights[1])
    for head in range(heads):
        value[head] = linear[:, head * HEAD : head * HEAD + HEAD].astype(LOW)
    forward(1, 0, 0)
    for flow in (0, 1):
        keep(flow, 0).start()
    own_sends(1)
    w_loads[2].wait()
    turned(weights[2], query)
    level(0, 1)
    own_sends(2)
    for count in range(2, levels + 1):
        level(0, count)
    level(1, 1)
    own_sends(3)
    for head in range(heads):
        complete(head)

        @pl.loop(0, PROMPT_DEV // block)
        def _(index, head=head):
            attend_rows(head, pl.multiple_of(index * block, block), own_places, False)

        for count in range(2, levels + 1):
            level(head + 1, count)
        level(head + 2, 1)
        own_sends(head + 4)
        for start in range(PROMPT_DEV, rows, block):
            attend_rows(head, start, other_places, True)
    for head in range(heads):
        for flow in (0, 1):
            write(flow, head).wait()
            for mask in masks:
                came_by(flow, head, mask).wait_send()


def gather_attend(members, readers, w_query, w_key, w_value, states, table):
    rows, depth = states.shape
    width = w_query.shape[1]
    heads = width // HEAD
    smem = pl.BlockSpec(memory_space=pltpu.SMEM)
    row_heads = (heads, rows, HEAD)
    every = (heads, members, PROMPT_DEV, HEAD)
    return pl.pallas_call(
        functools.partial(gather_attend_kernel, members),
        out_shape=[
            shape((rows, depth), LOW),
            shape(row_heads, LOW),
            shape(row_heads, LOW),
            shape(row_heads, LOW),
            shape((rows, HEAD), WIDE),
            shape((rows, HEAD), WIDE),
            shape((rows, width), LOW),
            shape(row_heads, WIDE),
            shape(row_heads, WIDE),
            shape(every, LOW),
            shape(every, LOW),
        ],
        in_specs=[smem] * 3 + [ANY] * 4 + [VMEM],
        out_specs=[VMEM] * 9 + [ANY] * 2,
        scratch_shapes=[
            pltpu.VMEM((rows, depth), WIDE),
            pltpu.VMEM((3, depth, width), LOW),
            DMA((4,)),
            DMA((3,)),
            DMA((2, heads, members)),
            DMA((2, heads, members)),
            DMA((2, heads)),
            DMA((2, heads)),
        ]
        + [pltpu.VMEM(every[1:], LOW)] * (2 * heads),
        compiler_params=pltpu.CompilerParams(
            collective_id=6, has_side_effects=True, vmem_limit_bytes=VMEM_LIMIT
        ),
        name="gather_attend",
    )(
        *readers,
        w_query,
        w_key,
        w_value,
        states,
        table,
    )


def back_owner_kernel(
    members,
    count,
    group_id,
    slice_start,
    cont_group,
    keys_in,
    values_in,
    query_in,
    key_in,
    value_in,
    attended_in,
    log_total_in,
    branch_low,
    w_out,
    cosine,
    sine,
    own_early,
    own_late,
    d_query,
    d_key,
    d_value,
    early_out,
    late_out,
    query,
    key,
    value,
    attended,
    log_total,
    d_mixed,
    d_queries,
    own_keys,
    own_values,
    other_keys,
    other_values,
    load_sem,
    *refs,
):
    take = taker(refs)
    member = lax.axis_index("dp")
    heads, rows = query.shape[0], query.shape[1]
    keys_all, values_all = take(heads), take(heads)
    out_send, out_recv = take(2)
    here = lax.axis_index("tensor")
    size = own_early.shape[0]
    own_rows = pl.ds(pl.multiple_of(here * size, size), size)
    told = ((own_early, early_out), (own_late, late_out))

    def tell(which, distance):
        source, target = told[which]
        return remote(
            source,
            target.at[own_rows],
            out_send.at[which, distance - 1],
            out_recv.at[which, distance - 1],
            (member, lax.rem(here + distance, count)),
        )

    half = pairs = members // 2
    parity = lax.rem(member, 2)
    order = bits_of(pairs)
    moves, flows, sides = [], [], []
    for way in (order, order[::-1]):
        mine, leaving, theirs = take(3)
        local_free, send_sem, recv_sem = take(3)
        refs_of = take(4)
        sides.append((mine, leaving, theirs, send_sem, recv_sem))
        per_head = []
        for head in range(heads):

            def own(mask, target, columns, mine=mine, theirs=theirs, head=head):
                return mine[head, target, :, columns].astype(WIDE) + theirs[
                    head, target, :, columns
                ].astype(WIDE)

            per_head.append(Halving(pairs, way, own, [ref.at[head] for ref in refs_of]))
        flows.append(per_head)
    partner = (flip(member, 1), lax.axis_index("tensor"))

    sources = (keys_in, values_in, query_in, key_in, value_in, attended_in, log_total_in)

    def load(index, head):
        if index < 2:
            target = (keys_all, values_all)[index][head]
        else:
            target = (query, key, value, attended, log_total)[index - 2].at[head]
        return pltpu.make_async_copy(
            sources[index].at[head], target, load_sem.at[index, head]
        )

    for head in range(heads):
        for index in range(len(sources)):
            load(index, head).start()

    def across(flow, head):
        _, leaving, theirs, send_sem, recv_sem = sides[flow]
        return remote(
            leaving.at[head], theirs.at[head], send_sem.at[head], recv_sem.at[head], partner
        )

    own_group, other_group = group_id[member], cont_group[0]
    own_start = slice_start[member]
    own_places = [place_of(group_id, slice_start, own_group, rank) for rank in range(half)]
    other_places = [place_of(group_id, slice_start, other_group, rank) for rank in range(half)]
    across_line = [(member, lax.rem(here + distance, count)) for distance in range(1, count)]
    hail(member_peers(members) + across_line)
    linear = dot(branch_low[...], w_out[...], 1, 1)
    for head in range(heads):
        d_mixed[head] = linear[:, head * HEAD : head * HEAD + HEAD].astype(LOW)
    heed(member_peers(members) + across_line)
    for which, (source, target) in enumerate(told):
        for distance in range(1, count):
            tell(which, distance).start()
        target[own_rows] = source[...]
    late = rows - PROMPT_DEV

    def back(scores, queries, keys, values, d_attended, log_sum, center):
        probabilities = jnp.exp2(scores - log_sum)
        d_scores = (probabilities * (dot(d_attended, values, 1, 1) - center)).astype(LOW)
        return (
            dot(d_scores, keys),
            dot(d_scores, queries, 0, 0),
            dot(probabilities.astype(LOW), d_attended, 0, 0),
        )

    def rows_of(head, start, count):
        span = pl.ds(start, count)
        d_attended = d_mixed[head, span]
        center = jnp.sum(d_attended.astype(WIDE) * attended[head, span], axis=-1, keepdims=True)
        return query[head, span], d_attended, log_total[head, span][:, :1], center

    def prompt_rank(head, rank):
        queries, d_attended, log_sum, center = rows_of(head, 0, PROMPT_DEV)
        place = own_places[rank]
        keys, values = keys_all[head][place], values_all[head][place]
        scores = dot(queries, keys, 1, 1) * SCALE_TWO
        at = lax.broadcasted_iota(jnp.int32, scores.shape, 0) + own_start
        to = lax.broadcasted_iota(jnp.int32, scores.shape, 1) + rank * PROMPT_DEV
        scores = jnp.where(to <= at, scores, NEGATIVE)
        more, d_keys, d_values = back(
            scores, queries, keys, values, d_attended, log_sum, center
        )
        early = pl.ds(0, PROMPT_DEV)
        if rank:
            d_queries[early] += more
        else:
            d_queries[early] = more
        own_keys[rank] = d_keys
        own_values[rank] = d_values

    def late_part(head):
        queries, d_attended, log_sum, center = rows_of(head, PROMPT_DEV, late)
        span = pl.ds(PROMPT_DEV, late)
        keys, values = key[head, span], value[head, span]
        scores = jnp.where(own_part(late), dot(queries, keys, 1, 1) * SCALE_TWO, NEGATIVE)
        total, d_keys, d_values = back(
            scores, queries, keys, values, d_attended, log_sum, center
        )
        columns = pl.ds(head * HEAD, HEAD)
        d_key[span, columns] = rotate(d_keys * SCALE, cosine[span], -sine[span]).astype(LOW)
        d_value[span, columns] = d_values.astype(LOW)
        for rank in range(half):
            place = other_places[rank]
            keys, values = keys_all[head][place], values_all[head][place]
            more, d_keys, d_values = back(
                dot(queries, keys, 1, 1) * SCALE_TWO, queries, keys, values, d_attended, log_sum, center
            )
            total += more
            other_keys[rank] = d_keys
            other_values[rank] = d_values
        d_queries[span] = total
        d_query[:, columns] = rotate(d_queries[...] * SCALE, cosine[...], -sine[...]).astype(LOW)

    def spread(head):
        for pair in range(pairs):
            for away in (0, 1):
                index = 2 * pair + (1 - parity if away else parity)
                rank = lax.div(slice_start[index], PROMPT_DEV)
                mine = jnp.where(group_id[index] == own_group, 1.0, 0.0)
                other = jnp.where(group_id[index] == other_group, 1.0, 0.0)
                for flow, (a, b, scale) in enumerate(
                    ((own_keys, other_keys, SCALE), (own_values, other_values, 1.0))
                ):
                    total = a[rank] * (mine * scale) + b[rank] * (other * scale)
                    sides[flow][away][head, pair] = total.astype(LOW)

    def begin(head):
        for flow in (0, 1):
            across(flow, head).start()

    def stage(head, index):
        if not 0 <= head < heads:
            return
        for flow in (0, 1):
            if not index:
                across(flow, head).wait_recv()
        for flow in (0, 1):
            for mask in flows[flow][head].steps(index):
                flows[flow][head].push(mask)

    def end(head):
        if not 0 <= head < heads:
            return
        early = pl.ds(0, PROMPT_DEV)
        columns = pl.ds(head * HEAD, HEAD)
        total = d_queries.at[early]
        flows[0][head].end(total)
        d_key[early, columns] = rotate(total[...], cosine[early], -sine[early]).astype(LOW)
        flows[1][head].end(d_value.at[early, columns])

    depth = len(order)
    for head in range(heads):
        for index in range(len(sources)):
            load(index, head).wait()
        for rank in range(half):
            prompt_rank(head, rank)
            if rank == 0:
                stage(head - 1, 0)
            if rank == half - 1:
                for index in range(1, depth):
                    stage(head - 1, index)
        late_part(head)
        spread(head)
        begin(head)
        end(head - 1)
    for index in range(depth):
        stage(heads - 1, index)
    end(heads - 1)
    for flow in (0, 1):
        for head in range(heads):
            across(flow, head).wait_send()
            flows[flow][head].sent()
    for which in range(len(told)):
        for distance in range(1, count):
            tell(which, distance).wait()


def back_owner(
    members,
    count,
    readers,
    keys_all,
    values_all,
    query,
    key,
    value,
    branch_low,
    w_out,
    attended,
    log_total,
    cosine,
    sine,
    own_early,
    own_late,
):
    heads, rows, _ = query.shape
    width = heads * HEAD
    pairs = members // 2
    smem = pl.BlockSpec(memory_space=pltpu.SMEM)
    every = pltpu.VMEM((members, PROMPT_DEV, HEAD), LOW)
    side = pltpu.VMEM((heads, pairs, PROMPT_DEV, HEAD), LOW)
    step = pltpu.VMEM((heads, pairs - 1, PROMPT_DEV, HEAD), LOW)
    flow = [side] * 3 + [DMA((heads,))] * 3 + [step] * 2 + [DMA((heads, pairs - 1, 1))] * 2
    total = pltpu.VMEM((pairs, PROMPT_DEV, HEAD), WIDE)
    return pl.pallas_call(
        functools.partial(back_owner_kernel, members, count),
        out_shape=[shape((rows, width), LOW)] * 3
        + [shape((count * own_early.shape[0], own_early.shape[1]), LOW)] * 2,
        in_specs=[smem] * 3 + [ANY] * 7 + [VMEM] * 6,
        out_specs=[VMEM] * 5,
        scratch_shapes=[
            pltpu.VMEM((heads, rows, HEAD), LOW),
            pltpu.VMEM((heads, rows, HEAD), LOW),
            pltpu.VMEM((heads, rows, HEAD), LOW),
            pltpu.VMEM((heads, rows, HEAD), WIDE),
            pltpu.VMEM((heads, rows, HEAD), WIDE),
            pltpu.VMEM((heads, rows, HEAD), LOW),
            pltpu.VMEM((rows, HEAD), WIDE),
            total,
            total,
            total,
            total,
            DMA((7, heads)),
        ]
        + [every] * (2 * heads)
        + [DMA((2, count - 1))] * 2
        + flow * 2,
        compiler_params=pltpu.CompilerParams(
            collective_id=7, has_side_effects=True, vmem_limit_bytes=VMEM_LIMIT
        ),
        name="back_owner",
    )(
        *readers,
        keys_all,
        values_all,
        query,
        key,
        value,
        attended,
        log_total,
        branch_low,
        w_out,
        cosine,
        sine,
        own_early,
        own_late,
    )


def middle_kernel(
    count,
    mixed,
    w_out,
    states,
    cotangent_in,
    w_gate_in,
    w_up_in,
    w_down_in,
    act,
    resid,
    own_early,
    out_low_out,
    ffn_late,
    d_act_out,
    hidden_out,
    d_gate_out,
    d_up_out,
    part,
    cotangent,
    out_low,
    d_hidden,
    w_gate,
    w_up,
    w_down,
    rows_in,
    ffn_total,
    d_total,
    ffn,
    hidden,
    d_gate,
    d_up,
    state_sem,
    cot_sem,
    weight_sem,
    out_sem,
    *refs,
):
    line = Line(count, refs[: Line.scratch_count])
    out_line = Line(count, refs[Line.scratch_count :])
    rows, size = resid.shape[0], line.rows
    fetch = pltpu.make_async_copy(
        states.at[pl.ds(pl.multiple_of(line.here * rows, rows), rows)], resid, state_sem
    )
    slots, step, _ = cotangent.shape

    def cot_load(index):
        return pltpu.make_async_copy(
            cotangent_in.at[pl.ds(index * step, step)],
            cotangent.at[index % slots],
            cot_sem.at[index % slots],
        )

    down_load, gate_load, up_load = [
        pltpu.make_async_copy(source, target, weight_sem.at[index])
        for index, (source, target) in enumerate(
            ((w_down_in, w_down), (w_gate_in, w_gate), (w_up_in, w_up))
        )
    ]
    fetch.start()
    for index in range(slots):
        cot_load(index).start()
    for load in (down_load, gate_load, up_load):
        load.start()
    hail(line.peers())
    tile = 512
    for start in range(0, part.shape[1], tile):
        columns = pl.ds(start, tile)
        part[:, columns] = dot(mixed[...], w_out[:, columns]).astype(LOW)
    heed(line.peers())
    fetch.wait()

    def finish(group):
        span = pl.ds(group * size, size)
        resid[span] += line.total[...]
        act[line.span(group, line.here)] = norm_rows(resid[span])[0].astype(LOW)

    leaving = []

    def leave(source, target):
        copy = pltpu.make_async_copy(source, target, out_sem.at[len(leaving)])
        copy.start()
        leaving.append(copy)

    def cast():
        steps = out_low.shape[0] // step
        for index in range(steps):
            cot_load(index).wait()
            out_low[pl.ds(index * step, step)] = cotangent[index % slots].astype(LOW)
            if index + slots < steps:
                cot_load(index + slots).start()
        leave(out_low, out_low_out)
        down_load.wait()

    def inner(start):
        span = pl.ds(start, tile)
        d_hidden[:, span] = dot(out_low[...], w_down[span], 1, 1).astype(LOW)

    units, block = d_hidden.shape[1], 512
    starts = list(range(0, units, tile))

    def inners(some):
        def run():
            for start in some:
                inner(start)

        return run

    def begin(group):
        if not group:
            gate_load.wait()
            up_load.wait()
        for chunk in range(count):
            rows_in[pl.ds(chunk * size, size)] = act[line.span(group, chunk)]
        ffn_total[...] = jnp.zeros_like(ffn_total)
        d_total[...] = jnp.zeros_like(d_total)

    def feed(group, first, last):
        @pl.loop(first, last)
        def _(index):
            columns = pl.ds(pl.multiple_of(index * block, block), block)
            gate = dot(rows_in[...], w_gate[:, columns])
            up = dot(rows_in[...], w_up[:, columns])
            sigmoid = jax.nn.sigmoid(gate)
            swish = gate * sigmoid
            d_inner = jnp.concatenate(
                [d_hidden[line.span(group, chunk), columns] for chunk in range(count)]
            ).astype(WIDE)
            new_hidden = (swish * up).astype(LOW)
            new_gate = (d_inner * up * sigmoid * (1.0 + gate * (1.0 - sigmoid))).astype(LOW)
            new_up = (d_inner * swish).astype(LOW)
            for chunk in range(count):
                own = slice(chunk * size, chunk * size + size)
                hidden[chunk, group, :, columns] = new_hidden[own]
                d_gate[chunk, group, :, columns] = new_gate[own]
                d_up[chunk, group, :, columns] = new_up[own]
            for start in range(0, part.shape[1], tile):
                out = pl.ds(start, tile)
                ffn_total[:, out] += dot(new_hidden, w_down[columns, out])
                d_total[:, out] += dot(new_gate, w_gate[out, columns], 1, 1) + dot(
                    new_up, w_up[out, columns], 1, 1
                )

    def end(group):
        own = pl.ds(pl.multiple_of(line.here * size, size), size)
        ffn_total[own] += resid[pl.ds(group * size, size)]
        ffn[group] = ffn_total[...].astype(LOW)
        if group:
            leave(ffn.at[group], ffn_late)
        for chunk in range(count):
            span = line.span(group, chunk)
            part[span] = d_total[pl.ds(chunk * size, size)].astype(LOW)
            leave(part.at[span], d_act_out.at[span])
        for source, target in (
            (hidden, hidden_out),
            (d_gate, d_gate_out),
            (d_up, d_up_out),
        ):
            leave(source.at[:, group], target.at[:, group])

    blocks = units // block
    third = -(-blocks // 3)

    def opening():
        begin(0)
        feed(0, 0, third)

    def closing():
        feed(0, 2 * third, blocks)
        end(0)

    line.reduce(
        part,
        act,
        finish,
        [
            cast,
            inners(starts[:1]),
            inners(starts[1:2]),
            inners(starts[2:]),
            opening,
            lambda: feed(0, third, 2 * third),
            closing,
        ],
    )
    early = ffn.at[0]
    out_line.scatter_slot(0, 0, early)
    begin(1)
    feed(1, 0, third)
    out_line.scatter_slot(0, 1, early)
    feed(1, third, 2 * third)
    for slot in range(2, count - 1):
        out_line.scatter_slot(0, slot, early)
    feed(1, 2 * third, blocks)
    end(1)
    out_line.scatter_end(0, early)
    own_early[...] = out_line.total[...].astype(LOW)
    for copy in leaving:
        copy.wait()
    line.sent(act)
    out_line.sent()


def middle(count, mixed, w_out, states, cotangent, w_gate, w_up, w_down):
    rows, depth = states.shape
    units = w_down.shape[0]
    size = rows // count // GROUPS
    split = (count, GROUPS, size)
    inside = (*split, units)
    some = (GROUPS, rows // GROUPS, depth)
    outs = pl.pallas_call(
        functools.partial(middle_kernel, count),
        out_shape=[
            shape((rows, depth), LOW),
            shape((rows // count, depth), WIDE),
            shape((size, depth), LOW),
            shape((rows, depth), LOW),
            shape(some[1:], LOW),
            shape((rows, depth), LOW),
            shape(inside, LOW),
            shape(inside, LOW),
            shape(inside, LOW),
        ],
        in_specs=[VMEM] * 2 + [ANY] * 5,
        out_specs=[VMEM] * 3 + [ANY] * 6,
        scratch_shapes=[
            pltpu.VMEM((rows, depth), LOW),
            pltpu.VMEM((2, 64, depth), WIDE),
            pltpu.VMEM((rows, depth), LOW),
            pltpu.VMEM((rows, units), LOW),
            pltpu.VMEM((depth, units), LOW),
            pltpu.VMEM((depth, units), LOW),
            pltpu.VMEM((units, depth), LOW),
            pltpu.VMEM(some[1:], LOW),
            pltpu.VMEM(some[1:], WIDE),
            pltpu.VMEM(some[1:], WIDE),
            pltpu.VMEM(some, LOW),
            pltpu.VMEM(inside, LOW),
            pltpu.VMEM(inside, LOW),
            pltpu.VMEM(inside, LOW),
            DMA,
            DMA((2,)),
            DMA((3,)),
            DMA(((4 + count) * GROUPS,)),
        ]
        + Line.scratch(count, GROUPS, rows // count, depth)
        + Line.scratch(count, 1, size, depth),
        compiler_params=pltpu.CompilerParams(
            collective_id=2, has_side_effects=True, vmem_limit_bytes=VMEM_LIMIT
        ),
        name="middle",
    )(mixed, w_out, states, cotangent, w_gate, w_up, w_down)
    return [*outs[:6], *(out.reshape(rows, -1) for out in outs[6:])]


def second_kernel(
    count,
    pairs,
    d_act_in,
    ffn_in,
    resid_in,
    cotangent,
    act,
    d_gate,
    d_up,
    branch_low,
    grad_resid,
    own_out,
    grad_gate,
    grad_up,
    d_act,
    ffn,
    resid,
    cot_sem,
    load_sem,
    *refs,
):
    take = taker(refs)
    line = Line(count, take(Line.scratch_count))
    out_line = Line(count, take(Line.scratch_count))
    lhs = Lhs(act, take(4))
    rights = [Rhs([source], take(4)) for source in (d_gate, d_up)]
    order = bits_of(pairs)
    flows = [
        Halving(pairs, way, product_of(lhs, right), take(4), *take(1))
        for way, right in zip((order, order[::-1]), rights)
    ]
    rows = resid.shape[0]
    fetch = pltpu.make_async_copy(
        cotangent.at[pl.ds(pl.multiple_of(line.here * rows, rows), rows)], grad_resid, cot_sem
    )
    peers = line.peers() + member_peers(2 * pairs)
    hail(peers)
    loads = [
        pltpu.make_async_copy(source, target, load_sem.at[index])
        for index, (source, target) in enumerate(
            ((d_act_in, d_act), (ffn_in, ffn), (resid_in, resid))
        )
    ]
    fetch.start()
    for load in loads:
        load.start()
    heed(peers)
    lhs.start()
    for piece in range(flows[0].pieces):
        for right in rights:
            right.start(piece)
    fetch.wait()
    for load in loads:
        load.wait()

    def finish(group):
        span = pl.ds(group * line.rows, line.rows)
        normed, inverse = norm_rows(resid[span])
        grad_resid[span] += norm_back(line.total[...], normed, inverse)
        branch_low[line.span(group, line.here)] = grad_resid[span].astype(LOW)

    sides = [(lhs, right, flow) for right, flow in zip(rights, flows)]
    ahead, early, others, settle, late = beside(order, sides)

    def out_slot(slot):
        return lambda: out_line.scatter_slot(0, slot, ffn)

    slots = [out_slot(slot) for slot in range(count - 1)]

    def fourth():
        settle()
        slots[0]()

    line.reduce(d_act, branch_low, finish, [ahead, early, others, fourth, late] + slots[1:])
    out_line.scatter_end(0, ffn)
    own_out[...] = out_line.total[...].astype(LOW)
    flows[0].end(grad_gate)
    flows[1].end(grad_up)
    for flow in flows:
        flow.sent()
    for move in [lhs] + rights:
        move.sent()
    line.sent(branch_low)
    out_line.sent()


def beside(order, sides):
    masks = [flow.steps(0) for _, _, flow in sides]

    def ahead():
        for (lhs, rhs, flow), (mask, *_) in zip(sides[:2], masks):
            lhs.ready()
            rhs.ready(0)
            flow.push_piece(mask, 0)

    def early():
        for at, ((lhs, rhs, flow), (mask, *_)) in enumerate(zip(sides, masks)):
            if at > 1:
                lhs.ready()
            for piece in range(0 if at > 1 else 1, flow.pieces):
                rhs.ready(piece)
                flow.push_piece(mask, piece)

    def others():
        for index in range(1, len(masks[0])):
            for (_, _, flow), steps in zip(sides, masks):
                flow.push(steps[index])

    def settle():
        for _, _, flow in sides:
            flow.settle()

    def late():
        for stage in range(1, len(order)):
            for index in range(len(sides[0][2].steps(stage))):
                for _, _, flow in sides:
                    flow.push(flow.steps(stage)[index])

    return [ahead, early, others, settle, late]


def second(count, members, d_act, ffn, resid, cotangent, act, d_gate, d_up):
    rows, depth = cotangent.shape
    units = d_gate.shape[1]
    pairs = members // 2
    block = depth // members
    return pl.pallas_call(
        functools.partial(second_kernel, count, pairs),
        out_shape=[
            shape((rows, depth), LOW),
            shape((rows // count, depth), WIDE),
            shape((ffn.shape[0] // count, depth), LOW),
            shape((block, units), LOW),
            shape((block, units), LOW),
        ],
        in_specs=[ANY] * 7,
        out_specs=[VMEM] * 5,
        scratch_shapes=[
            pltpu.VMEM(d_act.shape, LOW),
            pltpu.VMEM(ffn.shape, LOW),
            pltpu.VMEM(resid.shape, WIDE),
            DMA,
            DMA((3,)),
        ]
        + Line.scratch(count, GROUPS, rows // count, depth)
        + Line.scratch(count, 1, ffn.shape[0] // count, depth)
        + Lhs.scratch(pairs, rows, block)
        + Rhs.scratch(rows, units) * 2
        + (Halving.scratch(pairs, block, units) + [pltpu.VMEM((block, units), WIDE)]) * 2,
        compiler_params=pltpu.CompilerParams(
            collective_id=3, has_side_effects=True, vmem_limit_bytes=VMEM_LIMIT
        ),
        name="second",
    )(d_act, ffn, resid, cotangent, in_blocks(act, members), d_gate, d_up)


def owner_kernel(
    pairs,
    d_keys_all,
    d_values_all,
    d_key_own,
    d_value_own,
    cosine,
    sine,
    d_key,
    d_value,
    *refs,
):
    take = taker(refs)
    parity = lax.rem(lax.axis_index("dp"), 2)
    order = bits_of(pairs)
    width = d_key.shape[1]
    moves, flows = [], []
    for way, source in zip((order, order[::-1]), (d_keys_all, d_values_all)):
        mine, theirs = take(2)
        moves.append(
            Pairwise(
                [
                    (
                        source.at[2 * pair + parity],
                        mine.at[pair],
                        source.at[2 * pair + 1 - parity],
                        theirs.at[pair],
                    )
                    for pair in range(pairs)
                ],
                take(3),
            )
        )

        def own(mask, target, columns, mine=mine, theirs=theirs):
            return mine[target, :, columns].astype(WIDE) + theirs[target, :, columns].astype(WIDE)

        flows.append(Halving(pairs, way, own, take(4)))
    (total,) = take(1)
    greet(member_peers(2 * pairs))
    for move in moves:
        move.start()
    for move, flow in zip(moves, flows):
        move.ready()
        flow.push(flow.masks[0])
    late = pl.ds(PROMPT_DEV, d_key.shape[0] - PROMPT_DEV)
    d_key[late] = d_key_own[...]
    d_value[late] = d_value_own[...]
    for index in range(1, pairs - 1):
        for flow in flows:
            flow.push(flow.masks[index])
    early = pl.ds(0, PROMPT_DEV)
    flows[0].end(total)
    for start in range(0, width, HEAD):
        d_key[early, start : start + HEAD] = rotate(
            total[:, start : start + HEAD], cosine[early], -sine[early]
        ).astype(LOW)
    flows[1].end(d_value.at[early])
    for move, flow in zip(moves, flows):
        flow.sent()
        move.sent()


def owner(members, d_keys_all, d_values_all, d_key_own, d_value_own, cosine, sine):
    width = d_key_own.shape[1]
    rows = cosine.shape[0]
    pairs = members // 2
    flow = (
        [pltpu.VMEM((pairs, PROMPT_DEV, width), LOW)] * 2
        + Pairwise.sems(pairs)
        + Halving.scratch(pairs, PROMPT_DEV, width)
    )
    return pl.pallas_call(
        functools.partial(owner_kernel, pairs),
        out_shape=[shape((rows, width), LOW)] * 2,
        in_specs=[ANY, ANY] + [VMEM] * 4,
        out_specs=[VMEM] * 2,
        scratch_shapes=flow * 2 + [pltpu.VMEM((PROMPT_DEV, width), WIDE)],
        compiler_params=pltpu.CompilerParams(
            collective_id=4, has_side_effects=True, vmem_limit_bytes=VMEM_LIMIT
        ),
        name="owner",
    )(d_keys_all, d_values_all, d_key_own, d_value_own, cosine, sine)


def first_kernel(
    count,
    pairs,
    grad_resid,
    d_query,
    d_key,
    d_value,
    w_query,
    w_key,
    w_value,
    states,
    act,
    mixed,
    branch_low,
    hidden,
    out_low,
    far_query,
    far_key,
    far_value,
    input_grad,
    grad_down,
    grad_out,
    grad_query,
    grad_key,
    grad_value,
    inner_total,
    part,
    state,
    weight,
    state_sem,
    weight_sem,
    *refs,
):
    take = taker(refs)
    line = Line(count, take(Line.scratch_count))
    order = bits_of(pairs)
    sides = []
    for left, rights, way in (
        (out_low, (hidden,), order),
        (act, (far_query, far_key, far_value), order[::-1]),
        (branch_low, (mixed,), order[::-1]),
    ):
        lhs, rhs = Lhs(left, take(4)), Rhs(rights, take(4))
        sides.append((lhs, rhs, Halving(pairs, way, product_of(lhs, rhs), take(4), *take(1))))
    rows = state.shape[0]
    fetch = pltpu.make_async_copy(
        states.at[pl.ds(pl.multiple_of(line.here * rows, rows), rows)], state, state_sem
    )
    loads = [
        pltpu.make_async_copy(source, weight.at[index], weight_sem.at[index])
        for index, source in enumerate((w_query, w_key, w_value))
    ]
    for load in loads:
        load.start()
    fetch.start()
    greet(line.peers() + member_peers(2 * pairs))
    for lhs, rhs, _ in sides[:2]:
        lhs.start()
        rhs.start(0)
    for at, (lhs, rhs, flow) in enumerate(sides):
        if at > 1:
            lhs.start()
        for piece in range(0 if at > 1 else 1, flow.pieces):
            rhs.start(piece)
    for load in loads:
        load.wait()
    tile = 512
    for start in range(0, part.shape[1], tile):
        columns = pl.ds(start, tile)
        part[:, columns] = (
            dot(d_query[...], weight[0, columns], 1, 1)
            + dot(d_key[...], weight[1, columns], 1, 1)
            + dot(d_value[...], weight[2, columns], 1, 1)
        )
    fetch.wait()

    def finish(group):
        span = pl.ds(group * line.rows, line.rows)
        normed, inverse = norm_rows(state[span])
        input_grad[line.span(group, line.here)] = (
            grad_resid[span] + norm_back(line.total[...], normed, inverse)
        ).astype(LOW)

    line.reduce(part, input_grad, finish, beside(order, sides))
    for (_, _, flow), target in zip(sides, (grad_down, inner_total, grad_out)):
        flow.end(target)
    width = grad_query.shape[1]
    for index, target in enumerate((grad_query, grad_key, grad_value)):
        target[...] = inner_total[:, index * width : index * width + width]
    for lhs, rhs, flow in sides:
        flow.sent()
        lhs.sent()
        rhs.sent()
    line.sent(input_grad)


def first(
    count,
    members,
    grad_resid,
    weights,
    states,
    act,
    mixed,
    branch_low,
    hidden,
    out_low,
    d_query,
    d_key,
    d_value,
):
    rows, depth = states.shape
    width = d_query.shape[1]
    units = hidden.shape[1]
    pairs = members // 2
    block = depth // members
    scratch = []
    for wide in (units, 3 * width, width):
        scratch += Lhs.scratch(pairs, rows, block) + Rhs.scratch(rows, wide)
        scratch += Halving.scratch(pairs, block, wide) + [pltpu.VMEM((block, wide), WIDE)]
    return pl.pallas_call(
        functools.partial(first_kernel, count, pairs),
        out_shape=[
            shape((rows, depth), LOW),
            shape((block, units), LOW),
        ]
        + [shape((block, width), LOW)] * 4,
        in_specs=[VMEM] * 4 + [ANY] * 12,
        out_specs=[VMEM] * 6,
        scratch_shapes=[
            pltpu.VMEM((block, 3 * width), LOW),
            pltpu.VMEM((rows, depth), WIDE),
            pltpu.VMEM((rows // count, depth), WIDE),
            pltpu.VMEM((3, depth, width), LOW),
            DMA,
            DMA((3,)),
        ]
        + Line.scratch(count, GROUPS, rows // count, depth)
        + scratch,
        compiler_params=pltpu.CompilerParams(
            collective_id=5, has_side_effects=True, vmem_limit_bytes=VMEM_LIMIT
        ),
        name="first",
    )(
        grad_resid,
        d_query,
        d_key,
        d_value,
        *weights,
        states,
        in_blocks(act, members),
        mixed,
        in_blocks(branch_low, members),
        hidden,
        in_blocks(out_low, members),
        d_query,
        d_key,
        d_value,
    )


def widen_kernel(flat, early, late, *refs):
    count = len(refs) // 2
    sources, whole, targets = refs[:count], refs[count], refs[count + 1 :]
    half = early.shape[0]
    whole[pl.ds(0, half)] = early[...].astype(WIDE)
    whole[pl.ds(half, half)] = late[...].astype(WIDE)
    for index, (source, target) in enumerate(zip(sources, targets)):
        values = source[...].astype(WIDE)
        target[...] = values if index < flat else values.T


def widen(count, early, late, plain, turned):
    def rows(array):
        return pl.BlockSpec((array.shape[0] // count, array.shape[1]), lambda i: (i, 0))

    def columns(array):
        return pl.BlockSpec((array.shape[0], array.shape[1] // count), lambda i: (0, i))

    flipped = [shape(array.shape[::-1], WIDE) for array in turned]
    whole = shape((2 * early.shape[0], early.shape[1]), WIDE)
    return pl.pallas_call(
        functools.partial(widen_kernel, len(plain)),
        out_shape=[whole] + [shape(array.shape, WIDE) for array in plain] + flipped,
        grid=(count,),
        in_specs=[rows(array) for array in (early, late, *plain)]
        + [columns(array) for array in turned],
        out_specs=[rows(array) for array in (whole, *plain, *flipped)],
        compiler_params=pltpu.CompilerParams(vmem_limit_bytes=VMEM_LIMIT),
        name="widen",
    )(early, late, *plain, *turned)


def body(
    states,
    w_query,
    w_key,
    w_value,
    w_out,
    w_gate,
    w_up,
    w_down,
    group_id,
    slice_start,
    cont_group,
    cotangent,
):
    rows = states.shape[0]
    members = lax.axis_size("dp")
    count = lax.axis_size("tensor")
    frequency = 10000.0 ** (-np.arange(HEAD // 2) * 2.0 / HEAD)
    frequency = np.concatenate([frequency, frequency]).astype(np.float32)
    sign = np.repeat([-1.0, 1.0], HEAD // 2).astype(np.float32)
    readers = (group_id, slice_start, cont_group)
    merged = members * PROMPT_DEV * w_query.shape[1] * 2 * 4 <= 16 * 2**20
    if merged:
        table = jnp.stack([frequency, sign])
        act_one, query, key, value, cosine, sine, mixed, attended, log_total, *everyones = (
            gather_attend(members, readers, w_query, w_key, w_value, states, table)
        )
    else:
        index = jnp.arange(rows, dtype=jnp.int32)
        everyone = jnp.arange(members, dtype=jnp.int32)
        own_start = jnp.sum(jnp.where(everyone == lax.axis_index("dp"), slice_start, 0))
        prompt = members // 2 * PROMPT_DEV
        positions = jnp.where(index < PROMPT_DEV, own_start + index, prompt + index - PROMPT_DEV)
        angles = positions.astype(WIDE)[:, None] * frequency[None, :]
        cosine = jnp.cos(angles)
        sine = jnp.sin(angles) * sign[None, :]
        act_one, query, key, value, *everyones = project(
            members, states, w_query, w_key, w_value, cosine, sine
        )
        mixed, attended, log_total = attend(readers, query, key, value, *everyones)
    act_two, resid, own_early, out_low, ffn_late, d_act_two, hidden, d_gate, d_up = middle(
        count, mixed, w_out, states, cotangent, w_gate, w_up, w_down
    )
    branch_low, grad_resid, own_late, grad_gate, grad_up = second(
        count, members, d_act_two, ffn_late, resid, cotangent, act_two, d_gate, d_up
    )
    kept = (query, key, value, branch_low, w_out, attended, log_total, cosine, sine)
    if merged:
        d_query, d_key, d_value, early_out, late_out = back_owner(
            members, count, readers, *everyones, *kept, own_early, own_late
        )
    else:
        d_query, *d_everyones = attend_back(
            readers, query, key, value, *everyones, branch_low, w_out, attended, log_total, cosine, sine
        )
        d_key, d_value = owner(members, *d_everyones, cosine, sine)
        early_out, late_out = [
            lax.all_gather(own, "tensor", axis=0, tiled=True) for own in (own_early, own_late)
        ]
    input_grad, grad_down, grad_out, *grad_inner = first(
        count,
        members,
        grad_resid,
        (w_query, w_key, w_value),
        states,
        act_one,
        mixed,
        branch_low,
        hidden,
        out_low,
        d_query,
        d_key,
        d_value,
    )
    *plain, grad_out, grad_down = widen(
        count,
        early_out,
        late_out,
        (input_grad, *grad_inner, grad_gate, grad_up),
        (grad_out, grad_down),
    )
    return (*plain[:5], grad_out, *plain[5:], grad_down)


def solution(mesh):
    placed = (
        P("dp", None),
        P(None, "tensor"),
        P(None, "tensor"),
        P(None, "tensor"),
        P("tensor", None),
        P(None, "tensor"),
        P(None, "tensor"),
        P("tensor", None),
        P(),
        P(),
        P("dp"),
        P("dp", None),
    )
    return jax.shard_map(
        body,
        mesh=mesh,
        in_specs=placed,
        out_specs=(
            P("dp", None),
            P("dp", None),
            P("dp", "tensor"),
            P("dp", "tensor"),
            P("dp", "tensor"),
            P("tensor", "dp"),
            P("dp", "tensor"),
            P("dp", "tensor"),
            P("tensor", "dp"),
        ),
        check_vma=False,
    )
```

```python
import functools

import jax
import jax.numpy as jnp
import numpy as np
from jax import lax
from jax.experimental import pallas as pl
from jax.experimental.pallas import tpu as pltpu
from jax.sharding import PartitionSpec as P

HEAD = 128
PROMPT_DEV = 384
EPSILON = 1e-05
NEGATIVE = -1e30
SCALE = HEAD ** (-0.5)
SCALE_TWO = float(SCALE * np.log2(np.e))
LOW = jnp.bfloat16
WIDE = jnp.float32
MESH = pl.DeviceIdType.MESH
ANY = pl.BlockSpec(memory_space=pl.ANY)
VMEM = pl.BlockSpec(memory_space=pltpu.VMEM)
DMA = pltpu.SemaphoreType.DMA
VMEM_LIMIT = 63 * 2**20
GROUPS = 2
PIECE = 512


def dot(left, right, left_dim=1, right_dim=0):
    return lax.dot_general(
        left, right, (((left_dim,), (right_dim,)), ((), ())), preferred_element_type=WIDE
    )


def shape(dims, dtype):
    return jax.ShapeDtypeStruct(dims, dtype)


def norm_rows(values):
    row_mean = jnp.mean(values, axis=-1, keepdims=True)
    centred = values - row_mean
    inverse = lax.rsqrt(jnp.mean(centred * centred, axis=-1, keepdims=True) + EPSILON)
    return centred * inverse, inverse


def norm_back(gradient, normed, inverse):
    return inverse * (
        gradient
        - jnp.mean(gradient, axis=-1, keepdims=True)
        - normed * jnp.mean(gradient * normed, axis=-1, keepdims=True)
    )


def rotate(values, cosine, sine):
    return values * cosine + pltpu.roll(values, HEAD // 2, 1) * sine


def flip(index, mask):
    out, bit = index, 1
    while bit <= mask:
        if mask & bit:
            out = out + bit * (1 - 2 * lax.rem(lax.div(index, bit), 2))
        bit *= 2
    return out


def bits_of(count):
    return list(range(count.bit_length() - 1))


def hail(peers):
    barrier = pltpu.get_barrier_semaphore()
    for peer in peers:
        pl.semaphore_signal(barrier, inc=1, device_id=peer, device_id_type=MESH)


def heed(peers):
    pl.semaphore_wait(pltpu.get_barrier_semaphore(), len(peers))


def greet(peers):
    hail(peers)
    heed(peers)


def remote(source, target, send_sem, recv_sem, device):
    return pltpu.make_async_remote_copy(
        src_ref=source,
        dst_ref=target,
        send_sem=send_sem,
        recv_sem=recv_sem,
        device_id=device,
        device_id_type=MESH,
    )


class Line:
    scratch_count = 10

    @staticmethod
    def scratch(count, groups, rows, width):
        rows = rows // groups
        return [
            pltpu.VMEM((rows, width), WIDE),
            pltpu.VMEM((groups, count, rows, width), LOW),
            pltpu.VMEM((groups, count, rows, width), LOW),
            pltpu.VMEM((groups, count, rows, width), LOW),
            DMA((groups, count)),
            DMA((groups, count)),
            DMA((groups, count)),
            DMA((groups, count)),
            DMA((groups, count)),
            DMA((groups, count)),
        ]

    def __init__(self, count, refs):
        self.count = count
        (
            self.total,
            self.outgoing,
            self.from_left,
            self.from_right,
            self.out_sem,
            self.left_sem,
            self.right_sem,
            self.to_right_sem,
            self.to_left_sem,
            self.got_sem,
        ) = refs
        self.groups = self.outgoing.shape[0]
        self.rows = self.total.shape[0]
        self.here = lax.axis_index("tensor")
        member = lax.axis_index("dp")
        self.right = (member, lax.rem(self.here + 1, count))
        self.left = (member, lax.rem(self.here + count - 1, count))

    def peers(self):
        return [self.left, self.right]

    def span(self, group, chunk):
        start = chunk * (self.rows * self.groups) + group * self.rows
        return pl.ds(pl.multiple_of(start, self.rows), self.rows)

    def rightward(self, group, chunk):
        return remote(
            self.outgoing.at[group, chunk],
            self.from_left.at[group, chunk],
            self.out_sem.at[group, chunk],
            self.left_sem.at[group, chunk],
            self.right,
        )

    def leftward(self, group, chunk):
        return remote(
            self.outgoing.at[group, chunk],
            self.from_right.at[group, chunk],
            self.out_sem.at[group, chunk],
            self.right_sem.at[group, chunk],
            self.left,
        )

    def add_and_pass(self, group, chunk, part, right, wait):
        copy, came = (self.rightward, self.from_left) if right else (self.leftward, self.from_right)
        total = part[self.span(group, chunk)].astype(WIDE)
        if wait:
            copy(group, chunk).wait_recv()
            total += came[group, chunk].astype(WIDE)
        self.outgoing[group, chunk] = total.astype(LOW)
        copy(group, chunk).start()

    def scatter_slot(self, group, slot, part):
        here, count = self.here, self.count
        ahead, back = count - 1 + here - slot, slot - (count - 1 - here)
        if slot == 0:

            @pl.when(here == 0)
            def _():
                self.add_and_pass(group, ahead, part, True, False)

            @pl.when(here == count - 1)
            def _():
                self.add_and_pass(group, back, part, False, False)

            return
        for wait in (False, True):

            @pl.when((here <= slot) & ((here > 0) if wait else (here == 0)))
            def _(wait=wait):
                self.add_and_pass(group, ahead, part, True, wait)

            @pl.when(
                (count - 1 - here <= slot) & ((here < count - 1) if wait else (here == count - 1))
            )
            def _(wait=wait):
                self.add_and_pass(group, back, part, False, wait)

    def scatter_end(self, group, part):
        here = self.here
        last = self.count - 1

        def left():
            self.rightward(group, here).wait_recv()
            return self.from_left[group, here].astype(WIDE)

        def right():
            self.leftward(group, here).wait_recv()
            return self.from_right[group, here].astype(WIDE)

        @pl.when(here == 0)
        def _():
            self.total[...] = part[self.span(group, here)].astype(WIDE) + right()

        @pl.when(here == last)
        def _():
            self.total[...] = part[self.span(group, here)].astype(WIDE) + left()

        @pl.when((here > 0) & (here < last))
        def _():
            self.total[...] = part[self.span(group, here)].astype(WIDE) + left() + right()

    def passing(self, whole, group, chunk, right):
        ref = whole.at[self.span(group, chunk)]
        return remote(
            ref,
            ref,
            (self.to_right_sem if right else self.to_left_sem).at[group, chunk],
            self.got_sem.at[group, chunk],
            self.right if right else self.left,
        )

    def gather_slot(self, whole, group, distance):
        here, count = self.here, self.count

        @pl.when(here - distance >= 0)
        def _():
            if distance:
                self.passing(whole, group, here - distance, True).wait_recv()

            @pl.when(here < count - 1)
            def _():
                self.passing(whole, group, here - distance, True).start()

        @pl.when(here + distance <= count - 1)
        def _():
            if distance:
                self.passing(whole, group, here + distance, False).wait_recv()

            @pl.when(here > 0)
            def _():
                self.passing(whole, group, here + distance, False).start()

    def reduce(self, part, whole, finish, beside=()):
        beside = list(beside)
        last = self.count - 1
        self.scatter_slot(0, 0, part)
        for group in range(self.groups):
            for slot in range(1, last):
                if beside:
                    beside.pop(0)()
                self.scatter_slot(group, slot, part)
                if group:
                    self.gather_slot(whole, group - 1, slot)
            if group + 1 < self.groups:
                self.scatter_slot(group + 1, 0, part)
            if group:
                self.gather_slot(whole, group - 1, last)
            self.scatter_end(group, part)
            finish(group)
            self.gather_slot(whole, group, 0)
        for distance in range(1, self.count):
            if beside:
                beside.pop(0)()
            self.gather_slot(whole, self.groups - 1, distance)
        for act in beside:
            act()

    def sent(self, whole=None):
        here, count = self.here, self.count
        for group in range(self.groups):
            for chunk in range(count):

                @pl.when(here != chunk)
                def _(group=group, chunk=chunk):
                    self.rightward(group, chunk).wait_send()

                if whole is None:
                    continue

                @pl.when((chunk <= here) & (here < count - 1))
                def _(group=group, chunk=chunk):
                    self.passing(whole, group, chunk, True).wait_send()

                @pl.when((chunk >= here) & (here > 0))
                def _(group=group, chunk=chunk):
                    self.passing(whole, group, chunk, False).wait_send()


class Halving:
    @staticmethod
    def masks_of(pairs, order):
        def stage(mask):
            return min(order.index(bit) for bit in order if mask >> bit & 1)

        return sorted(range(1, pairs), key=lambda mask: (stage(mask), -mask.bit_count()))

    @staticmethod
    def scratch(pairs, block, width):
        count = pairs - 1
        pieces = max(1, width // PIECE)
        return [
            pltpu.VMEM((count, block, width), LOW),
            pltpu.VMEM((count, block, width), LOW),
            DMA((count, pieces)),
            DMA((count, pieces)),
        ]

    def __init__(self, pairs, order, own, refs, kept=None):
        self.order, self.own, self.kept = order, own, kept
        self.send, self.recv, self.send_sem, self.recv_sem = refs
        self.masks = Halving.masks_of(pairs, order)
        self.pieces = self.send_sem.shape[1]
        self.piece = self.send.shape[2] // self.pieces
        self.member = lax.axis_index("dp")
        self.tensor = lax.axis_index("tensor")
        self.high = lax.div(self.member, 2)

    def stage(self, mask):
        return min(
            [self.order.index(bit) for bit in self.order if mask >> bit & 1],
            default=len(self.order),
        )

    def steps(self, stage):
        return [mask for mask in self.masks if self.stage(mask) == stage]

    def columns(self, piece):
        return pl.ds(piece * self.piece, self.piece)

    def copy(self, mask, piece):
        index = self.masks.index(mask)
        bit = 1 << self.order[self.stage(mask)]
        return remote(
            self.send.at[index, :, self.columns(piece)],
            self.recv.at[index, :, self.columns(piece)],
            self.send_sem.at[index, piece],
            self.recv_sem.at[index, piece],
            (flip(self.member, bit * 2), self.tensor),
        )

    def settle(self):
        for piece in range(self.pieces):
            columns = self.columns(piece)
            self.kept[:, columns] = self.own(0, flip(self.high, 0), columns)

    def fill(self, mask, piece, out):
        columns = self.columns(piece)
        if self.kept is not None and not mask:
            total = self.kept[:, columns]
        else:
            total = self.own(mask, flip(self.high, mask), columns)
        for bit in self.order[: self.stage(mask)]:
            slot = mask | 1 << bit
            self.copy(slot, piece).wait_recv()
            total += self.recv[self.masks.index(slot), :, columns].astype(WIDE)
        out[:, columns] = total.astype(out.dtype)

    def push_piece(self, mask, piece):
        self.fill(mask, piece, self.send.at[self.masks.index(mask)])
        self.copy(mask, piece).start()

    def push(self, mask):
        for piece in range(self.pieces):
            self.push_piece(mask, piece)

    def end(self, out):
        for piece in range(self.pieces):
            self.fill(0, piece, out)

    def sent(self):
        for mask in self.masks:
            for piece in range(self.pieces):
                self.copy(mask, piece).wait_send()


class Pairwise:
    def __init__(self, moves, refs):
        self.moves, self.done = moves, False
        self.local_sem, self.send_sem, self.recv_sem = refs
        member = lax.axis_index("dp")
        self.partner = (flip(member, 1), lax.axis_index("tensor"))

    @staticmethod
    def sems(count):
        return [DMA((count,)), DMA((count,)), DMA((count,))]

    def local(self, index):
        source, target, _, _ = self.moves[index]
        return pltpu.make_async_copy(source, target, self.local_sem.at[index])

    def across(self, index):
        _, _, source, target = self.moves[index]
        return remote(
            source, target, self.send_sem.at[index], self.recv_sem.at[index], self.partner
        )

    def start(self, index=None):
        for index in range(len(self.moves)) if index is None else [index]:
            self.across(index).start()
            self.local(index).start()

    def ready(self, index=None):
        if index is None and self.done:
            return
        self.done = index is None
        for index in range(len(self.moves)) if index is None else [index]:
            self.local(index).wait()
            self.across(index).wait_recv()

    def sent(self):
        for index in range(len(self.moves)):
            self.across(index).wait_send()


class Lhs(Pairwise):
    @staticmethod
    def scratch(pairs, rows, block):
        return [pltpu.VMEM((pairs, 2 * rows, block), LOW)] + Pairwise.sems(pairs)

    def __init__(self, source, refs):
        self.held = refs[0]
        pairs, rows, block = self.held.shape
        rows = rows // 2
        parity = lax.rem(lax.axis_index("dp"), 2)

        def columns(index):
            if len(source.shape) == 3:
                return source.at[index]
            return source.at[:, pl.ds(pl.multiple_of(index * block, block), block)]

        super().__init__(
            [
                (
                    columns(2 * pair + parity),
                    self.held.at[pair, pl.ds(0, rows)],
                    columns(2 * pair + 1 - parity),
                    self.held.at[pair, pl.ds(rows, rows)],
                )
                for pair in range(pairs)
            ],
            refs[1:],
        )


class Rhs(Pairwise):
    @staticmethod
    def scratch(rows, width):
        return [pltpu.VMEM((2 * rows, width), LOW)] + Pairwise.sems(width // PIECE)

    def __init__(self, sources, refs):
        self.held = refs[0]
        rows = self.held.shape[0] // 2
        moves, at = [], 0
        for source in sources:
            for start in range(0, source.shape[1], PIECE):
                columns = pl.ds(at, PIECE)
                at += PIECE
                here = source.at[:, pl.ds(start, PIECE)]
                moves.append(
                    (
                        here,
                        self.held.at[pl.ds(0, rows), columns],
                        here,
                        self.held.at[pl.ds(rows, rows), columns],
                    )
                )
        super().__init__(moves, refs[1:])


def product_of(lhs, rhs):
    def own(mask, target, columns):
        return dot(lhs.held[target], rhs.held[:, columns], 0, 0)

    return own


def taker(refs):
    refs = list(refs)

    def take(count):
        out = refs[:count]
        del refs[:count]
        return out

    return take


def in_blocks(left, members):
    block = left.shape[1] // members
    if block % 128 == 0:
        return left
    return left.reshape(left.shape[0], members, block).transpose(1, 0, 2)


def member_peers(members):
    member, tensor = lax.axis_index("dp"), lax.axis_index("tensor")
    return [(flip(member, 1 << bit), tensor) for bit in bits_of(members)]


def project_kernel(
    members,
    states,
    w_query,
    w_key,
    w_value,
    cosine,
    sine,
    act,
    query,
    key,
    value,
    keys_all,
    values_all,
    send_sem,
    recv_sem,
    local_sem,
):
    member, tensor = lax.axis_index("dp"), lax.axis_index("tensor")
    width = query.shape[1]
    greet(member_peers(members))
    rows = 64
    for start in range(0, states.shape[0], rows):
        span = pl.ds(start, rows)
        act[span] = norm_rows(states[span])[0].astype(LOW)

    def turned(weight, out):
        linear = dot(act[...], weight[...])
        for start in range(0, width, HEAD):
            out[:, start : start + HEAD] = rotate(
                linear[:, start : start + HEAD], cosine[...], sine[...]
            ).astype(LOW)

    high = [bit for bit in bits_of(members) if bit]
    orders = (high + [0], high[::-1] + [0])
    owns, alls = (key, value), (keys_all, values_all)

    def copy(flow, mask, bit):
        slot = mask | 1 << bit
        place = alls[flow].at[flip(member, mask)]
        return remote(
            place if mask else owns[flow].at[pl.ds(0, PROMPT_DEV)],
            place,
            send_sem.at[flow, slot],
            recv_sem.at[flow, slot],
            (flip(member, 1 << bit), tensor),
        )

    def forward(flow, mask):
        order = orders[flow]
        last = max([order.index(bit) for bit in order if mask >> bit & 1], default=-1)
        for bit in order[last + 1 :]:
            copy(flow, mask, bit).start()

    def came_by(flow, mask):
        order = orders[flow]
        bit = order[max(order.index(bit) for bit in order if mask >> bit & 1)]
        return copy(flow, mask ^ 1 << bit, bit)

    def keep(flow):
        return pltpu.make_async_copy(
            owns[flow].at[pl.ds(0, PROMPT_DEV)], alls[flow].at[member], local_sem.at[flow]
        )

    turned(w_key, key)
    forward(0, 0)
    value[...] = dot(act[...], w_value[...]).astype(LOW)
    forward(1, 0)
    keep(0).start()
    keep(1).start()
    turned(w_query, query)
    masks = range(1, members)
    inner = sorted([mask for mask in masks if not mask & 1], key=lambda mask: mask.bit_count())
    for mask in inner:
        for flow in (0, 1):
            turn = flow if not mask & 2 else flow
            came_by(turn, mask).wait_recv()
            forward(turn, mask)
    for mask in masks:
        if mask & 1:
            for flow in (0, 1):
                came_by(flow, mask).wait_recv()
    for flow in (0, 1):
        keep(flow).wait()
        for mask in masks:
            came_by(flow, mask).wait_send()


def project(members, states, w_query, w_key, w_value, cosine, sine):
    rows, depth = states.shape
    width = w_query.shape[1]
    return pl.pallas_call(
        functools.partial(project_kernel, members),
        out_shape=[
            shape((rows, depth), LOW),
            shape((rows, width), LOW),
            shape((rows, width), LOW),
            shape((rows, width), LOW),
            shape((members, PROMPT_DEV, width), LOW),
            shape((members, PROMPT_DEV, width), LOW),
        ],
        in_specs=[VMEM] * 6,
        out_specs=[VMEM] * 4 + [ANY] * 2,
        scratch_shapes=[DMA((2, members)), DMA((2, members)), DMA((2,))],
        compiler_params=pltpu.CompilerParams(
            collective_id=1, has_side_effects=True, vmem_limit_bytes=VMEM_LIMIT
        ),
        name="project",
    )(states, w_query, w_key, w_value, cosine, sine)


def make_plan(half, group_id, slice_start, cont_group, plan):
    member = lax.axis_index("dp")
    own, other = group_id[member], cont_group[0]
    plan[0] = lax.div(slice_start[member], PROMPT_DEV)

    def step(index, _):
        rank = lax.div(slice_start[index], PROMPT_DEV)

        @pl.when(group_id[index] == own)
        def _():
            plan[1 + rank] = index

        @pl.when(group_id[index] == other)
        def _():
            plan[1 + half + rank] = index

        return 0

    lax.fori_loop(0, 2 * half, step, 0)


def attend_kernel(
    half,
    group_id,
    slice_start,
    cont_group,
    query,
    key,
    value,
    keys_all,
    values_all,
    mixed,
    attended,
    log_total,
    plan,
):
    @pl.when(pl.program_id(0) == 0)
    def _():
        make_plan(half, group_id, slice_start, cont_group, plan)

    def part(start, count, steps, offset):
        span = pl.ds(start, count)
        queries = query[span]
        allowed = lax.broadcasted_iota(jnp.int32, (count, count), 0) >= lax.broadcasted_iota(
            jnp.int32, (count, count), 1
        )
        scores = jnp.where(allowed, dot(queries, key[span], 1, 1) * SCALE, NEGATIVE)
        top = jnp.max(scores, axis=-1, keepdims=True)
        weights = jnp.exp(scores - top)
        total = jnp.sum(weights, axis=-1, keepdims=True)
        result = dot(weights.astype(LOW), value[span])

        def step(index, carry):
            top, total, result = carry
            place = plan[offset + index]
            scores = dot(queries, keys_all[place], 1, 1) * SCALE
            higher = jnp.maximum(top, jnp.max(scores, axis=-1, keepdims=True))
            fade = jnp.exp(top - higher)
            weights = jnp.exp(scores - higher)
            total = total * fade + jnp.sum(weights, axis=-1, keepdims=True)
            result = result * fade + dot(weights.astype(LOW), values_all[place])
            return higher, total, result

        top, total, result = lax.fori_loop(0, steps, step, (top, total, result))
        result = result / total
        mixed[span] = result.astype(LOW)
        attended[span] = result
        log_total[span] = jnp.broadcast_to(top + jnp.log(total), (count, HEAD))

    part(0, PROMPT_DEV, plan[0], 1)
    part(PROMPT_DEV, query.shape[0] - PROMPT_DEV, half, 1 + half)


def attend(readers, query, key, value, keys_all, values_all):
    rows, width = query.shape
    members = keys_all.shape[0]
    head = pl.BlockSpec((rows, HEAD), lambda h, *_: (0, h))
    every = pl.BlockSpec((members, PROMPT_DEV, HEAD), lambda h, *_: (0, 0, h))
    return pl.pallas_call(
        functools.partial(attend_kernel, members // 2),
        out_shape=[
            shape((rows, width), LOW),
            shape((rows, width), WIDE),
            shape((rows, width), WIDE),
        ],
        grid_spec=pltpu.PrefetchScalarGridSpec(
            num_scalar_prefetch=3,
            grid=(width // HEAD,),
            in_specs=[head, head, head, every, every],
            out_specs=[head, head, head],
            scratch_shapes=[pltpu.SMEM((members + 1,), jnp.int32)],
        ),
        compiler_params=pltpu.CompilerParams(vmem_limit_bytes=VMEM_LIMIT),
        name="attend",
    )(*readers, query, key, value, keys_all, values_all)


def attend_back_kernel(
    half,
    group_id,
    slice_start,
    cont_group,
    query,
    key,
    value,
    keys_all,
    values_all,
    branch_low,
    w_out,
    attended,
    log_total,
    cosine,
    sine,
    d_query,
    d_keys_all,
    d_values_all,
    d_key_own,
    d_value_own,
    d_mixed,
    key_total,
    value_total,
    plan,
):
    @pl.when(pl.program_id(0) == 0)
    def _():
        make_plan(half, group_id, slice_start, cont_group, plan)

    d_mixed[...] = dot(branch_low[...], w_out[...], 1, 1).astype(LOW)
    key_total[...] = jnp.zeros_like(key_total)
    value_total[...] = jnp.zeros_like(value_total)

    def part(start, count, steps, offset):
        span = pl.ds(start, count)
        queries, d_attended = query[span], d_mixed[span]
        log_sum = log_total[span][:, :1]
        center = jnp.sum(d_attended.astype(WIDE) * attended[span], axis=-1, keepdims=True)

        def back(scores, keys, values):
            probabilities = jnp.exp(scores - log_sum)
            d_scores = (probabilities * (dot(d_attended, values, 1, 1) - center)).astype(LOW)
            return (
                dot(d_scores, keys),
                dot(d_scores, queries, 0, 0),
                dot(probabilities.astype(LOW), d_attended, 0, 0),
            )

        allowed = lax.broadcasted_iota(jnp.int32, (count, count), 0) >= lax.broadcasted_iota(
            jnp.int32, (count, count), 1
        )
        scores = jnp.where(allowed, dot(queries, key[span], 1, 1) * SCALE, NEGATIVE)
        d_queries, d_own_keys, d_own_values = back(scores, key[span], value[span])

        def step(index, d_queries):
            place = plan[offset + index]
            keys, values = keys_all[place], values_all[place]
            more, d_keys, d_values = back(dot(queries, keys, 1, 1) * SCALE, keys, values)
            key_total[place] += d_keys
            value_total[place] += d_values
            return d_queries + more

        d_queries = lax.fori_loop(0, steps, step, d_queries) * SCALE
        d_query[span] = rotate(d_queries, cosine[span], -sine[span]).astype(LOW)
        return d_own_keys, d_own_values

    member = lax.axis_index("dp")
    d_own_keys, d_own_values = part(0, PROMPT_DEV, plan[0], 1)
    key_total[member] += d_own_keys
    value_total[member] += d_own_values
    d_own_keys, d_own_values = part(PROMPT_DEV, query.shape[0] - PROMPT_DEV, half, 1 + half)
    late = pl.ds(PROMPT_DEV, query.shape[0] - PROMPT_DEV)
    d_key_own[...] = rotate(d_own_keys * SCALE, cosine[late], -sine[late]).astype(LOW)
    d_value_own[...] = d_own_values.astype(LOW)
    d_keys_all[...] = (key_total[...] * SCALE).astype(LOW)
    d_values_all[...] = value_total[...].astype(LOW)


def attend_back(
    readers,
    query,
    key,
    value,
    keys_all,
    values_all,
    branch_low,
    w_out,
    attended,
    log_total,
    cosine,
    sine,
):
    rows, width = query.shape
    members = keys_all.shape[0]
    depth = branch_low.shape[1]
    late = rows - PROMPT_DEV
    heads = width // HEAD
    head = pl.BlockSpec((rows, HEAD), lambda h, *_: (0, h))
    every = pl.BlockSpec((members, PROMPT_DEV, HEAD), lambda h, *_: (0, 0, h))
    own = pl.BlockSpec((late, HEAD), lambda h, *_: (0, h))
    table = pl.BlockSpec((rows, HEAD), lambda h, *_: (0, 0))
    return pl.pallas_call(
        functools.partial(attend_back_kernel, members // 2),
        out_shape=[
            shape((rows, width), LOW),
            shape((members, PROMPT_DEV, width), LOW),
            shape((members, PROMPT_DEV, width), LOW),
            shape((late, width), LOW),
            shape((late, width), LOW),
        ],
        grid_spec=pltpu.PrefetchScalarGridSpec(
            num_scalar_prefetch=3,
            grid=(heads,),
            in_specs=[
                head,
                head,
                head,
                every,
                every,
                pl.BlockSpec((rows, depth), lambda h, *_: (0, 0)),
                pl.BlockSpec((HEAD, depth), lambda h, *_: (h, 0)),
                head,
                head,
                table,
                table,
            ],
            out_specs=[head, every, every, own, own],
            scratch_shapes=[
                pltpu.VMEM((rows, HEAD), LOW),
                pltpu.VMEM((members, PROMPT_DEV, HEAD), WIDE),
                pltpu.VMEM((members, PROMPT_DEV, HEAD), WIDE),
                pltpu.SMEM((members + 1,), jnp.int32),
            ],
        ),
        compiler_params=pltpu.CompilerParams(vmem_limit_bytes=VMEM_LIMIT),
        name="attend_back",
    )(
        *readers,
        query,
        key,
        value,
        keys_all,
        values_all,
        branch_low,
        w_out,
        attended,
        log_total,
        cosine,
        sine,
    )


def place_of(group_id, slice_start, group, rank):
    place = 0
    for index in range(group_id.shape[0]):
        found = (group_id[index] == group) & (slice_start[index] == rank * PROMPT_DEV)
        place = jnp.maximum(place, jnp.where(found, index, 0))
    return place


def own_part(rows):
    return lax.broadcasted_iota(jnp.int32, (rows, rows), 0) >= lax.broadcasted_iota(
        jnp.int32, (rows, rows), 1
    )


def gather_attend_kernel(
    members,
    group_id,
    slice_start,
    cont_group,
    w_query_in,
    w_key_in,
    w_value_in,
    states_in,
    table,
    act,
    query,
    key,
    value,
    cosine,
    sine,
    mixed,
    attended,
    log_total,
    keys_out,
    values_out,
    states,
    weights,
    load_sem,
    weight_sem,
    send_sem,
    recv_sem,
    keep_sem,
    out_sem,
    *every,
):
    member, tensor = lax.axis_index("dp"), lax.axis_index("tensor")
    heads = query.shape[0]
    keys_all, values_all = every[:heads], every[heads:]
    half = members // 2
    rows = states.shape[0]
    chunks = load_sem.shape[0]
    size = rows // chunks
    loads = []
    for index in range(chunks):
        span = pl.ds(index * size, size)
        loads.append(pltpu.make_async_copy(states_in.at[span], states.at[span], load_sem.at[index]))
    w_loads = [
        pltpu.make_async_copy(source, weights.at[index], weight_sem.at[index])
        for index, source in enumerate((w_key_in, w_value_in, w_query_in))
    ]
    for load in loads[:1] + w_loads[:1] + loads[1:] + w_loads[1:]:
        load.start()
    hail(member_peers(members))
    index = lax.broadcasted_iota(jnp.int32, cosine.shape, 0)
    prompt = half * PROMPT_DEV - PROMPT_DEV
    positions = index + jnp.where(index < PROMPT_DEV, slice_start[member], prompt)
    angles = positions.astype(WIDE) * table[:1]
    cosine[...] = jnp.cos(angles)
    sine[...] = jnp.sin(angles) * table[1:2]
    step = 64
    for index in range(chunks):
        loads[index].wait()
        for start in range(index * size, index * size + size, step):
            span = pl.ds(start, step)
            act[span] = norm_rows(states[span])[0].astype(LOW)

    def turned(weight, out):
        linear = dot(act[...], weight)
        for head in range(heads):
            out[head] = rotate(
                linear[:, head * HEAD : head * HEAD + HEAD], cosine[...], sine[...]
            ).astype(LOW)

    high = [bit for bit in bits_of(members) if bit]
    orders = (high + [0], high[::-1] + [0])
    owns, alls = (key, value), (keys_all, values_all)
    early = pl.ds(0, PROMPT_DEV)

    def copy(flow, head, mask, bit):
        slot = mask | 1 << bit
        place = alls[flow][head].at[flip(member, mask)]
        return remote(
            place if mask else owns[flow].at[head, early],
            place,
            send_sem.at[flow, head, slot],
            recv_sem.at[flow, head, slot],
            (flip(member, 1 << bit), tensor),
        )

    def forward(flow, head, mask):
        order = orders[flow]
        last = max([order.index(bit) for bit in order if mask >> bit & 1], default=-1)
        for bit in order[last + 1 :]:
            copy(flow, head, mask, bit).start()

    def came_by(flow, head, mask):
        order = orders[flow]
        bit = order[max(order.index(bit) for bit in order if mask >> bit & 1)]
        return copy(flow, head, mask ^ 1 << bit, bit)

    def keep(flow, head):
        return pltpu.make_async_copy(
            owns[flow].at[head, early], alls[flow][head].at[member], keep_sem.at[flow, head]
        )

    def write(flow, head):
        return pltpu.make_async_copy(
            alls[flow][head], (keys_out, values_out)[flow].at[head], out_sem.at[flow, head]
        )

    masks = range(1, members)
    levels = len(high)

    def own_sends(head):
        if head < heads:
            for flow in (0, 1):
                forward(flow, head, 0)
            for flow in (0, 1):
                keep(flow, head).start()

    def level(head, count):
        if head < heads:
            for mask in masks:
                if not mask & 1 and mask.bit_count() == count:
                    for flow in (0, 1):
                        came_by(flow, head, mask).wait_recv()
                        forward(flow, head, mask)

    def complete(head):
        for flow in (0, 1):
            for mask in masks:
                if mask & 1:
                    came_by(flow, head, mask).wait_recv()
            keep(flow, head).wait()
            write(flow, head).start()

    own_group, other_group = group_id[member], cont_group[0]
    own_start = slice_start[member]
    own_places = [place_of(group_id, slice_start, own_group, rank) for rank in range(half)]
    other_places = [place_of(group_id, slice_start, other_group, rank) for rank in range(half)]
    block = 128

    def attend_rows(head, start, places, whole):
        span = pl.ds(start, block)
        queries = query[head, span]
        scores, values = [], []
        for rank, place in enumerate(places):
            score = dot(queries, keys_all[head][place], 1, 1) * SCALE_TWO
            if not whole:
                at = lax.broadcasted_iota(jnp.int32, score.shape, 0) + (own_start + start)
                to = lax.broadcasted_iota(jnp.int32, score.shape, 1) + rank * PROMPT_DEV
                score = jnp.where(to <= at, score, NEGATIVE)
            scores.append(score)
            values.append(values_all[head][place])
        if whole:
            score = dot(queries, key[head, span], 1, 1) * SCALE_TWO
            scores.append(jnp.where(own_part(block), score, NEGATIVE))
            values.append(value[head, span])
        top = functools.reduce(
            jnp.maximum, [jnp.max(score, axis=-1, keepdims=True) for score in scores]
        )
        total = jnp.zeros_like(top)
        result = jnp.zeros((block, HEAD), WIDE)
        for score, held in zip(scores, values):
            weight = jnp.exp2(score - top)
            total += jnp.sum(weight, axis=-1, keepdims=True)
            result += dot(weight.astype(LOW), held)
        result = result / total
        mixed[span, head * HEAD : head * HEAD + HEAD] = result.astype(LOW)
        attended[head, span] = result
        log_total[head, span] = jnp.broadcast_to(top + jnp.log2(total), (block, HEAD))

    w_loads[0].wait()
    turned(weights[0], key)
    heed(member_peers(members))
    forward(0, 0, 0)
    w_loads[1].wait()
    linear = dot(act[...], weights[1])
    for head in range(heads):
        value[head] = linear[:, head * HEAD : head * HEAD + HEAD].astype(LOW)
    forward(1, 0, 0)
    for flow in (0, 1):
        keep(flow, 0).start()
    own_sends(1)
    w_loads[2].wait()
    turned(weights[2], query)
    level(0, 1)
    own_sends(2)
    for count in range(2, levels + 1):
        level(0, count)
    level(1, 1)
    own_sends(3)
    for head in range(heads):
        complete(head)

        @pl.loop(0, PROMPT_DEV // block)
        def _(index, head=head):
            attend_rows(head, pl.multiple_of(index * block, block), own_places, False)

        for count in range(2, levels + 1):
            level(head + 1, count)
        level(head + 2, 1)
        own_sends(head + 4)
        for start in range(PROMPT_DEV, rows, block):
            attend_rows(head, start, other_places, True)
    for head in range(heads):
        for flow in (0, 1):
            write(flow, head).wait()
            for mask in masks:
                came_by(flow, head, mask).wait_send()


def gather_attend(members, readers, w_query, w_key, w_value, states, table):
    rows, depth = states.shape
    width = w_query.shape[1]
    heads = width // HEAD
    smem = pl.BlockSpec(memory_space=pltpu.SMEM)
    row_heads = (heads, rows, HEAD)
    every = (heads, members, PROMPT_DEV, HEAD)
    return pl.pallas_call(
        functools.partial(gather_attend_kernel, members),
        out_shape=[
            shape((rows, depth), LOW),
            shape(row_heads, LOW),
            shape(row_heads, LOW),
            shape(row_heads, LOW),
            shape((rows, HEAD), WIDE),
            shape((rows, HEAD), WIDE),
            shape((rows, width), LOW),
            shape(row_heads, WIDE),
            shape(row_heads, WIDE),
            shape(every, LOW),
            shape(every, LOW),
        ],
        in_specs=[smem] * 3 + [ANY] * 4 + [VMEM],
        out_specs=[VMEM] * 9 + [ANY] * 2,
        scratch_shapes=[
            pltpu.VMEM((rows, depth), WIDE),
            pltpu.VMEM((3, depth, width), LOW),
            DMA((4,)),
            DMA((3,)),
            DMA((2, heads, members)),
            DMA((2, heads, members)),
            DMA((2, heads)),
            DMA((2, heads)),
        ]
        + [pltpu.VMEM(every[1:], LOW)] * (2 * heads),
        compiler_params=pltpu.CompilerParams(
            collective_id=6, has_side_effects=True, vmem_limit_bytes=VMEM_LIMIT
        ),
        name="gather_attend",
    )(
        *readers,
        w_query,
        w_key,
        w_value,
        states,
        table,
    )


def back_owner_kernel(
    members,
    count,
    group_id,
    slice_start,
    cont_group,
    keys_in,
    values_in,
    query_in,
    key_in,
    value_in,
    attended_in,
    log_total_in,
    branch_low,
    w_out,
    cosine,
    sine,
    own_early,
    own_late,
    d_query,
    d_key,
    d_value,
    early_out,
    late_out,
    query,
    key,
    value,
    attended,
    log_total,
    d_mixed,
    d_queries,
    own_keys,
    own_values,
    other_keys,
    other_values,
    load_sem,
    *refs,
):
    take = taker(refs)
    member = lax.axis_index("dp")
    heads, rows = query.shape[0], query.shape[1]
    keys_all, values_all = take(heads), take(heads)
    out_send, out_recv = take(2)
    here = lax.axis_index("tensor")
    size = own_early.shape[0]
    own_rows = pl.ds(pl.multiple_of(here * size, size), size)
    told = ((own_early, early_out), (own_late, late_out))

    def tell(which, distance):
        source, target = told[which]
        return remote(
            source,
            target.at[own_rows],
            out_send.at[which, distance - 1],
            out_recv.at[which, distance - 1],
            (member, lax.rem(here + distance, count)),
        )

    half = pairs = members // 2
    parity = lax.rem(member, 2)
    order = bits_of(pairs)
    moves, flows, sides = [], [], []
    for way in (order, order[::-1]):
        mine, leaving, theirs = take(3)
        local_free, send_sem, recv_sem = take(3)
        refs_of = take(4)
        sides.append((mine, leaving, theirs, send_sem, recv_sem))
        per_head = []
        for head in range(heads):

            def own(mask, target, columns, mine=mine, theirs=theirs, head=head):
                return mine[head, target, :, columns].astype(WIDE) + theirs[
                    head, target, :, columns
                ].astype(WIDE)

            per_head.append(Halving(pairs, way, own, [ref.at[head] for ref in refs_of]))
        flows.append(per_head)
    partner = (flip(member, 1), lax.axis_index("tensor"))

    sources = (keys_in, values_in, query_in, key_in, value_in, attended_in, log_total_in)

    def load(index, head):
        if index < 2:
            target = (keys_all, values_all)[index][head]
        else:
            target = (query, key, value, attended, log_total)[index - 2].at[head]
        return pltpu.make_async_copy(
            sources[index].at[head], target, load_sem.at[index, head]
        )

    for head in range(heads):
        for index in range(len(sources)):
            load(index, head).start()

    def across(flow, head):
        _, leaving, theirs, send_sem, recv_sem = sides[flow]
        return remote(
            leaving.at[head], theirs.at[head], send_sem.at[head], recv_sem.at[head], partner
        )

    own_group, other_group = group_id[member], cont_group[0]
    own_start = slice_start[member]
    own_places = [place_of(group_id, slice_start, own_group, rank) for rank in range(half)]
    other_places = [place_of(group_id, slice_start, other_group, rank) for rank in range(half)]
    across_line = [(member, lax.rem(here + distance, count)) for distance in range(1, count)]
    hail(member_peers(members) + across_line)
    linear = dot(branch_low[...], w_out[...], 1, 1)
    for head in range(heads):
        d_mixed[head] = linear[:, head * HEAD : head * HEAD + HEAD].astype(LOW)
    heed(member_peers(members) + across_line)
    for which, (source, target) in enumerate(told):
        for distance in range(1, count):
            tell(which, distance).start()
        target[own_rows] = source[...]
    late = rows - PROMPT_DEV

    def back(scores, queries, keys, values, d_attended, log_sum, center):
        probabilities = jnp.exp2(scores - log_sum)
        d_scores = (probabilities * (dot(d_attended, values, 1, 1) - center)).astype(LOW)
        return (
            dot(d_scores, keys),
            dot(d_scores, queries, 0, 0),
            dot(probabilities.astype(LOW), d_attended, 0, 0),
        )

    def rows_of(head, start, count):
        span = pl.ds(start, count)
        d_attended = d_mixed[head, span]
        center = jnp.sum(d_attended.astype(WIDE) * attended[head, span], axis=-1, keepdims=True)
        return query[head, span], d_attended, log_total[head, span][:, :1], center

    def prompt_rank(head, rank):
        queries, d_attended, log_sum, center = rows_of(head, 0, PROMPT_DEV)
        place = own_places[rank]
        keys, values = keys_all[head][place], values_all[head][place]
        scores = dot(queries, keys, 1, 1) * SCALE_TWO
        at = lax.broadcasted_iota(jnp.int32, scores.shape, 0) + own_start
        to = lax.broadcasted_iota(jnp.int32, scores.shape, 1) + rank * PROMPT_DEV
        scores = jnp.where(to <= at, scores, NEGATIVE)
        more, d_keys, d_values = back(
            scores, queries, keys, values, d_attended, log_sum, center
        )
        early = pl.ds(0, PROMPT_DEV)
        if rank:
            d_queries[early] += more
        else:
            d_queries[early] = more
        own_keys[rank] = d_keys
        own_values[rank] = d_values

    def late_part(head):
        queries, d_attended, log_sum, center = rows_of(head, PROMPT_DEV, late)
        span = pl.ds(PROMPT_DEV, late)
        keys, values = key[head, span], value[head, span]
        scores = jnp.where(own_part(late), dot(queries, keys, 1, 1) * SCALE_TWO, NEGATIVE)
        total, d_keys, d_values = back(
            scores, queries, keys, values, d_attended, log_sum, center
        )
        columns = pl.ds(head * HEAD, HEAD)
        d_key[span, columns] = rotate(d_keys * SCALE, cosine[span], -sine[span]).astype(LOW)
        d_value[span, columns] = d_values.astype(LOW)
        for rank in range(half):
            place = other_places[rank]
            keys, values = keys_all[head][place], values_all[head][place]
            more, d_keys, d_values = back(
                dot(queries, keys, 1, 1) * SCALE_TWO, queries, keys, values, d_attended, log_sum, center
            )
            total += more
            other_keys[rank] = d_keys
            other_values[rank] = d_values
        d_queries[span] = total
        d_query[:, columns] = rotate(d_queries[...] * SCALE, cosine[...], -sine[...]).astype(LOW)

    def spread(head):
        for pair in range(pairs):
            for away in (0, 1):
                index = 2 * pair + (1 - parity if away else parity)
                rank = lax.div(slice_start[index], PROMPT_DEV)
                mine = jnp.where(group_id[index] == own_group, 1.0, 0.0)
                other = jnp.where(group_id[index] == other_group, 1.0, 0.0)
                for flow, (a, b, scale) in enumerate(
                    ((own_keys, other_keys, SCALE), (own_values, other_values, 1.0))
                ):
                    total = a[rank] * (mine * scale) + b[rank] * (other * scale)
                    sides[flow][away][head, pair] = total.astype(LOW)

    def begin(head):
        for flow in (0, 1):
            across(flow, head).start()

    def stage(head, index):
        if not 0 <= head < heads:
            return
        for flow in (0, 1):
            if not index:
                across(flow, head).wait_recv()
        for flow in (0, 1):
            for mask in flows[flow][head].steps(index):
                flows[flow][head].push(mask)

    def end(head):
        if not 0 <= head < heads:
            return
        early = pl.ds(0, PROMPT_DEV)
        columns = pl.ds(head * HEAD, HEAD)
        total = d_queries.at[early]
        flows[0][head].end(total)
        d_key[early, columns] = rotate(total[...], cosine[early], -sine[early]).astype(LOW)
        flows[1][head].end(d_value.at[early, columns])

    depth = len(order)
    for head in range(heads):
        for index in range(len(sources)):
            load(index, head).wait()
        for rank in range(half):
            prompt_rank(head, rank)
            if rank == 0:
                stage(head - 1, 0)
            if rank == half - 1:
                for index in range(1, depth):
                    stage(head - 1, index)
        late_part(head)
        spread(head)
        begin(head)
        end(head - 1)
    for index in range(depth):
        stage(heads - 1, index)
    end(heads - 1)
    for flow in (0, 1):
        for head in range(heads):
            across(flow, head).wait_send()
            flows[flow][head].sent()
    for which in range(len(told)):
        for distance in range(1, count):
            tell(which, distance).wait()


def back_owner(
    members,
    count,
    readers,
    keys_all,
    values_all,
    query,
    key,
    value,
    branch_low,
    w_out,
    attended,
    log_total,
    cosine,
    sine,
    own_early,
    own_late,
):
    heads, rows, _ = query.shape
    width = heads * HEAD
    pairs = members // 2
    smem = pl.BlockSpec(memory_space=pltpu.SMEM)
    every = pltpu.VMEM((members, PROMPT_DEV, HEAD), LOW)
    side = pltpu.VMEM((heads, pairs, PROMPT_DEV, HEAD), LOW)
    step = pltpu.VMEM((heads, pairs - 1, PROMPT_DEV, HEAD), LOW)
    flow = [side] * 3 + [DMA((heads,))] * 3 + [step] * 2 + [DMA((heads, pairs - 1, 1))] * 2
    total = pltpu.VMEM((pairs, PROMPT_DEV, HEAD), WIDE)
    return pl.pallas_call(
        functools.partial(back_owner_kernel, members, count),
        out_shape=[shape((rows, width), LOW)] * 3
        + [shape((count * own_early.shape[0], own_early.shape[1]), LOW)] * 2,
        in_specs=[smem] * 3 + [ANY] * 7 + [VMEM] * 6,
        out_specs=[VMEM] * 5,
        scratch_shapes=[
            pltpu.VMEM((heads, rows, HEAD), LOW),
            pltpu.VMEM((heads, rows, HEAD), LOW),
            pltpu.VMEM((heads, rows, HEAD), LOW),
            pltpu.VMEM((heads, rows, HEAD), WIDE),
            pltpu.VMEM((heads, rows, HEAD), WIDE),
            pltpu.VMEM((heads, rows, HEAD), LOW),
            pltpu.VMEM((rows, HEAD), WIDE),
            total,
            total,
            total,
            total,
            DMA((7, heads)),
        ]
        + [every] * (2 * heads)
        + [DMA((2, count - 1))] * 2
        + flow * 2,
        compiler_params=pltpu.CompilerParams(
            collective_id=7, has_side_effects=True, vmem_limit_bytes=VMEM_LIMIT
        ),
        name="back_owner",
    )(
        *readers,
        keys_all,
        values_all,
        query,
        key,
        value,
        attended,
        log_total,
        branch_low,
        w_out,
        cosine,
        sine,
        own_early,
        own_late,
    )


def middle_kernel(
    count,
    mixed,
    w_out,
    states,
    cotangent_in,
    w_gate_in,
    w_up_in,
    w_down_in,
    act,
    resid,
    own_early,
    out_low_out,
    ffn_late,
    d_act_out,
    hidden_out,
    d_gate_out,
    d_up_out,
    part,
    cotangent,
    out_low,
    d_hidden,
    w_gate,
    w_up,
    w_down,
    rows_in,
    ffn_total,
    d_total,
    ffn,
    hidden,
    d_gate,
    d_up,
    state_sem,
    cot_sem,
    weight_sem,
    out_sem,
    *refs,
):
    line = Line(count, refs[: Line.scratch_count])
    out_line = Line(count, refs[Line.scratch_count :])
    rows, size = resid.shape[0], line.rows
    fetch = pltpu.make_async_copy(
        states.at[pl.ds(pl.multiple_of(line.here * rows, rows), rows)], resid, state_sem
    )
    slots, step, _ = cotangent.shape

    def cot_load(index):
        return pltpu.make_async_copy(
            cotangent_in.at[pl.ds(index * step, step)],
            cotangent.at[index % slots],
            cot_sem.at[index % slots],
        )

    down_load, gate_load, up_load = [
        pltpu.make_async_copy(source, target, weight_sem.at[index])
        for index, (source, target) in enumerate(
            ((w_down_in, w_down), (w_gate_in, w_gate), (w_up_in, w_up))
        )
    ]
    fetch.start()
    for index in range(slots):
        cot_load(index).start()
    hail(line.peers())
    tile = 512
    for start in range(0, part.shape[1], tile):
        columns = pl.ds(start, tile)
        part[:, columns] = dot(mixed[...], w_out[:, columns]).astype(LOW)
    heed(line.peers())
    fetch.wait()

    def finish(group):
        span = pl.ds(group * size, size)
        resid[span] += line.total[...]
        act[line.span(group, line.here)] = norm_rows(resid[span])[0].astype(LOW)

    leaving = []

    def leave(source, target):
        copy = pltpu.make_async_copy(source, target, out_sem.at[len(leaving)])
        copy.start()
        leaving.append(copy)

    def cast():
        steps = out_low.shape[0] // step
        for index in range(steps):
            cot_load(index).wait()
            out_low[pl.ds(index * step, step)] = cotangent[index % slots].astype(LOW)
            if index + slots < steps:
                cot_load(index + slots).start()
            if index + slots == steps:
                for load in (down_load, gate_load, up_load):
                    load.start()
        leave(out_low, out_low_out)

    def inner(start):
        span = pl.ds(start, tile)
        d_hidden[:, span] = dot(out_low[...], w_down[span], 1, 1).astype(LOW)

    units, block = d_hidden.shape[1], 512
    starts = list(range(0, units, tile))

    def inners(some):
        def run():
            if some[0] == 0:
                down_load.wait()
            for start in some:
                inner(start)

        return run

    def begin(group):
        if not group:
            gate_load.wait()
            up_load.wait()
        for chunk in range(count):
            rows_in[pl.ds(chunk * size, size)] = act[line.span(group, chunk)]
        ffn_total[...] = jnp.zeros_like(ffn_total)
        d_total[...] = jnp.zeros_like(d_total)

    def feed(group, first, last):
        @pl.loop(first, last)
        def _(index):
            columns = pl.ds(pl.multiple_of(index * block, block), block)
            gate = dot(rows_in[...], w_gate[:, columns])
            up = dot(rows_in[...], w_up[:, columns])
            sigmoid = jax.nn.sigmoid(gate)
            swish = gate * sigmoid
            d_inner = jnp.concatenate(
                [d_hidden[line.span(group, chunk), columns] for chunk in range(count)]
            ).astype(WIDE)
            new_hidden = (swish * up).astype(LOW)
            new_gate = (d_inner * up * sigmoid * (1.0 + gate * (1.0 - sigmoid))).astype(LOW)
            new_up = (d_inner * swish).astype(LOW)
            for chunk in range(count):
                own = slice(chunk * size, chunk * size + size)
                hidden[chunk, group, :, columns] = new_hidden[own]
                d_gate[chunk, group, :, columns] = new_gate[own]
                d_up[chunk, group, :, columns] = new_up[own]
            for start in range(0, part.shape[1], tile):
                out = pl.ds(start, tile)
                ffn_total[:, out] += dot(new_hidden, w_down[columns, out])
                d_total[:, out] += dot(new_gate, w_gate[out, columns], 1, 1) + dot(
                    new_up, w_up[out, columns], 1, 1
                )

    def end(group):
        own = pl.ds(pl.multiple_of(line.here * size, size), size)
        ffn_total[own] += resid[pl.ds(group * size, size)]
        ffn[group] = ffn_total[...].astype(LOW)
        if group:
            leave(ffn.at[group], ffn_late)
        for chunk in range(count):
            span = line.span(group, chunk)
            part[span] = d_total[pl.ds(chunk * size, size)].astype(LOW)
            leave(part.at[span], d_act_out.at[span])
        for source, target in (
            (hidden, hidden_out),
            (d_gate, d_gate_out),
            (d_up, d_up_out),
        ):
            leave(source.at[:, group], target.at[:, group])

    blocks = units // block
    third = -(-blocks // 3)

    def opening():
        begin(0)
        feed(0, 0, third)

    def closing():
        feed(0, 2 * third, blocks)
        end(0)

    line.reduce(
        part,
        act,
        finish,
        [
            cast,
            inners(starts[:1]),
            inners(starts[1:2]),
            inners(starts[2:]),
            opening,
            lambda: feed(0, third, 2 * third),
            closing,
        ],
    )
    early = ffn.at[0]
    out_line.scatter_slot(0, 0, early)
    begin(1)
    feed(1, 0, third)
    out_line.scatter_slot(0, 1, early)
    feed(1, third, 2 * third)
    for slot in range(2, count - 1):
        out_line.scatter_slot(0, slot, early)
    feed(1, 2 * third, blocks)
    end(1)
    out_line.scatter_end(0, early)
    own_early[...] = out_line.total[...].astype(LOW)
    for copy in leaving:
        copy.wait()
    line.sent(act)
    out_line.sent()


def middle(count, mixed, w_out, states, cotangent, w_gate, w_up, w_down):
    rows, depth = states.shape
    units = w_down.shape[0]
    size = rows // count // GROUPS
    split = (count, GROUPS, size)
    inside = (*split, units)
    some = (GROUPS, rows // GROUPS, depth)
    outs = pl.pallas_call(
        functools.partial(middle_kernel, count),
        out_shape=[
            shape((rows, depth), LOW),
            shape((rows // count, depth), WIDE),
            shape((size, depth), LOW),
            shape((rows, depth), LOW),
            shape(some[1:], LOW),
            shape((rows, depth), LOW),
            shape(inside, LOW),
            shape(inside, LOW),
            shape(inside, LOW),
        ],
        in_specs=[VMEM] * 2 + [ANY] * 5,
        out_specs=[VMEM] * 3 + [ANY] * 6,
        scratch_shapes=[
            pltpu.VMEM((rows, depth), LOW),
            pltpu.VMEM((2, 64, depth), WIDE),
            pltpu.VMEM((rows, depth), LOW),
            pltpu.VMEM((rows, units), LOW),
            pltpu.VMEM((depth, units), LOW),
            pltpu.VMEM((depth, units), LOW),
            pltpu.VMEM((units, depth), LOW),
            pltpu.VMEM(some[1:], LOW),
            pltpu.VMEM(some[1:], WIDE),
            pltpu.VMEM(some[1:], WIDE),
            pltpu.VMEM(some, LOW),
            pltpu.VMEM(inside, LOW),
            pltpu.VMEM(inside, LOW),
            pltpu.VMEM(inside, LOW),
            DMA,
            DMA((2,)),
            DMA((3,)),
            DMA(((4 + count) * GROUPS,)),
        ]
        + Line.scratch(count, GROUPS, rows // count, depth)
        + Line.scratch(count, 1, size, depth),
        compiler_params=pltpu.CompilerParams(
            collective_id=2, has_side_effects=True, vmem_limit_bytes=VMEM_LIMIT
        ),
        name="middle",
    )(mixed, w_out, states, cotangent, w_gate, w_up, w_down)
    return [*outs[:6], *(out.reshape(rows, -1) for out in outs[6:])]


def second_kernel(
    count,
    pairs,
    d_act_in,
    ffn_in,
    resid_in,
    cotangent,
    act,
    d_gate,
    d_up,
    branch_low,
    grad_resid,
    own_out,
    grad_gate,
    grad_up,
    d_act,
    ffn,
    resid,
    cot_sem,
    load_sem,
    *refs,
):
    take = taker(refs)
    line = Line(count, take(Line.scratch_count))
    out_line = Line(count, take(Line.scratch_count))
    lhs = Lhs(act, take(4))
    rights = [Rhs([source], take(4)) for source in (d_gate, d_up)]
    order = bits_of(pairs)
    flows = [
        Halving(pairs, way, product_of(lhs, right), take(4), *take(1))
        for way, right in zip((order, order[::-1]), rights)
    ]
    rows = resid.shape[0]
    fetch = pltpu.make_async_copy(
        cotangent.at[pl.ds(pl.multiple_of(line.here * rows, rows), rows)], grad_resid, cot_sem
    )
    peers = line.peers() + member_peers(2 * pairs)
    hail(peers)
    loads = [
        pltpu.make_async_copy(source, target, load_sem.at[index])
        for index, (source, target) in enumerate(
            ((d_act_in, d_act), (ffn_in, ffn), (resid_in, resid))
        )
    ]
    fetch.start()
    for load in loads:
        load.start()
    heed(peers)
    lhs.start()
    for piece in range(flows[0].pieces):
        for right in rights:
            right.start(piece)
    fetch.wait()
    for load in loads:
        load.wait()

    def finish(group):
        span = pl.ds(group * line.rows, line.rows)
        normed, inverse = norm_rows(resid[span])
        grad_resid[span] += norm_back(line.total[...], normed, inverse)
        branch_low[line.span(group, line.here)] = grad_resid[span].astype(LOW)

    sides = [(lhs, right, flow) for right, flow in zip(rights, flows)]
    ahead, early, others, settle, late = beside(order, sides)

    def out_slot(slot):
        return lambda: out_line.scatter_slot(0, slot, ffn)

    slots = [out_slot(slot) for slot in range(count - 1)]

    def fourth():
        settle()
        slots[0]()

    line.reduce(d_act, branch_low, finish, [ahead, early, others, fourth, late] + slots[1:])
    out_line.scatter_end(0, ffn)
    own_out[...] = out_line.total[...].astype(LOW)
    flows[0].end(grad_gate)
    flows[1].end(grad_up)
    for flow in flows:
        flow.sent()
    for move in [lhs] + rights:
        move.sent()
    line.sent(branch_low)
    out_line.sent()


def beside(order, sides):
    masks = [flow.steps(0) for _, _, flow in sides]

    def ahead():
        for (lhs, rhs, flow), (mask, *_) in zip(sides[:2], masks):
            lhs.ready()
            rhs.ready(0)
            flow.push_piece(mask, 0)

    def early():
        for at, ((lhs, rhs, flow), (mask, *_)) in enumerate(zip(sides, masks)):
            if at > 1:
                lhs.ready()
            for piece in range(0 if at > 1 else 1, flow.pieces):
                rhs.ready(piece)
                flow.push_piece(mask, piece)

    def others():
        for index in range(1, len(masks[0])):
            for (_, _, flow), steps in zip(sides, masks):
                flow.push(steps[index])

    def settle():
        for _, _, flow in sides:
            flow.settle()

    def late():
        for stage in range(1, len(order)):
            for index in range(len(sides[0][2].steps(stage))):
                for _, _, flow in sides:
                    flow.push(flow.steps(stage)[index])

    return [ahead, early, others, settle, late]


def second(count, members, d_act, ffn, resid, cotangent, act, d_gate, d_up):
    rows, depth = cotangent.shape
    units = d_gate.shape[1]
    pairs = members // 2
    block = depth // members
    return pl.pallas_call(
        functools.partial(second_kernel, count, pairs),
        out_shape=[
            shape((rows, depth), LOW),
            shape((rows // count, depth), WIDE),
            shape((ffn.shape[0] // count, depth), LOW),
            shape((block, units), LOW),
            shape((block, units), LOW),
        ],
        in_specs=[ANY] * 7,
        out_specs=[VMEM] * 5,
        scratch_shapes=[
            pltpu.VMEM(d_act.shape, LOW),
            pltpu.VMEM(ffn.shape, LOW),
            pltpu.VMEM(resid.shape, WIDE),
            DMA,
            DMA((3,)),
        ]
        + Line.scratch(count, GROUPS, rows // count, depth)
        + Line.scratch(count, 1, ffn.shape[0] // count, depth)
        + Lhs.scratch(pairs, rows, block)
        + Rhs.scratch(rows, units) * 2
        + (Halving.scratch(pairs, block, units) + [pltpu.VMEM((block, units), WIDE)]) * 2,
        compiler_params=pltpu.CompilerParams(
            collective_id=3, has_side_effects=True, vmem_limit_bytes=VMEM_LIMIT
        ),
        name="second",
    )(d_act, ffn, resid, cotangent, in_blocks(act, members), d_gate, d_up)


def owner_kernel(
    pairs,
    d_keys_all,
    d_values_all,
    d_key_own,
    d_value_own,
    cosine,
    sine,
    d_key,
    d_value,
    *refs,
):
    take = taker(refs)
    parity = lax.rem(lax.axis_index("dp"), 2)
    order = bits_of(pairs)
    width = d_key.shape[1]
    moves, flows = [], []
    for way, source in zip((order, order[::-1]), (d_keys_all, d_values_all)):
        mine, theirs = take(2)
        moves.append(
            Pairwise(
                [
                    (
                        source.at[2 * pair + parity],
                        mine.at[pair],
                        source.at[2 * pair + 1 - parity],
                        theirs.at[pair],
                    )
                    for pair in range(pairs)
                ],
                take(3),
            )
        )

        def own(mask, target, columns, mine=mine, theirs=theirs):
            return mine[target, :, columns].astype(WIDE) + theirs[target, :, columns].astype(WIDE)

        flows.append(Halving(pairs, way, own, take(4)))
    (total,) = take(1)
    greet(member_peers(2 * pairs))
    for move in moves:
        move.start()
    for move, flow in zip(moves, flows):
        move.ready()
        flow.push(flow.masks[0])
    late = pl.ds(PROMPT_DEV, d_key.shape[0] - PROMPT_DEV)
    d_key[late] = d_key_own[...]
    d_value[late] = d_value_own[...]
    for index in range(1, pairs - 1):
        for flow in flows:
            flow.push(flow.masks[index])
    early = pl.ds(0, PROMPT_DEV)
    flows[0].end(total)
    for start in range(0, width, HEAD):
        d_key[early, start : start + HEAD] = rotate(
            total[:, start : start + HEAD], cosine[early], -sine[early]
        ).astype(LOW)
    flows[1].end(d_value.at[early])
    for move, flow in zip(moves, flows):
        flow.sent()
        move.sent()


def owner(members, d_keys_all, d_values_all, d_key_own, d_value_own, cosine, sine):
    width = d_key_own.shape[1]
    rows = cosine.shape[0]
    pairs = members // 2
    flow = (
        [pltpu.VMEM((pairs, PROMPT_DEV, width), LOW)] * 2
        + Pairwise.sems(pairs)
        + Halving.scratch(pairs, PROMPT_DEV, width)
    )
    return pl.pallas_call(
        functools.partial(owner_kernel, pairs),
        out_shape=[shape((rows, width), LOW)] * 2,
        in_specs=[ANY, ANY] + [VMEM] * 4,
        out_specs=[VMEM] * 2,
        scratch_shapes=flow * 2 + [pltpu.VMEM((PROMPT_DEV, width), WIDE)],
        compiler_params=pltpu.CompilerParams(
            collective_id=4, has_side_effects=True, vmem_limit_bytes=VMEM_LIMIT
        ),
        name="owner",
    )(d_keys_all, d_values_all, d_key_own, d_value_own, cosine, sine)


def first_kernel(
    count,
    pairs,
    grad_resid,
    d_query,
    d_key,
    d_value,
    w_query,
    w_key,
    w_value,
    states,
    act,
    mixed,
    branch_low,
    hidden,
    out_low,
    far_query,
    far_key,
    far_value,
    input_grad,
    grad_down,
    grad_out,
    grad_query,
    grad_key,
    grad_value,
    inner_total,
    part,
    state,
    weight,
    state_sem,
    weight_sem,
    *refs,
):
    take = taker(refs)
    line = Line(count, take(Line.scratch_count))
    order = bits_of(pairs)
    sides = []
    for left, rights, way in (
        (out_low, (hidden,), order),
        (act, (far_query, far_key, far_value), order[::-1]),
        (branch_low, (mixed,), order[::-1]),
    ):
        lhs, rhs = Lhs(left, take(4)), Rhs(rights, take(4))
        sides.append((lhs, rhs, Halving(pairs, way, product_of(lhs, rhs), take(4), *take(1))))
    rows = state.shape[0]
    fetch = pltpu.make_async_copy(
        states.at[pl.ds(pl.multiple_of(line.here * rows, rows), rows)], state, state_sem
    )
    loads = [
        pltpu.make_async_copy(source, weight.at[index], weight_sem.at[index])
        for index, source in enumerate((w_query, w_key, w_value))
    ]
    for load in loads:
        load.start()
    fetch.start()
    greet(line.peers() + member_peers(2 * pairs))
    for lhs, rhs, _ in sides[:2]:
        lhs.start()
        rhs.start(0)
    for at, (lhs, rhs, flow) in enumerate(sides):
        if at > 1:
            lhs.start()
        for piece in range(0 if at > 1 else 1, flow.pieces):
            rhs.start(piece)
    for load in loads:
        load.wait()
    tile = 512
    for start in range(0, part.shape[1], tile):
        columns = pl.ds(start, tile)
        part[:, columns] = (
            dot(d_query[...], weight[0, columns], 1, 1)
            + dot(d_key[...], weight[1, columns], 1, 1)
            + dot(d_value[...], weight[2, columns], 1, 1)
        )
    fetch.wait()

    def finish(group):
        span = pl.ds(group * line.rows, line.rows)
        normed, inverse = norm_rows(state[span])
        input_grad[line.span(group, line.here)] = (
            grad_resid[span] + norm_back(line.total[...], normed, inverse)
        ).astype(LOW)

    line.reduce(part, input_grad, finish, beside(order, sides))
    for (_, _, flow), target in zip(sides, (grad_down, inner_total, grad_out)):
        flow.end(target)
    width = grad_query.shape[1]
    for index, target in enumerate((grad_query, grad_key, grad_value)):
        target[...] = inner_total[:, index * width : index * width + width]
    for lhs, rhs, flow in sides:
        flow.sent()
        lhs.sent()
        rhs.sent()
    line.sent(input_grad)


def first(
    count,
    members,
    grad_resid,
    weights,
    states,
    act,
    mixed,
    branch_low,
    hidden,
    out_low,
    d_query,
    d_key,
    d_value,
):
    rows, depth = states.shape
    width = d_query.shape[1]
    units = hidden.shape[1]
    pairs = members // 2
    block = depth // members
    scratch = []
    for wide in (units, 3 * width, width):
        scratch += Lhs.scratch(pairs, rows, block) + Rhs.scratch(rows, wide)
        scratch += Halving.scratch(pairs, block, wide) + [pltpu.VMEM((block, wide), WIDE)]
    return pl.pallas_call(
        functools.partial(first_kernel, count, pairs),
        out_shape=[
            shape((rows, depth), LOW),
            shape((block, units), LOW),
        ]
        + [shape((block, width), LOW)] * 4,
        in_specs=[VMEM] * 4 + [ANY] * 12,
        out_specs=[VMEM] * 6,
        scratch_shapes=[
            pltpu.VMEM((block, 3 * width), LOW),
            pltpu.VMEM((rows, depth), WIDE),
            pltpu.VMEM((rows // count, depth), WIDE),
            pltpu.VMEM((3, depth, width), LOW),
            DMA,
            DMA((3,)),
        ]
        + Line.scratch(count, GROUPS, rows // count, depth)
        + scratch,
        compiler_params=pltpu.CompilerParams(
            collective_id=5, has_side_effects=True, vmem_limit_bytes=VMEM_LIMIT
        ),
        name="first",
    )(
        grad_resid,
        d_query,
        d_key,
        d_value,
        *weights,
        states,
        in_blocks(act, members),
        mixed,
        in_blocks(branch_low, members),
        hidden,
        in_blocks(out_low, members),
        d_query,
        d_key,
        d_value,
    )


def widen_kernel(flat, early, late, *refs):
    count = len(refs) // 2
    sources, whole, targets = refs[:count], refs[count], refs[count + 1 :]
    half = early.shape[0]
    whole[pl.ds(0, half)] = early[...].astype(WIDE)
    whole[pl.ds(half, half)] = late[...].astype(WIDE)
    for index, (source, target) in enumerate(zip(sources, targets)):
        values = source[...].astype(WIDE)
        target[...] = values if index < flat else values.T


def widen(count, early, late, plain, turned):
    def rows(array):
        return pl.BlockSpec((array.shape[0] // count, array.shape[1]), lambda i: (i, 0))

    def columns(array):
        return pl.BlockSpec((array.shape[0], array.shape[1] // count), lambda i: (0, i))

    flipped = [shape(array.shape[::-1], WIDE) for array in turned]
    whole = shape((2 * early.shape[0], early.shape[1]), WIDE)
    return pl.pallas_call(
        functools.partial(widen_kernel, len(plain)),
        out_shape=[whole] + [shape(array.shape, WIDE) for array in plain] + flipped,
        grid=(count,),
        in_specs=[rows(array) for array in (early, late, *plain)]
        + [columns(array) for array in turned],
        out_specs=[rows(array) for array in (whole, *plain, *flipped)],
        compiler_params=pltpu.CompilerParams(vmem_limit_bytes=VMEM_LIMIT),
        name="widen",
    )(early, late, *plain, *turned)


def body(
    states,
    w_query,
    w_key,
    w_value,
    w_out,
    w_gate,
    w_up,
    w_down,
    group_id,
    slice_start,
    cont_group,
    cotangent,
):
    rows = states.shape[0]
    members = lax.axis_size("dp")
    count = lax.axis_size("tensor")
    frequency = 10000.0 ** (-np.arange(HEAD // 2) * 2.0 / HEAD)
    frequency = np.concatenate([frequency, frequency]).astype(np.float32)
    sign = np.repeat([-1.0, 1.0], HEAD // 2).astype(np.float32)
    readers = (group_id, slice_start, cont_group)
    merged = members * PROMPT_DEV * w_query.shape[1] * 2 * 4 <= 16 * 2**20
    if merged:
        table = jnp.stack([frequency, sign])
        act_one, query, key, value, cosine, sine, mixed, attended, log_total, *everyones = (
            gather_attend(members, readers, w_query, w_key, w_value, states, table)
        )
    else:
        index = jnp.arange(rows, dtype=jnp.int32)
        everyone = jnp.arange(members, dtype=jnp.int32)
        own_start = jnp.sum(jnp.where(everyone == lax.axis_index("dp"), slice_start, 0))
        prompt = members // 2 * PROMPT_DEV
        positions = jnp.where(index < PROMPT_DEV, own_start + index, prompt + index - PROMPT_DEV)
        angles = positions.astype(WIDE)[:, None] * frequency[None, :]
        cosine = jnp.cos(angles)
        sine = jnp.sin(angles) * sign[None, :]
        act_one, query, key, value, *everyones = project(
            members, states, w_query, w_key, w_value, cosine, sine
        )
        mixed, attended, log_total = attend(readers, query, key, value, *everyones)
    act_two, resid, own_early, out_low, ffn_late, d_act_two, hidden, d_gate, d_up = middle(
        count, mixed, w_out, states, cotangent, w_gate, w_up, w_down
    )
    branch_low, grad_resid, own_late, grad_gate, grad_up = second(
        count, members, d_act_two, ffn_late, resid, cotangent, act_two, d_gate, d_up
    )
    kept = (query, key, value, branch_low, w_out, attended, log_total, cosine, sine)
    if merged:
        d_query, d_key, d_value, early_out, late_out = back_owner(
            members, count, readers, *everyones, *kept, own_early, own_late
        )
    else:
        d_query, *d_everyones = attend_back(
            readers, query, key, value, *everyones, branch_low, w_out, attended, log_total, cosine, sine
        )
        d_key, d_value = owner(members, *d_everyones, cosine, sine)
        early_out, late_out = [
            lax.all_gather(own, "tensor", axis=0, tiled=True) for own in (own_early, own_late)
        ]
    input_grad, grad_down, grad_out, *grad_inner = first(
        count,
        members,
        grad_resid,
        (w_query, w_key, w_value),
        states,
        act_one,
        mixed,
        branch_low,
        hidden,
        out_low,
        d_query,
        d_key,
        d_value,
    )
    *plain, grad_out, grad_down = widen(
        count,
        early_out,
        late_out,
        (input_grad, *grad_inner, grad_gate, grad_up),
        (grad_out, grad_down),
    )
    return (*plain[:5], grad_out, *plain[5:], grad_down)


def solution(mesh):
    placed = (
        P("dp", None),
        P(None, "tensor"),
        P(None, "tensor"),
        P(None, "tensor"),
        P("tensor", None),
        P(None, "tensor"),
        P(None, "tensor"),
        P("tensor", None),
        P(),
        P(),
        P("dp"),
        P("dp", None),
    )
    return jax.shard_map(
        body,
        mesh=mesh,
        in_specs=placed,
        out_specs=(
            P("dp", None),
            P("dp", None),
            P("dp", "tensor"),
            P("dp", "tensor"),
            P("dp", "tensor"),
            P("tensor", "dp"),
            P("dp", "tensor"),
            P("dp", "tensor"),
            P("tensor", "dp"),
        ),
        check_vma=False,
    )
```

```python
import functools

import jax
import jax.numpy as jnp
import numpy as np
from jax import lax
from jax.experimental import pallas as pl
from jax.experimental.pallas import tpu as pltpu
from jax.sharding import PartitionSpec as P

HEAD = 128
PROMPT_DEV = 384
EPSILON = 1e-05
NEGATIVE = -1e30
SCALE = HEAD ** (-0.5)
SCALE_TWO = float(SCALE * np.log2(np.e))
LOW = jnp.bfloat16
WIDE = jnp.float32
MESH = pl.DeviceIdType.MESH
ANY = pl.BlockSpec(memory_space=pl.ANY)
VMEM = pl.BlockSpec(memory_space=pltpu.VMEM)
DMA = pltpu.SemaphoreType.DMA
VMEM_LIMIT = 63 * 2**20
GROUPS = 2
PIECE = 512


def dot(left, right, left_dim=1, right_dim=0):
    return lax.dot_general(
        left, right, (((left_dim,), (right_dim,)), ((), ())), preferred_element_type=WIDE
    )


def shape(dims, dtype):
    return jax.ShapeDtypeStruct(dims, dtype)


def norm_rows(values):
    row_mean = jnp.mean(values, axis=-1, keepdims=True)
    centred = values - row_mean
    inverse = lax.rsqrt(jnp.mean(centred * centred, axis=-1, keepdims=True) + EPSILON)
    return centred * inverse, inverse


def norm_back(gradient, normed, inverse):
    return inverse * (
        gradient
        - jnp.mean(gradient, axis=-1, keepdims=True)
        - normed * jnp.mean(gradient * normed, axis=-1, keepdims=True)
    )


def rotate(values, cosine, sine):
    return values * cosine + pltpu.roll(values, HEAD // 2, 1) * sine


def flip(index, mask):
    out, bit = index, 1
    while bit <= mask:
        if mask & bit:
            out = out + bit * (1 - 2 * lax.rem(lax.div(index, bit), 2))
        bit *= 2
    return out


def bits_of(count):
    return list(range(count.bit_length() - 1))


def hail(peers):
    barrier = pltpu.get_barrier_semaphore()
    for peer in peers:
        pl.semaphore_signal(barrier, inc=1, device_id=peer, device_id_type=MESH)


def heed(peers):
    pl.semaphore_wait(pltpu.get_barrier_semaphore(), len(peers))


def greet(peers):
    hail(peers)
    heed(peers)


def remote(source, target, send_sem, recv_sem, device):
    return pltpu.make_async_remote_copy(
        src_ref=source,
        dst_ref=target,
        send_sem=send_sem,
        recv_sem=recv_sem,
        device_id=device,
        device_id_type=MESH,
    )


class Line:
    scratch_count = 10

    @staticmethod
    def scratch(count, groups, rows, width):
        rows = rows // groups
        return [
            pltpu.VMEM((rows, width), WIDE),
            pltpu.VMEM((groups, count, rows, width), LOW),
            pltpu.VMEM((groups, count, rows, width), LOW),
            pltpu.VMEM((groups, count, rows, width), LOW),
            DMA((groups, count)),
            DMA((groups, count)),
            DMA((groups, count)),
            DMA((groups, count)),
            DMA((groups, count)),
            DMA((groups, count)),
        ]

    def __init__(self, count, refs):
        self.count = count
        (
            self.total,
            self.outgoing,
            self.from_left,
            self.from_right,
            self.out_sem,
            self.left_sem,
            self.right_sem,
            self.to_right_sem,
            self.to_left_sem,
            self.got_sem,
        ) = refs
        self.groups = self.outgoing.shape[0]
        self.rows = self.total.shape[0]
        self.here = lax.axis_index("tensor")
        member = lax.axis_index("dp")
        self.right = (member, lax.rem(self.here + 1, count))
        self.left = (member, lax.rem(self.here + count - 1, count))

    def peers(self):
        return [self.left, self.right]

    def span(self, group, chunk):
        start = chunk * (self.rows * self.groups) + group * self.rows
        return pl.ds(pl.multiple_of(start, self.rows), self.rows)

    def rightward(self, group, chunk):
        return remote(
            self.outgoing.at[group, chunk],
            self.from_left.at[group, chunk],
            self.out_sem.at[group, chunk],
            self.left_sem.at[group, chunk],
            self.right,
        )

    def leftward(self, group, chunk):
        return remote(
            self.outgoing.at[group, chunk],
            self.from_right.at[group, chunk],
            self.out_sem.at[group, chunk],
            self.right_sem.at[group, chunk],
            self.left,
        )

    def add_and_pass(self, group, chunk, part, right, wait):
        copy, came = (self.rightward, self.from_left) if right else (self.leftward, self.from_right)
        total = part[self.span(group, chunk)].astype(WIDE)
        if wait:
            copy(group, chunk).wait_recv()
            total += came[group, chunk].astype(WIDE)
        self.outgoing[group, chunk] = total.astype(LOW)
        copy(group, chunk).start()

    def scatter_slot(self, group, slot, part):
        here, count = self.here, self.count
        ahead, back = count - 1 + here - slot, slot - (count - 1 - here)
        if slot == 0:

            @pl.when(here == 0)
            def _():
                self.add_and_pass(group, ahead, part, True, False)

            @pl.when(here == count - 1)
            def _():
                self.add_and_pass(group, back, part, False, False)

            return
        for wait in (False, True):

            @pl.when((here <= slot) & ((here > 0) if wait else (here == 0)))
            def _(wait=wait):
                self.add_and_pass(group, ahead, part, True, wait)

            @pl.when(
                (count - 1 - here <= slot) & ((here < count - 1) if wait else (here == count - 1))
            )
            def _(wait=wait):
                self.add_and_pass(group, back, part, False, wait)

    def scatter_end(self, group, part):
        here = self.here
        last = self.count - 1

        def left():
            self.rightward(group, here).wait_recv()
            return self.from_left[group, here].astype(WIDE)

        def right():
            self.leftward(group, here).wait_recv()
            return self.from_right[group, here].astype(WIDE)

        @pl.when(here == 0)
        def _():
            self.total[...] = part[self.span(group, here)].astype(WIDE) + right()

        @pl.when(here == last)
        def _():
            self.total[...] = part[self.span(group, here)].astype(WIDE) + left()

        @pl.when((here > 0) & (here < last))
        def _():
            self.total[...] = part[self.span(group, here)].astype(WIDE) + left() + right()

    def passing(self, whole, group, chunk, right):
        ref = whole.at[self.span(group, chunk)]
        return remote(
            ref,
            ref,
            (self.to_right_sem if right else self.to_left_sem).at[group, chunk],
            self.got_sem.at[group, chunk],
            self.right if right else self.left,
        )

    def gather_slot(self, whole, group, distance):
        here, count = self.here, self.count

        @pl.when(here - distance >= 0)
        def _():
            if distance:
                self.passing(whole, group, here - distance, True).wait_recv()

            @pl.when(here < count - 1)
            def _():
                self.passing(whole, group, here - distance, True).start()

        @pl.when(here + distance <= count - 1)
        def _():
            if distance:
                self.passing(whole, group, here + distance, False).wait_recv()

            @pl.when(here > 0)
            def _():
                self.passing(whole, group, here + distance, False).start()

    def reduce(self, part, whole, finish, beside=()):
        beside = list(beside)
        last = self.count - 1
        self.scatter_slot(0, 0, part)
        for group in range(self.groups):
            for slot in range(1, last):
                if beside:
                    beside.pop(0)()
                self.scatter_slot(group, slot, part)
                if group:
                    self.gather_slot(whole, group - 1, slot)
            if group + 1 < self.groups:
                self.scatter_slot(group + 1, 0, part)
            if group:
                self.gather_slot(whole, group - 1, last)
            self.scatter_end(group, part)
            finish(group)
            self.gather_slot(whole, group, 0)
        for distance in range(1, self.count):
            if beside:
                beside.pop(0)()
            self.gather_slot(whole, self.groups - 1, distance)
        for act in beside:
            act()

    def sent(self, whole=None):
        here, count = self.here, self.count
        for group in range(self.groups):
            for chunk in range(count):

                @pl.when(here != chunk)
                def _(group=group, chunk=chunk):
                    self.rightward(group, chunk).wait_send()

                if whole is None:
                    continue

                @pl.when((chunk <= here) & (here < count - 1))
                def _(group=group, chunk=chunk):
                    self.passing(whole, group, chunk, True).wait_send()

                @pl.when((chunk >= here) & (here > 0))
                def _(group=group, chunk=chunk):
                    self.passing(whole, group, chunk, False).wait_send()


class Halving:
    @staticmethod
    def masks_of(pairs, order):
        def stage(mask):
            return min(order.index(bit) for bit in order if mask >> bit & 1)

        return sorted(range(1, pairs), key=lambda mask: (stage(mask), -mask.bit_count()))

    @staticmethod
    def scratch(pairs, block, width):
        count = pairs - 1
        pieces = max(1, width // PIECE)
        return [
            pltpu.VMEM((count, block, width), LOW),
            pltpu.VMEM((count, block, width), LOW),
            DMA((count, pieces)),
            DMA((count, pieces)),
        ]

    def __init__(self, pairs, order, own, refs, kept=None):
        self.order, self.own, self.kept = order, own, kept
        self.send, self.recv, self.send_sem, self.recv_sem = refs
        self.masks = Halving.masks_of(pairs, order)
        self.pieces = self.send_sem.shape[1]
        self.piece = self.send.shape[2] // self.pieces
        self.member = lax.axis_index("dp")
        self.tensor = lax.axis_index("tensor")
        self.high = lax.div(self.member, 2)

    def stage(self, mask):
        return min(
            [self.order.index(bit) for bit in self.order if mask >> bit & 1],
            default=len(self.order),
        )

    def steps(self, stage):
        return [mask for mask in self.masks if self.stage(mask) == stage]

    def columns(self, piece):
        return pl.ds(piece * self.piece, self.piece)

    def copy(self, mask, piece):
        index = self.masks.index(mask)
        bit = 1 << self.order[self.stage(mask)]
        return remote(
            self.send.at[index, :, self.columns(piece)],
            self.recv.at[index, :, self.columns(piece)],
            self.send_sem.at[index, piece],
            self.recv_sem.at[index, piece],
            (flip(self.member, bit * 2), self.tensor),
        )

    def settle(self):
        for piece in range(self.pieces):
            columns = self.columns(piece)
            self.kept[:, columns] = self.own(0, flip(self.high, 0), columns)

    def fill(self, mask, piece, out):
        columns = self.columns(piece)
        if self.kept is not None and not mask:
            total = self.kept[:, columns]
        else:
            total = self.own(mask, flip(self.high, mask), columns)
        for bit in self.order[: self.stage(mask)]:
            slot = mask | 1 << bit
            self.copy(slot, piece).wait_recv()
            total += self.recv[self.masks.index(slot), :, columns].astype(WIDE)
        out[:, columns] = total.astype(out.dtype)

    def push_piece(self, mask, piece):
        self.fill(mask, piece, self.send.at[self.masks.index(mask)])
        self.copy(mask, piece).start()

    def push(self, mask):
        for piece in range(self.pieces):
            self.push_piece(mask, piece)

    def end(self, out):
        for piece in range(self.pieces):
            self.fill(0, piece, out)

    def sent(self):
        for mask in self.masks:
            for piece in range(self.pieces):
                self.copy(mask, piece).wait_send()


class Pairwise:
    def __init__(self, moves, refs):
        self.moves, self.done = moves, False
        self.local_sem, self.send_sem, self.recv_sem = refs
        member = lax.axis_index("dp")
        self.partner = (flip(member, 1), lax.axis_index("tensor"))

    @staticmethod
    def sems(count):
        return [DMA((count,)), DMA((count,)), DMA((count,))]

    def local(self, index):
        source, target, _, _ = self.moves[index]
        return pltpu.make_async_copy(source, target, self.local_sem.at[index])

    def across(self, index):
        _, _, source, target = self.moves[index]
        return remote(
            source, target, self.send_sem.at[index], self.recv_sem.at[index], self.partner
        )

    def start(self, index=None):
        for index in range(len(self.moves)) if index is None else [index]:
            self.across(index).start()
            self.local(index).start()

    def ready(self, index=None):
        if index is None and self.done:
            return
        self.done = index is None
        for index in range(len(self.moves)) if index is None else [index]:
            self.local(index).wait()
            self.across(index).wait_recv()

    def sent(self):
        for index in range(len(self.moves)):
            self.across(index).wait_send()


class Lhs(Pairwise):
    @staticmethod
    def scratch(pairs, rows, block):
        return [pltpu.VMEM((pairs, 2 * rows, block), LOW)] + Pairwise.sems(pairs)

    def __init__(self, source, refs):
        self.held = refs[0]
        pairs, rows, block = self.held.shape
        rows = rows // 2
        parity = lax.rem(lax.axis_index("dp"), 2)

        def columns(index):
            if len(source.shape) == 3:
                return source.at[index]
            return source.at[:, pl.ds(pl.multiple_of(index * block, block), block)]

        super().__init__(
            [
                (
                    columns(2 * pair + parity),
                    self.held.at[pair, pl.ds(0, rows)],
                    columns(2 * pair + 1 - parity),
                    self.held.at[pair, pl.ds(rows, rows)],
                )
                for pair in range(pairs)
            ],
            refs[1:],
        )


class Rhs(Pairwise):
    @staticmethod
    def scratch(rows, width):
        return [pltpu.VMEM((2 * rows, width), LOW)] + Pairwise.sems(width // PIECE)

    def __init__(self, sources, refs):
        self.held = refs[0]
        rows = self.held.shape[0] // 2
        moves, at = [], 0
        for source in sources:
            for start in range(0, source.shape[1], PIECE):
                columns = pl.ds(at, PIECE)
                at += PIECE
                here = source.at[:, pl.ds(start, PIECE)]
                moves.append(
                    (
                        here,
                        self.held.at[pl.ds(0, rows), columns],
                        here,
                        self.held.at[pl.ds(rows, rows), columns],
                    )
                )
        super().__init__(moves, refs[1:])


def product_of(lhs, rhs):
    def own(mask, target, columns):
        return dot(lhs.held[target], rhs.held[:, columns], 0, 0)

    return own


def taker(refs):
    refs = list(refs)

    def take(count):
        out = refs[:count]
        del refs[:count]
        return out

    return take


def in_blocks(left, members):
    block = left.shape[1] // members
    if block % 128 == 0:
        return left
    return left.reshape(left.shape[0], members, block).transpose(1, 0, 2)


def member_peers(members):
    member, tensor = lax.axis_index("dp"), lax.axis_index("tensor")
    return [(flip(member, 1 << bit), tensor) for bit in bits_of(members)]


def project_kernel(
    members,
    states,
    w_query,
    w_key,
    w_value,
    cosine,
    sine,
    act,
    query,
    key,
    value,
    keys_all,
    values_all,
    send_sem,
    recv_sem,
    local_sem,
):
    member, tensor = lax.axis_index("dp"), lax.axis_index("tensor")
    width = query.shape[1]
    greet(member_peers(members))
    rows = 64
    for start in range(0, states.shape[0], rows):
        span = pl.ds(start, rows)
        act[span] = norm_rows(states[span])[0].astype(LOW)

    def turned(weight, out):
        linear = dot(act[...], weight[...])
        for start in range(0, width, HEAD):
            out[:, start : start + HEAD] = rotate(
                linear[:, start : start + HEAD], cosine[...], sine[...]
            ).astype(LOW)

    high = [bit for bit in bits_of(members) if bit]
    orders = (high + [0], high[::-1] + [0])
    owns, alls = (key, value), (keys_all, values_all)

    def copy(flow, mask, bit):
        slot = mask | 1 << bit
        place = alls[flow].at[flip(member, mask)]
        return remote(
            place if mask else owns[flow].at[pl.ds(0, PROMPT_DEV)],
            place,
            send_sem.at[flow, slot],
            recv_sem.at[flow, slot],
            (flip(member, 1 << bit), tensor),
        )

    def forward(flow, mask):
        order = orders[flow]
        last = max([order.index(bit) for bit in order if mask >> bit & 1], default=-1)
        for bit in order[last + 1 :]:
            copy(flow, mask, bit).start()

    def came_by(flow, mask):
        order = orders[flow]
        bit = order[max(order.index(bit) for bit in order if mask >> bit & 1)]
        return copy(flow, mask ^ 1 << bit, bit)

    def keep(flow):
        return pltpu.make_async_copy(
            owns[flow].at[pl.ds(0, PROMPT_DEV)], alls[flow].at[member], local_sem.at[flow]
        )

    turned(w_key, key)
    forward(0, 0)
    value[...] = dot(act[...], w_value[...]).astype(LOW)
    forward(1, 0)
    keep(0).start()
    keep(1).start()
    turned(w_query, query)
    masks = range(1, members)
    inner = sorted([mask for mask in masks if not mask & 1], key=lambda mask: mask.bit_count())
    for mask in inner:
        for flow in (0, 1):
            turn = flow if not mask & 2 else flow
            came_by(turn, mask).wait_recv()
            forward(turn, mask)
    for mask in masks:
        if mask & 1:
            for flow in (0, 1):
                came_by(flow, mask).wait_recv()
    for flow in (0, 1):
        keep(flow).wait()
        for mask in masks:
            came_by(flow, mask).wait_send()


def project(members, states, w_query, w_key, w_value, cosine, sine):
    rows, depth = states.shape
    width = w_query.shape[1]
    return pl.pallas_call(
        functools.partial(project_kernel, members),
        out_shape=[
            shape((rows, depth), LOW),
            shape((rows, width), LOW),
            shape((rows, width), LOW),
            shape((rows, width), LOW),
            shape((members, PROMPT_DEV, width), LOW),
            shape((members, PROMPT_DEV, width), LOW),
        ],
        in_specs=[VMEM] * 6,
        out_specs=[VMEM] * 4 + [ANY] * 2,
        scratch_shapes=[DMA((2, members)), DMA((2, members)), DMA((2,))],
        compiler_params=pltpu.CompilerParams(
            collective_id=1, has_side_effects=True, vmem_limit_bytes=VMEM_LIMIT
        ),
        name="project",
    )(states, w_query, w_key, w_value, cosine, sine)


def make_plan(half, group_id, slice_start, cont_group, plan):
    member = lax.axis_index("dp")
    own, other = group_id[member], cont_group[0]
    plan[0] = lax.div(slice_start[member], PROMPT_DEV)

    def step(index, _):
        rank = lax.div(slice_start[index], PROMPT_DEV)

        @pl.when(group_id[index] == own)
        def _():
            plan[1 + rank] = index

        @pl.when(group_id[index] == other)
        def _():
            plan[1 + half + rank] = index

        return 0

    lax.fori_loop(0, 2 * half, step, 0)


def attend_kernel(
    half,
    group_id,
    slice_start,
    cont_group,
    query,
    key,
    value,
    keys_all,
    values_all,
    mixed,
    attended,
    log_total,
    plan,
):
    @pl.when(pl.program_id(0) == 0)
    def _():
        make_plan(half, group_id, slice_start, cont_group, plan)

    def part(start, count, steps, offset):
        span = pl.ds(start, count)
        queries = query[span]
        allowed = lax.broadcasted_iota(jnp.int32, (count, count), 0) >= lax.broadcasted_iota(
            jnp.int32, (count, count), 1
        )
        scores = jnp.where(allowed, dot(queries, key[span], 1, 1) * SCALE, NEGATIVE)
        top = jnp.max(scores, axis=-1, keepdims=True)
        weights = jnp.exp(scores - top)
        total = jnp.sum(weights, axis=-1, keepdims=True)
        result = dot(weights.astype(LOW), value[span])

        def step(index, carry):
            top, total, result = carry
            place = plan[offset + index]
            scores = dot(queries, keys_all[place], 1, 1) * SCALE
            higher = jnp.maximum(top, jnp.max(scores, axis=-1, keepdims=True))
            fade = jnp.exp(top - higher)
            weights = jnp.exp(scores - higher)
            total = total * fade + jnp.sum(weights, axis=-1, keepdims=True)
            result = result * fade + dot(weights.astype(LOW), values_all[place])
            return higher, total, result

        top, total, result = lax.fori_loop(0, steps, step, (top, total, result))
        result = result / total
        mixed[span] = result.astype(LOW)
        attended[span] = result
        log_total[span] = jnp.broadcast_to(top + jnp.log(total), (count, HEAD))

    part(0, PROMPT_DEV, plan[0], 1)
    part(PROMPT_DEV, query.shape[0] - PROMPT_DEV, half, 1 + half)


def attend(readers, query, key, value, keys_all, values_all):
    rows, width = query.shape
    members = keys_all.shape[0]
    head = pl.BlockSpec((rows, HEAD), lambda h, *_: (0, h))
    every = pl.BlockSpec((members, PROMPT_DEV, HEAD), lambda h, *_: (0, 0, h))
    return pl.pallas_call(
        functools.partial(attend_kernel, members // 2),
        out_shape=[
            shape((rows, width), LOW),
            shape((rows, width), WIDE),
            shape((rows, width), WIDE),
        ],
        grid_spec=pltpu.PrefetchScalarGridSpec(
            num_scalar_prefetch=3,
            grid=(width // HEAD,),
            in_specs=[head, head, head, every, every],
            out_specs=[head, head, head],
            scratch_shapes=[pltpu.SMEM((members + 1,), jnp.int32)],
        ),
        compiler_params=pltpu.CompilerParams(vmem_limit_bytes=VMEM_LIMIT),
        name="attend",
    )(*readers, query, key, value, keys_all, values_all)


def attend_back_kernel(
    half,
    group_id,
    slice_start,
    cont_group,
    query,
    key,
    value,
    keys_all,
    values_all,
    branch_low,
    w_out,
    attended,
    log_total,
    cosine,
    sine,
    d_query,
    d_keys_all,
    d_values_all,
    d_key_own,
    d_value_own,
    d_mixed,
    key_total,
    value_total,
    plan,
):
    @pl.when(pl.program_id(0) == 0)
    def _():
        make_plan(half, group_id, slice_start, cont_group, plan)

    d_mixed[...] = dot(branch_low[...], w_out[...], 1, 1).astype(LOW)
    key_total[...] = jnp.zeros_like(key_total)
    value_total[...] = jnp.zeros_like(value_total)

    def part(start, count, steps, offset):
        span = pl.ds(start, count)
        queries, d_attended = query[span], d_mixed[span]
        log_sum = log_total[span][:, :1]
        center = jnp.sum(d_attended.astype(WIDE) * attended[span], axis=-1, keepdims=True)

        def back(scores, keys, values):
            probabilities = jnp.exp(scores - log_sum)
            d_scores = (probabilities * (dot(d_attended, values, 1, 1) - center)).astype(LOW)
            return (
                dot(d_scores, keys),
                dot(d_scores, queries, 0, 0),
                dot(probabilities.astype(LOW), d_attended, 0, 0),
            )

        allowed = lax.broadcasted_iota(jnp.int32, (count, count), 0) >= lax.broadcasted_iota(
            jnp.int32, (count, count), 1
        )
        scores = jnp.where(allowed, dot(queries, key[span], 1, 1) * SCALE, NEGATIVE)
        d_queries, d_own_keys, d_own_values = back(scores, key[span], value[span])

        def step(index, d_queries):
            place = plan[offset + index]
            keys, values = keys_all[place], values_all[place]
            more, d_keys, d_values = back(dot(queries, keys, 1, 1) * SCALE, keys, values)
            key_total[place] += d_keys
            value_total[place] += d_values
            return d_queries + more

        d_queries = lax.fori_loop(0, steps, step, d_queries) * SCALE
        d_query[span] = rotate(d_queries, cosine[span], -sine[span]).astype(LOW)
        return d_own_keys, d_own_values

    member = lax.axis_index("dp")
    d_own_keys, d_own_values = part(0, PROMPT_DEV, plan[0], 1)
    key_total[member] += d_own_keys
    value_total[member] += d_own_values
    d_own_keys, d_own_values = part(PROMPT_DEV, query.shape[0] - PROMPT_DEV, half, 1 + half)
    late = pl.ds(PROMPT_DEV, query.shape[0] - PROMPT_DEV)
    d_key_own[...] = rotate(d_own_keys * SCALE, cosine[late], -sine[late]).astype(LOW)
    d_value_own[...] = d_own_values.astype(LOW)
    d_keys_all[...] = (key_total[...] * SCALE).astype(LOW)
    d_values_all[...] = value_total[...].astype(LOW)


def attend_back(
    readers,
    query,
    key,
    value,
    keys_all,
    values_all,
    branch_low,
    w_out,
    attended,
    log_total,
    cosine,
    sine,
):
    rows, width = query.shape
    members = keys_all.shape[0]
    depth = branch_low.shape[1]
    late = rows - PROMPT_DEV
    heads = width // HEAD
    head = pl.BlockSpec((rows, HEAD), lambda h, *_: (0, h))
    every = pl.BlockSpec((members, PROMPT_DEV, HEAD), lambda h, *_: (0, 0, h))
    own = pl.BlockSpec((late, HEAD), lambda h, *_: (0, h))
    table = pl.BlockSpec((rows, HEAD), lambda h, *_: (0, 0))
    return pl.pallas_call(
        functools.partial(attend_back_kernel, members // 2),
        out_shape=[
            shape((rows, width), LOW),
            shape((members, PROMPT_DEV, width), LOW),
            shape((members, PROMPT_DEV, width), LOW),
            shape((late, width), LOW),
            shape((late, width), LOW),
        ],
        grid_spec=pltpu.PrefetchScalarGridSpec(
            num_scalar_prefetch=3,
            grid=(heads,),
            in_specs=[
                head,
                head,
                head,
                every,
                every,
                pl.BlockSpec((rows, depth), lambda h, *_: (0, 0)),
                pl.BlockSpec((HEAD, depth), lambda h, *_: (h, 0)),
                head,
                head,
                table,
                table,
            ],
            out_specs=[head, every, every, own, own],
            scratch_shapes=[
                pltpu.VMEM((rows, HEAD), LOW),
                pltpu.VMEM((members, PROMPT_DEV, HEAD), WIDE),
                pltpu.VMEM((members, PROMPT_DEV, HEAD), WIDE),
                pltpu.SMEM((members + 1,), jnp.int32),
            ],
        ),
        compiler_params=pltpu.CompilerParams(vmem_limit_bytes=VMEM_LIMIT),
        name="attend_back",
    )(
        *readers,
        query,
        key,
        value,
        keys_all,
        values_all,
        branch_low,
        w_out,
        attended,
        log_total,
        cosine,
        sine,
    )


def place_of(group_id, slice_start, group, rank):
    place = 0
    for index in range(group_id.shape[0]):
        found = (group_id[index] == group) & (slice_start[index] == rank * PROMPT_DEV)
        place = jnp.maximum(place, jnp.where(found, index, 0))
    return place


def own_part(rows):
    return lax.broadcasted_iota(jnp.int32, (rows, rows), 0) >= lax.broadcasted_iota(
        jnp.int32, (rows, rows), 1
    )


def gather_attend_kernel(
    members,
    group_id,
    slice_start,
    cont_group,
    w_query_in,
    w_key_in,
    w_value_in,
    states_in,
    table,
    act,
    query,
    key,
    value,
    cosine,
    sine,
    mixed,
    attended,
    log_total,
    keys_out,
    values_out,
    states,
    weights,
    load_sem,
    weight_sem,
    send_sem,
    recv_sem,
    keep_sem,
    out_sem,
    *every,
):
    member, tensor = lax.axis_index("dp"), lax.axis_index("tensor")
    heads = query.shape[0]
    keys_all, values_all = every[:heads], every[heads:]
    half = members // 2
    rows = states.shape[0]
    chunks = load_sem.shape[0]
    size = rows // chunks
    loads = []
    for index in range(chunks):
        span = pl.ds(index * size, size)
        loads.append(pltpu.make_async_copy(states_in.at[span], states.at[span], load_sem.at[index]))
    w_loads = [
        pltpu.make_async_copy(source, weights.at[index], weight_sem.at[index])
        for index, source in enumerate((w_key_in, w_value_in, w_query_in))
    ]
    for load in loads[:1] + w_loads[:1] + loads[1:] + w_loads[1:]:
        load.start()
    hail(member_peers(members))
    index = lax.broadcasted_iota(jnp.int32, cosine.shape, 0)
    prompt = half * PROMPT_DEV - PROMPT_DEV
    positions = index + jnp.where(index < PROMPT_DEV, slice_start[member], prompt)
    angles = positions.astype(WIDE) * table[:1]
    cosine[...] = jnp.cos(angles)
    sine[...] = jnp.sin(angles) * table[1:2]
    step = 64
    for index in range(chunks):
        loads[index].wait()
        for start in range(index * size, index * size + size, step):
            span = pl.ds(start, step)
            act[span] = norm_rows(states[span])[0].astype(LOW)

    def turned(weight, out):
        linear = dot(act[...], weight)
        for head in range(heads):
            out[head] = rotate(
                linear[:, head * HEAD : head * HEAD + HEAD], cosine[...], sine[...]
            ).astype(LOW)

    high = [bit for bit in bits_of(members) if bit]
    orders = (high + [0], high[::-1] + [0])
    owns, alls = (key, value), (keys_all, values_all)
    early = pl.ds(0, PROMPT_DEV)

    def copy(flow, head, mask, bit):
        slot = mask | 1 << bit
        place = alls[flow][head].at[flip(member, mask)]
        return remote(
            place if mask else owns[flow].at[head, early],
            place,
            send_sem.at[flow, head, slot],
            recv_sem.at[flow, head, slot],
            (flip(member, 1 << bit), tensor),
        )

    def forward(flow, head, mask):
        order = orders[flow]
        last = max([order.index(bit) for bit in order if mask >> bit & 1], default=-1)
        for bit in order[last + 1 :]:
            copy(flow, head, mask, bit).start()

    def came_by(flow, head, mask):
        order = orders[flow]
        bit = order[max(order.index(bit) for bit in order if mask >> bit & 1)]
        return copy(flow, head, mask ^ 1 << bit, bit)

    def keep(flow, head):
        return pltpu.make_async_copy(
            owns[flow].at[head, early], alls[flow][head].at[member], keep_sem.at[flow, head]
        )

    def write(flow, head):
        return pltpu.make_async_copy(
            alls[flow][head], (keys_out, values_out)[flow].at[head], out_sem.at[flow, head]
        )

    masks = range(1, members)
    levels = len(high)

    def own_sends(head):
        if head < heads:
            for flow in (0, 1):
                forward(flow, head, 0)
            for flow in (0, 1):
                keep(flow, head).start()

    def level(head, count):
        if head < heads:
            for mask in masks:
                if not mask & 1 and mask.bit_count() == count:
                    for flow in (0, 1):
                        came_by(flow, head, mask).wait_recv()
                        forward(flow, head, mask)

    def complete(head):
        for flow in (0, 1):
            for mask in masks:
                if mask & 1:
                    came_by(flow, head, mask).wait_recv()
            keep(flow, head).wait()
            write(flow, head).start()

    own_group, other_group = group_id[member], cont_group[0]
    own_start = slice_start[member]
    own_places = [place_of(group_id, slice_start, own_group, rank) for rank in range(half)]
    other_places = [place_of(group_id, slice_start, other_group, rank) for rank in range(half)]
    block = 128

    def attend_rows(head, start, places, whole):
        span = pl.ds(start, block)
        queries = query[head, span]
        scores, values = [], []
        for rank, place in enumerate(places):
            score = dot(queries, keys_all[head][place], 1, 1) * SCALE_TWO
            if not whole:
                at = lax.broadcasted_iota(jnp.int32, score.shape, 0) + (own_start + start)
                to = lax.broadcasted_iota(jnp.int32, score.shape, 1) + rank * PROMPT_DEV
                score = jnp.where(to <= at, score, NEGATIVE)
            scores.append(score)
            values.append(values_all[head][place])
        if whole:
            score = dot(queries, key[head, span], 1, 1) * SCALE_TWO
            scores.append(jnp.where(own_part(block), score, NEGATIVE))
            values.append(value[head, span])
        top = functools.reduce(
            jnp.maximum, [jnp.max(score, axis=-1, keepdims=True) for score in scores]
        )
        total = jnp.zeros_like(top)
        result = jnp.zeros((block, HEAD), WIDE)
        for score, held in zip(scores, values):
            weight = jnp.exp2(score - top)
            total += jnp.sum(weight, axis=-1, keepdims=True)
            result += dot(weight.astype(LOW), held)
        result = result / total
        mixed[span, head * HEAD : head * HEAD + HEAD] = result.astype(LOW)
        attended[head, span] = result
        log_total[head, span] = jnp.broadcast_to(top + jnp.log2(total), (block, HEAD))

    w_loads[0].wait()
    turned(weights[0], key)
    heed(member_peers(members))
    forward(0, 0, 0)
    w_loads[1].wait()
    linear = dot(act[...], weights[1])
    for head in range(heads):
        value[head] = linear[:, head * HEAD : head * HEAD + HEAD].astype(LOW)
    forward(1, 0, 0)
    for flow in (0, 1):
        keep(flow, 0).start()
    own_sends(1)
    w_loads[2].wait()
    turned(weights[2], query)
    level(0, 1)
    own_sends(2)
    for count in range(2, levels + 1):
        level(0, count)
    level(1, 1)
    own_sends(3)
    for head in range(heads):
        complete(head)

        @pl.loop(0, PROMPT_DEV // block)
        def _(index, head=head):
            attend_rows(head, pl.multiple_of(index * block, block), own_places, False)

        for count in range(2, levels + 1):
            level(head + 1, count)
        level(head + 2, 1)
        own_sends(head + 4)
        for start in range(PROMPT_DEV, rows, block):
            attend_rows(head, start, other_places, True)
    for head in range(heads):
        for flow in (0, 1):
            write(flow, head).wait()
            for mask in masks:
                came_by(flow, head, mask).wait_send()


def gather_attend(members, readers, w_query, w_key, w_value, states, table):
    rows, depth = states.shape
    width = w_query.shape[1]
    heads = width // HEAD
    smem = pl.BlockSpec(memory_space=pltpu.SMEM)
    row_heads = (heads, rows, HEAD)
    every = (heads, members, PROMPT_DEV, HEAD)
    return pl.pallas_call(
        functools.partial(gather_attend_kernel, members),
        out_shape=[
            shape((rows, depth), LOW),
            shape(row_heads, LOW),
            shape(row_heads, LOW),
            shape(row_heads, LOW),
            shape((rows, HEAD), WIDE),
            shape((rows, HEAD), WIDE),
            shape((rows, width), LOW),
            shape(row_heads, WIDE),
            shape(row_heads, WIDE),
            shape(every, LOW),
            shape(every, LOW),
        ],
        in_specs=[smem] * 3 + [ANY] * 4 + [VMEM],
        out_specs=[VMEM] * 9 + [ANY] * 2,
        scratch_shapes=[
            pltpu.VMEM((rows, depth), WIDE),
            pltpu.VMEM((3, depth, width), LOW),
            DMA((4,)),
            DMA((3,)),
            DMA((2, heads, members)),
            DMA((2, heads, members)),
            DMA((2, heads)),
            DMA((2, heads)),
        ]
        + [pltpu.VMEM(every[1:], LOW)] * (2 * heads),
        compiler_params=pltpu.CompilerParams(
            collective_id=6, has_side_effects=True, vmem_limit_bytes=VMEM_LIMIT
        ),
        name="gather_attend",
    )(
        *readers,
        w_query,
        w_key,
        w_value,
        states,
        table,
    )


def back_owner_kernel(
    members,
    count,
    group_id,
    slice_start,
    cont_group,
    keys_in,
    values_in,
    query_in,
    key_in,
    value_in,
    attended_in,
    log_total_in,
    branch_low,
    w_out,
    cosine,
    sine,
    own_early,
    own_late,
    d_query,
    d_key,
    d_value,
    early_out,
    late_out,
    query,
    key,
    value,
    attended,
    log_total,
    d_mixed,
    d_queries,
    own_keys,
    own_values,
    other_keys,
    other_values,
    load_sem,
    *refs,
):
    take = taker(refs)
    member = lax.axis_index("dp")
    heads, rows = query.shape[0], query.shape[1]
    keys_all, values_all = take(heads), take(heads)
    out_send, out_recv = take(2)
    here = lax.axis_index("tensor")
    size = own_early.shape[0]
    own_rows = pl.ds(pl.multiple_of(here * size, size), size)
    told = ((own_early, early_out), (own_late, late_out))

    def tell(which, distance):
        source, target = told[which]
        return remote(
            source,
            target.at[own_rows],
            out_send.at[which, distance - 1],
            out_recv.at[which, distance - 1],
            (member, lax.rem(here + distance, count)),
        )

    half = pairs = members // 2
    parity = lax.rem(member, 2)
    order = bits_of(pairs)
    moves, flows, sides = [], [], []
    for way in (order, order[::-1]):
        mine, leaving, theirs = take(3)
        local_free, send_sem, recv_sem = take(3)
        refs_of = take(4)
        sides.append((mine, leaving, theirs, send_sem, recv_sem))
        per_head = []
        for head in range(heads):

            def own(mask, target, columns, mine=mine, theirs=theirs, head=head):
                return mine[head, target, :, columns].astype(WIDE) + theirs[
                    head, target, :, columns
                ].astype(WIDE)

            per_head.append(Halving(pairs, way, own, [ref.at[head] for ref in refs_of]))
        flows.append(per_head)
    partner = (flip(member, 1), lax.axis_index("tensor"))

    sources = (keys_in, values_in, query_in, key_in, value_in, attended_in, log_total_in)

    def load(index, head):
        if index < 2:
            target = (keys_all, values_all)[index][head]
        else:
            target = (query, key, value, attended, log_total)[index - 2].at[head]
        return pltpu.make_async_copy(
            sources[index].at[head], target, load_sem.at[index, head]
        )

    for head in range(heads):
        for index in range(len(sources)):
            load(index, head).start()

    def across(flow, head):
        _, leaving, theirs, send_sem, recv_sem = sides[flow]
        return remote(
            leaving.at[head], theirs.at[head], send_sem.at[head], recv_sem.at[head], partner
        )

    own_group, other_group = group_id[member], cont_group[0]
    own_start = slice_start[member]
    own_places = [place_of(group_id, slice_start, own_group, rank) for rank in range(half)]
    other_places = [place_of(group_id, slice_start, other_group, rank) for rank in range(half)]
    across_line = [(member, lax.rem(here + distance, count)) for distance in range(1, count)]
    hail(member_peers(members) + across_line)
    linear = dot(branch_low[...], w_out[...], 1, 1)
    for head in range(heads):
        d_mixed[head] = linear[:, head * HEAD : head * HEAD + HEAD].astype(LOW)
    heed(member_peers(members) + across_line)
    for which, (source, target) in enumerate(told):
        for distance in range(1, count):
            tell(which, distance).start()
        target[own_rows] = source[...]
    late = rows - PROMPT_DEV

    def back(scores, queries, keys, values, d_attended, log_sum, center):
        probabilities = jnp.exp2(scores - log_sum)
        d_scores = (probabilities * (dot(d_attended, values, 1, 1) - center)).astype(LOW)
        return (
            dot(d_scores, keys),
            dot(d_scores, queries, 0, 0),
            dot(probabilities.astype(LOW), d_attended, 0, 0),
        )

    def rows_of(head, start, count):
        span = pl.ds(start, count)
        d_attended = d_mixed[head, span]
        center = jnp.sum(d_attended.astype(WIDE) * attended[head, span], axis=-1, keepdims=True)
        return query[head, span], d_attended, log_total[head, span][:, :1], center

    def prompt_rank(head, rank):
        queries, d_attended, log_sum, center = rows_of(head, 0, PROMPT_DEV)
        place = own_places[rank]
        keys, values = keys_all[head][place], values_all[head][place]
        scores = dot(queries, keys, 1, 1) * SCALE_TWO
        at = lax.broadcasted_iota(jnp.int32, scores.shape, 0) + own_start
        to = lax.broadcasted_iota(jnp.int32, scores.shape, 1) + rank * PROMPT_DEV
        scores = jnp.where(to <= at, scores, NEGATIVE)
        more, d_keys, d_values = back(
            scores, queries, keys, values, d_attended, log_sum, center
        )
        early = pl.ds(0, PROMPT_DEV)
        if rank:
            d_queries[early] += more
        else:
            d_queries[early] = more
        own_keys[rank] = d_keys
        own_values[rank] = d_values

    def late_part(head):
        queries, d_attended, log_sum, center = rows_of(head, PROMPT_DEV, late)
        span = pl.ds(PROMPT_DEV, late)
        keys, values = key[head, span], value[head, span]
        scores = jnp.where(own_part(late), dot(queries, keys, 1, 1) * SCALE_TWO, NEGATIVE)
        total, d_keys, d_values = back(
            scores, queries, keys, values, d_attended, log_sum, center
        )
        columns = pl.ds(head * HEAD, HEAD)
        d_key[span, columns] = rotate(d_keys * SCALE, cosine[span], -sine[span]).astype(LOW)
        d_value[span, columns] = d_values.astype(LOW)
        for rank in range(half):
            place = other_places[rank]
            keys, values = keys_all[head][place], values_all[head][place]
            more, d_keys, d_values = back(
                dot(queries, keys, 1, 1) * SCALE_TWO, queries, keys, values, d_attended, log_sum, center
            )
            total += more
            other_keys[rank] = d_keys
            other_values[rank] = d_values
        d_queries[span] = total
        d_query[:, columns] = rotate(d_queries[...] * SCALE, cosine[...], -sine[...]).astype(LOW)

    def spread(head, flow):
        a, b, scale = ((own_keys, other_keys, SCALE), (own_values, other_values, 1.0))[flow]
        for pair in range(pairs):
            for away in (0, 1):
                index = 2 * pair + (1 - parity if away else parity)
                rank = lax.div(slice_start[index], PROMPT_DEV)
                mine = jnp.where(group_id[index] == own_group, 1.0, 0.0)
                other = jnp.where(group_id[index] == other_group, 1.0, 0.0)
                total = a[rank] * (mine * scale) + b[rank] * (other * scale)
                sides[flow][away][head, pair] = total.astype(LOW)

    def begin(head):
        for flow in (0, 1):
            spread(head, flow)
            across(flow, head).start()

    def stage(head, index):
        if not 0 <= head < heads:
            return
        for flow in (0, 1):
            if not index:
                across(flow, head).wait_recv()
        for flow in (0, 1):
            for mask in flows[flow][head].steps(index):
                flows[flow][head].push(mask)

    def end(head):
        if not 0 <= head < heads:
            return
        early = pl.ds(0, PROMPT_DEV)
        columns = pl.ds(head * HEAD, HEAD)
        total = d_queries.at[early]
        flows[0][head].end(total)
        d_key[early, columns] = rotate(total[...], cosine[early], -sine[early]).astype(LOW)
        flows[1][head].end(d_value.at[early, columns])

    depth = len(order)
    for head in range(heads):
        for index in range(len(sources)):
            load(index, head).wait()
        for rank in range(half):
            prompt_rank(head, rank)
            if rank == 0:
                stage(head - 1, 0)
            if rank == half - 1:
                for index in range(1, depth):
                    stage(head - 1, index)
        late_part(head)
        begin(head)
        end(head - 1)
    for index in range(depth):
        stage(heads - 1, index)
    end(heads - 1)
    for flow in (0, 1):
        for head in range(heads):
            across(flow, head).wait_send()
            flows[flow][head].sent()
    for which in range(len(told)):
        for distance in range(1, count):
            tell(which, distance).wait()


def back_owner(
    members,
    count,
    readers,
    keys_all,
    values_all,
    query,
    key,
    value,
    branch_low,
    w_out,
    attended,
    log_total,
    cosine,
    sine,
    own_early,
    own_late,
):
    heads, rows, _ = query.shape
    width = heads * HEAD
    pairs = members // 2
    smem = pl.BlockSpec(memory_space=pltpu.SMEM)
    every = pltpu.VMEM((members, PROMPT_DEV, HEAD), LOW)
    side = pltpu.VMEM((heads, pairs, PROMPT_DEV, HEAD), LOW)
    step = pltpu.VMEM((heads, pairs - 1, PROMPT_DEV, HEAD), LOW)
    flow = [side] * 3 + [DMA((heads,))] * 3 + [step] * 2 + [DMA((heads, pairs - 1, 1))] * 2
    total = pltpu.VMEM((pairs, PROMPT_DEV, HEAD), WIDE)
    return pl.pallas_call(
        functools.partial(back_owner_kernel, members, count),
        out_shape=[shape((rows, width), LOW)] * 3
        + [shape((count * own_early.shape[0], own_early.shape[1]), LOW)] * 2,
        in_specs=[smem] * 3 + [ANY] * 7 + [VMEM] * 6,
        out_specs=[VMEM] * 5,
        scratch_shapes=[
            pltpu.VMEM((heads, rows, HEAD), LOW),
            pltpu.VMEM((heads, rows, HEAD), LOW),
            pltpu.VMEM((heads, rows, HEAD), LOW),
            pltpu.VMEM((heads, rows, HEAD), WIDE),
            pltpu.VMEM((heads, rows, HEAD), WIDE),
            pltpu.VMEM((heads, rows, HEAD), LOW),
            pltpu.VMEM((rows, HEAD), WIDE),
            total,
            total,
            total,
            total,
            DMA((7, heads)),
        ]
        + [every] * (2 * heads)
        + [DMA((2, count - 1))] * 2
        + flow * 2,
        compiler_params=pltpu.CompilerParams(
            collective_id=7, has_side_effects=True, vmem_limit_bytes=VMEM_LIMIT
        ),
        name="back_owner",
    )(
        *readers,
        keys_all,
        values_all,
        query,
        key,
        value,
        attended,
        log_total,
        branch_low,
        w_out,
        cosine,
        sine,
        own_early,
        own_late,
    )


def middle_kernel(
    count,
    mixed,
    w_out,
    states,
    cotangent_in,
    w_gate_in,
    w_up_in,
    w_down_in,
    act,
    resid,
    own_early,
    out_low_out,
    ffn_late,
    d_act_out,
    hidden_out,
    d_gate_out,
    d_up_out,
    part,
    cotangent,
    out_low,
    d_hidden,
    w_gate,
    w_up,
    w_down,
    rows_in,
    ffn_total,
    d_total,
    ffn,
    hidden,
    d_gate,
    d_up,
    state_sem,
    cot_sem,
    weight_sem,
    out_sem,
    *refs,
):
    line = Line(count, refs[: Line.scratch_count])
    out_line = Line(count, refs[Line.scratch_count :])
    rows, size = resid.shape[0], line.rows
    fetch = pltpu.make_async_copy(
        states.at[pl.ds(pl.multiple_of(line.here * rows, rows), rows)], resid, state_sem
    )
    slots, step, _ = cotangent.shape

    def cot_load(index):
        return pltpu.make_async_copy(
            cotangent_in.at[pl.ds(index * step, step)],
            cotangent.at[index % slots],
            cot_sem.at[index % slots],
        )

    down_load, gate_load, up_load = [
        pltpu.make_async_copy(source, target, weight_sem.at[index])
        for index, (source, target) in enumerate(
            ((w_down_in, w_down), (w_gate_in, w_gate), (w_up_in, w_up))
        )
    ]
    fetch.start()
    for index in range(slots):
        cot_load(index).start()
    hail(line.peers())
    tile = 512
    for start in range(0, part.shape[1], tile):
        columns = pl.ds(start, tile)
        part[:, columns] = dot(mixed[...], w_out[:, columns]).astype(LOW)
    heed(line.peers())
    fetch.wait()

    def finish(group):
        span = pl.ds(group * size, size)
        resid[span] += line.total[...]
        act[line.span(group, line.here)] = norm_rows(resid[span])[0].astype(LOW)

    leaving = []

    def leave(source, target):
        copy = pltpu.make_async_copy(source, target, out_sem.at[len(leaving)])
        copy.start()
        leaving.append(copy)

    def cast():
        steps = out_low.shape[0] // step
        for index in range(steps):
            cot_load(index).wait()
            out_low[pl.ds(index * step, step)] = cotangent[index % slots].astype(LOW)
            if index + slots < steps:
                cot_load(index + slots).start()
            if index + slots == steps:
                for load in (down_load, gate_load, up_load):
                    load.start()
        leave(out_low, out_low_out)

    def inner(start):
        span = pl.ds(start, tile)
        d_hidden[:, span] = dot(out_low[...], w_down[span], 1, 1).astype(LOW)

    units, block = d_hidden.shape[1], 512
    starts = list(range(0, units, tile))

    def inners(some):
        def run():
            if some[0] == 0:
                down_load.wait()
            for start in some:
                inner(start)

        return run

    def begin(group):
        if not group:
            gate_load.wait()
            up_load.wait()
        for chunk in range(count):
            rows_in[pl.ds(chunk * size, size)] = act[line.span(group, chunk)]
        ffn_total[...] = jnp.zeros_like(ffn_total)
        d_total[...] = jnp.zeros_like(d_total)

    def feed(group, first, last):
        @pl.loop(first, last)
        def _(index):
            columns = pl.ds(pl.multiple_of(index * block, block), block)
            gate = dot(rows_in[...], w_gate[:, columns])
            up = dot(rows_in[...], w_up[:, columns])
            sigmoid = jax.nn.sigmoid(gate)
            swish = gate * sigmoid
            d_inner = jnp.concatenate(
                [d_hidden[line.span(group, chunk), columns] for chunk in range(count)]
            ).astype(WIDE)
            new_hidden = (swish * up).astype(LOW)
            new_gate = (d_inner * up * sigmoid * (1.0 + gate * (1.0 - sigmoid))).astype(LOW)
            new_up = (d_inner * swish).astype(LOW)
            for chunk in range(count):
                own = slice(chunk * size, chunk * size + size)
                hidden[chunk, group, :, columns] = new_hidden[own]
                d_gate[chunk, group, :, columns] = new_gate[own]
                d_up[chunk, group, :, columns] = new_up[own]
            for start in range(0, part.shape[1], tile):
                out = pl.ds(start, tile)
                ffn_total[:, out] += dot(new_hidden, w_down[columns, out])
                d_total[:, out] += dot(new_gate, w_gate[out, columns], 1, 1) + dot(
                    new_up, w_up[out, columns], 1, 1
                )

    def end(group):
        own = pl.ds(pl.multiple_of(line.here * size, size), size)
        ffn_total[own] += resid[pl.ds(group * size, size)]
        ffn[group] = ffn_total[...].astype(LOW)
        if group:
            leave(ffn.at[group], ffn_late)
        for chunk in range(count):
            span = line.span(group, chunk)
            part[span] = d_total[pl.ds(chunk * size, size)].astype(LOW)
            leave(part.at[span], d_act_out.at[span])
        for source, target in (
            (hidden, hidden_out),
            (d_gate, d_gate_out),
            (d_up, d_up_out),
        ):
            leave(source.at[:, group], target.at[:, group])

    blocks = units // block
    third = -(-blocks // 3)

    def opening():
        begin(0)
        feed(0, 0, third)

    def closing():
        feed(0, 2 * third, blocks)
        end(0)

    line.reduce(
        part,
        act,
        finish,
        [
            cast,
            inners(starts[:1]),
            inners(starts[1:2]),
            inners(starts[2:]),
            opening,
            lambda: feed(0, third, 2 * third),
            closing,
        ],
    )
    early = ffn.at[0]
    out_line.scatter_slot(0, 0, early)
    begin(1)
    feed(1, 0, third)
    out_line.scatter_slot(0, 1, early)
    feed(1, third, 2 * third)
    for slot in range(2, count - 1):
        out_line.scatter_slot(0, slot, early)
    feed(1, 2 * third, blocks)
    end(1)
    out_line.scatter_end(0, early)
    own_early[...] = out_line.total[...].astype(LOW)
    for copy in leaving:
        copy.wait()
    line.sent(act)
    out_line.sent()


def middle(count, mixed, w_out, states, cotangent, w_gate, w_up, w_down):
    rows, depth = states.shape
    units = w_down.shape[0]
    size = rows // count // GROUPS
    split = (count, GROUPS, size)
    inside = (*split, units)
    some = (GROUPS, rows // GROUPS, depth)
    outs = pl.pallas_call(
        functools.partial(middle_kernel, count),
        out_shape=[
            shape((rows, depth), LOW),
            shape((rows // count, depth), WIDE),
            shape((size, depth), LOW),
            shape((rows, depth), LOW),
            shape(some[1:], LOW),
            shape((rows, depth), LOW),
            shape(inside, LOW),
            shape(inside, LOW),
            shape(inside, LOW),
        ],
        in_specs=[VMEM] * 2 + [ANY] * 5,
        out_specs=[VMEM] * 3 + [ANY] * 6,
        scratch_shapes=[
            pltpu.VMEM((rows, depth), LOW),
            pltpu.VMEM((2, 64, depth), WIDE),
            pltpu.VMEM((rows, depth), LOW),
            pltpu.VMEM((rows, units), LOW),
            pltpu.VMEM((depth, units), LOW),
            pltpu.VMEM((depth, units), LOW),
            pltpu.VMEM((units, depth), LOW),
            pltpu.VMEM(some[1:], LOW),
            pltpu.VMEM(some[1:], WIDE),
            pltpu.VMEM(some[1:], WIDE),
            pltpu.VMEM(some, LOW),
            pltpu.VMEM(inside, LOW),
            pltpu.VMEM(inside, LOW),
            pltpu.VMEM(inside, LOW),
            DMA,
            DMA((2,)),
            DMA((3,)),
            DMA(((4 + count) * GROUPS,)),
        ]
        + Line.scratch(count, GROUPS, rows // count, depth)
        + Line.scratch(count, 1, size, depth),
        compiler_params=pltpu.CompilerParams(
            collective_id=2, has_side_effects=True, vmem_limit_bytes=VMEM_LIMIT
        ),
        name="middle",
    )(mixed, w_out, states, cotangent, w_gate, w_up, w_down)
    return [*outs[:6], *(out.reshape(rows, -1) for out in outs[6:])]


def second_kernel(
    count,
    pairs,
    d_act_in,
    ffn_in,
    resid_in,
    cotangent,
    act,
    d_gate,
    d_up,
    branch_low,
    grad_resid,
    own_out,
    grad_gate,
    grad_up,
    d_act,
    ffn,
    resid,
    cot_sem,
    load_sem,
    *refs,
):
    take = taker(refs)
    line = Line(count, take(Line.scratch_count))
    out_line = Line(count, take(Line.scratch_count))
    lhs = Lhs(act, take(4))
    rights = [Rhs([source], take(4)) for source in (d_gate, d_up)]
    order = bits_of(pairs)
    flows = [
        Halving(pairs, way, product_of(lhs, right), take(4), *take(1))
        for way, right in zip((order, order[::-1]), rights)
    ]
    rows = resid.shape[0]
    fetch = pltpu.make_async_copy(
        cotangent.at[pl.ds(pl.multiple_of(line.here * rows, rows), rows)], grad_resid, cot_sem
    )
    peers = line.peers() + member_peers(2 * pairs)
    hail(peers)
    loads = [
        pltpu.make_async_copy(source, target, load_sem.at[index])
        for index, (source, target) in enumerate(
            ((d_act_in, d_act), (ffn_in, ffn), (resid_in, resid))
        )
    ]
    fetch.start()
    for load in loads:
        load.start()
    heed(peers)
    lhs.start()
    for piece in range(flows[0].pieces):
        for right in rights:
            right.start(piece)
    fetch.wait()
    for load in loads:
        load.wait()

    def finish(group):
        span = pl.ds(group * line.rows, line.rows)
        normed, inverse = norm_rows(resid[span])
        grad_resid[span] += norm_back(line.total[...], normed, inverse)
        branch_low[line.span(group, line.here)] = grad_resid[span].astype(LOW)

    sides = [(lhs, right, flow) for right, flow in zip(rights, flows)]
    ahead, early, others, settle, late = beside(order, sides)

    def out_slot(slot):
        return lambda: out_line.scatter_slot(0, slot, ffn)

    slots = [out_slot(slot) for slot in range(count - 1)]

    def fourth():
        settle()
        slots[0]()

    line.reduce(d_act, branch_low, finish, [ahead, early, others, fourth, late] + slots[1:])
    out_line.scatter_end(0, ffn)
    own_out[...] = out_line.total[...].astype(LOW)
    flows[0].end(grad_gate)
    flows[1].end(grad_up)
    for flow in flows:
        flow.sent()
    for move in [lhs] + rights:
        move.sent()
    line.sent(branch_low)
    out_line.sent()


def beside(order, sides):
    masks = [flow.steps(0) for _, _, flow in sides]

    def ahead():
        for (lhs, rhs, flow), (mask, *_) in zip(sides[:2], masks):
            lhs.ready()
            rhs.ready(0)
            flow.push_piece(mask, 0)

    def early():
        for at, ((lhs, rhs, flow), (mask, *_)) in enumerate(zip(sides, masks)):
            if at > 1:
                lhs.ready()
            for piece in range(0 if at > 1 else 1, flow.pieces):
                rhs.ready(piece)
                flow.push_piece(mask, piece)

    def others():
        for index in range(1, len(masks[0])):
            for (_, _, flow), steps in zip(sides, masks):
                flow.push(steps[index])

    def settle():
        for _, _, flow in sides:
            flow.settle()

    def late():
        for stage in range(1, len(order)):
            for index in range(len(sides[0][2].steps(stage))):
                for _, _, flow in sides:
                    flow.push(flow.steps(stage)[index])

    return [ahead, early, others, settle, late]


def second(count, members, d_act, ffn, resid, cotangent, act, d_gate, d_up):
    rows, depth = cotangent.shape
    units = d_gate.shape[1]
    pairs = members // 2
    block = depth // members
    return pl.pallas_call(
        functools.partial(second_kernel, count, pairs),
        out_shape=[
            shape((rows, depth), LOW),
            shape((rows // count, depth), WIDE),
            shape((ffn.shape[0] // count, depth), LOW),
            shape((block, units), LOW),
            shape((block, units), LOW),
        ],
        in_specs=[ANY] * 7,
        out_specs=[VMEM] * 5,
        scratch_shapes=[
            pltpu.VMEM(d_act.shape, LOW),
            pltpu.VMEM(ffn.shape, LOW),
            pltpu.VMEM(resid.shape, WIDE),
            DMA,
            DMA((3,)),
        ]
        + Line.scratch(count, GROUPS, rows // count, depth)
        + Line.scratch(count, 1, ffn.shape[0] // count, depth)
        + Lhs.scratch(pairs, rows, block)
        + Rhs.scratch(rows, units) * 2
        + (Halving.scratch(pairs, block, units) + [pltpu.VMEM((block, units), WIDE)]) * 2,
        compiler_params=pltpu.CompilerParams(
            collective_id=3, has_side_effects=True, vmem_limit_bytes=VMEM_LIMIT
        ),
        name="second",
    )(d_act, ffn, resid, cotangent, in_blocks(act, members), d_gate, d_up)


def owner_kernel(
    pairs,
    d_keys_all,
    d_values_all,
    d_key_own,
    d_value_own,
    cosine,
    sine,
    d_key,
    d_value,
    *refs,
):
    take = taker(refs)
    parity = lax.rem(lax.axis_index("dp"), 2)
    order = bits_of(pairs)
    width = d_key.shape[1]
    moves, flows = [], []
    for way, source in zip((order, order[::-1]), (d_keys_all, d_values_all)):
        mine, theirs = take(2)
        moves.append(
            Pairwise(
                [
                    (
                        source.at[2 * pair + parity],
                        mine.at[pair],
                        source.at[2 * pair + 1 - parity],
                        theirs.at[pair],
                    )
                    for pair in range(pairs)
                ],
                take(3),
            )
        )

        def own(mask, target, columns, mine=mine, theirs=theirs):
            return mine[target, :, columns].astype(WIDE) + theirs[target, :, columns].astype(WIDE)

        flows.append(Halving(pairs, way, own, take(4)))
    (total,) = take(1)
    greet(member_peers(2 * pairs))
    for move in moves:
        move.start()
    for move, flow in zip(moves, flows):
        move.ready()
        flow.push(flow.masks[0])
    late = pl.ds(PROMPT_DEV, d_key.shape[0] - PROMPT_DEV)
    d_key[late] = d_key_own[...]
    d_value[late] = d_value_own[...]
    for index in range(1, pairs - 1):
        for flow in flows:
            flow.push(flow.masks[index])
    early = pl.ds(0, PROMPT_DEV)
    flows[0].end(total)
    for start in range(0, width, HEAD):
        d_key[early, start : start + HEAD] = rotate(
            total[:, start : start + HEAD], cosine[early], -sine[early]
        ).astype(LOW)
    flows[1].end(d_value.at[early])
    for move, flow in zip(moves, flows):
        flow.sent()
        move.sent()


def owner(members, d_keys_all, d_values_all, d_key_own, d_value_own, cosine, sine):
    width = d_key_own.shape[1]
    rows = cosine.shape[0]
    pairs = members // 2
    flow = (
        [pltpu.VMEM((pairs, PROMPT_DEV, width), LOW)] * 2
        + Pairwise.sems(pairs)
        + Halving.scratch(pairs, PROMPT_DEV, width)
    )
    return pl.pallas_call(
        functools.partial(owner_kernel, pairs),
        out_shape=[shape((rows, width), LOW)] * 2,
        in_specs=[ANY, ANY] + [VMEM] * 4,
        out_specs=[VMEM] * 2,
        scratch_shapes=flow * 2 + [pltpu.VMEM((PROMPT_DEV, width), WIDE)],
        compiler_params=pltpu.CompilerParams(
            collective_id=4, has_side_effects=True, vmem_limit_bytes=VMEM_LIMIT
        ),
        name="owner",
    )(d_keys_all, d_values_all, d_key_own, d_value_own, cosine, sine)


def first_kernel(
    count,
    pairs,
    grad_resid,
    d_query,
    d_key,
    d_value,
    w_query,
    w_key,
    w_value,
    states,
    act,
    mixed,
    branch_low,
    hidden,
    out_low,
    far_query,
    far_key,
    far_value,
    input_grad,
    grad_down,
    grad_out,
    grad_query,
    grad_key,
    grad_value,
    inner_total,
    part,
    state,
    weight,
    state_sem,
    weight_sem,
    *refs,
):
    take = taker(refs)
    line = Line(count, take(Line.scratch_count))
    order = bits_of(pairs)
    sides = []
    for left, rights, way in (
        (out_low, (hidden,), order),
        (act, (far_query, far_key, far_value), order[::-1]),
        (branch_low, (mixed,), order[::-1]),
    ):
        lhs, rhs = Lhs(left, take(4)), Rhs(rights, take(4))
        sides.append((lhs, rhs, Halving(pairs, way, product_of(lhs, rhs), take(4), *take(1))))
    rows = state.shape[0]
    fetch = pltpu.make_async_copy(
        states.at[pl.ds(pl.multiple_of(line.here * rows, rows), rows)], state, state_sem
    )
    loads = [
        pltpu.make_async_copy(source, weight.at[index], weight_sem.at[index])
        for index, source in enumerate((w_query, w_key, w_value))
    ]
    for load in loads:
        load.start()
    fetch.start()
    greet(line.peers() + member_peers(2 * pairs))
    for lhs, rhs, _ in sides[:2]:
        lhs.start()
        rhs.start(0)
    for at, (lhs, rhs, flow) in enumerate(sides):
        if at > 1:
            lhs.start()
        for piece in range(0 if at > 1 else 1, flow.pieces):
            rhs.start(piece)
    for load in loads:
        load.wait()
    tile = 512
    for start in range(0, part.shape[1], tile):
        columns = pl.ds(start, tile)
        part[:, columns] = (
            dot(d_query[...], weight[0, columns], 1, 1)
            + dot(d_key[...], weight[1, columns], 1, 1)
            + dot(d_value[...], weight[2, columns], 1, 1)
        )
    fetch.wait()

    def finish(group):
        span = pl.ds(group * line.rows, line.rows)
        normed, inverse = norm_rows(state[span])
        input_grad[line.span(group, line.here)] = (
            grad_resid[span] + norm_back(line.total[...], normed, inverse)
        ).astype(LOW)

    line.reduce(part, input_grad, finish, beside(order, sides))
    for (_, _, flow), target in zip(sides, (grad_down, inner_total, grad_out)):
        flow.end(target)
    width = grad_query.shape[1]
    for index, target in enumerate((grad_query, grad_key, grad_value)):
        target[...] = inner_total[:, index * width : index * width + width]
    for lhs, rhs, flow in sides:
        flow.sent()
        lhs.sent()
        rhs.sent()
    line.sent(input_grad)


def first(
    count,
    members,
    grad_resid,
    weights,
    states,
    act,
    mixed,
    branch_low,
    hidden,
    out_low,
    d_query,
    d_key,
    d_value,
):
    rows, depth = states.shape
    width = d_query.shape[1]
    units = hidden.shape[1]
    pairs = members // 2
    block = depth // members
    scratch = []
    for wide in (units, 3 * width, width):
        scratch += Lhs.scratch(pairs, rows, block) + Rhs.scratch(rows, wide)
        scratch += Halving.scratch(pairs, block, wide) + [pltpu.VMEM((block, wide), WIDE)]
    return pl.pallas_call(
        functools.partial(first_kernel, count, pairs),
        out_shape=[
            shape((rows, depth), LOW),
            shape((block, units), LOW),
        ]
        + [shape((block, width), LOW)] * 4,
        in_specs=[VMEM] * 4 + [ANY] * 12,
        out_specs=[VMEM] * 6,
        scratch_shapes=[
            pltpu.VMEM((block, 3 * width), LOW),
            pltpu.VMEM((rows, depth), WIDE),
            pltpu.VMEM((rows // count, depth), WIDE),
            pltpu.VMEM((3, depth, width), LOW),
            DMA,
            DMA((3,)),
        ]
        + Line.scratch(count, GROUPS, rows // count, depth)
        + scratch,
        compiler_params=pltpu.CompilerParams(
            collective_id=5, has_side_effects=True, vmem_limit_bytes=VMEM_LIMIT
        ),
        name="first",
    )(
        grad_resid,
        d_query,
        d_key,
        d_value,
        *weights,
        states,
        in_blocks(act, members),
        mixed,
        in_blocks(branch_low, members),
        hidden,
        in_blocks(out_low, members),
        d_query,
        d_key,
        d_value,
    )


def widen_kernel(flat, early, late, *refs):
    count = len(refs) // 2
    sources, whole, targets = refs[:count], refs[count], refs[count + 1 :]
    half = early.shape[0]
    whole[pl.ds(0, half)] = early[...].astype(WIDE)
    whole[pl.ds(half, half)] = late[...].astype(WIDE)
    for index, (source, target) in enumerate(zip(sources, targets)):
        values = source[...].astype(WIDE)
        target[...] = values if index < flat else values.T


def widen(count, early, late, plain, turned):
    def rows(array):
        return pl.BlockSpec((array.shape[0] // count, array.shape[1]), lambda i: (i, 0))

    def columns(array):
        return pl.BlockSpec((array.shape[0], array.shape[1] // count), lambda i: (0, i))

    flipped = [shape(array.shape[::-1], WIDE) for array in turned]
    whole = shape((2 * early.shape[0], early.shape[1]), WIDE)
    return pl.pallas_call(
        functools.partial(widen_kernel, len(plain)),
        out_shape=[whole] + [shape(array.shape, WIDE) for array in plain] + flipped,
        grid=(count,),
        in_specs=[rows(array) for array in (early, late, *plain)]
        + [columns(array) for array in turned],
        out_specs=[rows(array) for array in (whole, *plain, *flipped)],
        compiler_params=pltpu.CompilerParams(vmem_limit_bytes=VMEM_LIMIT),
        name="widen",
    )(early, late, *plain, *turned)


def body(
    states,
    w_query,
    w_key,
    w_value,
    w_out,
    w_gate,
    w_up,
    w_down,
    group_id,
    slice_start,
    cont_group,
    cotangent,
):
    rows = states.shape[0]
    members = lax.axis_size("dp")
    count = lax.axis_size("tensor")
    frequency = 10000.0 ** (-np.arange(HEAD // 2) * 2.0 / HEAD)
    frequency = np.concatenate([frequency, frequency]).astype(np.float32)
    sign = np.repeat([-1.0, 1.0], HEAD // 2).astype(np.float32)
    readers = (group_id, slice_start, cont_group)
    merged = members * PROMPT_DEV * w_query.shape[1] * 2 * 4 <= 16 * 2**20
    if merged:
        table = jnp.stack([frequency, sign])
        act_one, query, key, value, cosine, sine, mixed, attended, log_total, *everyones = (
            gather_attend(members, readers, w_query, w_key, w_value, states, table)
        )
    else:
        index = jnp.arange(rows, dtype=jnp.int32)
        everyone = jnp.arange(members, dtype=jnp.int32)
        own_start = jnp.sum(jnp.where(everyone == lax.axis_index("dp"), slice_start, 0))
        prompt = members // 2 * PROMPT_DEV
        positions = jnp.where(index < PROMPT_DEV, own_start + index, prompt + index - PROMPT_DEV)
        angles = positions.astype(WIDE)[:, None] * frequency[None, :]
        cosine = jnp.cos(angles)
        sine = jnp.sin(angles) * sign[None, :]
        act_one, query, key, value, *everyones = project(
            members, states, w_query, w_key, w_value, cosine, sine
        )
        mixed, attended, log_total = attend(readers, query, key, value, *everyones)
    act_two, resid, own_early, out_low, ffn_late, d_act_two, hidden, d_gate, d_up = middle(
        count, mixed, w_out, states, cotangent, w_gate, w_up, w_down
    )
    branch_low, grad_resid, own_late, grad_gate, grad_up = second(
        count, members, d_act_two, ffn_late, resid, cotangent, act_two, d_gate, d_up
    )
    kept = (query, key, value, branch_low, w_out, attended, log_total, cosine, sine)
    if merged:
        d_query, d_key, d_value, early_out, late_out = back_owner(
            members, count, readers, *everyones, *kept, own_early, own_late
        )
    else:
        d_query, *d_everyones = attend_back(
            readers, query, key, value, *everyones, branch_low, w_out, attended, log_total, cosine, sine
        )
        d_key, d_value = owner(members, *d_everyones, cosine, sine)
        early_out, late_out = [
            lax.all_gather(own, "tensor", axis=0, tiled=True) for own in (own_early, own_late)
        ]
    input_grad, grad_down, grad_out, *grad_inner = first(
        count,
        members,
        grad_resid,
        (w_query, w_key, w_value),
        states,
        act_one,
        mixed,
        branch_low,
        hidden,
        out_low,
        d_query,
        d_key,
        d_value,
    )
    *plain, grad_out, grad_down = widen(
        count,
        early_out,
        late_out,
        (input_grad, *grad_inner, grad_gate, grad_up),
        (grad_out, grad_down),
    )
    return (*plain[:5], grad_out, *plain[5:], grad_down)


def solution(mesh):
    placed = (
        P("dp", None),
        P(None, "tensor"),
        P(None, "tensor"),
        P(None, "tensor"),
        P("tensor", None),
        P(None, "tensor"),
        P(None, "tensor"),
        P("tensor", None),
        P(),
        P(),
        P("dp"),
        P("dp", None),
    )
    return jax.shard_map(
        body,
        mesh=mesh,
        in_specs=placed,
        out_specs=(
            P("dp", None),
            P("dp", None),
            P("dp", "tensor"),
            P("dp", "tensor"),
            P("dp", "tensor"),
            P("tensor", "dp"),
            P("dp", "tensor"),
            P("dp", "tensor"),
            P("tensor", "dp"),
        ),
        check_vma=False,
    )
```
